32 devices in a mesh: batch: 8 (over y, x, core), seq: 4 (over z).
Axes of the slice: x: 2, y: 2, z: 4, core: 2. Of those that a mesh axis runs over, the one named last changes fastest.
Arguments:
- byte_values: int32 [16, 2048], P('batch', 'seq'), may hold values from 0 to 258
- segments: int32 [16, 2048], P('batch'), may hold values from 0 to 3, as said below
- byte_mask: int32 [16, 2048], P('batch', 'seq'), may hold values from 0 to 1, as said below
- embedding: bfloat16 [259, 768], replicated, may hold values from -6 to 6
- filter_weight: float32 [4, 768], replicated, may hold values from -3 to 3
- score_weight: float32 [768], replicated, may hold values from -0.4375 to 0.4375
- first_gain: float32 [768], replicated, may hold values from 0.1 to 1.9
- query_weight: bfloat16 [768, 768], replicated, may hold values from -0.109375 to 0.109375
- key_weight: bfloat16 [768, 768], replicated, may hold values from -0.109375 to 0.109375
- value_weight: bfloat16 [768, 768], replicated, may hold values from -0.21875 to 0.21875
- merge_weight: bfloat16 [768, 768], replicated, may hold values from -0.875 to 0.875
- position_bias: float32 [32, 12], replicated, may hold values from -4 to 4
- second_gain: float32 [768], replicated, may hold values from 0.1 to 1.9
- gate_weight: bfloat16 [768, 2048], replicated, may hold values from -0.21875 to 0.21875
- up_weight: bfloat16 [768, 2048], replicated, may hold values from -0.21875 to 0.21875
- down_weight: bfloat16 [2048, 768], replicated, may hold values from -0.125 to 0.125
- cotangent: bfloat16 [16, 1024, 768], P('batch', 'seq'), may hold values from -6 to 6
Outputs:
- layer_output: bfloat16 [16, 1024, 768], P('batch', 'seq')
- embed_grad: float32 [259, 768], replicated
- filter_grad: float32 [4, 768], replicated
- score_grad: float32 [768], replicated
- first_grad: float32 [768], replicated
- query_grad: float32 [768, 768], P('batch', 'seq')
- key_grad: float32 [768, 768], P('batch', 'seq')
- value_grad: float32 [768, 768], P('batch', 'seq')
- merge_grad: float32 [768, 768], P('batch', 'seq')
- bias_grad: float32 [32, 12], replicated
- second_grad: float32 [768], replicated
- gate_grad: float32 [768, 2048], P('batch', 'seq')
- up_grad: float32 [768, 2048], P('batch', 'seq')
- down_grad: float32 [2048, 768], P('batch', 'seq')
The draws below stay inside these ranges and needn't reach their ends.
Inputs may be any that keep to these rules, and one draw needn't show every extreme that they name: Within a row the numbers never fall. Each row has segments 0, 1, 2, 3 in order: segment 1 runs from a byte below 129 to a byte at or beyond 2048 - 512 // 2, segment 3 holds exactly the bytes whose byte_mask is 0. `byte_mask`: 0 exactly on a tail of each row of 1 to 128 bytes.
All inputs are finite; a program needn't handle non-finite values.
Results may differ from the reference program's by a relative error of at most 0.02.
Values may be sent and summed in bfloat16 or wider, within the bound.
No kernel may reach another device: no remote copies, remote signals or barrier semaphores. Data moves between devices by JAX's collectives and lax.ppermute only.
A program may use at most 320 MiB of HBM per device.

```python
import math
import jax
import jax.numpy as jnp
import numpy as np
from jax import lax

D = 768
H = 12
DH = 64
FF = 2048
VOCAB = 259
BUCKETS = 32
ROW = 2048
ROWS = 16
BYTE_DEV = 512
LTOK = 1024


def row_bounds(key):
    quarter = BYTE_DEV // 4
    pieces = jax.random.split(key, 3)
    start = jax.random.randint(pieces[0], (ROWS, 1), 1, quarter + 1)
    tail = jax.random.randint(pieces[1], (ROWS, 1), 1, quarter + 1)
    padding = jax.random.randint(pieces[2], (ROWS, 1), 1, quarter + 1)
    place = jnp.arange(ROW).astype(jnp.int32)[None, :]
    used = ROW - padding
    return (place, start, used - tail, used)


def draw_segments(key, part):
    place, start, finish, used = row_bounds(key)
    first = (place >= start).astype(jnp.int32)
    second = (place >= finish).astype(jnp.int32)
    third = (place >= used).astype(jnp.int32)
    return first + second + third


def draw_byte_mask(key, part):
    place, start, finish, used = row_bounds(key)
    return (place < used).astype(jnp.int32)


def touch_ends(values, stream_key, smallest, top_value):
    spot = [jax.random.randint(jax.random.fold_in(stream_key, axis), (), 0, length) for axis, length in enumerate(values.shape)]
    main_axis = values.shape.index(max(values.shape))
    beside = spot[:main_axis] + [(spot[main_axis] + 1) % values.shape[main_axis]] + spot[main_axis + 1:]
    return values.at[tuple(spot)].set(smallest).at[tuple(beside)].set(top_value)


def shard_levels(key, shape, cuts, smallest, high):
    def one(position, shards_of):
        draws = jax.random.uniform(jax.random.fold_in(jax.random.fold_in(key, 6), position), (shards_of,), jnp.float32, smallest / len(cuts), high / len(cuts))
        return jnp.repeat(jnp.exp(draws), shape[position] // shards_of).reshape((-1,) + (1,) * (len(shape) - position - 1))

    loudness = one(*cuts[0])
    for cut in cuts[1:]:
        loudness = loudness * one(*cut)
    return loudness


def cumulative_ranks(count, skew):
    portions = [(1 << 20) // math.isqrt(rank ** skew) + 1 for rank in range(1, count + 1)]
    scale = 1 + sum(portions) // (1 << 30)
    return np.cumsum(np.array([max(1, weight // scale) for weight in portions]))


def skewed_ids(own_key, shape, count, slope):
    listing = cumulative_ranks(count, slope)
    lot = jax.random.randint(jax.random.fold_in(own_key, 1), shape, 0, int(listing[count - 1]))
    grade = jnp.searchsorted(jnp.asarray(listing, jnp.int32), lot, side="right")
    return jax.random.permutation(jax.random.fold_in(own_key, 2), count)[grade].astype(jnp.int32)


def normal_values(own_key, shape, spread, reach, cuts=(), dtype=jnp.bfloat16):
    level = shard_levels(own_key, shape, cuts, -0.22, 0.18) if cuts else 1.0
    drawn = jax.random.normal(own_key, shape, jnp.float32) * spread * level
    return jnp.minimum(jnp.maximum(drawn, -reach), reach).astype(dtype)


def setup_inputs(seed: int = 0) -> dict:
    arg_keys = jax.random.split(jax.random.key(seed), 18)
    return {
        "byte_values": touch_ends(skewed_ids(arg_keys[0], (ROWS, ROW), VOCAB, 2), jax.random.fold_in(arg_keys[0], 3), 0, VOCAB - 1).astype(jnp.int32),
        "segments": draw_segments(jax.random.fold_in(arg_keys[17], 71), 0),
        "byte_mask": draw_byte_mask(jax.random.fold_in(arg_keys[17], 71), 0),
        "embedding": normal_values(arg_keys[3], (VOCAB, D), 1.0, 6.0),
        "filter_weight": normal_values(arg_keys[4], (4, D), 0.5, 3.0, (), jnp.float32),
        "score_weight": normal_values(arg_keys[5], (D,), (D // 4) ** -0.5, 0.4375, (), jnp.float32),
        "first_gain": jnp.clip(1.0 + 0.18 * jax.random.normal(arg_keys[6], (D,), jnp.float32), 0.1, 1.9),
        "query_weight": normal_values(arg_keys[7], (D, D), (4 * D) ** -0.5, 0.109375),
        "key_weight": normal_values(arg_keys[8], (D, D), (4 * D) ** -0.5, 0.109375),
        "value_weight": normal_values(arg_keys[9], (D, D), D ** -0.5, 0.21875),
        "merge_weight": normal_values(arg_keys[10], (D, D), (D // 16) ** -0.5, 0.875),
        "position_bias": normal_values(arg_keys[11], (BUCKETS, H), 1.0, 4.0, (), jnp.float32),
        "second_gain": jnp.clip(1.0 + 0.18 * jax.random.normal(arg_keys[12], (D,), jnp.float32), 0.1, 1.9),
        "gate_weight": normal_values(arg_keys[13], (D, FF), D ** -0.5, 0.21875),
        "up_weight": normal_values(arg_keys[14], (D, FF), D ** -0.5, 0.21875),
        "down_weight": normal_values(arg_keys[15], (FF, D), FF ** -0.5, 0.125),
        "cotangent": normal_values(arg_keys[16], (ROWS, LTOK, D), 1.0, 6.0, ((0, 8), (1, 4))),
    }


EPS = 1e-06
LIMITS = (12, 16, 23, 32, 46, 64, 91)
HIGH = lax.Precision.HIGHEST

@jax.custom_vjp
def low(v):
    return lax.optimization_barrier(v.astype(jnp.bfloat16)).astype(jnp.float32)

@jax.custom_vjp
def low_back(v):
    return v

def low_keep(v):
    return (low(v), None)

def low_pass(kept, grad):
    return (grad,)

def back_keep(v):
    return (v, None)

def back_low(kept, grad):
    return (low(grad),)
low.defvjp(low_keep, low_pass)
low_back.defvjp(back_keep, back_low)

def buckets(query_pos, key_pos):
    relative = key_pos[None, :] - query_pos[:, None]
    distance = jnp.abs(relative)
    far = 8 + sum(((distance >= limit).astype(jnp.int32) for limit in LIMITS))
    near = jnp.where(distance < 8, distance, far)
    return (near + 16 * (relative > 0).astype(jnp.int32)).astype(jnp.int32)

def rms_norm(values, gain):
    return values * lax.rsqrt(lax.optimization_barrier(jnp.mean(values * values, axis=-1, keepdims=True)) + EPS) * gain

def byte_mixer(embedded, filters, score):
    length = embedded.shape[0]
    padded = jnp.pad(embedded, ((2, 1), (0, 0)))
    convolved = sum((filters[k] * padded[k:k + length] for k in range(4)))
    pooled = []
    for size in range(1, 5):
        count = -(-length // size)
        extended = jnp.pad(convolved, ((0, count * size - length), (0, 0)))
        means = lax.optimization_barrier(jnp.mean(extended.reshape(count, size, -1), axis=1))
        pooled.append(jnp.repeat(means, size, axis=0)[:length])
    stacked = jnp.stack(pooled)
    weights = jax.nn.softmax(jnp.dot(stacked, score, precision=HIGH), axis=0)
    mixed = lax.optimization_barrier(jnp.sum(weights[:, :, None] * stacked, axis=0))
    return lax.optimization_barrier(jnp.mean(mixed.reshape(length // 2, 2, -1), axis=1))

def block_row(stream, segs, bias, gain_a, wquery, wkey, wvalue, wmerge, gain_b, wgate, wup, wdown):
    length = stream.shape[0]
    normed = low(rms_norm(stream, gain_a))
    query = low(low_back(jnp.dot(normed, wquery, precision=HIGH))).reshape(length, H, DH)
    keys = low(low_back(jnp.dot(normed, wkey, precision=HIGH))).reshape(length, H, DH)
    values = low(low_back(jnp.dot(normed, wvalue, precision=HIGH))).reshape(length, H, DH)
    scores = jnp.einsum('qhd,khd->hqk', query, keys, precision=HIGH) + bias
    same = (segs[:, None] == segs[None, :])[None]
    scores = low_back(jnp.where(same, scores, -1e+30))
    probs = jax.nn.softmax(scores, axis=-1)
    attended = jnp.einsum('hqk,khd->qhd', low(probs), values, precision=HIGH).reshape(length, H * DH)
    attended = low(low_back(attended))
    resid = stream + low_back(jnp.dot(attended, wmerge, precision=HIGH))
    normed_two = low(rms_norm(resid, gain_b))
    gate = low_back(jnp.dot(normed_two, wgate, precision=HIGH))
    up_value = low_back(jnp.dot(normed_two, wup, precision=HIGH))
    hidden = low(jax.nn.gelu(gate) * up_value)
    return resid + low_back(jnp.dot(hidden, wdown, precision=HIGH))

def reference(byte_values, segments, byte_mask, embedding, filter_weight, score_weight, first_gain, query_weight, key_weight, value_weight, merge_weight, position_bias, second_gain, gate_weight, up_weight, down_weight, cotangent):
    positions = jnp.arange(LTOK).astype(jnp.int32)
    table = buckets(positions, positions)
    token_segments = segments[:, ::2]
    keep = byte_mask.astype(jnp.float32)[:, :, None]

    def forward(embed, filters, score, gain_a, wquery, wkey, wvalue, wmerge, bias_table, gain_b, wgate, wup, wdown):
        bias = jnp.transpose(bias_table[table], (2, 0, 1))

        def one_row(row):
            values, segs, mask_row = row
            embedded = embed[values] * mask_row
            stream = byte_mixer(embedded, filters, score)
            return block_row(stream, segs, bias, gain_a, wquery, wkey, wvalue, wmerge, gain_b, wgate, wup, wdown)
        return lax.map(jax.checkpoint(one_row), (byte_values, token_segments, keep))
    params = (embedding.astype(jnp.float32), filter_weight.astype(jnp.float32), score_weight.astype(jnp.float32), first_gain.astype(jnp.float32), query_weight.astype(jnp.float32), key_weight.astype(jnp.float32), value_weight.astype(jnp.float32), merge_weight.astype(jnp.float32), position_bias.astype(jnp.float32), second_gain.astype(jnp.float32), gate_weight.astype(jnp.float32), up_weight.astype(jnp.float32), down_weight.astype(jnp.float32))
    outputs, pullback = jax.vjp(forward, *params)
    grads = pullback(cotangent.astype(jnp.float32))
    return (outputs.astype(jnp.bfloat16), grads[0], grads[1], grads[2], grads[3], grads[4], grads[5], grads[6], grads[7], grads[8], grads[9], grads[10], grads[11], grads[12])
```

```python
import functools

import jax
import jax.numpy as jnp
from jax import lax
from jax.experimental import pallas as pl
from jax.experimental.pallas import tpu as pltpu
from jax.sharding import PartitionSpec as P

EPS = 1e-06
LIMITS = (12, 16, 23, 32, 46, 64, 91)
NEG = -1e30
LANES = 128
BLOCK = 128
FAR = 2
CUBE = 0.044715
SLOPE = 0.7978845608028654
MEGA = 1 << 20


def dot(a, b):
    return lax.dot_general(a, b, (((1,), (0,)), ((), ())), preferred_element_type=jnp.float32)


def dot_nt(a, b):
    return lax.dot_general(a, b, (((1,), (1,)), ((), ())), preferred_element_type=jnp.float32)


def params(megabytes):
    return pltpu.CompilerParams(vmem_limit_bytes=megabytes * MEGA)


def cost(flops, moved):
    return pl.CostEstimate(flops=int(flops), bytes_accessed=int(moved), transcendentals=0)


VMEM = pl.BlockSpec(memory_space=pltpu.VMEM)
SMEM = pl.BlockSpec(memory_space=pltpu.SMEM)


def bias_kernel(table_ref, out_ref):
    heads = out_ref.shape[0]
    spread = lax.broadcasted_iota(jnp.int32, (BLOCK, BLOCK), 0) - lax.broadcasted_iota(
        jnp.int32, (BLOCK, BLOCK), 1
    )

    def one_head(h, carry):
        def chain(distance, first):
            value = jnp.full((BLOCK, BLOCK), table_ref[first + 15, h], jnp.float32)
            for place in reversed(range(7)):
                value = jnp.where(distance < LIMITS[place], table_ref[first + 8 + place, h], value)
            for near in reversed(range(8)):
                value = jnp.where(distance < near + 1, table_ref[first + near, h], value)
            return value

        out_ref[h, 0] = jnp.full((BLOCK, BLOCK), table_ref[15, h], jnp.float32)
        out_ref[h, 1] = chain(BLOCK - spread, 0)
        before = chain(-spread, 0)
        after = chain(spread, 16)
        out_ref[h, 2] = jnp.where(spread > 0, after, before)
        out_ref[h, 3] = chain(BLOCK + spread, 16)
        out_ref[h, 4] = jnp.full((BLOCK, BLOCK), table_ref[31, h], jnp.float32)
        return carry

    lax.fori_loop(0, heads, one_head, 0)


def bias_tiles(table):
    heads = table.shape[1]
    shape = (heads, 2 * FAR + 1, BLOCK, BLOCK)
    return pl.pallas_call(
        bias_kernel,
        out_shape=jax.ShapeDtypeStruct(shape, jnp.float32),
        in_specs=[SMEM],
        out_specs=VMEM,
        compiler_params=params(16),
        cost_estimate=cost(heads * 2e6, heads * 5 * 65536),
        name="bias_tiles",
    )(table)


def chunk_of(c):
    return pl.ds(pl.multiple_of(c * LANES, LANES), LANES)


def down(x):
    return pltpu.roll(x, 1, 0)


def up(x):
    return pltpu.roll(x, x.shape[0] - 1, 0)


def lane_sum(x):
    return jnp.broadcast_to(jnp.sum(x, axis=1, keepdims=True), x.shape)


def offsets_of(rows):
    return {
        -2: down(rows[2]),
        -1: down(rows[3]),
        0: rows[0],
        1: rows[1],
        2: rows[2],
        3: rows[3],
        4: up(rows[0]),
        5: up(rows[1]),
    }


def spread_of(phase, j, one, two, three, four, coefs):
    pair = j - j % 2
    third = three / 3.0
    zero = jnp.zeros_like(third)
    half, quarter = two * 0.5, four * 0.25

    def add(o, value):
        coefs[o] = coefs[o] + value if o in coefs else value

    add(j, one + third)
    for o in (pair, pair + 1):
        add(o, half)
    for o in range(4):
        add(o, quarter)
    add(j + 1, jnp.where(phase <= 1, third, zero))
    add(j + 2, jnp.where(phase == 0, third, zero))
    add(j - 1, jnp.where(phase >= 1, third, zero))
    add(j - 2, jnp.where(phase == 2, third, zero))


def pooled_dots(phase, j, dots):
    pair = j - j % 2
    zero = jnp.zeros_like(dots[0])
    two = 0.5 * (dots[pair] + dots[pair + 1])
    four = 0.25 * ((dots[0] + dots[1]) + (dots[2] + dots[3]))
    three = dots[j] + jnp.where(phase <= 1, dots[j + 1], zero)
    three = three + jnp.where(phase == 0, dots[j + 2], zero)
    three = three + jnp.where(phase >= 1, dots[j - 1], zero)
    three = three + jnp.where(phase == 2, dots[j - 2], zero)
    return dots[j], two, three / 3.0, four


def convolve(e, taps):
    em2, em3, ep0 = down(e[2]), down(e[3]), up(e[0])
    f0, f1, f2, f3 = taps
    return [
        f0 * em2 + f1 * em3 + f2 * e[0] + f3 * e[1],
        f0 * em3 + f1 * e[0] + f2 * e[1] + f3 * e[2],
        f0 * e[0] + f1 * e[1] + f2 * e[2] + f3 * e[3],
        f0 * e[1] + f1 * e[2] + f2 * e[3] + f3 * ep0,
    ]


def mixer_weights(info_ref, ids_ref, emb_ref, filt_ref, score_ref, e_ref, c_ref, acc_ref, row_len):
    count = ids_ref.shape[1]
    words, features = emb_ref.shape
    chunks = features // LANES
    group = info_ref[4] // 4
    vocab = lax.broadcasted_iota(jnp.int32, (count, words), 1)
    for j in range(4):
        hot = jnp.where(ids_ref[j] == vocab, 1.0, 0.0).astype(jnp.bfloat16)
        e_ref[j] = dot(hot, emb_ref[...])
        acc_ref[j] = jnp.zeros((count, LANES), jnp.float32)

    def one_chunk(c, carry):
        lanes = chunk_of(c)
        e = [e_ref[j, :, lanes] for j in range(4)]
        conv = convolve(e, [filt_ref[k : k + 1, lanes] for k in range(4)])
        for j in range(4):
            c_ref[j, :, lanes] = conv[j]
            acc_ref[j] += conv[j] * score_ref[:, lanes]
        return carry

    lax.fori_loop(0, chunks, one_chunk, 0)
    rows = lax.broadcasted_iota(jnp.int32, (count, LANES), 0)
    places = jnp.where(rows == count - 1, -1, rows) + group
    inside = [(4 * places + j < row_len) for j in range(4)]
    dots = [jnp.where(inside[j], lane_sum(acc_ref[j]), 0.0) for j in range(4)]
    dots = offsets_of(dots)
    phases, weights = [], []
    for j in range(4):
        phase = lax.rem(places + 3 + j, 3)
        scores = pooled_dots(phase, j, dots)
        highest = jnp.maximum(jnp.maximum(scores[0], scores[1]), jnp.maximum(scores[2], scores[3]))
        powers = [jnp.exp(score - highest) for score in scores]
        share = 1.0 / ((powers[0] + powers[1]) + (powers[2] + powers[3]))
        phases.append(phase)
        weights.append([power * share for power in powers])
    limits = {o: (4 * places + o < row_len) for o in (4, 5)}
    return phases, weights, limits


def token_coefs(phases, weights, limits, scale):
    result = []
    for h in range(2):
        coefs = {}
        for j in (2 * h, 2 * h + 1):
            spread_of(phases[j], j, *weights[j], coefs)
        for o in coefs:
            if o in limits:
                coefs[o] = jnp.where(limits[o], coefs[o], 0.0)
            coefs[o] = coefs[o] * scale
        result.append(coefs)
    return result


def mixer_kernel(
    row_len,
    info_ref,
    ids_ref,
    emb_ref,
    filt_ref,
    score_ref,
    gain_ref,
    wq_ref,
    wk_ref,
    wv_ref,
    stream_ref,
    normed_ref,
    q_ref,
    k_ref,
    v_ref,
    e_ref,
    c_ref,
    acc_ref,
    coef_ref,
    square_ref,
    root_ref,
):
    tokens, features = stream_ref.shape
    groups = tokens // 2
    chunks = features // LANES
    phases, weights, limits = mixer_weights(
        info_ref, ids_ref, emb_ref, filt_ref, score_ref, e_ref, c_ref, acc_ref, row_len
    )
    coefs = token_coefs(phases, weights, limits, 0.5)
    names = [(h, o) for h in range(2) for o in sorted(coefs[h])]
    for place, (h, o) in enumerate(names):
        coef_ref[place] = coefs[h][o][:groups]
    square_ref[...] = jnp.zeros_like(square_ref)

    def one_chunk(c, carry):
        lanes = chunk_of(c)
        conv = {
            o: value[:groups]
            for o, value in offsets_of([c_ref[j, :, lanes] for j in range(4)]).items()
        }
        for h in range(2):
            mixed = None
            for place, (side, o) in enumerate(names):
                if side == h:
                    term = coef_ref[place] * conv[o]
                    mixed = term if mixed is None else mixed + term
            root_ref[pl.ds(h, groups, stride=2), :] = mixed
            square_ref[h] += mixed * mixed
        stream_ref[:, lanes] = root_ref[...]
        return carry

    lax.fori_loop(0, chunks, one_chunk, 0)
    for h in range(2):
        root = lax.rsqrt(lane_sum(square_ref[h]) / features + EPS)
        root_ref[pl.ds(h, groups, stride=2), :] = root

    def norm_chunk(c, carry):
        lanes = chunk_of(c)
        normed = stream_ref[:, lanes] * root_ref[...] * gain_ref[:, lanes]
        normed_ref[:, lanes] = normed.astype(jnp.bfloat16)
        return carry

    lax.fori_loop(0, chunks, norm_chunk, 0)
    for w_ref, out_ref in ((wk_ref, k_ref), (wv_ref, v_ref), (wq_ref, q_ref)):
        out_ref[...] = dot(normed_ref[...], w_ref[...]).astype(jnp.bfloat16)


def mixer_forward(info, ids, emb, filt, score, gain, wq, wk, wv, tokens, row_len):
    features = emb.shape[1]
    count = ids.shape[1]
    groups = tokens // 2
    low = jax.ShapeDtypeStruct((tokens, features), jnp.bfloat16)
    full = jax.ShapeDtypeStruct((tokens, features), jnp.float32)
    return pl.pallas_call(
        functools.partial(mixer_kernel, row_len),
        out_shape=[full, low, low, low, low],
        in_specs=[SMEM] + [VMEM] * 8,
        out_specs=[VMEM] * 5,
        scratch_shapes=[
            pltpu.VMEM((4, count, features), jnp.float32),
            pltpu.VMEM((4, count, features), jnp.float32),
            pltpu.VMEM((4, count, LANES), jnp.float32),
            pltpu.VMEM((12, groups, LANES), jnp.float32),
            pltpu.VMEM((2, groups, LANES), jnp.float32),
            pltpu.VMEM((tokens, LANES), jnp.float32),
        ],
        compiler_params=params(40),
        cost_estimate=cost(2 * tokens * features * features * 8, 8e6),
        name="mixer_forward",
    )(info, ids, emb, filt, score, gain, wq, wk, wv)


def mixer_back_kernel(
    row_len,
    info_ref,
    ids_ref,
    flat_ref,
    emb_ref,
    filt_ref,
    score_ref,
    grad_ref,
    embed_ref,
    small_ref,
    e_ref,
    c_ref,
    acc_ref,
    coef_ref,
    dots_ref,
    high_ref,
    low_ref,
    turn_ref,
):
    tokens, features = grad_ref.shape
    groups = tokens // 2
    chunks = features // LANES
    count = ids_ref.shape[1]
    words = emb_ref.shape[0]
    phases, weights, limits = mixer_weights(
        info_ref, ids_ref, emb_ref, filt_ref, score_ref, e_ref, c_ref, acc_ref, row_len
    )
    coefs = token_coefs(phases, weights, limits, 0.5)
    names = [(h, o) for h in range(2) for o in sorted(coefs[h])]
    empty = jnp.zeros((count - groups, LANES), jnp.float32)
    dots_ref[...] = jnp.zeros_like(dots_ref)

    def token_grads(lanes):
        turn_ref[...] = grad_ref[:, lanes]
        return [
            jnp.concatenate([turn_ref[pl.ds(h, groups, stride=2), :], empty], axis=0)
            for h in range(2)
        ]

    def dots_chunk(c, carry):
        lanes = chunk_of(c)
        conv = offsets_of([c_ref[j, :, lanes] for j in range(4)])
        grads = token_grads(lanes)
        for place, (h, o) in enumerate(names):
            dots_ref[place] += grads[h] * conv[o]
        return carry

    lax.fori_loop(0, chunks, dots_chunk, 0)
    pulls = []
    for h in range(2):
        dots = {}
        for place, (side, o) in enumerate(names):
            if side == h:
                value = lane_sum(dots_ref[place]) * 0.5
                dots[o] = jnp.where(limits[o], value, 0.0) if o in limits else value
        for j in (2 * h, 2 * h + 1):
            grads = pooled_dots(phases[j], j, dots)
            mean = sum(weights[j][i] * grads[i] for i in range(4))
            pulls.append([weights[j][i] * (grads[i] - mean) for i in range(4)])
    score_coefs = token_coefs(phases, pulls, limits, 1.0)

    def gathered(by_token):
        first, second = by_token
        return [
            first[0] + second[0] + down(second[4]),
            first[1] + second[1] + down(second[5]),
            first[2] + second[2] + up(first[-2]),
            first[3] + second[3] + up(first[-1]),
        ]

    kappas = gathered(score_coefs)
    for j in range(4):
        coef_ref[4 * j] = coefs[0][j]
        coef_ref[4 * j + 1] = coefs[1][j]
        coef_ref[4 * j + 2] = down(coefs[1][4 + j]) if j < 2 else up(coefs[0][j - 4])
        coef_ref[4 * j + 3] = kappas[j]
    small_ref[...] = jnp.zeros_like(small_ref)

    def total(x):
        return jnp.sum(x, axis=0, keepdims=True)

    def grad_chunk(c, carry):
        lanes = chunk_of(c)
        first, second = token_grads(lanes)
        above, below = down(second), up(first)
        score = score_ref[:, lanes]
        taps = [filt_ref[k : k + 1, lanes] for k in range(4)]
        e = [e_ref[j, :, lanes] for j in range(4)]
        near = offsets_of(e)
        d = []
        score_sum = jnp.zeros((1, LANES), jnp.float32)
        tap_sums = [jnp.zeros((1, LANES), jnp.float32) for _ in range(4)]
        for j in range(4):
            beside = above if j < 2 else below
            kappa = coef_ref[4 * j + 3]
            value = (
                coef_ref[4 * j] * first
                + coef_ref[4 * j + 1] * second
                + coef_ref[4 * j + 2] * beside
                + kappa * score
            )
            d.append(value)
            score_sum = score_sum + total(kappa * c_ref[j, :, lanes])
            for k in range(4):
                tap_sums[k] = tap_sums[k] + total(value * near[j + k - 2])
        for k in range(4):
            small_ref[k : k + 1, lanes] = tap_sums[k]
        small_ref[4:5, lanes] = score_sum
        f0, f1, f2, f3 = taps
        d3m, d0p, d1p = down(d[3]), up(d[0]), up(d[1])
        back = [
            f0 * d[2] + f1 * d[1] + f2 * d[0] + f3 * d3m,
            f0 * d[3] + f1 * d[2] + f2 * d[1] + f3 * d[0],
            f0 * d0p + f1 * d[3] + f2 * d[2] + f3 * d[1],
            f0 * d1p + f1 * d0p + f2 * d[3] + f3 * d[2],
        ]
        for j in range(4):
            high = back[j].astype(jnp.bfloat16)
            high_ref[j * count : (j + 1) * count, lanes] = high
            low_ref[j * count : (j + 1) * count, lanes] = (
                back[j] - high.astype(jnp.float32)
            ).astype(jnp.bfloat16)
        return carry

    lax.fori_loop(0, chunks, grad_chunk, 0)
    vocab = lax.broadcasted_iota(jnp.int32, (words, 4 * count), 0)
    hot = jnp.where(flat_ref[...] == vocab, 1.0, 0.0).astype(jnp.bfloat16)
    embed_ref[...] = dot(hot, high_ref[...]) + dot(hot, low_ref[...])


def mixer_backward(info, ids, emb, filt, score, grad, row_len):
    tokens, features = grad.shape
    count = ids.shape[1]
    words = emb.shape[0]
    flat = ids.reshape(1, -1)
    return pl.pallas_call(
        functools.partial(mixer_back_kernel, row_len),
        out_shape=[
            jax.ShapeDtypeStruct((words, features), jnp.float32),
            jax.ShapeDtypeStruct((8, features), jnp.float32),
        ],
        in_specs=[SMEM] + [VMEM] * 6,
        out_specs=[VMEM] * 2,
        scratch_shapes=[
            pltpu.VMEM((4, count, features), jnp.float32),
            pltpu.VMEM((4, count, features), jnp.float32),
            pltpu.VMEM((4, count, LANES), jnp.float32),
            pltpu.VMEM((16, count, LANES), jnp.float32),
            pltpu.VMEM((12, count, LANES), jnp.float32),
            pltpu.VMEM((4 * count, features), jnp.bfloat16),
            pltpu.VMEM((4 * count, features), jnp.bfloat16),
            pltpu.VMEM((tokens, LANES), jnp.float32),
        ],
        compiler_params=params(48),
        cost_estimate=cost(2 * tokens * features * features * 8, 8e6),
        name="mixer_backward",
    )(info, ids, flat, emb, filt, score, grad)


def scores_of(info_ref, part, h, k_ref, q_low, bias_ref, row_seg_ref, col_seg_ref):
    keys, tokens = k_ref.shape[0], q_low.shape[0]
    base = info_ref[part]
    raw = dot_nt(k_ref[...], q_low)
    own = info_ref[3]
    seg_row = row_seg_ref[...]
    rows = []
    for kb in range(keys // BLOCK):
        tiles = [
            bias_ref[h, jnp.clip(base + kb - own - qb, -FAR, FAR) + FAR]
            for qb in range(tokens // BLOCK)
        ]
        value = raw[kb * BLOCK : (kb + 1) * BLOCK] + jnp.concatenate(tiles, axis=1)
        start = pl.multiple_of((base + kb) * BLOCK, BLOCK)
        same = col_seg_ref[pl.ds(start, BLOCK), :] == seg_row
        rows.append(jnp.where(same, value, NEG))
    return rows


def only_head(x, h, size):
    lane = lax.broadcasted_iota(jnp.int32, x.shape, 1)
    return jnp.where((lane >= h * size) & (lane < (h + 1) * size), x, jnp.zeros_like(x))


def attention_kernel(
    parts,
    size,
    info_ref,
    stream_ref,
    q_ref,
    *refs,
):
    k_refs, v_refs = refs[:parts], refs[parts : 2 * parts]
    (
        bias_ref,
        row_seg_ref,
        col_seg_ref,
        wm_ref,
        gain_ref,
        att_ref,
        lse_ref,
        resid_ref,
        normed_ref,
    ) = refs[2 * parts :]
    step = pl.program_id(0)
    features = stream_ref.shape[1]
    low = []
    for h in range(2):
        q_low = only_head(q_ref[...], h, size)
        rows = []
        for part in range(parts):
            rows.append(
                scores_of(info_ref, 5 + part, h, k_refs[part], q_low, bias_ref, row_seg_ref, col_seg_ref)
            )
        highest = None
        for row in sum(rows, []):
            top = jnp.max(row, axis=0, keepdims=True)
            highest = top if highest is None else jnp.maximum(highest, top)
        summed = None
        mixed = None
        for part in range(parts):
            powers = [jnp.exp(row - highest) for row in rows[part]]
            for power in powers:
                here = jnp.sum(power, axis=0, keepdims=True)
                summed = here if summed is None else summed + here
            weights = jnp.concatenate([power.astype(jnp.bfloat16) for power in powers], axis=0)
            turned = v_refs[part][...].T[h * size : (h + 1) * size]
            term = dot(turned, weights)
            mixed = term if mixed is None else mixed + term
        lse_ref[0, h : h + 1] = highest + jnp.log(summed)
        low.append(mixed * (1.0 / summed))
    turned = jnp.concatenate(low, axis=0)
    att_ref[...] = turned.astype(jnp.bfloat16)
    attended = turned.T.astype(jnp.bfloat16)
    added = dot(attended, wm_ref[...])

    @pl.when(step == 0)
    def _():
        resid_ref[...] = stream_ref[...] + added

    @pl.when(step > 0)
    def _():
        resid_ref[...] += added

    @pl.when(step == pl.num_programs(0) - 1)
    def _():
        resid = resid_ref[...]
        root = lax.rsqrt(jnp.sum(resid * resid, axis=1, keepdims=True) / features + EPS)
        normed_ref[...] = (resid * root * gain_ref[...]).astype(jnp.bfloat16)


def attention_forward(info, stream, q, ks, vs, bias, row_seg, col_seg, wm, gain):
    tokens, features = q.shape
    heads = bias.shape[0]
    size = features // heads
    pairs = heads // 2
    parts = len(ks)
    wide = 2 * size
    by_pair = [pl.BlockSpec((x.shape[0], wide), lambda p: (0, p)) for x in ks]
    whole = lambda shape: pl.BlockSpec(shape, lambda p: (0,) * len(shape))
    return pl.pallas_call(
        functools.partial(attention_kernel, parts, size),
        grid=(pairs,),
        out_shape=[
            jax.ShapeDtypeStruct((features, tokens), jnp.bfloat16),
            jax.ShapeDtypeStruct((pairs, 8, tokens), jnp.float32),
            jax.ShapeDtypeStruct((tokens, features), jnp.float32),
            jax.ShapeDtypeStruct((tokens, features), jnp.bfloat16),
        ],
        in_specs=[
            SMEM,
            whole(stream.shape),
            pl.BlockSpec((tokens, wide), lambda p: (0, p)),
            *by_pair,
            *by_pair,
            pl.BlockSpec((2,) + bias.shape[1:], lambda p: (p, 0, 0, 0)),
            whole(row_seg.shape),
            whole(col_seg.shape),
            pl.BlockSpec((wide, features), lambda p: (p, 0)),
            whole(gain.shape),
        ],
        out_specs=[
            pl.BlockSpec((wide, tokens), lambda p: (p, 0)),
            pl.BlockSpec((1, 8, tokens), lambda p: (p, 0, 0)),
            whole((tokens, features)),
            whole((tokens, features)),
        ],
        compiler_params=params(48),
        cost_estimate=cost(8 * tokens * 1024 * features * 4, 12e6),
        name="attention_forward",
    )(info, stream, q, *ks, *vs, bias, row_seg, col_seg, wm, gain)


def attention_back_kernel(
    parts,
    size,
    info_ref,
    q_ref,
    g_ref,
    *refs,
):
    k_refs, v_refs = refs[:parts], refs[parts : 2 * parts]
    bias_ref, row_seg_ref, col_seg_ref, lse_ref, dq_ref = refs[2 * parts : 2 * parts + 5]
    refs = refs[2 * parts + 5 :]
    dk_refs, dv_refs, tile_ref = refs[:parts], refs[parts : 2 * parts], refs[2 * parts]
    tokens = q_ref.shape[0]
    own = info_ref[3]
    turned_keys = [k_ref[...].T for k_ref in k_refs]
    dk = [None] * parts
    dv = [None] * parts
    low = []
    tile_ref[...] = jnp.zeros_like(tile_ref)
    for h in range(2):
        q_low = only_head(q_ref[...], h, size)
        g_low = only_head(g_ref[...], h, size)
        log_total = lse_ref[0, h : h + 1]
        shares, pulls = [], []
        correction = None
        for part in range(parts):
            rows = scores_of(
                info_ref, 5 + part, h, k_refs[part], q_low, bias_ref, row_seg_ref, col_seg_ref
            )
            probs = [jnp.exp(row - log_total) for row in rows]
            pull = dot_nt(v_refs[part][...], g_low)
            pull = [pull[i * BLOCK : (i + 1) * BLOCK] for i in range(len(rows))]
            for i in range(len(rows)):
                here = jnp.sum(probs[i] * pull[i], axis=0, keepdims=True)
                correction = here if correction is None else correction + here
            shares.append(probs)
            pulls.append(pull)
        turned = None
        for part in range(parts):
            base = info_ref[5 + part]
            grads = [p * (d - correction) for p, d in zip(shares[part], pulls[part])]
            blocks = tokens // BLOCK
            for delta in range(-blocks + 1, len(grads)):
                tile = None
                for kb in range(len(grads)):
                    qb = kb - delta
                    if 0 <= qb < blocks:
                        here = grads[kb][:, qb * BLOCK : (qb + 1) * BLOCK]
                        tile = here if tile is None else tile + here
                place = jnp.clip(base - own + delta, -FAR, FAR) + FAR
                tile_ref[h, place] += tile
            grads = jnp.concatenate([grad.astype(jnp.bfloat16) for grad in grads], axis=0)
            probs = jnp.concatenate([share.astype(jnp.bfloat16) for share in shares[part]], axis=0)
            term = dot(grads, q_low)
            dk[part] = term if dk[part] is None else dk[part] + term
            term = dot(probs, g_low)
            dv[part] = term if dv[part] is None else dv[part] + term
            term = dot(turned_keys[part][h * size : (h + 1) * size], grads)
            turned = term if turned is None else turned + term
        low.append(turned)
    dq_ref[...] = jnp.concatenate(low, axis=0).T.astype(jnp.bfloat16)
    for part in range(parts):
        dk_refs[part][...] = dk[part].astype(jnp.bfloat16)
        dv_refs[part][...] = dv[part].astype(jnp.bfloat16)


def attention_backward(info, q, g, ks, vs, bias, row_seg, col_seg, lse):
    tokens, features = q.shape
    heads = bias.shape[0]
    size = features // heads
    pairs = heads // 2
    parts = len(ks)
    wide = 2 * size
    by_pair = [pl.BlockSpec((x.shape[0], wide), lambda p: (0, p)) for x in ks]
    own = pl.BlockSpec((tokens, wide), lambda p: (0, p))
    whole = lambda shape: pl.BlockSpec(shape, lambda p: (0,) * len(shape))
    tiles = pl.BlockSpec((2,) + bias.shape[1:], lambda p: (p, 0, 0, 0))
    shapes = [jax.ShapeDtypeStruct(x.shape, jnp.bfloat16) for x in ks]
    result = pl.pallas_call(
        functools.partial(attention_back_kernel, parts, size),
        grid=(pairs,),
        out_shape=[jax.ShapeDtypeStruct(q.shape, jnp.bfloat16), *shapes, *shapes]
        + [jax.ShapeDtypeStruct(bias.shape, jnp.float32)],
        in_specs=[
            SMEM,
            own,
            own,
            *by_pair,
            *by_pair,
            tiles,
            whole(row_seg.shape),
            whole(col_seg.shape),
            pl.BlockSpec((1, 8, tokens), lambda p: (p, 0, 0)),
        ],
        out_specs=[own, *by_pair, *by_pair, tiles],
        compiler_params=params(56),
        cost_estimate=cost(14 * tokens * 1024 * features * 4, 16e6),
        name="attention_backward",
    )(info, q, g, *ks, *vs, bias, row_seg, col_seg, lse)
    return result[0], result[1 : 1 + parts], result[1 + parts : 1 + 2 * parts], result[-1]


def bucket_kernel(tile_ref, out_ref):
    heads = tile_ref.shape[0]
    wide = 2 * BLOCK
    lane = lax.broadcasted_iota(jnp.int32, (1, wide), 1)
    spot = lax.broadcasted_iota(jnp.int32, (wide, LANES), 1)
    entry = lax.broadcasted_iota(jnp.int32, (wide, LANES), 0)
    gap = entry - (BLOCK - 1)
    row = lax.broadcasted_iota(jnp.int32, (BLOCK, BLOCK), 0)
    column = lax.broadcasted_iota(jnp.int32, (BLOCK, BLOCK), 1)
    flip = jnp.where(row + column == BLOCK - 1, 1.0, 0.0).astype(jnp.bfloat16)
    hots = []
    for delta in (-1, 0, 1):
        relative = delta * BLOCK - gap
        distance = jnp.abs(relative)
        far = jnp.full_like(distance, 8)
        for limit in LIMITS:
            far = far + jnp.where(distance >= limit, 1, 0)
        bucket = jnp.where(distance < 8, distance, far) + jnp.where(relative > 0, 16, 0)
        hots.append(jnp.where(bucket == spot, 1.0, 0.0).astype(jnp.bfloat16))
    lanes = lax.broadcasted_iota(jnp.int32, (1, LANES), 1)

    def one_head(h, carry):
        result = jnp.where(lanes == 15, jnp.sum(tile_ref[h, 0]), 0.0)
        result = result + jnp.where(lanes == 31, jnp.sum(tile_ref[h, 2 * FAR]), 0.0)
        for delta in range(3):
            tile = tile_ref[h, 1 + delta]
            flipped = jnp.zeros_like(tile)
            for _ in range(3):
                high = tile.astype(jnp.bfloat16)
                flipped = flipped + dot(flip, high)
                tile = tile - high.astype(jnp.float32)
            padded = jnp.concatenate([flipped, jnp.zeros_like(tile)], axis=1)
            slid = pltpu.roll(padded, 0, 1, stride=1, stride_axis=0)
            sums = jnp.sum(slid, axis=0, keepdims=True)
            for _ in range(3):
                high = sums.astype(jnp.bfloat16)
                result = result + dot(jnp.broadcast_to(high, (8, wide)), hots[delta])[:1]
                sums = sums - high.astype(jnp.float32)
        out_ref[pl.ds(h, 1), :] = result
        return carry

    lax.fori_loop(0, heads, one_head, 0)


def bucket_sums(tiles, buckets):
    heads = tiles.shape[0]
    result = pl.pallas_call(
        bucket_kernel,
        out_shape=jax.ShapeDtypeStruct((heads, LANES), jnp.float32),
        in_specs=[VMEM],
        out_specs=VMEM,
        compiler_params=params(24),
        cost_estimate=cost(heads * 4e6, heads * 5 * 65536),
        name="bucket_sums",
    )(tiles)
    return result[:, :buckets]


def relative_rows(me, count, src_ref, dst_ref):
    size = src_ref.shape[0] // count
    for place in range(count):
        r = 2 * (place % (count // 2)) + place // (count // 2)
        start = pl.multiple_of((me ^ r) * size, 16)
        dst_ref[place * size : (place + 1) * size] = src_ref[pl.ds(start, size), :]


def feed_kernel(
    held,
    count,
    info_ref,
    normed_ref,
    resid_ref,
    *refs,
):
    cot_refs = refs[:held]
    (
        wg_ref,
        wu_ref,
        wd_ref,
        out_ref,
        grad_ref,
        gu_keep_ref,
        gu_send_ref,
        d_keep_ref,
        d_send_ref,
        cot_ref,
        cot_turned_ref,
        turned_ref,
        normed_turned_ref,
        acc_ref,
    ) = refs[held:]
    step = pl.program_id(0)
    core = info_ref[1]
    span = cot_refs[0].shape[0]

    @pl.when(step == 0)
    def _():
        for phase in range(held):
            start = pl.multiple_of(lax.rem(info_ref[2] + held - phase, held) * span, span)
            cot_ref[pl.ds(start, span), :] = cot_refs[phase][...]
        cot_turned_ref[...] = cot_ref[...].T
        turned_ref[...] = normed_ref[...].T
        relative_rows(info_ref[0], count, turned_ref, normed_turned_ref)

    normed, cot = normed_ref[...], cot_ref[...]
    gate = dot(normed, wg_ref[...])
    up_value = dot(normed, wu_ref[...])
    grad_hidden = dot_nt(cot, wd_ref[...])
    square = gate * gate
    bend = jnp.tanh(SLOPE * gate * (1.0 + CUBE * square))
    half = 0.5 * (1.0 + bend)
    gelu = gate * half
    slope = half + (0.5 * SLOPE) * gate * (1.0 - bend * bend) * (1.0 + (3.0 * CUBE) * square)
    hidden = (gelu * up_value).astype(jnp.bfloat16)
    grad_gate = (grad_hidden * up_value * slope).astype(jnp.bfloat16)
    grad_up = (grad_hidden * gelu).astype(jnp.bfloat16)
    result = dot(hidden, wd_ref[...])
    back = dot_nt(grad_gate, wg_ref[...]) + dot_nt(grad_up, wu_ref[...])

    @pl.when(step == 0)
    def _():
        acc_ref[...] = resid_ref[...] + result
        grad_ref[...] = back

    @pl.when(step > 0)
    def _():
        acc_ref[...] += result
        grad_ref[...] += back

    rb, cb = gu_keep_ref.shape[-2:]
    half_rows = count // 2 * rb
    turned = normed_turned_ref[...]
    for kind, grad in enumerate((grad_gate, grad_up)):
        part = dot(turned, grad).astype(jnp.bfloat16)
        for e in range(2):
            columns = part[:, e * cb : (e + 1) * cb]
            gu_keep_ref[:, kind, e] = columns[:half_rows].reshape(count // 2, rb, cb)
            gu_send_ref[:, kind, e] = columns[half_rows:].reshape(count // 2, rb, cb)
    part = dot(cot_turned_ref[...], hidden)
    first, second = part[:, :cb], part[:, cb:]
    mine = core == 0
    keep = jnp.where(mine, first, second).astype(jnp.bfloat16)
    send = jnp.where(mine, second, first).astype(jnp.bfloat16)
    d_keep_ref[0] = keep.reshape(count, rb, cb)
    d_send_ref[0] = send.reshape(count, rb, cb)

    @pl.when(step == pl.num_programs(0) - 1)
    def _():
        out_ref[...] = acc_ref[...].astype(jnp.bfloat16)


def feed_forward(info, normed, resid, cots, wg, wu, wd, count):
    tokens, features = normed.shape
    width = wg.shape[1]
    chips = count // 2
    rb, cb = features // count, width // count
    held = len(cots)
    whole = lambda shape: pl.BlockSpec(shape, lambda j, info: (0,) * len(shape))
    low = jnp.bfloat16
    gu = jax.ShapeDtypeStruct((chips, 2, count, rb, cb), low)
    dd = jax.ShapeDtypeStruct((chips, count, rb, cb), low)
    gu_spec = pl.BlockSpec((chips, 2, 2, rb, cb), lambda j, info: (0, 0, j, 0, 0))
    dd_spec = pl.BlockSpec((1, count, rb, cb), lambda j, info: (j ^ (info[0] // 2), 0, 0, 0))
    return pl.pallas_call(
        functools.partial(feed_kernel, held, count),
        grid_spec=pltpu.PrefetchScalarGridSpec(
            num_scalar_prefetch=1,
            grid=(chips,),
            in_specs=[
                whole(normed.shape),
                whole(resid.shape),
                *[whole(cot.shape) for cot in cots],
                pl.BlockSpec((features, 2 * cb), lambda j, info: (0, j)),
                pl.BlockSpec((features, 2 * cb), lambda j, info: (0, j)),
                pl.BlockSpec((2 * cb, features), lambda j, info: (j, 0)),
            ],
            out_specs=[
                whole((tokens, features)),
                whole((tokens, features)),
                gu_spec,
                gu_spec,
                dd_spec,
                dd_spec,
            ],
            scratch_shapes=[
                pltpu.VMEM((tokens, features), low),
                pltpu.VMEM((features, tokens), low),
                pltpu.VMEM((features, tokens), low),
                pltpu.VMEM((features, tokens), low),
                pltpu.VMEM((tokens, features), jnp.float32),
            ],
        ),
        out_shape=[
            jax.ShapeDtypeStruct((tokens, features), low),
            jax.ShapeDtypeStruct((tokens, features), jnp.float32),
            gu,
            gu,
            dd,
            dd,
        ],
        compiler_params=params(56),
        cost_estimate=cost(2 * tokens * features * width * 9, 30e6),
        name="feed_forward",
    )(info, normed, resid, *cots, wg, wu, wd)


def between_kernel(
    held,
    count,
    info_ref,
    grad_ref,
    resid_ref,
    gain_ref,
    *refs,
):
    cot_refs = refs[:held]
    (
        att_ref,
        wm_ref,
        out_ref,
        att_grad_ref,
        keep_ref,
        send_ref,
        gain_grad_ref,
        cot_ref,
        turned_ref,
    ) = refs[held:]
    features = resid_ref.shape[1]
    span = cot_refs[0].shape[0]
    for phase in range(held):
        start = pl.multiple_of(lax.rem(info_ref[2] + held - phase, held) * span, span)
        cot_ref[pl.ds(start, span), :] = cot_refs[phase][...]
    resid = resid_ref[...]
    root = lax.rsqrt(jnp.sum(resid * resid, axis=1, keepdims=True) / features + EPS)
    grad = grad_ref[...]
    unit = resid * root
    gain_grad_ref[...] = jnp.sum(grad * unit, axis=0, keepdims=True)
    pulled = grad * gain_ref[...]
    mean = jnp.sum(unit * pulled, axis=1, keepdims=True) / features
    result = cot_ref[...].astype(jnp.float32) + root * (pulled - unit * mean)
    out_ref[...] = result
    mixed = result.astype(jnp.bfloat16)
    att_grad_ref[...] = dot_nt(mixed, wm_ref[...]).astype(jnp.bfloat16)
    relative_rows(info_ref[0], count, att_ref, turned_ref)
    part = dot(turned_ref[...], mixed).astype(jnp.bfloat16)
    half = features // 2
    keep_ref[...] = part[:half].reshape(keep_ref.shape)
    send_ref[...] = part[half:].reshape(send_ref.shape)


def between(info, grad, resid, gain, cots, att, wm, count):
    tokens, features = grad.shape
    rb = features // count
    low = jnp.bfloat16
    piece = jax.ShapeDtypeStruct((count // 2, rb, features), low)
    return pl.pallas_call(
        functools.partial(between_kernel, len(cots), count),
        out_shape=[
            jax.ShapeDtypeStruct((tokens, features), jnp.float32),
            jax.ShapeDtypeStruct((tokens, features), low),
            piece,
            piece,
            jax.ShapeDtypeStruct((1, features), jnp.float32),
        ],
        in_specs=[SMEM] + [VMEM] * (5 + len(cots)),
        out_specs=[VMEM] * 5,
        scratch_shapes=[
            pltpu.VMEM((tokens, features), low),
            pltpu.VMEM((features, tokens), low),
        ],
        compiler_params=params(40),
        cost_estimate=cost(4 * tokens * features * features, 10e6),
        name="between",
    )(info, grad, resid, gain, *cots, att, wm)


def project_back_kernel(
    count,
    info_ref,
    dq_ref,
    dk_ref,
    dk_got_ref,
    dv_ref,
    dv_got_ref,
    normed_ref,
    stream_ref,
    grad_ref,
    gain_ref,
    wq_ref,
    wk_ref,
    wv_ref,
    keep_ref,
    send_ref,
    out_ref,
    gain_grad_ref,
    turned_ref,
    relative_ref,
):
    features = stream_ref.shape[1]
    turned_ref[...] = normed_ref[...].T
    relative_rows(info_ref[0], count, turned_ref, relative_ref)
    half = features // 2
    rb = features // count
    total = None

    def both(a_ref, b_ref):
        return (a_ref[...].astype(jnp.float32) + b_ref[...].astype(jnp.float32)).astype(jnp.bfloat16)

    grads = (dq_ref[...], both(dk_ref, dk_got_ref), both(dv_ref, dv_got_ref))
    for place, (grad, w_ref) in enumerate(zip(grads, (wq_ref, wk_ref, wv_ref))):
        part = dot(relative_ref[...], grad).astype(jnp.bfloat16)
        keep_ref[:, place] = part[:half].reshape(count // 2, rb, features)
        send_ref[:, place] = part[half:].reshape(count // 2, rb, features)
        term = dot_nt(grad, w_ref[...])
        total = term if total is None else total + term
    stream = stream_ref[...]
    root = lax.rsqrt(jnp.sum(stream * stream, axis=1, keepdims=True) / features + EPS)
    unit = stream * root
    gain_grad_ref[...] = jnp.sum(total * unit, axis=0, keepdims=True)
    pulled = total * gain_ref[...]
    mean = jnp.sum(unit * pulled, axis=1, keepdims=True) / features
    out_ref[...] = grad_ref[...] + root * (pulled - unit * mean)


def project_back(info, dq, dk, dk_got, dv, dv_got, normed, stream, grad, gain, wq, wk, wv, count):
    tokens, features = dq.shape
    rb = features // count
    low = jnp.bfloat16
    piece = jax.ShapeDtypeStruct((count // 2, 3, rb, features), low)
    return pl.pallas_call(
        functools.partial(project_back_kernel, count),
        out_shape=[
            piece,
            piece,
            jax.ShapeDtypeStruct((tokens, features), jnp.float32),
            jax.ShapeDtypeStruct((1, features), jnp.float32),
        ],
        in_specs=[SMEM] + [VMEM] * 12,
        out_specs=[VMEM] * 4,
        scratch_shapes=[
            pltpu.VMEM((features, tokens), low),
            pltpu.VMEM((features, tokens), low),
        ],
        compiler_params=params(48),
        cost_estimate=cost(12 * tokens * features * features, 20e6),
        name="project_back",
    )(info, dq, dk, dk_got, dv, dv_got, normed, stream, grad, gain, wq, wk, wv)


AXES = ("batch", "seq")


def across_cores(x):
    count = lax.axis_size("batch")
    return lax.ppermute(x, "batch", [(i, i ^ 1) for i in range(count)])


def bits_of(count):
    return count.bit_length() - 1


def over_batch(keep, send, split):
    got = across_cores(send)
    levels = bits_of(keep.shape[0])
    parts = []
    for piece, order in ((slice(0, split), range(levels)), (slice(split, None), reversed(range(levels)))):
        if not keep[:1, piece].size:
            continue
        part = (
            keep[:, piece].astype(jnp.float32) + got[:, piece].astype(jnp.float32)
        ).astype(jnp.bfloat16)
        done = []
        for bit in order:
            part = halve_step_at(part, bit, done)
            done.append(bit)
        parts.append(part[0])
    return parts


def halve_step_at(part, bit, done):
    count = lax.axis_size("batch")
    place = bit - sum(1 for other in done if other < bit)
    lead = part.shape[0]
    low = 1 << place
    split = part.reshape((lead // (2 * low), 2, low) + part.shape[1:])
    keep = split[:, 0].reshape((lead // 2,) + part.shape[1:])
    send = split[:, 1].reshape((lead // 2,) + part.shape[1:])
    got = lax.ppermute(send, "batch", [(i, i ^ (2 << bit)) for i in range(count)])
    return (keep.astype(jnp.float32) + got.astype(jnp.float32)).astype(jnp.bfloat16)


def over_seq(blocks):
    count = lax.axis_size("seq")
    place = lax.axis_index("seq")
    total = lax.dynamic_index_in_dim(blocks, place, 0, keepdims=False).astype(jnp.float32)
    for d in range(1, count):
        send = lax.dynamic_index_in_dim(blocks, place ^ d, 0, keepdims=False)
        got = lax.ppermute(send, "seq", [(i, i ^ d) for i in range(count)])
        total = total + got.astype(jnp.float32)
    return total


def sum_all(pack):
    count = lax.axis_size("batch")
    chips = count // 2
    me = lax.axis_index("batch")
    chip = me // 2
    core = me % 2
    seqs = lax.axis_size("seq")
    rows, features = pack.shape
    unit = 16 * count
    padded = jnp.pad(pack, ((0, -rows % unit), (0, 0))).astype(jnp.bfloat16)
    blocks = padded.reshape(2, chips, -1, features)
    got = across_cores(lax.dynamic_index_in_dim(blocks, 1 - core, 0, keepdims=False))
    mine = lax.dynamic_index_in_dim(blocks, core, 0, keepdims=False)
    mine = (mine.astype(jnp.float32) + got.astype(jnp.float32)).astype(jnp.bfloat16)
    terms = [lax.dynamic_index_in_dim(mine, chip, 0, keepdims=False)]
    for d in range(1, chips):
        send = lax.dynamic_index_in_dim(mine, chip ^ d, 0, keepdims=False)
        terms.append(lax.ppermute(send, "batch", [(i, i ^ (2 * d)) for i in range(count)]))
    terms = [term.astype(jnp.float32) for term in terms]
    while len(terms) > 1:
        terms = [terms[i] + terms[i + 1] for i in range(0, len(terms), 2)]
    total = terms[0].astype(jnp.bfloat16)
    terms = [total] + [
        lax.ppermute(total, "seq", [(i, i ^ d) for i in range(seqs)]) for d in range(1, seqs)
    ]
    terms = [term.astype(jnp.float32) for term in terms]
    while len(terms) > 1:
        terms = [terms[i] + terms[i + 1] for i in range(0, len(terms), 2)]
    total = terms[0].astype(jnp.bfloat16)
    shares = [total] + [
        lax.ppermute(total, "batch", [(i, i ^ (2 * d)) for i in range(count)])
        for d in range(1, chips)
    ]
    stacked = jnp.stack(shares)
    mine = jnp.take(stacked, jnp.arange(chips) ^ chip, axis=0)
    other = across_cores(mine)
    first = jnp.where(core == 0, mine, other)
    second = jnp.where(core == 0, other, mine)
    whole = jnp.stack([first, second]).reshape(-1, features)
    return whole[:rows].astype(jnp.float32)


class Plan:
    def __init__(self, held):
        self.count = lax.axis_size("batch")
        self.seqs = lax.axis_size("seq")
        self.held = held
        self.group = self.seqs // (2 * held)
        me = lax.axis_index("batch")
        place = lax.axis_index("seq")
        self.me, self.place = me, place
        self.core = me % 2
        self.row = place // self.group
        self.part = 2 * (place % self.group) + self.core
        self.parts = 2 * self.group
        self.perms = []
        for phase in range(held):
            perm = []
            for b in range(self.count):
                for s in range(self.seqs):
                    row = held * (b % 2) + (s + phase) % held
                    part = s // held
                    target = (b - b % 2 + part % 2, self.group * row + part // 2)
                    perm.append((b * self.seqs + s, target[0] * self.seqs + target[1]))
            self.perms.append(perm)

    def parts_of(self, x):
        parts = []
        for phase, perm in enumerate(self.perms):
            send = lax.dynamic_index_in_dim(x, (self.place + phase) % self.held, 0, keepdims=False)
            parts.append(lax.ppermute(send, AXES, perm))
        return parts

    def to_rows(self, x):
        held = self.held
        stacked = jnp.stack(self.parts_of(x))
        order = (self.row - jnp.arange(held)) % held
        taken = jnp.take(stacked, order, axis=0)
        return taken.reshape((-1,) + x.shape[2:])

    def from_rows(self, y):
        held = self.held
        blocks = y.reshape((held, -1) + y.shape[1:])
        parts = []
        for phase, perm in enumerate(self.perms):
            send = lax.dynamic_index_in_dim(
                blocks, (self.row - phase) % held, 0, keepdims=False
            )
            parts.append(lax.ppermute(send, AXES, [(b, a) for a, b in perm]))
        stacked = jnp.stack(parts)
        order = (jnp.arange(held) - self.place) % held
        return jnp.take(stacked, order, axis=0)

    def halo(self, x, width):
        ends = jnp.concatenate([x[:width], x[-width:]])
        other = across_cores(ends)
        before, after = other[width:], other[:width]
        far = jnp.full_like(before, -1)
        if self.group > 1:
            perm = []
            for b in range(self.count):
                for s in range(self.seqs):
                    if b % 2 == 1 and (s + 1) % self.group:
                        perm.append((b * self.seqs + s, (b - 1) * self.seqs + s + 1))
                    if b % 2 == 0 and s % self.group:
                        perm.append((b * self.seqs + s, (b + 1) * self.seqs + s - 1))
            there = lax.ppermute(ends, AXES, perm)
            inside = jnp.where(self.core == 0, self.part > 0, self.part < self.parts - 1)
            far = jnp.where(inside, jnp.where(self.core == 0, there[width:], there[:width]), -1)
        low = jnp.where(self.core == 1, before, far)
        high = jnp.where(self.core == 0, after, far)
        return jnp.concatenate([low, x, high])

    def gather(self, x):
        other = across_cores(x)
        pair = jnp.stack([jnp.where(self.core == 0, x, other), jnp.where(self.core == 0, other, x)])
        if self.group > 1:
            groups = [
                list(range(first, first + self.group))
                for first in range(0, self.seqs, self.group)
            ]
            pair = lax.all_gather(pair, "seq", axis_index_groups=groups)
        return pair.reshape((-1,) + x.shape[1:])

    def scatter(self, x):
        if self.group > 1:
            groups = [
                list(range(first, first + self.group))
                for first in range(0, self.seqs, self.group)
            ]
            x = lax.psum_scatter(
                x, "seq", scatter_dimension=0, axis_index_groups=groups, tiled=True
            )
        pair = x.reshape((2, -1) + x.shape[1:])
        got = across_cores(lax.dynamic_index_in_dim(pair, 1 - self.core, 0, keepdims=False))
        mine = lax.dynamic_index_in_dim(pair, self.core, 0, keepdims=False)
        return mine.astype(jnp.float32) + got.astype(jnp.float32)


def shards(
    byte_values,
    segments,
    byte_mask,
    embedding,
    filter_weight,
    score_weight,
    first_gain,
    query_weight,
    key_weight,
    value_weight,
    merge_weight,
    position_bias,
    second_gain,
    gate_weight,
    up_weight,
    down_weight,
    cotangent,
):
    count = lax.axis_size("batch")
    seqs = lax.axis_size("seq")
    held, width = byte_values.shape
    row_len = segments.shape[1]
    vocab, features = embedding.shape
    hidden_size = gate_weight.shape[1]
    heads = position_bias.shape[1]
    bucket_count = position_bias.shape[0]
    total = row_len // 2
    plan = Plan(held)
    tokens = total // plan.parts
    rb, cb = features // count, hidden_size // count
    blocks = tokens // BLOCK
    other_part = plan.part ^ 1

    bases = [plan.part * blocks, other_part * blocks] if plan.group == 1 else [0, 0]
    info = jnp.stack(
        [
            jnp.asarray(value, jnp.int32)
            for value in (
                plan.me,
                plan.core,
                plan.row % held,
                plan.part * blocks,
                plan.part * 2 * tokens,
                bases[0],
                bases[1],
                0,
            )
        ]
    )
    ids = plan.to_rows(jnp.where(byte_mask > 0, byte_values, -1))
    ids = plan.halo(ids, 4).reshape(-1, 4).T
    groups = tokens // 2
    spare = -(groups + 2) % 8
    ids = jnp.concatenate(
        [ids[:, 1:], jnp.full((4, spare), -1, jnp.int32), ids[:, :1]], axis=1
    )[:, :, None]
    bias = bias_tiles(position_bias)
    words = -(-vocab // LANES) * LANES
    emb = jnp.pad(embedding, ((0, words - vocab), (0, 0)))
    score_row = score_weight[None]
    gain_one, gain_two = first_gain[None], second_gain[None]
    stream, normed, q, k, v = mixer_forward(
        info,
        ids,
        emb,
        filter_weight,
        score_row,
        gain_one,
        query_weight,
        key_weight,
        value_weight,
        tokens,
        row_len,
    )
    if plan.group == 1:
        ks, vs = [k, across_cores(k)], [v, across_cores(v)]
    else:
        ks, vs = [plan.gather(k)], [plan.gather(v)]
    cots = plan.parts_of(cotangent)
    token_segments = segments[:, ::2]
    other_segments = across_cores(token_segments)
    both = jnp.concatenate([token_segments, other_segments])
    own_first = jnp.where(plan.row // held == plan.core, 0, held)
    row_segments = lax.dynamic_index_in_dim(both, own_first + plan.row % held, 0, keepdims=False)
    local_segments = lax.dynamic_slice_in_dim(row_segments, plan.part * tokens, tokens, 0)
    seg_row, seg_col = local_segments[None], row_segments[:, None]

    att, lse, resid, normed_two = attention_forward(
        info, stream, q, ks, vs, bias, seg_row, seg_col, merge_weight, gain_two
    )
    result, grad_two, gu_keep, gu_send, d_keep, d_send = feed_forward(
        info, normed_two, resid, cots, gate_weight, up_weight, down_weight, count
    )
    layer_output = plan.from_rows(result)
    chips = count // 2
    gu = over_batch(
        gu_keep.reshape(chips, 2 * count, rb, cb), gu_send.reshape(chips, 2 * count, rb, cb), count
    )
    dd = over_batch(d_keep, d_send, count // 2)

    grad_resid, att_grad, m_keep, m_send, second_part = between(
        info, grad_two, resid, gain_two, cots, att, merge_weight, count
    )
    merged = over_batch(m_keep[:, None], m_send[:, None], 1)
    dq, dks, dvs, tiles = attention_backward(
        info, q, att_grad, ks, vs, bias, seg_row, seg_col, lse
    )
    if plan.group == 1:
        dk, dk_got = dks[0], across_cores(dks[1])
        dv, dv_got = dvs[0], across_cores(dvs[1])
    else:
        dk, dv = plan.scatter(dks[0]).astype(jnp.bfloat16), plan.scatter(dvs[0]).astype(jnp.bfloat16)
        dk_got, dv_got = jnp.zeros_like(dk), jnp.zeros_like(dv)
    bias_part = bucket_sums(tiles, bucket_count)
    p_keep, p_send, grad_stream, first_part = project_back(
        info,
        dq,
        dk,
        dk_got,
        dv,
        dv_got,
        normed,
        stream,
        grad_resid,
        gain_one,
        query_weight,
        key_weight,
        value_weight,
        count,
    )
    mixed = over_batch(p_keep, p_send, 1)
    embed_part, small = mixer_backward(
        info, ids, emb, filter_weight, score_row, grad_stream, row_len
    )

    def feed_share(x):
        return over_seq(x.reshape(seqs, count // seqs, rb, cb))

    def mix_share(x):
        x = x.reshape(x.shape[0], rb, seqs, features // seqs).transpose(2, 0, 1, 3)
        return over_seq(x)

    gate_grad = feed_share(gu[0]).transpose(1, 0, 2).reshape(rb, -1)
    up_grad = feed_share(gu[1]).transpose(1, 0, 2).reshape(rb, -1)
    down_grad = feed_share(jnp.concatenate(dd)).reshape(-1, cb).T
    shares = mix_share(jnp.concatenate(merged + mixed))
    bias_row = jnp.pad(bias_part.T.reshape(1, -1), ((0, 0), (0, features - bias_part.size)))
    pack = jnp.concatenate([embed_part[:vocab], small[:5], first_part, second_part, bias_row])
    pack = sum_all(pack)
    return (
        layer_output,
        pack[:vocab],
        pack[vocab : vocab + 4],
        pack[vocab + 4],
        pack[vocab + 5],
        shares[1],
        shares[2],
        shares[3],
        shares[0],
        pack[vocab + 7, : bias_part.size].reshape(bucket_count, heads),
        pack[vocab + 6],
        gate_grad,
        up_grad,
        down_grad,
    )


def solution(mesh):
    in_specs = (
        P("batch", "seq"),
        P("batch", None),
        P("batch", "seq"),
        P(),
        P(),
        P(),
        P(),
        P(),
        P(),
        P(),
        P(),
        P(),
        P(),
        P(),
        P(),
        P(),
        P("batch", "seq", None),
    )
    out_specs = (
        P("batch", "seq", None),
        P(),
        P(),
        P(),
        P(),
        P("batch", "seq"),
        P("batch", "seq"),
        P("batch", "seq"),
        P("batch", "seq"),
        P(),
        P(),
        P("batch", "seq"),
        P("batch", "seq"),
        P("batch", "seq"),
    )
    return jax.shard_map(shards, mesh=mesh, in_specs=in_specs, out_specs=out_specs, check_vma=False)
```

```python
import functools

import jax
import jax.numpy as jnp
from jax import lax
from jax.experimental import pallas as pl
from jax.experimental.pallas import tpu as pltpu
from jax.sharding import PartitionSpec as P

EPS = 1e-06
LIMITS = (12, 16, 23, 32, 46, 64, 91)
NEG = -1e30
LANES = 128
BLOCK = 128
FAR = 2
CUBE = 0.044715
SLOPE = 0.7978845608028654
MEGA = 1 << 20


def dot(a, b):
    return lax.dot_general(a, b, (((1,), (0,)), ((), ())), preferred_element_type=jnp.float32)


def dot_nt(a, b):
    return lax.dot_general(a, b, (((1,), (1,)), ((), ())), preferred_element_type=jnp.float32)


def params(megabytes):
    return pltpu.CompilerParams(vmem_limit_bytes=megabytes * MEGA)


def cost(microseconds):
    return pl.CostEstimate(flops=int(microseconds * 1e+09), bytes_accessed=1, transcendentals=0)


VMEM = pl.BlockSpec(memory_space=pltpu.VMEM)
ANY = pl.BlockSpec(memory_space=pl.ANY)
HBM = pl.BlockSpec(memory_space=pltpu.HBM)
SMEM = pl.BlockSpec(memory_space=pltpu.SMEM)


def hbm(x):
    return pltpu.with_memory_space_constraint(x, pltpu.HBM)


def ordered(kernel, inputs, after):
    def with_others(*refs):
        kernel(*refs[:inputs], *refs[inputs + len(after) :])

    return with_others


def launch(name, kernel, ins, in_specs, outs, out_specs, megabytes, scratch=(), after=(), carry=(), microseconds=1.0
):
    given, made = len(ins), len(outs)
    skip = len(after) + len(carry)

    def body(*refs):
        rest = refs[given + skip :]
        kernel(*refs[:given], *rest[:made], *rest[made + len(carry) :])

    results = pl.pallas_call(
        body,
        out_shape=[*outs, *[jax.ShapeDtypeStruct(x.shape, x.dtype) for x in carry]],
        in_specs=[*in_specs, *[ANY] * skip],
        out_specs=[*out_specs, *[ANY] * len(carry)],
        scratch_shapes=list(scratch),
        input_output_aliases={given + len(after) + i: made + i for i in range(len(carry))},
        compiler_params=params(megabytes),
        cost_estimate=cost(microseconds),
        name=name,
    )(*ins, *after, *carry)
    return results[:made], results[made:]


def bias_kernel(table_ref, out_ref):
    heads = out_ref.shape[0]
    spread = lax.broadcasted_iota(jnp.int32, (BLOCK, BLOCK), 0) - lax.broadcasted_iota(
        jnp.int32, (BLOCK, BLOCK), 1
    )

    def one_head(h, carry):
        def chain(distance, first):
            value = jnp.full((BLOCK, BLOCK), table_ref[first + 15, h], jnp.float32)
            for place in reversed(range(7)):
                value = jnp.where(distance < LIMITS[place], table_ref[first + 8 + place, h], value)
            for near in reversed(range(8)):
                value = jnp.where(distance < near + 1, table_ref[first + near, h], value)
            return value

        out_ref[h, 0] = jnp.full((BLOCK, BLOCK), table_ref[15, h], jnp.float32)
        out_ref[h, 1] = chain(BLOCK - spread, 0)
        before = chain(-spread, 0)
        after = chain(spread, 16)
        out_ref[h, 2] = jnp.where(spread > 0, after, before)
        out_ref[h, 3] = chain(BLOCK + spread, 16)
        out_ref[h, 4] = jnp.full((BLOCK, BLOCK), table_ref[31, h], jnp.float32)
        return carry

    lax.fori_loop(0, heads, one_head, 0)


def bias_tiles(table):
    heads = table.shape[1]
    shape = (heads, 2 * FAR + 1, BLOCK, BLOCK)
    return pl.pallas_call(
        bias_kernel,
        out_shape=jax.ShapeDtypeStruct(shape, jnp.float32),
        in_specs=[SMEM],
        out_specs=VMEM,
        compiler_params=params(8),
        cost_estimate=cost(2.6),
        name="bias_tiles",
    )(table)


def chunk_of(c):
    return pl.ds(pl.multiple_of(c * LANES, LANES), LANES)


def down(x):
    return pltpu.roll(x, 1, 0)


def up(x):
    return pltpu.roll(x, x.shape[0] - 1, 0)


def lane_sum(x):
    return jnp.broadcast_to(jnp.sum(x, axis=1, keepdims=True), x.shape)


def offsets_of(rows):
    return {
        -2: down(rows[2]),
        -1: down(rows[3]),
        0: rows[0],
        1: rows[1],
        2: rows[2],
        3: rows[3],
        4: up(rows[0]),
        5: up(rows[1]),
    }


def spread_of(phase, j, one, two, three, four, coefs):
    pair = j - j % 2
    third = three / 3.0
    zero = jnp.zeros_like(third)
    half, quarter = two * 0.5, four * 0.25

    def add(o, value):
        coefs[o] = coefs[o] + value if o in coefs else value

    add(j, one + third)
    for o in (pair, pair + 1):
        add(o, half)
    for o in range(4):
        add(o, quarter)
    add(j + 1, jnp.where(phase <= 1, third, zero))
    add(j + 2, jnp.where(phase == 0, third, zero))
    add(j - 1, jnp.where(phase >= 1, third, zero))
    add(j - 2, jnp.where(phase == 2, third, zero))


def pooled_dots(phase, j, dots):
    pair = j - j % 2
    zero = jnp.zeros_like(dots[0])
    two = 0.5 * (dots[pair] + dots[pair + 1])
    four = 0.25 * ((dots[0] + dots[1]) + (dots[2] + dots[3]))
    three = dots[j] + jnp.where(phase <= 1, dots[j + 1], zero)
    three = three + jnp.where(phase == 0, dots[j + 2], zero)
    three = three + jnp.where(phase >= 1, dots[j - 1], zero)
    three = three + jnp.where(phase == 2, dots[j - 2], zero)
    return dots[j], two, three / 3.0, four


def convolve(e, taps):
    em2, em3, ep0 = down(e[2]), down(e[3]), up(e[0])
    f0, f1, f2, f3 = taps
    return [
        f0 * em2 + f1 * em3 + f2 * e[0] + f3 * e[1],
        f0 * em3 + f1 * e[0] + f2 * e[1] + f3 * e[2],
        f0 * e[0] + f1 * e[1] + f2 * e[2] + f3 * e[3],
        f0 * e[1] + f1 * e[2] + f2 * e[3] + f3 * ep0,
    ]


def mixer_weights(info_ref, ids_ref, emb_ref, filt_ref, score_ref, e_ref, c_ref, acc_ref, row_len):
    count = ids_ref.shape[0]
    words, features = emb_ref.shape
    chunks = features // LANES
    group = info_ref[4] // 4
    vocab = lax.broadcasted_iota(jnp.int32, (count, words), 1)
    for j in range(4):
        hot = jnp.where(ids_ref[:, j : j + 1] == vocab, 1.0, 0.0).astype(jnp.bfloat16)
        e_ref[j] = dot(hot, emb_ref[...])
        acc_ref[j] = jnp.zeros((count, LANES), jnp.float32)

    def one_chunk(c, carry):
        lanes = chunk_of(c)
        e = [e_ref[j, :, lanes] for j in range(4)]
        conv = convolve(e, [filt_ref[k : k + 1, lanes] for k in range(4)])
        for j in range(4):
            c_ref[j, :, lanes] = conv[j]
            acc_ref[j] += conv[j] * score_ref[:1, lanes]
        return carry

    lax.fori_loop(0, chunks, one_chunk, 0)
    rows = lax.broadcasted_iota(jnp.int32, (count, LANES), 0)
    places = jnp.where(rows == count - 1, -1, rows) + group
    inside = [(4 * places + j < row_len) for j in range(4)]
    dots = [jnp.where(inside[j], lane_sum(acc_ref[j]), 0.0) for j in range(4)]
    dots = offsets_of(dots)
    phases, weights = [], []
    for j in range(4):
        phase = lax.rem(places + 3 + j, 3)
        scores = pooled_dots(phase, j, dots)
        highest = jnp.maximum(jnp.maximum(scores[0], scores[1]), jnp.maximum(scores[2], scores[3]))
        powers = [jnp.exp(score - highest) for score in scores]
        share = 1.0 / ((powers[0] + powers[1]) + (powers[2] + powers[3]))
        phases.append(phase)
        weights.append([power * share for power in powers])
    limits = {o: (4 * places + o < row_len) for o in (4, 5)}
    return phases, weights, limits


def token_coefs(phases, weights, limits, scale):
    result = []
    for h in range(2):
        coefs = {}
        for j in (2 * h, 2 * h + 1):
            spread_of(phases[j], j, *weights[j], coefs)
        for o in coefs:
            if o in limits:
                coefs[o] = jnp.where(limits[o], coefs[o], 0.0)
            coefs[o] = coefs[o] * scale
        result.append(coefs)
    return result


def mixer_kernel(
    row_len,
    info_ref,
    ids_ref,
    emb_ref,
    filt_ref,
    score_ref,
    wq_ref,
    wk_ref,
    wv_ref,
    stream_ref,
    normed_ref,
    q_ref,
    kv_ref,
    e_ref,
    c_ref,
    acc_ref,
    coef_ref,
    square_ref,
    root_ref,
    weight_ref,
    sems,
):
    copies = [
        pltpu.make_async_copy(w_ref, weight_ref.at[i], sems.at[i])
        for i, w_ref in enumerate((wk_ref, wv_ref, wq_ref))
    ]
    for copy in copies:
        copy.start()
    tokens, features = stream_ref.shape
    groups = tokens // 2
    chunks = features // LANES
    phases, weights, limits = mixer_weights(
        info_ref, ids_ref, emb_ref, filt_ref, score_ref, e_ref, c_ref, acc_ref, row_len
    )
    coefs = token_coefs(phases, weights, limits, 0.5)
    names = [(h, o) for h in range(2) for o in sorted(coefs[h])]
    for place, (h, o) in enumerate(names):
        coef_ref[place] = coefs[h][o][:groups]
    square_ref[...] = jnp.zeros_like(square_ref)

    def one_chunk(c, carry):
        lanes = chunk_of(c)
        conv = {
            o: value[:groups]
            for o, value in offsets_of([c_ref[j, :, lanes] for j in range(4)]).items()
        }
        for h in range(2):
            mixed = None
            for place, (side, o) in enumerate(names):
                if side == h:
                    term = coef_ref[place] * conv[o]
                    mixed = term if mixed is None else mixed + term
            root_ref[pl.ds(h, groups, stride=2), :] = mixed
            square_ref[h] += mixed * mixed
        stream_ref[:, lanes] = root_ref[...]
        return carry

    lax.fori_loop(0, chunks, one_chunk, 0)
    for h in range(2):
        root = lax.rsqrt(lane_sum(square_ref[h]) / features + EPS)
        root_ref[pl.ds(h, groups, stride=2), :] = root

    def norm_chunk(c, carry):
        lanes = chunk_of(c)
        normed = stream_ref[:, lanes] * root_ref[...] * score_ref[1:2, lanes]
        normed_ref[:, lanes] = normed.astype(jnp.bfloat16)
        return carry

    lax.fori_loop(0, chunks, norm_chunk, 0)
    for i in range(2):
        copies[i].wait()
        kv_ref[i] = dot(normed_ref[...], weight_ref[i]).astype(jnp.bfloat16)
    copies[2].wait()
    q_ref[...] = dot(normed_ref[...], weight_ref[2]).astype(jnp.bfloat16)


def mixer_forward(info, ids, emb, filt, score, wq, wk, wv, tokens, row_len, after):
    features = emb.shape[1]
    count = ids.shape[0]
    groups = tokens // 2
    low = jax.ShapeDtypeStruct((tokens, features), jnp.bfloat16)
    full = jax.ShapeDtypeStruct((tokens, features), jnp.float32)
    return pl.pallas_call(
        ordered(functools.partial(mixer_kernel, row_len), 8, after),
        out_shape=[
            full,
            low,
            low,
            jax.ShapeDtypeStruct((2, tokens, features), jnp.bfloat16),
        ],
        in_specs=[SMEM] + [VMEM] * 4 + [HBM] * 3 + [ANY] * len(after),
        out_specs=[VMEM] * 4,
        scratch_shapes=[
            pltpu.VMEM((4, count, features), jnp.float32),
            pltpu.VMEM((4, count, features), jnp.float32),
            pltpu.VMEM((4, count, LANES), jnp.float32),
            pltpu.VMEM((12, groups, LANES), jnp.float32),
            pltpu.VMEM((2, groups, LANES), jnp.float32),
            pltpu.VMEM((tokens, LANES), jnp.float32),
            pltpu.VMEM((3, features, features), jnp.bfloat16),
            pltpu.SemaphoreType.DMA((3,)),
        ],
        compiler_params=params(24),
        cost_estimate=cost(10),
        name="mixer_forward",
    )(info, ids, emb, filt, score, wq, wk, wv, *after)


def mixer_back_kernel(
    row_len,
    vocab_size,
    info_ref,
    ids_ref,
    emb_ref,
    filt_ref,
    score_ref,
    grad_ref,
    first_ref,
    second_ref,
    bias_ref,
    *refs,
):
    (
        keep_ref,
        send_ref,
        e_ref,
        c_ref,
        acc_ref,
        coef_ref,
        dots_ref,
        high_ref,
        low_ref,
        turn_ref,
        embed_ref,
        small_ref,
    ) = refs[-12:]
    tokens, features = grad_ref.shape
    groups = tokens // 2
    chunks = features // LANES
    count = ids_ref.shape[0]
    phases, weights, limits = mixer_weights(
        info_ref, ids_ref, emb_ref, filt_ref, score_ref, e_ref, c_ref, acc_ref, row_len
    )
    coefs = token_coefs(phases, weights, limits, 0.5)
    names = [(h, o) for h in range(2) for o in sorted(coefs[h])]
    empty = jnp.zeros((count - groups, LANES), jnp.float32)
    dots_ref[...] = jnp.zeros_like(dots_ref)

    def token_grads(lanes):
        turn_ref[...] = grad_ref[:, lanes]
        return [
            jnp.concatenate([turn_ref[pl.ds(h, groups, stride=2), :], empty], axis=0)
            for h in range(2)
        ]

    def dots_chunk(c, carry):
        lanes = chunk_of(c)
        conv = offsets_of([c_ref[j, :, lanes] for j in range(4)])
        grads = token_grads(lanes)
        for place, (h, o) in enumerate(names):
            dots_ref[place] += grads[h] * conv[o]
        return carry

    lax.fori_loop(0, chunks, dots_chunk, 0)
    pulls = []
    for h in range(2):
        dots = {}
        for place, (side, o) in enumerate(names):
            if side == h:
                value = lane_sum(dots_ref[place]) * 0.5
                dots[o] = jnp.where(limits[o], value, 0.0) if o in limits else value
        for j in (2 * h, 2 * h + 1):
            grads = pooled_dots(phases[j], j, dots)
            mean = sum(weights[j][i] * grads[i] for i in range(4))
            pulls.append([weights[j][i] * (grads[i] - mean) for i in range(4)])
    score_coefs = token_coefs(phases, pulls, limits, 1.0)

    def gathered(by_token):
        first, second = by_token
        return [
            first[0] + second[0] + down(second[4]),
            first[1] + second[1] + down(second[5]),
            first[2] + second[2] + up(first[-2]),
            first[3] + second[3] + up(first[-1]),
        ]

    kappas = gathered(score_coefs)
    for j in range(4):
        coef_ref[4 * j] = coefs[0][j]
        coef_ref[4 * j + 1] = coefs[1][j]
        coef_ref[4 * j + 2] = down(coefs[1][4 + j]) if j < 2 else up(coefs[0][j - 4])
        coef_ref[4 * j + 3] = kappas[j]
    small_ref[...] = jnp.zeros_like(small_ref)

    def total(x):
        return jnp.sum(x, axis=0, keepdims=True)

    def grad_chunk(c, carry):
        lanes = chunk_of(c)
        first, second = token_grads(lanes)
        above, below = down(second), up(first)
        score = score_ref[:1, lanes]
        taps = [filt_ref[k : k + 1, lanes] for k in range(4)]
        e = [e_ref[j, :, lanes] for j in range(4)]
        near = offsets_of(e)
        d = []
        score_sum = jnp.zeros((1, LANES), jnp.float32)
        tap_sums = [jnp.zeros((1, LANES), jnp.float32) for _ in range(4)]
        for j in range(4):
            beside = above if j < 2 else below
            kappa = coef_ref[4 * j + 3]
            value = (
                coef_ref[4 * j] * first
                + coef_ref[4 * j + 1] * second
                + coef_ref[4 * j + 2] * beside
                + kappa * score
            )
            d.append(value)
            score_sum = score_sum + total(kappa * c_ref[j, :, lanes])
            for k in range(4):
                tap_sums[k] = tap_sums[k] + total(value * near[j + k - 2])
        for k in range(4):
            small_ref[k : k + 1, lanes] = tap_sums[k]
        small_ref[4:5, lanes] = score_sum
        f0, f1, f2, f3 = taps
        d3m, d0p, d1p = down(d[3]), up(d[0]), up(d[1])
        back = [
            f0 * d[2] + f1 * d[1] + f2 * d[0] + f3 * d3m,
            f0 * d[3] + f1 * d[2] + f2 * d[1] + f3 * d[0],
            f0 * d0p + f1 * d[3] + f2 * d[2] + f3 * d[1],
            f0 * d1p + f1 * d0p + f2 * d[3] + f3 * d[2],
        ]
        for j in range(4):
            high = back[j].astype(jnp.bfloat16)
            high_ref[j * count : (j + 1) * count, lanes] = high
            low_ref[j * count : (j + 1) * count, lanes] = (
                back[j] - high.astype(jnp.float32)
            ).astype(jnp.bfloat16)
        return carry

    lax.fori_loop(0, chunks, grad_chunk, 0)
    vocab = lax.broadcasted_iota(jnp.int32, (embed_ref.shape[0], count), 0)
    lane = lax.broadcasted_iota(jnp.int32, (count, LANES), 1)
    spread = jnp.zeros((count, LANES), jnp.float32)
    for j in range(4):
        spread = jnp.where(lane == j, ids_ref[:, j : j + 1].astype(jnp.float32), spread)
    spare = jnp.zeros((-count % LANES, LANES), jnp.float32)
    flat = jnp.concatenate([spread, spare], axis=0).T.astype(jnp.int32)
    hot = [
        jnp.where(flat[j : j + 1, :count] == vocab, 1.0, 0.0).astype(jnp.bfloat16) for j in range(4)
    ]
    total_grad = None
    for j in range(4):
        rows = slice(j * count, (j + 1) * count)
        here = dot(hot[j], high_ref[rows]) + dot(hot[j], low_ref[rows])
        total_grad = here if total_grad is None else total_grad + here
    embed_ref[...] = total_grad
    embed_ref[vocab_size : vocab_size + 5] = small_ref[:5]
    embed_ref[vocab_size + 5 : vocab_size + 6] = first_ref[...]
    embed_ref[vocab_size + 6 : vocab_size + 7] = second_ref[...]
    heads = bias_ref.shape[0]
    embed_ref[vocab_size + 7 : vocab_size + 7 + heads, :LANES] = bias_ref[...]
    share = keep_ref.shape[1]
    chips = keep_ref.shape[0]
    me = info_ref[0]
    for place in range(chips):
        for odd, out_ref in enumerate((keep_ref, send_ref)):
            start = pl.multiple_of((me ^ (2 * place + odd)) * share, 16)
            out_ref[place] = embed_ref[pl.ds(start, share), :].astype(jnp.bfloat16)


def mixer_backward(info, ids, emb, filt, score, grad, first, second, bias, row_len, vocab, embed_rows, devices, after):
    tokens, features = grad.shape
    count = ids.shape[0]
    words = embed_rows
    return pl.pallas_call(
        functools.partial(mixer_back_kernel, row_len, vocab),
        out_shape=[jax.ShapeDtypeStruct((devices // 2, words // devices, features), jnp.bfloat16)] * 2,
        in_specs=[SMEM] + [VMEM] * 8 + [ANY] * len(after),
        out_specs=[VMEM] * 2,
        scratch_shapes=[
            pltpu.VMEM((4, count, features), jnp.float32),
            pltpu.VMEM((4, count, features), jnp.float32),
            pltpu.VMEM((4, count, LANES), jnp.float32),
            pltpu.VMEM((16, count, LANES), jnp.float32),
            pltpu.VMEM((12, count, LANES), jnp.float32),
            pltpu.VMEM((4 * count, features), jnp.bfloat16),
            pltpu.VMEM((4 * count, features), jnp.bfloat16),
            pltpu.VMEM((tokens, LANES), jnp.float32),
            pltpu.VMEM((words, features), jnp.float32),
            pltpu.VMEM((8, features), jnp.float32),
        ],
        compiler_params=params(22),
        cost_estimate=cost(15.6),
        name="mixer_backward",
    )(info, ids, emb, filt, score, grad, first, second, bias, *after)


def segments_at(cut_ref, place):
    return sum(jnp.where(place >= cut_ref[i], 1, 0) for i in range(3))


def scores_of(info_ref, part, h, k_ref, q_low, bias_ref, cut_ref):
    keys, tokens = k_ref.shape[0], q_low.shape[0]
    base = info_ref[part]
    raw = dot_nt(k_ref[...], q_low)
    own = info_ref[3]
    seg_row = segments_at(cut_ref, own * BLOCK + lax.broadcasted_iota(jnp.int32, (1, tokens), 1))
    column = lax.broadcasted_iota(jnp.int32, (BLOCK, 1), 0)
    rows = []
    for kb in range(keys // BLOCK):
        tiles = [
            bias_ref[h, jnp.clip(base + kb - own - qb, -FAR, FAR) + FAR]
            for qb in range(tokens // BLOCK)
        ]
        value = raw[kb * BLOCK : (kb + 1) * BLOCK] + jnp.concatenate(tiles, axis=1)
        same = segments_at(cut_ref, (base + kb) * BLOCK + column) == seg_row
        rows.append(jnp.where(same, value, NEG))
    return rows


def only_head(x, h, size):
    lane = lax.broadcasted_iota(jnp.int32, x.shape, 1)
    return jnp.where((lane >= h * size) & (lane < (h + 1) * size), x, jnp.zeros_like(x))


def attention_kernel(
    size,
    carried,
    last,
    info_ref,
    q_ref,
    kv_ref,
    bias_ref,
    cut_ref,
    *refs,
):
    if carried:
        before_ref, state_ref, *refs = refs
    if last:
        stream_ref, wm_ref, gain_ref, att_ref, lse_ref, resid_ref, normed_ref = refs
    else:
        mixed_ref, stat_ref = refs
    step = pl.program_id(0)
    part = 5 + carried
    low = []
    for h in range(2):
        q_low = only_head(q_ref[...], h, size)
        rows = scores_of(info_ref, part, h, kv_ref.at[0], q_low, bias_ref, cut_ref)
        highest = None
        for row in rows:
            top = jnp.max(row, axis=0, keepdims=True)
            highest = top if highest is None else jnp.maximum(highest, top)
        if carried:
            highest = jnp.maximum(highest, state_ref[0, h : h + 1])
        powers = [jnp.exp(row - highest) for row in rows]
        summed = None
        for power in powers:
            here = jnp.sum(power, axis=0, keepdims=True)
            summed = here if summed is None else summed + here
        weights = jnp.concatenate([power.astype(jnp.bfloat16) for power in powers], axis=0)
        mixed = dot(kv_ref[1].T[h * size : (h + 1) * size], weights)
        if carried:
            shrink = jnp.exp(state_ref[0, h : h + 1] - highest)
            summed = summed + state_ref[0, 2 + h : 3 + h] * shrink
            mixed = mixed + before_ref[h * size : (h + 1) * size] * shrink
        if last:
            lse_ref[0, h : h + 1] = highest + jnp.log(summed)
            low.append(mixed * (1.0 / summed))
        else:
            stat_ref[0, h : h + 1] = highest
            stat_ref[0, 2 + h : 3 + h] = summed
            mixed_ref[h * size : (h + 1) * size] = mixed
    if not last:
        return
    features = stream_ref.shape[1]
    turned = jnp.concatenate(low, axis=0)
    att_ref[...] = turned.astype(jnp.bfloat16)
    attended = turned.T.astype(jnp.bfloat16)
    added = dot(attended, wm_ref[...])

    @pl.when(step == 0)
    def _():
        resid_ref[...] = stream_ref[...] + added

    @pl.when(step > 0)
    def _():
        resid_ref[...] += added

    @pl.when(step == pl.num_programs(0) - 1)
    def _():
        resid = resid_ref[...]
        root = lax.rsqrt(jnp.sum(resid * resid, axis=1, keepdims=True) / features + EPS)
        normed_ref[...] = (resid * root * gain_ref[2:3]).astype(jnp.bfloat16)


def attention_forward(name, info, q, kv, bias, cuts, carried=(), last=(), after=()):
    tokens, features = q.shape
    heads = bias.shape[0]
    size = features // heads
    pairs = heads // 2
    wide = 2 * size
    whole = lambda shape: pl.BlockSpec(shape, lambda p: (0,) * len(shape))
    by_rows = pl.BlockSpec((wide, tokens), lambda p: (p, 0))
    stat = pl.BlockSpec((1, 8, tokens), lambda p: (p, 0, 0))
    stat_shape = jax.ShapeDtypeStruct((pairs, 8, tokens), jnp.float32)
    ins = [info, q, kv, bias, cuts, *carried, *last]
    in_specs = [
        SMEM,
        pl.BlockSpec((tokens, wide), lambda p: (0, p)),
        pl.BlockSpec((2, kv.shape[1], wide), lambda p: (0, 0, p)),
        pl.BlockSpec((2,) + bias.shape[1:], lambda p: (p, 0, 0, 0)),
        SMEM,
    ]
    if carried:
        in_specs += [by_rows, stat]
    if last:
        stream, wm, gain = last
        in_specs += [
            whole(stream.shape),
            pl.BlockSpec((wide, features), lambda p: (p, 0)),
            whole(gain.shape),
        ]
        shapes = [
            jax.ShapeDtypeStruct((features, tokens), jnp.bfloat16),
            stat_shape,
            jax.ShapeDtypeStruct((tokens, features), jnp.float32),
            jax.ShapeDtypeStruct((tokens, features), jnp.bfloat16),
        ]
        out_specs = [by_rows, stat, whole((tokens, features)), whole((tokens, features))]
    else:
        shapes = [jax.ShapeDtypeStruct((features, tokens), jnp.float32), stat_shape]
        out_specs = [by_rows, stat]
    kernel = functools.partial(attention_kernel, size, int(bool(carried)), bool(last))
    return pl.pallas_call(
        ordered(kernel, len(ins), after),
        grid=(pairs,),
        out_shape=shapes,
        in_specs=in_specs + [ANY] * len(after),
        out_specs=out_specs,
        compiler_params=params(12),
        cost_estimate=cost(9),
        name=name,
    )(*ins, *after)


def attention_back_kernel(
    parts,
    size,
    info_ref,
    q_ref,
    g_ref,
    *refs,
):
    k_refs = [ref.at[0] for ref in refs[:parts]]
    v_refs = [ref.at[1] for ref in refs[:parts]]
    bias_ref, cut_ref, lse_ref = refs[parts : parts + 3]
    dq_ref, *dkv_refs, tile_ref = refs[-2 - parts :]
    tokens = q_ref.shape[0]
    own = info_ref[3]
    turned_keys = [k_ref[...].T for k_ref in k_refs]
    dk = [None] * parts
    dv = [None] * parts
    low = []
    tile_ref[...] = jnp.zeros_like(tile_ref)
    for h in range(2):
        q_low = only_head(q_ref[...], h, size)
        g_low = only_head(g_ref[...], h, size)
        log_total = lse_ref[0, h : h + 1]
        shares, pulls = [], []
        correction = None
        for part in range(parts):
            rows = scores_of(
                info_ref, 5 + part, h, k_refs[part], q_low, bias_ref, cut_ref
            )
            probs = [jnp.exp(row - log_total) for row in rows]
            pull = dot_nt(v_refs[part][...], g_low)
            pull = [pull[i * BLOCK : (i + 1) * BLOCK] for i in range(len(rows))]
            for i in range(len(rows)):
                here = jnp.sum(probs[i] * pull[i], axis=0, keepdims=True)
                correction = here if correction is None else correction + here
            shares.append(probs)
            pulls.append(pull)
        turned = None
        for part in range(parts):
            base = info_ref[5 + part]
            grads = [p * (d - correction) for p, d in zip(shares[part], pulls[part])]
            blocks = tokens // BLOCK
            for delta in range(-blocks + 1, len(grads)):
                tile = None
                for kb in range(len(grads)):
                    qb = kb - delta
                    if 0 <= qb < blocks:
                        here = grads[kb][:, qb * BLOCK : (qb + 1) * BLOCK]
                        tile = here if tile is None else tile + here
                place = jnp.clip(base - own + delta, -FAR, FAR) + FAR
                tile_ref[h, place] += tile
            grads = jnp.concatenate([grad.astype(jnp.bfloat16) for grad in grads], axis=0)
            probs = jnp.concatenate([share.astype(jnp.bfloat16) for share in shares[part]], axis=0)
            term = dot(grads, q_low)
            dk[part] = term if dk[part] is None else dk[part] + term
            term = dot(probs, g_low)
            dv[part] = term if dv[part] is None else dv[part] + term
            term = dot(turned_keys[part][h * size : (h + 1) * size], grads)
            turned = term if turned is None else turned + term
        low.append(turned)
    dq_ref[...] = jnp.concatenate(low, axis=0).T.astype(jnp.bfloat16)
    for part in range(parts):
        dkv_refs[part][0] = dk[part].astype(jnp.bfloat16)
        dkv_refs[part][1] = dv[part].astype(jnp.bfloat16)


def attention_backward(info, q, g, kvs, bias, cuts, lse, after):
    tokens, features = q.shape
    heads = bias.shape[0]
    size = features // heads
    pairs = heads // 2
    parts = len(kvs)
    wide = 2 * size
    by_pair = [pl.BlockSpec((2, x.shape[1], wide), lambda p: (0, 0, p)) for x in kvs]
    own = pl.BlockSpec((tokens, wide), lambda p: (0, p))
    whole = lambda shape: pl.BlockSpec(shape, lambda p: (0,) * len(shape))
    tiles = pl.BlockSpec((2,) + bias.shape[1:], lambda p: (p, 0, 0, 0))
    shapes = [jax.ShapeDtypeStruct(x.shape, jnp.bfloat16) for x in kvs]
    result = pl.pallas_call(
        functools.partial(attention_back_kernel, parts, size),
        grid=(pairs,),
        out_shape=[jax.ShapeDtypeStruct(q.shape, jnp.bfloat16), *shapes]
        + [jax.ShapeDtypeStruct(bias.shape, jnp.float32)],
        in_specs=[
            SMEM,
            own,
            own,
            *by_pair,
            tiles,
            SMEM,
            pl.BlockSpec((1, 8, tokens), lambda p: (p, 0, 0)),
            *[ANY] * len(after),
        ],
        out_specs=[own, *by_pair, tiles],
        compiler_params=params(14),
        cost_estimate=cost(28),
        name="attention_backward",
    )(info, q, g, *kvs, bias, cuts, lse, *after)
    return result[0], result[1 : 1 + parts], result[-1]


def bucket_kernel(tile_ref, out_ref):
    heads = tile_ref.shape[0]
    wide = 2 * BLOCK
    lane = lax.broadcasted_iota(jnp.int32, (1, wide), 1)
    spot = lax.broadcasted_iota(jnp.int32, (wide, LANES), 1)
    entry = lax.broadcasted_iota(jnp.int32, (wide, LANES), 0)
    gap = entry - (BLOCK - 1)
    row = lax.broadcasted_iota(jnp.int32, (BLOCK, BLOCK), 0)
    column = lax.broadcasted_iota(jnp.int32, (BLOCK, BLOCK), 1)
    flip = jnp.where(row + column == BLOCK - 1, 1.0, 0.0).astype(jnp.bfloat16)
    hots = []
    for delta in (-1, 0, 1):
        relative = delta * BLOCK - gap
        distance = jnp.abs(relative)
        far = jnp.full_like(distance, 8)
        for limit in LIMITS:
            far = far + jnp.where(distance >= limit, 1, 0)
        bucket = jnp.where(distance < 8, distance, far) + jnp.where(relative > 0, 16, 0)
        hots.append(jnp.where(bucket == spot, 1.0, 0.0).astype(jnp.bfloat16))
    lanes = lax.broadcasted_iota(jnp.int32, (1, LANES), 1)

    def one_head(h, carry):
        result = jnp.where(lanes == 15, jnp.sum(tile_ref[h, 0]), 0.0)
        result = result + jnp.where(lanes == 31, jnp.sum(tile_ref[h, 2 * FAR]), 0.0)
        for delta in range(3):
            tile = tile_ref[h, 1 + delta]
            flipped = jnp.zeros_like(tile)
            for _ in range(3):
                high = tile.astype(jnp.bfloat16)
                flipped = flipped + dot(flip, high)
                tile = tile - high.astype(jnp.float32)
            padded = jnp.concatenate([flipped, jnp.zeros_like(tile)], axis=1)
            slid = pltpu.roll(padded, 0, 1, stride=1, stride_axis=0)
            sums = jnp.sum(slid, axis=0, keepdims=True)
            for _ in range(3):
                high = sums.astype(jnp.bfloat16)
                result = result + dot(jnp.broadcast_to(high, (8, wide)), hots[delta])[:1]
                sums = sums - high.astype(jnp.float32)
        out_ref[pl.ds(h, 1), :] = result
        return carry

    lax.fori_loop(0, heads, one_head, 0)


def bucket_sums(tiles, after):
    heads = tiles.shape[0]
    result = pl.pallas_call(
        ordered(bucket_kernel, 1, after),
        out_shape=jax.ShapeDtypeStruct((heads, LANES), jnp.float32),
        in_specs=[VMEM] + [ANY] * len(after),
        out_specs=VMEM,
        compiler_params=params(6),
        cost_estimate=cost(6.6),
        name="bucket_sums",
    )(tiles, *after)
    return result


def relative_rows(me, count, src_ref, dst_ref):
    size = src_ref.shape[0] // count
    for place in range(count):
        r = 2 * (place % (count // 2)) + place // (count // 2)
        start = pl.multiple_of((me ^ r) * size, 16)
        dst_ref[place * size : (place + 1) * size] = src_ref[pl.ds(start, size), :]


def feed_kernel(
    held,
    count,
    half,
    info_ref,
    normed_ref,
    *refs,
):
    if half == 0:
        cot_refs = refs[:held]
        (
            resid_ref,
            wg_ref,
            wu_ref,
            wd_ref,
            acc_ref,
            grad_ref,
            gu_keep_ref,
            gu_send_ref,
            d_keep_ref,
            d_send_ref,
            cot_ref,
            cot_turned_ref,
            normed_turned_ref,
            turned_ref,
        ) = refs[held:]
        grad_in_ref = None
    else:
        (
            resid_ref,
            grad_in_ref,
            cot_ref,
            cot_turned_ref,
            normed_turned_ref,
            wg_ref,
            wu_ref,
            wd_ref,
            *out_refs,
            grad_ref,
            gu_keep_ref,
            gu_send_ref,
            d_keep_ref,
            d_send_ref,
            acc_ref,
        ) = refs
    step = pl.program_id(0)
    core = info_ref[1]
    if half == 0:
        span = cot_refs[0].shape[0]

        @pl.when(step == 0)
        def _():
            for phase in range(held):
                start = pl.multiple_of(lax.rem(info_ref[2] + held - phase, held) * span, span)
                cot_ref[pl.ds(start, span), :] = cot_refs[phase][...]
            cot_turned_ref[...] = cot_ref[...].T
            turned_ref[...] = normed_ref[...].T
            relative_rows(info_ref[0], count, turned_ref, normed_turned_ref)

    normed, cot = normed_ref[...], cot_ref[...]
    gate = dot(normed, wg_ref[...])
    up_value = dot(normed, wu_ref[...])
    grad_hidden = dot_nt(cot, wd_ref[...])
    square = gate * gate
    bend = jnp.tanh(SLOPE * gate * (1.0 + CUBE * square))
    middle = 0.5 * (1.0 + bend)
    gelu = gate * middle
    slope = middle + (0.5 * SLOPE) * gate * (1.0 - bend * bend) * (1.0 + (3.0 * CUBE) * square)
    hidden = (gelu * up_value).astype(jnp.bfloat16)
    grad_gate = (grad_hidden * up_value * slope).astype(jnp.bfloat16)
    grad_up = (grad_hidden * gelu).astype(jnp.bfloat16)
    rb, cb = gu_keep_ref.shape[-2:]
    half_rows = count // 2 * rb
    turned = normed_turned_ref[...]
    for kind, grad in enumerate((grad_gate, grad_up)):
        part = dot(turned, grad).astype(jnp.bfloat16)
        for e in range(2):
            columns = part[:, e * cb : (e + 1) * cb]
            gu_keep_ref[:, kind, e] = columns[:half_rows].reshape(count // 2, rb, cb)
            gu_send_ref[:, kind, e] = columns[half_rows:].reshape(count // 2, rb, cb)
    part = dot(cot_turned_ref[...], hidden)
    first, second = part[:, :cb], part[:, cb:]
    mine = core == 0
    keep = jnp.where(mine, first, second).astype(jnp.bfloat16)
    send = jnp.where(mine, second, first).astype(jnp.bfloat16)
    d_keep_ref[0] = keep.reshape(count, rb, cb)
    d_send_ref[0] = send.reshape(count, rb, cb)
    result = dot(hidden, wd_ref[...])
    back = dot_nt(grad_gate, wg_ref[...]) + dot_nt(grad_up, wu_ref[...])

    @pl.when(step == 0)
    def _():
        acc_ref[...] = resid_ref[...] + result
        grad_ref[...] = back if grad_in_ref is None else grad_in_ref[...] + back

    @pl.when(step > 0)
    def _():
        acc_ref[...] += result
        grad_ref[...] += back

    if half == 1:

        @pl.when(step == pl.num_programs(0) - 1)
        def _():
            span = out_refs[0].shape[0]
            for phase in range(held):
                start = pl.multiple_of(lax.rem(info_ref[2] + held - phase, held) * span, span)
                out_refs[phase][...] = acc_ref[pl.ds(start, span), :].astype(jnp.bfloat16)


def feed_forward(half, info, normed, ins, wg, wu, wd, held, count):
    tokens, features = normed.shape
    width = wg.shape[1]
    chips = count // 2
    steps = chips // 2
    rb, cb = features // count, width // count
    whole = lambda shape: pl.BlockSpec(shape, lambda j, info: (0,) * len(shape))
    low = jnp.bfloat16
    gu = jax.ShapeDtypeStruct((chips, 2, count // 2, rb, cb), low)
    dd = jax.ShapeDtypeStruct((steps, count, rb, cb), low)
    gu_spec = pl.BlockSpec((chips, 2, 2, rb, cb), lambda j, info: (0, 0, j, 0, 0))
    dd_spec = pl.BlockSpec(
        (1, count, rb, cb), lambda j, info: (j ^ ((info[0] // 2) % steps), 0, 0, 0)
    )
    natural, turned = (tokens, features), (features, tokens)
    full = jax.ShapeDtypeStruct(natural, jnp.float32)
    shapes = [full, gu, gu, dd, dd]
    specs = [whole(natural), gu_spec, gu_spec, dd_spec, dd_spec]
    if half == 0:
        shapes, specs = [full] + shapes, [whole(natural)] + specs
    else:
        span = (tokens // held, features)
        shapes = [jax.ShapeDtypeStruct(span, low)] * held + shapes
        specs = [whole(span)] * held + specs
    scratch = [pltpu.VMEM(natural, jnp.float32)]
    if half == 0:
        shapes += [
            jax.ShapeDtypeStruct(natural, low),
            jax.ShapeDtypeStruct(turned, low),
            jax.ShapeDtypeStruct(turned, low),
        ]
        specs += [whole(natural), whole(turned), whole(turned)]
        scratch = [pltpu.VMEM(turned, low)]
    return pl.pallas_call(
        functools.partial(feed_kernel, held, count, half),
        grid_spec=pltpu.PrefetchScalarGridSpec(
            num_scalar_prefetch=1,
            grid=(steps,),
            in_specs=[
                whole(normed.shape),
                *[whole(x.shape) for x in ins],
                pl.BlockSpec((features, 2 * cb), lambda j, info: (0, j + half * steps)),
                pl.BlockSpec((features, 2 * cb), lambda j, info: (0, j + half * steps)),
                pl.BlockSpec((2 * cb, features), lambda j, info: (j + half * steps, 0)),
            ],
            out_specs=specs,
            scratch_shapes=scratch,
        ),
        out_shape=shapes,
        compiler_params=params(28),
        cost_estimate=cost(11),
        name=f"feed_forward_{half}",
    )(info, normed, *ins, wg, wu, wd)


def between_kernel(
    count,
    info_ref,
    grad_ref,
    resid_ref,
    gain_ref,
    cot_ref,
    att_ref,
    wm_ref,
    *refs,
):
    out_ref, att_grad_ref, keep_ref, send_ref, gain_grad_ref, turned_ref = refs[-6:]
    features = resid_ref.shape[1]
    resid = resid_ref[...]
    root = lax.rsqrt(jnp.sum(resid * resid, axis=1, keepdims=True) / features + EPS)
    grad = grad_ref[...]
    unit = resid * root
    gain_grad_ref[...] = jnp.sum(grad * unit, axis=0, keepdims=True)
    pulled = grad * gain_ref[2:3]
    mean = jnp.sum(unit * pulled, axis=1, keepdims=True) / features
    result = cot_ref[...].astype(jnp.float32) + root * (pulled - unit * mean)
    out_ref[...] = result
    mixed = result.astype(jnp.bfloat16)
    att_grad_ref[...] = dot_nt(mixed, wm_ref[...]).astype(jnp.bfloat16)
    relative_rows(info_ref[0], count, att_ref, turned_ref)
    part = dot(turned_ref[...], mixed).astype(jnp.bfloat16)
    half = features // 2
    keep_ref[...] = part[:half].reshape(keep_ref.shape)
    send_ref[...] = part[half:].reshape(send_ref.shape)


def between(info, grad, resid, gain, cot, att, wm, count, after):
    tokens, features = grad.shape
    rb = features // count
    low = jnp.bfloat16
    piece = jax.ShapeDtypeStruct((count // 2, rb, features), low)
    return pl.pallas_call(
        functools.partial(between_kernel, count),
        out_shape=[
            jax.ShapeDtypeStruct((tokens, features), jnp.float32),
            jax.ShapeDtypeStruct((tokens, features), low),
            piece,
            piece,
            jax.ShapeDtypeStruct((1, features), jnp.float32),
        ],
        in_specs=[SMEM] + [VMEM] * 6 + [ANY] * len(after),
        out_specs=[VMEM] * 5,
        scratch_shapes=[pltpu.VMEM((features, tokens), low)],
        compiler_params=params(12),
        cost_estimate=cost(2.5),
        name="between",
    )(info, grad, resid, gain, cot, att, wm, *after)


def project_q_kernel(count, info_ref, dq_ref, normed_ref, wq_ref, keep_ref, send_ref, back_ref, turned_ref, plain_ref):
    plain_ref[...] = normed_ref[...].T
    relative_rows(info_ref[0], count, plain_ref, turned_ref)
    dq = dq_ref[...]
    part = dot(turned_ref[...], dq).astype(jnp.bfloat16)
    half = part.shape[0] // 2
    keep_ref[...] = part[:half].reshape(keep_ref.shape)
    send_ref[...] = part[half:].reshape(send_ref.shape)
    back_ref[...] = dot_nt(dq, wq_ref[...])


def project_q(info, dq, normed, wq, count, after):
    tokens, features = dq.shape
    low = jnp.bfloat16
    piece = jax.ShapeDtypeStruct((count // 2, features // count, features), low)
    outs, _ = launch(
        "project_q",
        functools.partial(project_q_kernel, count),
        [info, dq, normed, wq],
        [SMEM] + [VMEM] * 3,
        [
            piece,
            piece,
            jax.ShapeDtypeStruct((tokens, features), jnp.float32),
            jax.ShapeDtypeStruct((features, tokens), low),
        ],
        [VMEM] * 4,
        14,
        [pltpu.VMEM((features, tokens), low)],
        after=after,
    )
    return outs


def project_kv_kernel(
    mine_ref,
    got_ref,
    turned_ref,
    back_ref,
    stream_ref,
    grad_ref,
    gain_ref,
    wk_ref,
    wv_ref,
    k_keep_ref,
    k_send_ref,
    v_keep_ref,
    v_send_ref,
    out_ref,
    gain_grad_ref,
):
    features = stream_ref.shape[1]
    half = features // 2
    total = back_ref[...]
    for i, w_ref, keep_ref, send_ref in (
        (0, wk_ref, k_keep_ref, k_send_ref),
        (1, wv_ref, v_keep_ref, v_send_ref),
    ):
        grad = mine_ref[i] + got_ref[i]
        part = dot(turned_ref[...], grad).astype(jnp.bfloat16)
        keep_ref[...] = part[:half].reshape(keep_ref.shape)
        send_ref[...] = part[half:].reshape(send_ref.shape)
        total = total + dot_nt(grad, w_ref[...])
    stream = stream_ref[...]
    root = lax.rsqrt(jnp.sum(stream * stream, axis=1, keepdims=True) / features + EPS)
    unit = stream * root
    gain_grad_ref[...] = jnp.sum(total * unit, axis=0, keepdims=True)
    pulled = total * gain_ref[1:2]
    mean = jnp.sum(unit * pulled, axis=1, keepdims=True) / features
    out_ref[...] = grad_ref[...] + root * (pulled - unit * mean)


def project_kv(mine, got, turned, back, stream, grad, gain, wk, wv, count, after):
    tokens, features = stream.shape
    piece = jax.ShapeDtypeStruct((count // 2, features // count, features), jnp.bfloat16)
    outs, _ = launch(
        "project_kv",
        project_kv_kernel,
        [mine, got, turned, back, stream, grad, gain, wk, wv],
        [VMEM] * 9,
        [piece] * 4
        + [
            jax.ShapeDtypeStruct((tokens, features), jnp.float32),
            jax.ShapeDtypeStruct((1, features), jnp.float32),
        ],
        [VMEM] * 6,
        18,
        after=after,
    )
    return outs


def pick_of(pairs, info_ref):
    def tile(pair, at):
        return pairs[pair][0][at] + pairs[pair][1][at]

    def value(pick):
        if len(pick) == 2:
            return tile(*pick)
        return jnp.where(info_ref[7] == 0, tile(*pick[:2]), tile(*pick[2:]))

    return value


def tiles_of(pairs):
    return [tuple(x.reshape((-1,) + x.shape[-2:]) for x in pair) for pair in pairs]


def fold(name, info, pairs, picks, after=(), carry=()):
    pairs = tiles_of(pairs)
    shape = pairs[0][0].shape[1:]

    def kernel(info_ref, *refs):
        ins, outs = refs[: 2 * len(pairs)], refs[2 * len(pairs) :]
        value = pick_of([ins[2 * i : 2 * i + 2] for i in range(len(pairs))], info_ref)
        for out_ref, chosen in zip(outs, picks):
            for slot, pick in enumerate(chosen):
                out_ref[slot] = value(pick)

    return launch(
        name,
        kernel,
        [info, *sum(pairs, ())],
        [SMEM] + [VMEM] * (2 * len(pairs)),
        [jax.ShapeDtypeStruct((len(chosen),) + shape, jnp.bfloat16) for chosen in picks],
        [VMEM] * len(picks),
        16,
        after=after,
        carry=carry,
    )


def fold_seq(name, info, pairs, picks, seqs, slots, groups, width=None, after=(), carry=()):
    pairs = tiles_of(pairs)
    tall, wide = pairs[0][0].shape[1:]
    shape = (tall, width or wide)

    def kernel(info_ref, *refs):
        ins, outs, scratch_ref = refs[: 2 * len(pairs)], refs[2 * len(pairs) : -1], refs[-1]
        value = pick_of([ins[2 * i : 2 * i + 2] for i in range(len(pairs))], info_ref)
        here = info_ref[8]
        for pick, block, slot in picks:
            total = value(pick)
            if width is None:
                scratch_ref[block ^ here, slot] = total
            else:
                for s in range(seqs):
                    scratch_ref[s ^ here, slot] = total[:, s * width : (s + 1) * width]
        for out_ref, group in zip(outs, groups):
            for i, d in enumerate(group):
                out_ref[i * slots : (i + 1) * slots] = scratch_ref[d]

    return launch(
        name,
        kernel,
        [info, *sum(pairs, ())],
        [SMEM] + [VMEM] * (2 * len(pairs)),
        [jax.ShapeDtypeStruct((len(group) * slots,) + shape, jnp.bfloat16) for group in groups],
        [VMEM] * len(groups),
        16,
        [pltpu.VMEM((seqs, slots) + shape, jnp.bfloat16)],
        after=after,
        carry=carry,
    )


def summed(refs, at):
    terms = [ref[at].astype(jnp.float32) for ref in refs]
    while len(terms) > 1:
        terms = [terms[i] + terms[i + 1] for i in range(0, len(terms), 2)]
    return terms[0]


def feed_end_kernel(seqs, *refs):
    ins, (gate_ref, up_ref, down_ref) = refs[:seqs], refs[seqs:]
    slots, rb, cb = ins[0].shape
    each = slots // 3
    for q in range(each):
        gate_ref[:, q * cb : (q + 1) * cb] = summed(ins, q)
        up_ref[:, q * cb : (q + 1) * cb] = summed(ins, each + q)
    for q in range(each):
        down_ref[q * rb : (q + 1) * rb] = summed(ins, 2 * each + q)


def feed_end(ins, after):
    slots, rb, cb = ins[0].shape
    each = slots // 3
    wide = jax.ShapeDtypeStruct((rb, each * cb), jnp.float32)
    return pl.pallas_call(
        ordered(functools.partial(feed_end_kernel, len(ins)), len(ins), after),
        out_shape=[wide, wide, jax.ShapeDtypeStruct((each * rb, cb), jnp.float32)],
        in_specs=[VMEM] * len(ins) + [ANY] * len(after),
        out_specs=[VMEM] * 3,
        compiler_params=params(8),
        cost_estimate=cost(1),
        name="feed_end",
    )(*ins, *after)


def join_kernel(info_ref, *refs):
    held = len(refs) - 1
    for phase in range(held):
        refs[held][lax.rem(info_ref[8] + phase, held)] = refs[phase][...]


def join(info, parts, after):
    shape = (len(parts),) + parts[0].shape
    outs, _ = launch(
        "join",
        join_kernel,
        [info, *parts],
        [SMEM] + [VMEM] * len(parts),
        [jax.ShapeDtypeStruct(shape, parts[0].dtype)],
        [VMEM],
        8,
        after=after,
    )
    return outs[0]


def mix_end_kernel(seqs, *refs):
    for slot, out_ref in enumerate(refs[seqs:]):
        out_ref[...] = summed(refs[:seqs], slot)


def mix_end(ins, after):
    slots = ins[0].shape[0]
    return pl.pallas_call(
        ordered(functools.partial(mix_end_kernel, len(ins)), len(ins), after),
        out_shape=[jax.ShapeDtypeStruct(ins[0].shape[1:], jnp.float32)] * slots,
        in_specs=[VMEM] * len(ins) + [ANY] * len(after),
        out_specs=[VMEM] * slots,
        compiler_params=params(8),
        cost_estimate=cost(1),
        name="mix_end",
    )(*ins, *after)


def sum_kernel(count, *refs):
    refs[count][...] = summed(refs[:count], slice(None)).astype(jnp.bfloat16)


def sum_of(name, terms, after):
    return pl.pallas_call(
        ordered(functools.partial(sum_kernel, len(terms)), len(terms), after),
        out_shape=jax.ShapeDtypeStruct(terms[0].shape, jnp.bfloat16),
        in_specs=[VMEM] * len(terms) + [ANY] * len(after),
        out_specs=VMEM,
        compiler_params=params(8),
        cost_estimate=cost(1),
        name=name,
    )(*terms, *after)


def unpack_kernel(vocab, chips, info_ref, *refs):
    shares = refs[: 2 * chips]
    embed_ref, filter_ref, score_ref, first_ref, second_ref, bias_ref, whole_ref = refs[2 * chips :]
    share = shares[0].shape[1]
    me = info_ref[0]
    for place in range(chips):
        for odd in range(2):
            start = pl.multiple_of((me ^ (2 * place + odd)) * share, 16)
            whole_ref[pl.ds(start, share), :] = shares[odd * chips + place][0].astype(jnp.float32)
    embed_ref[...] = whole_ref[:vocab]
    filter_ref[...] = whole_ref[vocab : vocab + 4]
    score_ref[...] = whole_ref[vocab + 4 : vocab + 5]
    first_ref[...] = whole_ref[vocab + 5 : vocab + 6]
    second_ref[...] = whole_ref[vocab + 6 : vocab + 7]
    heads, buckets = bias_ref.shape
    bias_ref[...] = whole_ref[vocab + 7 : vocab + 7 + heads, :buckets]


def unpack(info, mine, others, vocab, buckets, heads, after):
    chips = len(mine)
    _, share, features = mine[0].shape
    full = lambda *shape: jax.ShapeDtypeStruct(shape, jnp.float32)
    return pl.pallas_call(
        ordered(functools.partial(unpack_kernel, vocab, chips), 1 + 2 * chips, after),
        out_shape=[
            full(vocab, features),
            full(4, features),
            full(1, features),
            full(1, features),
            full(1, features),
            full(heads, buckets),
        ],
        in_specs=[SMEM] + [VMEM] * (2 * chips) + [ANY] * len(after),
        out_specs=[VMEM] * 6,
        scratch_shapes=[pltpu.VMEM((2 * chips * share, features), jnp.float32)],
        compiler_params=params(8),
        cost_estimate=cost(1),
        name="unpack",
    )(info, *mine, *others, *after)


AXES = ("batch", "seq")


def across_cores(x):
    count = lax.axis_size("batch")
    return lax.ppermute(x, "batch", [(i, i ^ 1) for i in range(count)])


def across_chips(x, chip):
    count = lax.axis_size("batch")
    return lax.ppermute(x, "batch", [(i, i ^ (2 * chip)) for i in range(count)])


def across_seq(x, d):
    count = lax.axis_size("seq")
    return lax.ppermute(x, "seq", [(i, i ^ d) for i in range(count)])


class Halving:
    def __init__(self, pairs, where):
        self.pairs, self.where = pairs, where

    def split(self, chosen, bit):
        keys = [key for key in self.where if chosen(key)]
        keep = [key for key in keys if not key[-1] & (1 << bit)]
        send = [key[:-1] + (key[-1] | (1 << bit),) for key in keep]
        return keep, send

    def picks(self, keys):
        return [self.where[key] for key in keys]


def exchange(name, info, state, plans, after=(), carry=()):
    lists, kept = [], []
    for chosen, bit in plans:
        keep, send = state.split(chosen, bit)
        kept.append(keep)
        lists += [state.picks(keep), state.picks(send)]
    outs, carried = fold(name, info, state.pairs, lists, after, carry)
    pairs, where = [], {}
    for place, ((_, bit), keep) in enumerate(zip(plans, kept)):
        pairs.append((outs[2 * place], across_chips(outs[2 * place + 1], 1 << bit)))
        where.update({key: (place, slot) for slot, key in enumerate(keep)})
    return Halving(pairs, where), outs, carried


class Plan:
    def __init__(self, held):
        self.count = lax.axis_size("batch")
        self.seqs = lax.axis_size("seq")
        self.held = held
        self.group = self.seqs // (2 * held)
        me = lax.axis_index("batch")
        place = lax.axis_index("seq")
        self.me, self.place = me, place
        self.core = me % 2
        self.row = place // self.group
        self.part = 2 * (place % self.group) + self.core
        self.parts = 2 * self.group
        self.perms = []
        for phase in range(held):
            perm = []
            for b in range(self.count):
                for s in range(self.seqs):
                    row = held * (b % 2) + (s + phase) % held
                    part = s // held
                    target = (b - b % 2 + part % 2, self.group * row + part // 2)
                    perm.append((b * self.seqs + s, target[0] * self.seqs + target[1]))
            self.perms.append(perm)

    def parts_of(self, x):
        parts = []
        for phase, perm in enumerate(self.perms):
            send = lax.dynamic_index_in_dim(x, (self.place + phase) % self.held, 0, keepdims=False)
            parts.append(lax.ppermute(send, AXES, perm))
        return parts

    def bytes_of(self, x):
        held = self.held
        main = self.parts_of(x)
        ends = jnp.concatenate([x[:, :4], x[:, -4:]], axis=1)
        sides = []
        for phase in range(held):
            perm = []
            for b in range(self.count):
                for s in range(self.seqs):
                    row = held * (b % 2) + (s + phase) % held
                    part = s // held + {0: -1, held - 1: 1}.get(s % held, self.parts)
                    if 0 <= part < self.parts:
                        target = (b - b % 2 + part % 2, self.group * row + part // 2)
                        perm.append((b * self.seqs + s, target[0] * self.seqs + target[1]))
            send = lax.dynamic_index_in_dim(ends, (self.place + phase) % held, 0, keepdims=False)
            sides.append(lax.ppermute(send, AXES, perm))
        low = lax.dynamic_index_in_dim(
            jnp.stack(sides), (self.row + 1) % held, 0, keepdims=False
        )[4:]
        high = lax.dynamic_index_in_dim(jnp.stack(sides), self.row % held, 0, keepdims=False)[:4]
        low = jnp.where(self.part > 0, low, -1)
        high = jnp.where(self.part < self.parts - 1, high, -1)
        order = (self.row - jnp.arange(held)) % held
        middle = jnp.take(jnp.stack(main), order, axis=0).reshape(-1)
        return jnp.concatenate([low, middle, high]).reshape(-1, 4)

    def gather(self, x):
        other = across_cores(x)
        pair = jnp.stack([jnp.where(self.core == 0, x, other), jnp.where(self.core == 0, other, x)])
        if self.group > 1:
            groups = [
                list(range(first, first + self.group))
                for first in range(0, self.seqs, self.group)
            ]
            pair = lax.all_gather(pair, "seq", axis_index_groups=groups)
        return pair.reshape((-1,) + x.shape[1:])

    def scatter(self, x):
        if self.group > 1:
            groups = [
                list(range(first, first + self.group))
                for first in range(0, self.seqs, self.group)
            ]
            x = lax.psum_scatter(
                x, "seq", scatter_dimension=0, axis_index_groups=groups, tiled=True
            )
        pair = x.reshape((2, -1) + x.shape[1:])
        got = across_cores(lax.dynamic_index_in_dim(pair, 1 - self.core, 0, keepdims=False))
        mine = lax.dynamic_index_in_dim(pair, self.core, 0, keepdims=False)
        return mine.astype(jnp.float32) + got.astype(jnp.float32)


def shards(
    byte_values,
    segments,
    byte_mask,
    embedding,
    filter_weight,
    score_weight,
    first_gain,
    query_weight,
    key_weight,
    value_weight,
    merge_weight,
    position_bias,
    second_gain,
    gate_weight,
    up_weight,
    down_weight,
    cotangent,
):
    count = lax.axis_size("batch")
    seqs = lax.axis_size("seq")
    held, width = byte_values.shape
    row_len = segments.shape[1]
    vocab, features = embedding.shape
    hidden_size = gate_weight.shape[1]
    heads = position_bias.shape[1]
    bucket_count = position_bias.shape[0]
    total = row_len // 2
    plan = Plan(held)
    tokens = total // plan.parts
    chips = count // 2
    levels = chips.bit_length() - 1
    blocks = tokens // BLOCK
    other_part = plan.part ^ 1

    bases = [plan.part * blocks, other_part * blocks] if plan.group == 1 else [0, 0]
    info = jnp.stack(
        [
            jnp.asarray(value, jnp.int32)
            for value in (
                plan.me,
                plan.core,
                plan.row % held,
                plan.part * blocks,
                plan.part * 2 * tokens,
                bases[0],
                bases[1],
                plan.me // chips,
                plan.place,
            )
        ]
    )
    ids = plan.bytes_of(jnp.where(byte_mask > 0, byte_values, -1))
    groups = tokens // 2
    spare = -(groups + 2) % 8
    ids = jnp.concatenate([ids[1:], jnp.full((spare, 4), -1, jnp.int32), ids[:1]])
    cuts = jnp.sum((segments[:, :, None] < jnp.arange(1, 4)).astype(jnp.int32), axis=1)
    cuts = (cuts + 1) // 2
    both = jnp.concatenate([cuts, across_cores(cuts)])
    own_first = jnp.where(plan.row // held == plan.core, 0, held)
    cuts = lax.dynamic_index_in_dim(both, own_first + plan.row % held, 0, keepdims=False)
    bias = bias_tiles(position_bias)
    gate_weight, up_weight, down_weight = map(hbm, (gate_weight, up_weight, down_weight))
    query_weight, key_weight, value_weight = map(hbm, (query_weight, key_weight, value_weight))
    merge_weight, bias = hbm(merge_weight), hbm(bias)
    words = -(-(vocab + 7 + heads) // (16 * count)) * (16 * count)
    vectors = jnp.stack([score_weight, first_gain, second_gain])
    stream, normed, q, kv = mixer_forward(
        info,
        ids,
        embedding,
        filter_weight,
        vectors,
        query_weight,
        key_weight,
        value_weight,
        tokens,
        row_len,
        [bias],
    )
    q, normed = hbm(q), hbm(normed)
    ends = (stream, merge_weight, vectors)
    if plan.group == 1:
        kvs = [hbm(kv), across_cores(kv)]
        begun = attention_forward("attention_own", info, q, kvs[0], bias, cuts)
        att, lse, resid, normed_two = attention_forward(
            "attention_other", info, q, kvs[1], bias, cuts, begun, ends
        )
    else:
        kvs = [jnp.stack([plan.gather(kv[0]), plan.gather(kv[1])])]
        att, lse, resid, normed_two = attention_forward(
            "attention_all", info, q, kvs[0], bias, cuts, (), ends
        )
    cots = plan.parts_of(cotangent)

    weights = (gate_weight, up_weight, down_weight)
    acc, grad_two, *grads, cot, cot_turned, normed_turned = feed_forward(
        0, info, normed_two, [*cots, resid], *weights, held, count
    )
    halves = [grads]
    *results, grad_two, gu_keep, gu_send, d_keep, d_send = feed_forward(
        1,
        info,
        normed_two,
        [acc, grad_two, cot, cot_turned, normed_turned],
        *weights,
        held,
        count,
    )
    halves.append([gu_keep, gu_send, d_keep, d_send])
    out_parts = [
        lax.ppermute(x, AXES, [(b, a) for a, b in perm]) for x, perm in zip(results, plan.perms)
    ]
    early = count // 4

    def upwards(key):
        return key[0] == "down" or key[3] < early

    def downwards(key):
        return not upwards(key)

    states = []

    def start_half(half, after):
        gu_keep, gu_send, d_keep, d_send = halves[half]
        pairs = [(gu_keep, across_cores(gu_send)), (d_keep, across_cores(d_send))]
        where = {}
        for r in range(chips):
            for n in range(count):
                where["gu", half, 0, n, r] = (0, r * count + n)
        for r in range(chips // 2):
            for n in range(count):
                where["down", half, 0, n, r] = (1, r * count + n)
        state = Halving(pairs, where)
        first = None
        for level in range(levels - 1):
            state, outs, _ = exchange(
                f"feed_{half}_{level}",
                info,
                state,
                [(upwards, level), (downwards, levels - 1 - level)],
                after if level == 0 else (),
            )
            first = first or outs
        states.append(state)
        return first

    first = start_half(0, [grad_two])
    grad_resid, att_grad, m_keep, m_send, second_part = between(
        info, grad_two, resid, vectors, cot, att, merge_weight, count, [first[0]]
    )
    m_got = across_cores(m_send)
    first = start_half(1, [second_part])
    dq, dkvs, tiles = attention_backward(
        info, q, hbm(att_grad), kvs, bias, cuts, lse, [first[0]]
    )

    where = {}
    for half, state in enumerate(states):
        for key, (pair, slot) in state.where.items():
            where[key] = (2 * half + pair, slot)
    top = 1 << (levels - 1)
    for key in [key for key in where if key[0] == "down"]:
        _, half, kind, n, r = key
        mine, other = where["down", 0, 0, n, 0], where["down", 1, 0, n, 0]
        if half == 0:
            where["one", 2, 0, n, 0] = mine + other
            where["one", 2, 0, n, top] = other + mine
    where = {key: value for key, value in where.items() if key[0] != "down"}
    state = Halving(states[0].pairs + states[1].pairs, where)
    crossing = [dkvs[1]] if plan.group == 1 else []
    state, lasts, crossing = exchange(
        "feed_last",
        info,
        state,
        [
            (lambda key: key[0] == "one" or key[3] < early, levels - 1),
            (lambda key: key[0] == "gu" and key[3] >= early, 0),
        ],
        [dq],
        crossing,
    )
    if plan.group == 1:
        mine, got = hbm(dkvs[0]), across_cores(crossing[0])
    else:
        mine = jnp.stack([plan.scatter(dkvs[0][i]).astype(jnp.bfloat16) for i in range(2)])
        got = jnp.zeros_like(mine)
    q_keep, q_send, back, turned = project_q(info, hbm(dq), normed, query_weight, count, [lasts[0]])
    q_got = across_cores(q_send)
    k_keep, k_send, v_keep, v_send, grad_stream, first_part = project_kv(
        mine,
        got,
        turned,
        back,
        stream,
        hbm(grad_resid),
        vectors,
        key_weight,
        value_weight,
        count,
        [],
    )
    k_got, v_got = across_cores(k_send), across_cores(v_send)

    each = count // seqs
    picks = []
    for key, pick in state.where.items():
        if key[0] == "one":
            picks.append((pick, key[3] // each, 2 * each + key[3] % each))
        else:
            kind, block = key[3] // chips, key[1] * chips + key[3] % chips
            picks.append((pick, block // each, kind * each + block % each))
    slots = 3 * each
    groups = [list(range(0, seqs, 2)), list(range(1, seqs, 2))]
    (z_keep, z_send), _ = fold_seq(
        "feed_seq", info, state.pairs, picks, seqs, slots, groups, after=[first_part]
    )
    z_got = across_seq(z_send, 1)
    layer_output = join(info, out_parts, [z_keep])
    bias_part = bucket_sums(hbm(tiles), [layer_output])

    where = {}
    for r in range(chips):
        for kind in range(4):
            where["p", kind, r] = (kind, r)
    mixes = Halving([(q_keep, q_got), (k_keep, k_got), (v_keep, v_got), (hbm(m_keep), m_got)], where)

    def mix_step(mixes, level, after, carry=()):
        return exchange(
            f"mix_{level}",
            info,
            mixes,
            [
                (lambda key: key[1] in (1, 3), level),
                (lambda key: key[1] in (0, 2), levels - 1 - level),
            ],
            after,
            carry,
        )

    mixes, outs, _ = mix_step(mixes, 0, [bias_part])
    e_keep, e_send = mixer_backward(
        info,
        ids,
        embedding,
        filter_weight,
        vectors,
        grad_stream,
        first_part,
        second_part,
        bias_part,
        row_len,
        vocab,
        words,
        count,
        [outs[0]],
    )

    def feed_step(z_keep, z_got, step, after, carry):
        held_now = z_keep.shape[0] // slots
        lists = [
            [(0, d * slots + i) for d in range(first, held_now, 2) for i in range(slots)]
            for first in range(2)
        ]
        (z_keep, z_send), carried = fold(
            f"feed_seq_{step}", info, [(z_keep, z_got)], lists, after, carry
        )
        return z_keep, across_seq(z_send, step), carried

    step, carry = 2, [e_send]
    while step < seqs:
        z_keep, z_got, carry = feed_step(z_keep, z_got, step, [e_keep], carry)
        step *= 2
    last = z_keep
    for level in range(1, levels):
        mixes, outs, carry = mix_step(mixes, level, [last], carry)
        last = outs[0]
    e_got = across_cores(carry[0])

    parts, _ = fold(
        "small_cores", info, [(e_keep, e_got)], [[(0, r)] for r in range(chips)], [last]
    )
    share = sum_of(
        "small_chips", [parts[0]] + [across_chips(parts[r], r) for r in range(1, chips)], []
    )
    seq_parts = [share] + [across_seq(share, d) for d in range(1, seqs)]
    picks = [(pick, None, key[1]) for key, pick in mixes.where.items()]
    mix_sends, _ = fold_seq(
        "mix_seq",
        info,
        mixes.pairs,
        picks,
        seqs,
        4,
        [[d] for d in range(seqs)],
        features // seqs,
        after=[share],
    )
    mix_arrived = [mix_sends[0]] + [across_seq(mix_sends[d], d) for d in range(1, seqs)]
    gate_grad, up_grad, down_grad = feed_end([z_keep, z_got], [mix_sends[0]])
    share = sum_of("small_seq", seq_parts, [gate_grad])
    shares = [share] + [across_chips(share, r) for r in range(1, chips)]
    embed, filters, score, first, second, bias_sum = unpack(
        info, shares, [across_cores(x) for x in shares], vocab, bucket_count, heads, []
    )
    query_grad, key_grad, value_grad, merge_grad = mix_end(mix_arrived, [score])
    return (
        layer_output,
        embed,
        filters,
        score[0],
        first[0],
        query_grad,
        key_grad,
        value_grad,
        merge_grad,
        bias_sum.T,
        second[0],
        gate_grad,
        up_grad,
        down_grad.T,
    )


def solution(mesh):
    in_specs = (
        P("batch", "seq"),
        P("batch", None),
        P("batch", "seq"),
        P(),
        P(),
        P(),
        P(),
        P(),
        P(),
        P(),
        P(),
        P(),
        P(),
        P(),
        P(),
        P(),
        P("batch", "seq", None),
    )
    out_specs = (
        P("batch", "seq", None),
        P(),
        P(),
        P(),
        P(),
        P("batch", "seq"),
        P("batch", "seq"),
        P("batch", "seq"),
        P("batch", "seq"),
        P(),
        P(),
        P("batch", "seq"),
        P("batch", "seq"),
        P("batch", "seq"),
    )
    return jax.shard_map(shards, mesh=mesh, in_specs=in_specs, out_specs=out_specs, check_vma=False)
```

```python
import functools

import jax
import jax.numpy as jnp
from jax import lax
from jax.experimental import pallas as pl
from jax.experimental.pallas import tpu as pltpu
from jax.sharding import PartitionSpec as P

EPS = 1e-06
LIMITS = (12, 16, 23, 32, 46, 64, 91)
NEG = -1e30
LANES = 128
BLOCK = 128
FAR = 2
CUBE = 0.044715
SLOPE = 0.7978845608028654
MEGA = 1 << 20


def dot(a, b):
    return lax.dot_general(a, b, (((1,), (0,)), ((), ())), preferred_element_type=jnp.float32)


def dot_nt(a, b):
    return lax.dot_general(a, b, (((1,), (1,)), ((), ())), preferred_element_type=jnp.float32)


def params(megabytes):
    return pltpu.CompilerParams(vmem_limit_bytes=megabytes * MEGA)


def cost(microseconds):
    return pl.CostEstimate(flops=int(microseconds * 1e+09), bytes_accessed=1, transcendentals=0)


VMEM = pl.BlockSpec(memory_space=pltpu.VMEM)
ANY = pl.BlockSpec(memory_space=pl.ANY)
HBM = pl.BlockSpec(memory_space=pltpu.HBM)
AUTO = pl.BlockSpec()
SMEM = pl.BlockSpec(memory_space=pltpu.SMEM)


def hbm(x):
    return pltpu.with_memory_space_constraint(x, pltpu.HBM)


def ordered(kernel, inputs, after):
    def with_others(*refs):
        kernel(*refs[:inputs], *refs[inputs + len(after) :])

    return with_others


def launch(name, kernel, ins, in_specs, outs, out_specs, megabytes, scratch=(), after=(), carry=(), microseconds=1.0
):
    given, made = len(ins), len(outs)
    skip = len(after) + len(carry)

    def body(*refs):
        rest = refs[given + skip :]
        kernel(*refs[:given], *rest[:made], *rest[made + len(carry) :])

    results = pl.pallas_call(
        body,
        out_shape=[*outs, *[jax.ShapeDtypeStruct(x.shape, x.dtype) for x in carry]],
        in_specs=[*in_specs, *[ANY] * skip],
        out_specs=[*out_specs, *[ANY] * len(carry)],
        scratch_shapes=list(scratch),
        input_output_aliases={given + len(after) + i: made + i for i in range(len(carry))},
        compiler_params=params(megabytes),
        cost_estimate=cost(microseconds),
        name=name,
    )(*ins, *after, *carry)
    return results[:made], results[made:]


def bucket_of(relative):
    distance = jnp.abs(relative)
    far = jnp.full_like(distance, 8)
    for limit in LIMITS:
        far = far + jnp.where(distance >= limit, 1, 0)
    return jnp.where(distance < 8, distance, far) + jnp.where(relative > 0, 16, 0)


def split_three(x):
    parts = []
    for _ in range(3):
        high = x.astype(jnp.bfloat16)
        parts.append(high)
        x = x - high.astype(jnp.float32)
    return parts


def bias_kernel(table_ref, out_ref, tile_ref, sems):
    copies = []
    heads, buckets = table_ref.shape
    wide = 2 * BLOCK
    parts = split_three(table_ref[...])
    bucket = lax.broadcasted_iota(jnp.int32, (buckets, wide), 0)
    entry = lax.broadcasted_iota(jnp.int32, (buckets, wide), 1)
    gap = jnp.where(entry < BLOCK, entry, entry - wide)
    for delta in range(3):
        hot = jnp.where(bucket_of((delta - 1) * BLOCK - gap) == bucket, 1.0, 0.0)
        hot = hot.astype(jnp.bfloat16)
        rows = (dot(parts[2], hot) + dot(parts[1], hot)) + dot(parts[0], hot)
        for h in range(heads):
            row = jnp.broadcast_to(rows[h : h + 1], (BLOCK, wide))
            tile_ref[delta, h] = pltpu.roll(row, 0, 1, stride=1, stride_axis=0)[:, :BLOCK]
        copies.append(pltpu.make_async_copy(tile_ref.at[delta], out_ref.at[delta], sems.at[delta]))
        copies[-1].start()
    for copy in copies:
        copy.wait()


def bias_tiles(table):
    outs, _ = launch(
        "bias_tiles",
        bias_kernel,
        [table],
        [VMEM],
        [pltpu.HBM((3, table.shape[0], BLOCK, BLOCK), jnp.float32)],
        [HBM],
        6,
        [
            pltpu.VMEM((3, table.shape[0], BLOCK, BLOCK), jnp.float32),
            pltpu.SemaphoreType.DMA((3,)),
        ],
        microseconds=2,
    )
    return outs[0]


def fill_tiles(near_ref, h, tile_ref):
    for delta in range(3):
        tile_ref[1 + delta] = near_ref[delta, h]
    tile_ref[0] = jnp.broadcast_to(near_ref[0, h, :1, BLOCK - 1 :], (BLOCK, BLOCK))
    tile_ref[4] = jnp.broadcast_to(near_ref[2, h, BLOCK - 1 :, :1], (BLOCK, BLOCK))


def by_head(turned, size):
    empty = jnp.zeros((size, turned.shape[1]), turned.dtype)
    left = jnp.concatenate([turned[:size], empty], axis=0)
    right = jnp.concatenate([empty, turned[size:]], axis=0)
    return jnp.concatenate([left, right], axis=1)


def lower_rows(cut_ref, start, rows, heads):
    count = rows[0].shape[1] if rows else heads[1]
    place = start + lax.broadcasted_iota(jnp.int32, (16, count), 1)
    row = lax.broadcasted_iota(jnp.int32, (16, count), 0)
    segment = sum(jnp.where(place >= cut_ref[i], 1, 0) for i in range(3))
    mask = jnp.where((row < 4) & (segment != row), NEG, 0.0)
    blocks = []
    for head in range(heads[0]):
        block = mask
        if rows:
            for i, part in enumerate(split_three(rows[head])):
                block = jnp.where(row == 4 + i, part.astype(jnp.float32), block)
        blocks.append(block.astype(jnp.bfloat16))
    block = jnp.concatenate(blocks, axis=1)
    return jnp.concatenate([block, jnp.zeros((LANES - 16, block.shape[1]), jnp.bfloat16)], axis=0)


def segment_hots(cut_ref, start, count, inside, outside):
    place = start + lax.broadcasted_iota(jnp.int32, (count, LANES), 0)
    lane = lax.broadcasted_iota(jnp.int32, (count, LANES), 1)
    segment = sum(jnp.where(place >= cut_ref[i], 1, 0) for i in range(3))
    value = jnp.where(segment == lane, inside, outside)
    return jnp.where(lane < 4, value, 0.0).astype(jnp.bfloat16)


def chunk_of(c):
    return pl.ds(pl.multiple_of(c * LANES, LANES), LANES)


def down(x):
    return pltpu.roll(x, 1, 0)


def up(x):
    return pltpu.roll(x, x.shape[0] - 1, 0)


def lane_sum(x):
    return jnp.broadcast_to(jnp.sum(x, axis=1, keepdims=True), x.shape)


def offsets_of(rows):
    return {
        -2: down(rows[2]),
        -1: down(rows[3]),
        0: rows[0],
        1: rows[1],
        2: rows[2],
        3: rows[3],
        4: up(rows[0]),
        5: up(rows[1]),
    }


def spread_of(phase, j, one, two, three, four, coefs):
    pair = j - j % 2
    third = three / 3.0
    zero = jnp.zeros_like(third)
    half, quarter = two * 0.5, four * 0.25

    def add(o, value):
        coefs[o] = coefs[o] + value if o in coefs else value

    add(j, one + third)
    for o in (pair, pair + 1):
        add(o, half)
    for o in range(4):
        add(o, quarter)
    add(j + 1, jnp.where(phase <= 1, third, zero))
    add(j + 2, jnp.where(phase == 0, third, zero))
    add(j - 1, jnp.where(phase >= 1, third, zero))
    add(j - 2, jnp.where(phase == 2, third, zero))


def pooled_dots(phase, j, dots):
    pair = j - j % 2
    zero = jnp.zeros_like(dots[0])
    two = 0.5 * (dots[pair] + dots[pair + 1])
    four = 0.25 * ((dots[0] + dots[1]) + (dots[2] + dots[3]))
    three = dots[j] + jnp.where(phase <= 1, dots[j + 1], zero)
    three = three + jnp.where(phase == 0, dots[j + 2], zero)
    three = three + jnp.where(phase >= 1, dots[j - 1], zero)
    three = three + jnp.where(phase == 2, dots[j - 2], zero)
    return dots[j], two, three / 3.0, four


def convolve(e, taps):
    em2, em3, ep0 = down(e[2]), down(e[3]), up(e[0])
    f0, f1, f2, f3 = taps
    return [
        f0 * em2 + f1 * em3 + f2 * e[0] + f3 * e[1],
        f0 * em3 + f1 * e[0] + f2 * e[1] + f3 * e[2],
        f0 * e[0] + f1 * e[1] + f2 * e[2] + f3 * e[3],
        f0 * e[1] + f1 * e[2] + f2 * e[3] + f3 * ep0,
    ]


def mixer_weights(info_ref, ids_ref, emb_ref, filt_ref, score_ref, e_ref, c_ref, acc_ref, row_len):
    count = ids_ref.shape[0]
    words, features = emb_ref.shape
    chunks = features // LANES
    group = info_ref[4] // 4
    vocab = lax.broadcasted_iota(jnp.int32, (count, words), 1)
    for j in range(4):
        hot = jnp.where(ids_ref[:, j : j + 1] == vocab, 1.0, 0.0).astype(jnp.bfloat16)
        e_ref[j] = dot(hot, emb_ref[...])
        acc_ref[j] = jnp.zeros((count, LANES), jnp.float32)

    def one_chunk(c, carry):
        lanes = chunk_of(c)
        e = [e_ref[j, :, lanes] for j in range(4)]
        conv = convolve(e, [filt_ref[k : k + 1, lanes] for k in range(4)])
        for j in range(4):
            c_ref[j, :, lanes] = conv[j]
            acc_ref[j] += conv[j] * score_ref[:1, lanes]
        return carry

    lax.fori_loop(0, chunks, one_chunk, 0)
    rows = lax.broadcasted_iota(jnp.int32, (count, LANES), 0)
    places = jnp.where(rows == count - 1, -1, rows) + group
    inside = [(4 * places + j < row_len) for j in range(4)]
    dots = [jnp.where(inside[j], lane_sum(acc_ref[j]), 0.0) for j in range(4)]
    dots = offsets_of(dots)
    phases, weights = [], []
    for j in range(4):
        phase = lax.rem(places + 3 + j, 3)
        scores = pooled_dots(phase, j, dots)
        highest = jnp.maximum(jnp.maximum(scores[0], scores[1]), jnp.maximum(scores[2], scores[3]))
        powers = [jnp.exp(score - highest) for score in scores]
        share = 1.0 / ((powers[0] + powers[1]) + (powers[2] + powers[3]))
        phases.append(phase)
        weights.append([power * share for power in powers])
    limits = {o: (4 * places + o < row_len) for o in (4, 5)}
    return phases, weights, limits


def token_coefs(phases, weights, limits, scale):
    result = []
    for h in range(2):
        coefs = {}
        for j in (2 * h, 2 * h + 1):
            spread_of(phases[j], j, *weights[j], coefs)
        for o in coefs:
            if o in limits:
                coefs[o] = jnp.where(limits[o], coefs[o], 0.0)
            coefs[o] = coefs[o] * scale
        result.append(coefs)
    return result


def mixer_kernel(
    row_len,
    info_ref,
    ids_ref,
    emb_ref,
    filt_ref,
    score_ref,
    wq_ref,
    wk_ref,
    wv_ref,
    stream_out_ref,
    normed_out_ref,
    q_ref,
    kv_ref,
    e_ref,
    c_ref,
    acc_ref,
    coef_ref,
    square_ref,
    root_ref,
    weight_ref,
    sems,
    stream_ref,
    normed_ref,
):
    copies = [
        pltpu.make_async_copy(w_ref, weight_ref.at[i], sems.at[i])
        for i, w_ref in enumerate((wk_ref, wv_ref, wq_ref))
    ]
    for copy in copies:
        copy.start()
    tokens, features = stream_ref.shape
    groups = tokens // 2
    chunks = features // LANES
    phases, weights, limits = mixer_weights(
        info_ref, ids_ref, emb_ref, filt_ref, score_ref, e_ref, c_ref, acc_ref, row_len
    )
    coefs = token_coefs(phases, weights, limits, 0.5)
    names = [(h, o) for h in range(2) for o in sorted(coefs[h])]
    for place, (h, o) in enumerate(names):
        coef_ref[place] = coefs[h][o][:groups]
    square_ref[...] = jnp.zeros_like(square_ref)

    def one_chunk(c, carry):
        lanes = chunk_of(c)
        conv = {
            o: value[:groups]
            for o, value in offsets_of([c_ref[j, :, lanes] for j in range(4)]).items()
        }
        for h in range(2):
            mixed = None
            for place, (side, o) in enumerate(names):
                if side == h:
                    term = coef_ref[place] * conv[o]
                    mixed = term if mixed is None else mixed + term
            root_ref[pl.ds(h, groups, stride=2), :] = mixed
            square_ref[h] += mixed * mixed
        stream_ref[:, lanes] = root_ref[...]
        return carry

    lax.fori_loop(0, chunks, one_chunk, 0)
    for h in range(2):
        root = lax.rsqrt(lane_sum(square_ref[h]) / features + EPS)
        root_ref[pl.ds(h, groups, stride=2), :] = root

    def norm_chunk(c, carry):
        lanes = chunk_of(c)
        normed = stream_ref[:, lanes] * root_ref[...] * score_ref[1:2, lanes]
        normed_ref[:, lanes] = normed.astype(jnp.bfloat16)
        return carry

    lax.fori_loop(0, chunks, norm_chunk, 0)
    kept = [
        pltpu.make_async_copy(stream_ref, stream_out_ref, sems.at[3]),
        pltpu.make_async_copy(normed_ref, normed_out_ref, sems.at[4]),
    ]
    for copy in kept:
        copy.start()
    for i in range(2):
        copies[i].wait()
        kv_ref[i] = dot(normed_ref[...], weight_ref[i]).astype(jnp.bfloat16)
    copies[2].wait()
    q_ref[...] = dot(normed_ref[...], weight_ref[2]).astype(jnp.bfloat16)
    for copy in kept:
        copy.wait()


def mixer_forward(info, ids, emb, filt, score, wq, wk, wv, tokens, row_len, after):
    features = emb.shape[1]
    count = ids.shape[0]
    groups = tokens // 2
    low = jax.ShapeDtypeStruct((tokens, features), jnp.bfloat16)
    return pl.pallas_call(
        ordered(functools.partial(mixer_kernel, row_len), 8, after),
        out_shape=[
            pltpu.HBM((tokens, features), jnp.float32),
            pltpu.HBM((tokens, features), jnp.bfloat16),
            low,
            jax.ShapeDtypeStruct((2, tokens, features), jnp.bfloat16),
        ],
        in_specs=[SMEM] + [VMEM] * 4 + [HBM] * 3 + [ANY] * len(after),
        out_specs=[HBM, HBM, VMEM, VMEM],
        scratch_shapes=[
            pltpu.VMEM((4, count, features), jnp.float32),
            pltpu.VMEM((4, count, features), jnp.float32),
            pltpu.VMEM((4, count, LANES), jnp.float32),
            pltpu.VMEM((12, groups, LANES), jnp.float32),
            pltpu.VMEM((2, groups, LANES), jnp.float32),
            pltpu.VMEM((tokens, LANES), jnp.float32),
            pltpu.VMEM((3, features, features), jnp.bfloat16),
            pltpu.SemaphoreType.DMA((5,)),
            pltpu.VMEM((tokens, features), jnp.float32),
            pltpu.VMEM((tokens, features), jnp.bfloat16),
        ],
        compiler_params=params(24),
        cost_estimate=cost(10),
        name="mixer_forward",
    )(info, ids, emb, filt, score, wq, wk, wv, *after)


def mixer_back_kernel(
    row_len,
    vocab_size,
    info_ref,
    ids_ref,
    emb_ref,
    filt_ref,
    score_ref,
    grad_ref,
    first_ref,
    second_ref,
    bias_ref,
    *refs,
):
    (
        keep_ref,
        send_ref,
        e_ref,
        c_ref,
        acc_ref,
        coef_ref,
        dots_ref,
        high_ref,
        low_ref,
        turn_ref,
        embed_ref,
        small_ref,
    ) = refs[-12:]
    tokens, features = grad_ref.shape
    groups = tokens // 2
    chunks = features // LANES
    count = ids_ref.shape[0]
    phases, weights, limits = mixer_weights(
        info_ref, ids_ref, emb_ref, filt_ref, score_ref, e_ref, c_ref, acc_ref, row_len
    )
    coefs = token_coefs(phases, weights, limits, 0.5)
    names = [(h, o) for h in range(2) for o in sorted(coefs[h])]
    empty = jnp.zeros((count - groups, LANES), jnp.float32)
    dots_ref[...] = jnp.zeros_like(dots_ref)

    def token_grads(lanes):
        turn_ref[...] = grad_ref[:, lanes]
        return [
            jnp.concatenate([turn_ref[pl.ds(h, groups, stride=2), :], empty], axis=0)
            for h in range(2)
        ]

    def dots_chunk(c, carry):
        lanes = chunk_of(c)
        conv = offsets_of([c_ref[j, :, lanes] for j in range(4)])
        grads = token_grads(lanes)
        for place, (h, o) in enumerate(names):
            dots_ref[place] += grads[h] * conv[o]
        return carry

    lax.fori_loop(0, chunks, dots_chunk, 0)
    pulls = []
    for h in range(2):
        dots = {}
        for place, (side, o) in enumerate(names):
            if side == h:
                value = lane_sum(dots_ref[place]) * 0.5
                dots[o] = jnp.where(limits[o], value, 0.0) if o in limits else value
        for j in (2 * h, 2 * h + 1):
            grads = pooled_dots(phases[j], j, dots)
            mean = sum(weights[j][i] * grads[i] for i in range(4))
            pulls.append([weights[j][i] * (grads[i] - mean) for i in range(4)])
    score_coefs = token_coefs(phases, pulls, limits, 1.0)

    def gathered(by_token):
        first, second = by_token
        return [
            first[0] + second[0] + down(second[4]),
            first[1] + second[1] + down(second[5]),
            first[2] + second[2] + up(first[-2]),
            first[3] + second[3] + up(first[-1]),
        ]

    kappas = gathered(score_coefs)
    for j in range(4):
        coef_ref[4 * j] = coefs[0][j]
        coef_ref[4 * j + 1] = coefs[1][j]
        coef_ref[4 * j + 2] = down(coefs[1][4 + j]) if j < 2 else up(coefs[0][j - 4])
        coef_ref[4 * j + 3] = kappas[j]
    small_ref[...] = jnp.zeros_like(small_ref)

    def total(x):
        return jnp.sum(x, axis=0, keepdims=True)

    def grad_chunk(c, carry):
        lanes = chunk_of(c)
        first, second = token_grads(lanes)
        above, below = down(second), up(first)
        score = score_ref[:1, lanes]
        taps = [filt_ref[k : k + 1, lanes] for k in range(4)]
        e = [e_ref[j, :, lanes] for j in range(4)]
        near = offsets_of(e)
        d = []
        score_sum = jnp.zeros((1, LANES), jnp.float32)
        tap_sums = [jnp.zeros((1, LANES), jnp.float32) for _ in range(4)]
        for j in range(4):
            beside = above if j < 2 else below
            kappa = coef_ref[4 * j + 3]
            value = (
                coef_ref[4 * j] * first
                + coef_ref[4 * j + 1] * second
                + coef_ref[4 * j + 2] * beside
                + kappa * score
            )
            d.append(value)
            score_sum = score_sum + total(kappa * c_ref[j, :, lanes])
            for k in range(4):
                tap_sums[k] = tap_sums[k] + total(value * near[j + k - 2])
        for k in range(4):
            small_ref[k : k + 1, lanes] = tap_sums[k]
        small_ref[4:5, lanes] = score_sum
        f0, f1, f2, f3 = taps
        d3m, d0p, d1p = down(d[3]), up(d[0]), up(d[1])
        back = [
            f0 * d[2] + f1 * d[1] + f2 * d[0] + f3 * d3m,
            f0 * d[3] + f1 * d[2] + f2 * d[1] + f3 * d[0],
            f0 * d0p + f1 * d[3] + f2 * d[2] + f3 * d[1],
            f0 * d1p + f1 * d0p + f2 * d[3] + f3 * d[2],
        ]
        for j in range(4):
            high = back[j].astype(jnp.bfloat16)
            high_ref[j * count : (j + 1) * count, lanes] = high
            low_ref[j * count : (j + 1) * count, lanes] = (
                back[j] - high.astype(jnp.float32)
            ).astype(jnp.bfloat16)
        return carry

    lax.fori_loop(0, chunks, grad_chunk, 0)
    vocab = lax.broadcasted_iota(jnp.int32, (embed_ref.shape[0], count), 0)
    lane = lax.broadcasted_iota(jnp.int32, (count, LANES), 1)
    spread = jnp.zeros((count, LANES), jnp.float32)
    for j in range(4):
        spread = jnp.where(lane == j, ids_ref[:, j : j + 1].astype(jnp.float32), spread)
    spare = jnp.zeros((-count % LANES, LANES), jnp.float32)
    flat = jnp.concatenate([spread, spare], axis=0).T.astype(jnp.int32)
    hot = [
        jnp.where(flat[j : j + 1, :count] == vocab, 1.0, 0.0).astype(jnp.bfloat16) for j in range(4)
    ]
    total_grad = None
    for j in range(4):
        rows = slice(j * count, (j + 1) * count)
        here = dot(hot[j], high_ref[rows]) + dot(hot[j], low_ref[rows])
        total_grad = here if total_grad is None else total_grad + here
    embed_ref[...] = total_grad
    embed_ref[vocab_size : vocab_size + 5] = small_ref[:5]
    embed_ref[vocab_size + 5 : vocab_size + 6] = first_ref[...]
    embed_ref[vocab_size + 6 : vocab_size + 7] = second_ref[...]
    heads = bias_ref.shape[0]
    embed_ref[vocab_size + 7 : vocab_size + 7 + heads, :LANES] = bias_ref[...]
    share = keep_ref.shape[1]
    chips = keep_ref.shape[0]
    me = info_ref[0]
    for place in range(chips):
        for odd, out_ref in enumerate((keep_ref, send_ref)):
            start = pl.multiple_of((me ^ (2 * place + odd)) * share, 16)
            out_ref[place] = embed_ref[pl.ds(start, share), :].astype(jnp.bfloat16)


def mixer_backward(info, ids, emb, filt, score, grad, first, second, bias, row_len, vocab, embed_rows, devices, after):
    tokens, features = grad.shape
    count = ids.shape[0]
    words = embed_rows
    return pl.pallas_call(
        functools.partial(mixer_back_kernel, row_len, vocab),
        out_shape=[jax.ShapeDtypeStruct((devices // 2, words // devices, features), jnp.bfloat16)] * 2,
        in_specs=[SMEM] + [VMEM] * 8 + [ANY] * len(after),
        out_specs=[VMEM] * 2,
        scratch_shapes=[
            pltpu.VMEM((4, count, features), jnp.float32),
            pltpu.VMEM((4, count, features), jnp.float32),
            pltpu.VMEM((4, count, LANES), jnp.float32),
            pltpu.VMEM((16, count, LANES), jnp.float32),
            pltpu.VMEM((12, count, LANES), jnp.float32),
            pltpu.VMEM((4 * count, features), jnp.bfloat16),
            pltpu.VMEM((4 * count, features), jnp.bfloat16),
            pltpu.VMEM((tokens, LANES), jnp.float32),
            pltpu.VMEM((words, features), jnp.float32),
            pltpu.VMEM((8, features), jnp.float32),
        ],
        compiler_params=params(22),
        cost_estimate=cost(15.6),
        name="mixer_backward",
    )(info, ids, emb, filt, score, grad, first, second, bias, *after)


def scores_of(info_ref, part, raw, tile_ref):
    keys, tokens = raw.shape
    base, own = info_ref[part], info_ref[3]
    rows = []
    for kb in range(keys // BLOCK):
        tiles = [
            tile_ref[jnp.clip(base + kb - own - qb, -FAR, FAR) + FAR]
            for qb in range(tokens // BLOCK)
        ]
        rows.append(raw[kb * BLOCK : (kb + 1) * BLOCK] + jnp.concatenate(tiles, axis=1))
    return rows


def only_head(x, h, size):
    lane = lax.broadcasted_iota(jnp.int32, x.shape, 1)
    return jnp.where((lane >= h * size) & (lane < (h + 1) * size), x, jnp.zeros_like(x))


def attention_kernel(
    size,
    carried,
    last,
    info_ref,
    q_ref,
    kv_ref,
    bias_ref,
    cut_ref,
    *refs,
):
    if last:
        *refs, plain_ref, weight_ref, sems = refs
    *refs, tile_ref, q_low_ref, k_hot_ref = refs
    if carried:
        before_ref, state_ref, *refs = refs
    if last:
        stream_ref, wm_ref, gain_ref, att_ref, lse_ref, resid_ref, normed_ref = refs
    else:
        mixed_ref, stat_ref = refs
    step = pl.program_id(0)
    part = 5 + carried
    low = []
    tokens = q_ref.shape[0]

    @pl.when(step == 0)
    def _():
        q_low_ref[...] = lower_rows(cut_ref, info_ref[3] * BLOCK, [], (2, tokens))
        k_hot_ref[...] = segment_hots(cut_ref, info_ref[part] * BLOCK, kv_ref.shape[1], 1.0, 0.0)

    both = jnp.concatenate([by_head(q_ref[...].T, size), q_low_ref[...]], axis=0)
    raws = dot(jnp.concatenate([kv_ref[0], k_hot_ref[...]], axis=1), both)
    turned = kv_ref[1].T
    ones = jnp.ones((16, turned.shape[1]), jnp.bfloat16)
    for h in range(2):
        fill_tiles(bias_ref, h, tile_ref.at[h])
    for h in range(2):
        raw = raws[:, h * tokens : (h + 1) * tokens]
        rows = scores_of(info_ref, part, raw, tile_ref.at[h])
        highest = None
        for row in rows:
            top = jnp.max(row, axis=0, keepdims=True)
            highest = top if highest is None else jnp.maximum(highest, top)
        if carried:
            highest = jnp.maximum(highest, state_ref[0, h : h + 1])
        weights = jnp.concatenate([jnp.exp(row - highest).astype(jnp.bfloat16) for row in rows], axis=0)
        mixed = dot(jnp.concatenate([turned[h * size : (h + 1) * size], ones], axis=0), weights)
        mixed, summed = mixed[:size], mixed[size : size + 1]
        if carried:
            shrink = jnp.exp(state_ref[0, h : h + 1] - highest)
            summed = summed + state_ref[0, 2 + h : 3 + h] * shrink
            mixed = mixed + before_ref[h * size : (h + 1) * size] * shrink
        if last:
            lse_ref[0, h : h + 1] = highest + jnp.log(summed)
            low.append(mixed * (1.0 / summed))
        else:
            stat_ref[0, h : h + 1] = highest
            stat_ref[0, 2 + h : 3 + h] = summed
            mixed_ref[h * size : (h + 1) * size] = mixed
    if not last:
        return
    features = stream_ref.shape[1]
    turned = jnp.concatenate(low, axis=0)
    att_ref[...] = turned
    plain_ref[step] = turned.T.astype(jnp.bfloat16)
    copies = [
        pltpu.make_async_copy(wm_ref, weight_ref, sems.at[0]),
        pltpu.make_async_copy(stream_ref, resid_ref, sems.at[1]),
    ]

    @pl.when(step == 0)
    def _():
        for copy in copies:
            copy.start()

    @pl.when(step == pl.num_programs(0) - 1)
    def _():
        for copy in copies:
            copy.wait()
        attended = jnp.concatenate([plain_ref[p] for p in range(plain_ref.shape[0])], axis=1)
        resid = resid_ref[...] + dot(attended, weight_ref[...])
        resid_ref[...] = resid
        root = lax.rsqrt(jnp.sum(resid * resid, axis=1, keepdims=True) / features + EPS)
        normed_ref[...] = (resid * root * gain_ref[2:3]).astype(jnp.bfloat16)


def attention_forward(name, size, info, q, kv, bias, cuts, carried=(), last=(), carry=()):
    tokens, features = q.shape
    heads = features // size
    pairs = heads // 2
    wide = 2 * size
    whole = lambda shape: pl.BlockSpec(shape, lambda p: (0,) * len(shape))
    by_rows = pl.BlockSpec((wide, tokens), lambda p: (p, 0))
    stat = pl.BlockSpec((1, 8, tokens), lambda p: (p, 0, 0))
    stat_shape = jax.ShapeDtypeStruct((pairs, 8, tokens), jnp.float32)
    ins = [info, q, kv, bias, cuts, *carried, *last]
    in_specs = [
        SMEM,
        pl.BlockSpec((tokens, wide), lambda p: (0, p)),
        pl.BlockSpec((2, kv.shape[1], wide), lambda p: (0, 0, p)),
        pl.BlockSpec((3, 2, BLOCK, BLOCK), lambda p: (0, p, 0, 0)),
        SMEM,
    ]
    if carried:
        in_specs += [by_rows, stat]
    if last:
        stream, wm, gain = last
        in_specs += [
            HBM,
            HBM,
            whole(gain.shape),
        ]
        shapes = [
            jax.ShapeDtypeStruct((features, tokens), jnp.float32),
            stat_shape,
            jax.ShapeDtypeStruct((tokens, features), jnp.float32),
            jax.ShapeDtypeStruct((tokens, features), jnp.bfloat16),
        ]
        out_specs = [by_rows, stat, whole((tokens, features)), whole((tokens, features))]
    else:
        shapes = [jax.ShapeDtypeStruct((features, tokens), jnp.float32), stat_shape]
        out_specs = [by_rows, stat]
    merging = [
        pltpu.VMEM((pairs, tokens, wide), jnp.bfloat16),
        pltpu.VMEM((features, features), jnp.bfloat16),
        pltpu.SemaphoreType.DMA((2,)),
    ]
    kernel = functools.partial(attention_kernel, size, int(bool(carried)), bool(last))
    made = len(shapes)

    def body(*refs):
        rest = refs[len(ins) + len(carry) :]
        kernel(*refs[: len(ins)], *rest[:made], *rest[made + len(carry) :])

    results = pl.pallas_call(
        body,
        grid=(pairs,),
        out_shape=[*shapes, *[jax.ShapeDtypeStruct(x.shape, x.dtype) for x in carry]],
        in_specs=in_specs + [ANY] * len(carry),
        out_specs=[*out_specs, *[ANY] * len(carry)],
        input_output_aliases={len(ins) + i: made + i for i in range(len(carry))},
        scratch_shapes=[
            pltpu.VMEM((2, 2 * FAR + 1, BLOCK, BLOCK), jnp.float32),
            pltpu.VMEM((LANES, 2 * tokens), jnp.bfloat16),
            pltpu.VMEM((kv.shape[1], LANES), jnp.bfloat16),
            *(merging if last else []),
        ],
        compiler_params=params(12),
        cost_estimate=cost(9),
        name=name,
    )(*ins, *carry)
    return results[:made], results[made:]


def diagonal_sums(tile_ref, sums_ref):
    wide = 2 * BLOCK
    row = lax.broadcasted_iota(jnp.int32, (BLOCK, BLOCK), 0)
    column = lax.broadcasted_iota(jnp.int32, (BLOCK, BLOCK), 1)
    flip = jnp.where(row + column == BLOCK - 1, 1.0, 0.0).astype(jnp.bfloat16)
    near = jnp.concatenate([tile_ref[h, 1 + delta] for h in range(2) for delta in range(3)], axis=1)
    high = near.astype(jnp.bfloat16)
    rest = (near - high.astype(jnp.float32)).astype(jnp.bfloat16)
    flipped = dot(flip, high) + dot(flip, rest)
    empty = jnp.zeros((BLOCK, BLOCK), jnp.float32)
    for h in range(2):
        for delta in range(3):
            start = (3 * h + delta) * BLOCK
            padded = jnp.concatenate([flipped[:, start : start + BLOCK], empty], axis=1)
            slid = pltpu.roll(padded, 0, 1, stride=1, stride_axis=0)
            place = 5 * h + 1 + delta
            sums_ref[0, place : place + 1] = jnp.sum(slid, axis=0, keepdims=True)
        for far in (0, 2 * FAR):
            place = 5 * h + far
            total = jnp.sum(tile_ref[h, far], axis=0, keepdims=True)
            sums_ref[0, place : place + 1] = jnp.concatenate([total, empty[:1]], axis=1)


def attention_back_kernel(
    parts,
    size,
    info_ref,
    q_ref,
    g_ref,
    *refs,
):
    kv_refs = refs[:parts]
    bias_ref, cut_ref, lse_ref, att_ref = refs[parts : parts + 4]
    dq_ref, *dkv_refs, sums_ref, bias_tile_ref, tile_ref = refs[-4 - 2 * parts : len(refs) - parts]
    k_hot_refs = refs[len(refs) - parts :]
    tokens = q_ref.shape[0]
    blocks = tokens // BLOCK
    own = info_ref[3]
    for h in range(2):
        fill_tiles(bias_ref, h, bias_tile_ref.at[h])

    @pl.when(pl.program_id(0) == 0)
    def _():
        lane = lax.broadcasted_iota(jnp.int32, (1, LANES), 1)
        one = jnp.where((lane >= 4) & (lane < 7), 1.0, 0.0).astype(jnp.bfloat16)
        for part in range(parts):
            hots = segment_hots(cut_ref, info_ref[5 + part] * BLOCK, kv_refs[part].shape[1], 1.0, 0.0)
            k_hot_refs[part][...] = hots + one

    q_both = jnp.concatenate([only_head(q_ref[...], h, size) for h in range(2)], axis=0)
    g_both = jnp.concatenate([only_head(g_ref[...], h, size) for h in range(2)], axis=0)
    turned = g_ref[...].T
    logs = [-lse_ref[0, h : h + 1] for h in range(2)]
    q_wide = jnp.concatenate(
        [by_head(q_ref[...].T, size), lower_rows(cut_ref, own * BLOCK, logs, (2, tokens))], axis=0
    )
    g_wide = by_head(turned, size)
    products = turned.astype(jnp.float32) * att_ref[...]
    correction = jnp.concatenate(
        [jnp.sum(products[h * size : (h + 1) * size], axis=0, keepdims=True) for h in range(2)], axis=1
    )
    tile_ref[...] = jnp.zeros_like(tile_ref)
    dq = None
    for part in range(parts):
        base = info_ref[5 + part]
        keys = kv_refs[part].shape[1]
        hots = k_hot_refs[part][...]
        raw = dot(jnp.concatenate([kv_refs[part][0], hots], axis=1), q_wide)
        pull = dot(kv_refs[part][1], g_wide)
        shares, grads, sums = [], [], {}
        for kb in range(keys // BLOCK):
            rows = slice(kb * BLOCK, (kb + 1) * BLOCK)
            tiles = [
                bias_tile_ref[h, jnp.clip(base + kb - own - qb, -FAR, FAR) + FAR]
                for h in range(2)
                for qb in range(blocks)
            ]
            probs = jnp.exp(raw[rows] + jnp.concatenate(tiles, axis=1))
            grad = probs * (pull[rows] - correction)
            shares.append(probs.astype(jnp.bfloat16))
            grads.append(grad.astype(jnp.bfloat16))
            for h in range(2):
                for qb in range(blocks):
                    start = (h * blocks + qb) * BLOCK
                    here = grad[:, start : start + BLOCK]
                    key = (h, kb - qb)
                    sums[key] = sums[key] + here if key in sums else here
        for (h, delta), tile in sums.items():
            place = jnp.clip(base - own + delta, -FAR, FAR) + FAR
            tile_ref[h, place] += tile
        shares = jnp.concatenate(shares, axis=0)
        grads = jnp.concatenate(grads, axis=0)
        dkv_refs[part][0] = dot(grads, q_both).astype(jnp.bfloat16)
        dkv_refs[part][1] = dot(shares, g_both).astype(jnp.bfloat16)
        term = dot(kv_refs[part][0].T, grads)
        dq = term if dq is None else dq + term
    dq = jnp.concatenate([dq[:size, :tokens], dq[size:, tokens:]], axis=0)
    dq_ref[...] = dq.T.astype(jnp.bfloat16)
    diagonal_sums(tile_ref, sums_ref)


def attention_backward(size, info, q, g, kvs, bias, cuts, lse, att, after):
    tokens, features = q.shape
    pairs = features // size // 2
    parts = len(kvs)
    wide = 2 * size
    by_pair = [pl.BlockSpec((2, x.shape[1], wide), lambda p: (0, 0, p)) for x in kvs]
    own = pl.BlockSpec((tokens, wide), lambda p: (0, p))
    sums = pl.BlockSpec((1, 16, 2 * BLOCK), lambda p: (p, 0, 0))
    tiles = pltpu.VMEM((2, 2 * FAR + 1, BLOCK, BLOCK), jnp.float32)
    shapes = [jax.ShapeDtypeStruct(x.shape, jnp.bfloat16) for x in kvs]
    if parts > 1:
        shapes[0] = pltpu.HBM(kvs[0].shape, jnp.bfloat16)
    result = pl.pallas_call(
        functools.partial(attention_back_kernel, parts, size),
        grid=(pairs,),
        out_shape=[pltpu.HBM(q.shape, jnp.bfloat16), *shapes]
        + [jax.ShapeDtypeStruct((pairs, 16, 2 * BLOCK), jnp.float32)],
        in_specs=[
            SMEM,
            own,
            own,
            *by_pair,
            pl.BlockSpec((3, 2, BLOCK, BLOCK), lambda p: (0, p, 0, 0)),
            SMEM,
            pl.BlockSpec((1, 8, tokens), lambda p: (p, 0, 0)),
            pl.BlockSpec((wide, tokens), lambda p: (p, 0)),
            *[ANY] * len(after),
        ],
        out_specs=[own, *by_pair, sums],
        scratch_shapes=[
            tiles,
            tiles,
            *[pltpu.VMEM((x.shape[1], LANES), jnp.bfloat16) for x in kvs],
        ],
        compiler_params=params(18),
        cost_estimate=cost(20),
        name="attention_backward",
    )(info, q, g, *kvs, bias, cuts, lse, att, *after)
    return result[0], result[1 : 1 + parts], result[-1]


def bucket_kernel(sums_ref, out_ref):
    pairs = sums_ref.shape[0]
    wide = 2 * BLOCK
    spot = lax.broadcasted_iota(jnp.int32, (wide, LANES), 1)
    entry = lax.broadcasted_iota(jnp.int32, (wide, LANES), 0)
    gap = entry - (BLOCK - 1)
    total = None
    for delta in range(5):
        if delta in (0, 2 * FAR):
            hot = jnp.where(spot == (15 if delta == 0 else 31), 1.0, 0.0)
        else:
            hot = jnp.where(spot == bucket_of((delta - FAR) * BLOCK - gap), 1.0, 0.0)
        hot = hot.astype(jnp.bfloat16)
        rows = [sums_ref[p, 5 * h + delta : 5 * h + delta + 1] for p in range(pairs) for h in range(2)]
        rows = jnp.concatenate(rows, axis=0)
        for part in split_three(rows):
            here = dot(part, hot)
            total = here if total is None else total + here
    out_ref[...] = total


def bucket_sums(sums, after):
    outs, _ = launch(
        "bucket_sums",
        bucket_kernel,
        [sums],
        [VMEM],
        [jax.ShapeDtypeStruct((2 * sums.shape[0], LANES), jnp.float32)],
        [VMEM],
        4,
        after=after,
    )
    return outs[0]


def relative_rows(me, count, src_ref, dst_ref):
    size = src_ref.shape[0] // count
    for place in range(count):
        r = 2 * (place % (count // 2)) + place // (count // 2)
        start = pl.multiple_of((me ^ r) * size, 16)
        dst_ref[place * size : (place + 1) * size] = src_ref[pl.ds(start, size), :]


def feed_kernel(
    held,
    count,
    half,
    info_ref,
    normed_ref,
    *refs,
):
    if half == 0:
        cot_refs = refs[:held]
        (
            resid_ref,
            wg_ref,
            wu_ref,
            wd_ref,
            acc_ref,
            grad_ref,
            gu_keep_ref,
            gu_send_ref,
            d_keep_ref,
            d_send_ref,
            cot_ref,
            cot_turned_ref,
            normed_turned_ref,
            turned_ref,
        ) = refs[held:]
        grad_in_ref = None
    else:
        (
            resid_ref,
            grad_in_ref,
            cot_ref,
            cot_turned_ref,
            normed_turned_ref,
            wg_ref,
            wu_ref,
            wd_ref,
            *out_refs,
            grad_ref,
            gu_keep_ref,
            gu_send_ref,
            d_keep_ref,
            d_send_ref,
            acc_ref,
        ) = refs
    step = pl.program_id(0)
    core = info_ref[1]
    if half == 0:
        span = cot_refs[0].shape[0]

        @pl.when(step == 0)
        def _():
            for phase in range(held):
                start = pl.multiple_of(lax.rem(info_ref[2] + held - phase, held) * span, span)
                cot_ref[pl.ds(start, span), :] = cot_refs[phase][...]
            cot_turned_ref[...] = cot_ref[...].T
            turned_ref[...] = normed_ref[...].T
            relative_rows(info_ref[0], count, turned_ref, normed_turned_ref)

    normed, cot = normed_ref[...], cot_ref[...]
    gate = dot(normed, wg_ref[...])
    up_value = dot(normed, wu_ref[...])
    grad_hidden = dot_nt(cot, wd_ref[...])
    square = gate * gate
    bend = jnp.tanh(gate * (SLOPE + (SLOPE * CUBE) * square))
    middle = 0.5 + 0.5 * bend
    gelu = gate * middle
    slope = middle * (1.0 + (1.0 - bend) * (gate * (SLOPE + (3.0 * SLOPE * CUBE) * square)))
    hidden = (gelu * up_value).astype(jnp.bfloat16)
    grad_gate = (grad_hidden * up_value * slope).astype(jnp.bfloat16)
    grad_up = (grad_hidden * gelu).astype(jnp.bfloat16)
    rb, cb = gu_keep_ref.shape[-2:]
    half_rows = count // 2 * rb
    turned = normed_turned_ref[...]
    for kind, grad in enumerate((grad_gate, grad_up)):
        part = dot(turned, grad).astype(jnp.bfloat16)
        for e in range(2):
            columns = part[:, e * cb : (e + 1) * cb]
            gu_keep_ref[:, kind, e] = columns[:half_rows].reshape(count // 2, rb, cb)
            gu_send_ref[:, kind, e] = columns[half_rows:].reshape(count // 2, rb, cb)
    part = dot(cot_turned_ref[...], hidden)
    first, second = part[:, :cb], part[:, cb:]
    mine = core == 0
    keep = jnp.where(mine, first, second).astype(jnp.bfloat16)
    send = jnp.where(mine, second, first).astype(jnp.bfloat16)
    d_keep_ref[0] = keep.reshape(count, rb, cb)
    d_send_ref[0] = send.reshape(count, rb, cb)
    result = dot(hidden, wd_ref[...])
    back = dot_nt(grad_gate, wg_ref[...]) + dot_nt(grad_up, wu_ref[...])

    @pl.when(step == 0)
    def _():
        acc_ref[...] = resid_ref[...] + result
        grad_ref[...] = back if grad_in_ref is None else grad_in_ref[...] + back

    @pl.when(step > 0)
    def _():
        acc_ref[...] += result
        grad_ref[...] += back

    if half == 1:

        @pl.when(step == pl.num_programs(0) - 1)
        def _():
            span = out_refs[0].shape[0]
            for phase in range(held):
                start = pl.multiple_of(lax.rem(info_ref[2] + held - phase, held) * span, span)
                out_refs[phase][...] = acc_ref[pl.ds(start, span), :].astype(jnp.bfloat16)


def feed_forward(half, info, normed, ins, wg, wu, wd, held, count):
    tokens, features = normed.shape
    width = wg.shape[1]
    chips = count // 2
    steps = chips // 2
    rb, cb = features // count, width // count
    whole = lambda shape: pl.BlockSpec(shape, lambda j, info: (0,) * len(shape))
    low = jnp.bfloat16
    gu = jax.ShapeDtypeStruct((chips, 2, count // 2, rb, cb), low)
    dd = jax.ShapeDtypeStruct((steps, count, rb, cb), low)
    gu_spec = pl.BlockSpec((chips, 2, 2, rb, cb), lambda j, info: (0, 0, j, 0, 0))
    dd_spec = pl.BlockSpec(
        (1, count, rb, cb), lambda j, info: (j ^ ((info[0] // 2) % steps), 0, 0, 0)
    )
    natural, turned = (tokens, features), (features, tokens)
    full = jax.ShapeDtypeStruct(natural, jnp.float32)
    shapes = [full, gu, gu, dd, dd]
    specs = [whole(natural), gu_spec, gu_spec, dd_spec, dd_spec]
    if half == 0:
        shapes, specs = [full] + shapes, [whole(natural)] + specs
    else:
        span = (tokens // held, features)
        shapes = [jax.ShapeDtypeStruct(span, low)] * held + shapes
        specs = [whole(span)] * held + specs
    scratch = [pltpu.VMEM(natural, jnp.float32)]
    if half == 0:
        shapes += [
            jax.ShapeDtypeStruct(natural, low),
            jax.ShapeDtypeStruct(turned, low),
            jax.ShapeDtypeStruct(turned, low),
        ]
        specs += [whole(natural), whole(turned), whole(turned)]
        scratch = [pltpu.VMEM(turned, low)]
    return pl.pallas_call(
        functools.partial(feed_kernel, held, count, half),
        grid_spec=pltpu.PrefetchScalarGridSpec(
            num_scalar_prefetch=1,
            grid=(steps,),
            in_specs=[
                whole(normed.shape),
                *[whole(x.shape) for x in ins],
                pl.BlockSpec((features, 2 * cb), lambda j, info: (0, j + half * steps)),
                pl.BlockSpec((features, 2 * cb), lambda j, info: (0, j + half * steps)),
                pl.BlockSpec((2 * cb, features), lambda j, info: (j + half * steps, 0)),
            ],
            out_specs=specs,
            scratch_shapes=scratch,
        ),
        out_shape=shapes,
        compiler_params=params(28),
        cost_estimate=cost(11),
        name=f"feed_forward_{half}",
    )(info, normed, *ins, wg, wu, wd)


def between_kernel(
    count,
    info_ref,
    grad_ref,
    resid_ref,
    gain_ref,
    cot_ref,
    att_ref,
    wm_ref,
    *refs,
):
    (
        out_hbm_ref,
        att_grad_ref,
        keep_hbm_ref,
        send_ref,
        gain_grad_ref,
        turned_ref,
        low_ref,
        out_ref,
        keep_ref,
        sems,
    ) = refs[-10:]
    features = resid_ref.shape[1]
    resid = resid_ref[...]
    root = lax.rsqrt(jnp.sum(resid * resid, axis=1, keepdims=True) / features + EPS)
    grad = grad_ref[...]
    unit = resid * root
    gain_grad_ref[...] = jnp.sum(grad * unit, axis=0, keepdims=True)
    pulled = grad * gain_ref[2:3]
    mean = jnp.sum(unit * pulled, axis=1, keepdims=True) / features
    result = cot_ref[...].astype(jnp.float32) + root * (pulled - unit * mean)
    out_ref[...] = result
    copies = [
        pltpu.make_async_copy(out_ref, out_hbm_ref, sems.at[0]),
        pltpu.make_async_copy(keep_ref, keep_hbm_ref, sems.at[1]),
    ]
    copies[0].start()
    mixed = result.astype(jnp.bfloat16)
    low_ref[...] = att_ref[...].astype(jnp.bfloat16)
    relative_rows(info_ref[0], count, low_ref, turned_ref)
    part = dot(turned_ref[...], mixed).astype(jnp.bfloat16)
    half = features // 2
    keep_ref[...] = part[:half].reshape(keep_ref.shape)
    copies[1].start()
    send_ref[...] = part[half:].reshape(send_ref.shape)
    att_grad_ref[...] = dot_nt(mixed, wm_ref[...]).astype(jnp.bfloat16)
    for copy in copies:
        copy.wait()


def between(info, grad, resid, gain, cot, att, wm, count, after, carry):
    tokens, features = grad.shape
    rb = features // count
    low = jnp.bfloat16
    piece = jax.ShapeDtypeStruct((count // 2, rb, features), low)
    ins = [info, grad, resid, gain, cot, att, wm]
    return launch(
        "between",
        functools.partial(between_kernel, count),
        ins,
        [SMEM] + [VMEM] * 6,
        [
            pltpu.HBM((tokens, features), jnp.float32),
            jax.ShapeDtypeStruct((tokens, features), low),
            pltpu.HBM(piece.shape, low),
            piece,
            jax.ShapeDtypeStruct((1, features), jnp.float32),
        ],
        [HBM, VMEM, HBM, VMEM, VMEM],
        16,
        [
            pltpu.VMEM((features, tokens), low),
            pltpu.VMEM((features, tokens), low),
            pltpu.VMEM((tokens, features), jnp.float32),
            pltpu.VMEM(piece.shape, low),
            pltpu.SemaphoreType.DMA((2,)),
        ],
        after=after,
        carry=carry,
        microseconds=3,
    )


def project_q_kernel(
    count,
    info_ref,
    dq_ref,
    normed_ref,
    wq_ref,
    other_ref,
    keep_ref,
    send_ref,
    back_ref,
    turned_ref,
    plain_ref,
):
    plain_ref[...] = normed_ref[...].T
    relative_rows(info_ref[0], count, plain_ref, turned_ref)
    dq = dq_ref[...]
    part = dot(turned_ref[...], dq).astype(jnp.bfloat16)
    half = part.shape[0] // 2
    keep_ref[...] = part[:half].reshape(keep_ref.shape)
    send_ref[0] = part[half:].reshape(send_ref.shape[1:])
    send_ref[1] = other_ref[...]
    back_ref[...] = dot_nt(dq, wq_ref[...])


def project_q(info, dq, normed, wq, other, count, after):
    tokens, features = dq.shape
    low = jnp.bfloat16
    piece = jax.ShapeDtypeStruct((count // 2, features // count, features), low)
    outs, _ = launch(
        "project_q",
        functools.partial(project_q_kernel, count),
        [info, dq, normed, wq, other],
        [SMEM] + [VMEM] * 4,
        [
            piece,
            jax.ShapeDtypeStruct((2,) + piece.shape, low),
            jax.ShapeDtypeStruct((tokens, features), jnp.float32),
            jax.ShapeDtypeStruct((features, tokens), low),
        ],
        [VMEM] * 4,
        14,
        [pltpu.VMEM((features, tokens), low)],
        after=after,
    )
    return outs


def project_kv_kernel(
    mine_ref,
    got_ref,
    turned_ref,
    back_ref,
    stream_ref,
    grad_ref,
    gain_ref,
    wk_ref,
    wv_ref,
    keep_ref,
    send_ref,
    out_ref,
    gain_grad_ref,
):
    features = stream_ref.shape[1]
    half = features // 2
    total = back_ref[...]
    for i, w_ref in enumerate((wk_ref, wv_ref)):
        grad = mine_ref[i] + got_ref[i]
        part = dot(turned_ref[...], grad).astype(jnp.bfloat16)
        keep_ref[i] = part[:half].reshape(keep_ref.shape[1:])
        send_ref[i] = part[half:].reshape(send_ref.shape[1:])
        total = total + dot_nt(grad, w_ref[...])
    stream = stream_ref[...]
    root = lax.rsqrt(jnp.sum(stream * stream, axis=1, keepdims=True) / features + EPS)
    unit = stream * root
    gain_grad_ref[...] = jnp.sum(total * unit, axis=0, keepdims=True)
    pulled = total * gain_ref[1:2]
    mean = jnp.sum(unit * pulled, axis=1, keepdims=True) / features
    out_ref[...] = grad_ref[...] + root * (pulled - unit * mean)


def project_kv(mine, got, turned, back, stream, grad, gain, wk, wv, count, after):
    tokens, features = stream.shape
    piece = jax.ShapeDtypeStruct((2, count // 2, features // count, features), jnp.bfloat16)
    outs, _ = launch(
        "project_kv",
        project_kv_kernel,
        [mine, got, turned, back, stream, grad, gain, wk, wv],
        [VMEM] * 9,
        [piece] * 2
        + [
            jax.ShapeDtypeStruct((tokens, features), jnp.float32),
            jax.ShapeDtypeStruct((1, features), jnp.float32),
        ],
        [VMEM] * 4,
        18,
        after=after,
    )
    return outs


def pick_of(pairs, info_ref):
    def tile(pair, at):
        first, second = at if isinstance(at, tuple) else (at, at)
        return pairs[pair][0][first] + pairs[pair][1][second]

    def value(pick):
        if len(pick) == 2:
            return tile(*pick)
        return jnp.where(info_ref[7] == 0, tile(*pick[:2]), tile(*pick[2:]))

    return value


def tiles_of(pairs):
    return [tuple(x.reshape((-1,) + x.shape[-2:]) for x in pair) for pair in pairs]


def fold(name, info, pairs, picks, after=(), carry=()):
    pairs = tiles_of(pairs)
    shape = pairs[0][0].shape[1:]

    def kernel(info_ref, *refs):
        ins, outs = refs[: 2 * len(pairs)], refs[2 * len(pairs) :]
        value = pick_of([ins[2 * i : 2 * i + 2] for i in range(len(pairs))], info_ref)
        for out_ref, chosen in zip(outs, picks):
            for slot, pick in enumerate(chosen):
                out_ref[slot] = value(pick)

    return launch(
        name,
        kernel,
        [info, *sum(pairs, ())],
        [SMEM] + [VMEM] * (2 * len(pairs)),
        [jax.ShapeDtypeStruct((len(chosen),) + shape, jnp.bfloat16) for chosen in picks],
        [VMEM] * len(picks),
        16,
        after=after,
        carry=carry,
    )


def lane_tiles(width):
    whole = width // LANES
    rest = width - whole * LANES
    return whole, rest, LANES // rest if rest else 1


def tile_count(pieces, width):
    whole, rest, each = lane_tiles(width)
    return pieces * whole + (-(-pieces // each) if rest else 0)


def pack_lanes(pieces):
    width = pieces[0].shape[1]
    whole, rest, each = lane_tiles(width)
    tiles = [piece[:, i * LANES : (i + 1) * LANES] for piece in pieces for i in range(whole)]
    if rest:
        ends = [piece[:, whole * LANES :] for piece in pieces]
        for i in range(0, len(ends), each):
            group = ends[i : i + each]
            spare = LANES - rest * len(group)
            if spare:
                group = group + [jnp.zeros((group[0].shape[0], spare), group[0].dtype)]
            tiles.append(jnp.concatenate(group, axis=1))
    return tiles


def unpack_lanes(tiles, pieces, width):
    whole, rest, each = lane_tiles(width)
    result = []
    for piece in range(pieces):
        parts = [tiles[piece * whole + i] for i in range(whole)]
        if rest:
            tile = tiles[pieces * whole + piece // each]
            start = piece % each * rest
            parts.append(tile[:, start : start + rest])
        result.append(jnp.concatenate(parts, axis=1) if len(parts) > 1 else parts[0])
    return result


def fold_seq(name, info, pairs, picks, seqs, slots, groups, width=None, after=(), carry=()):
    pairs = tiles_of(pairs)
    tall, wide = pairs[0][0].shape[1:]
    shape = (tall, LANES if width else wide)

    def kernel(info_ref, *refs):
        ins, outs, scratch_ref = refs[: 2 * len(pairs)], refs[2 * len(pairs) : -1], refs[-1]
        value = pick_of([ins[2 * i : 2 * i + 2] for i in range(len(pairs))], info_ref)
        here = info_ref[8]
        if width is None:
            for pick, block, slot in picks:
                scratch_ref[block ^ here, slot] = value(pick)
        else:
            totals = [value(pick) for pick, _, _ in sorted(picks, key=lambda x: x[2])]
            for s in range(seqs):
                pieces = [total[:, s * width : (s + 1) * width] for total in totals]
                for slot, tile in enumerate(pack_lanes(pieces)):
                    scratch_ref[s ^ here, slot] = tile
        for out_ref, group in zip(outs, groups):
            for i, d in enumerate(group):
                out_ref[i * slots : (i + 1) * slots] = scratch_ref[d]

    return launch(
        name,
        kernel,
        [info, *sum(pairs, ())],
        [SMEM] + [VMEM] * (2 * len(pairs)),
        [jax.ShapeDtypeStruct((len(group) * slots,) + shape, jnp.bfloat16) for group in groups],
        [VMEM] * len(groups),
        16,
        [pltpu.VMEM((seqs, slots) + shape, jnp.bfloat16)],
        after=after,
        carry=carry,
    )


def summed(refs, at):
    terms = [ref[at].astype(jnp.float32) for ref in refs]
    while len(terms) > 1:
        terms = [terms[i] + terms[i + 1] for i in range(0, len(terms), 2)]
    return terms[0]


def feed_end_kernel(seqs, *refs):
    ins, (gate_ref, up_ref, down_ref) = refs[:seqs], refs[seqs:]
    slots, rb, cb = ins[0].shape
    each = slots // 3
    for q in range(each):
        gate_ref[:, q * cb : (q + 1) * cb] = summed(ins, q)
        up_ref[:, q * cb : (q + 1) * cb] = summed(ins, each + q)
    for q in range(each):
        down_ref[q * rb : (q + 1) * rb] = summed(ins, 2 * each + q)


def feed_end(ins, after):
    slots, rb, cb = ins[0].shape
    each = slots // 3
    wide = pltpu.HBM((rb, each * cb), jnp.float32)
    return pl.pallas_call(
        ordered(functools.partial(feed_end_kernel, len(ins)), len(ins), after),
        out_shape=[wide, wide, pltpu.HBM((each * rb, cb), jnp.float32)],
        in_specs=[VMEM] * len(ins) + [ANY] * len(after),
        out_specs=[AUTO] * 3,
        compiler_params=params(8),
        cost_estimate=cost(1),
        name="feed_end",
    )(*ins, *after)


def join_kernel(info_ref, *refs):
    held = len(refs) - 1
    for phase in range(held):
        refs[held][lax.rem(info_ref[8] + phase, held)] = refs[phase][...]


def join(info, parts, after):
    shape = (len(parts),) + parts[0].shape
    outs, _ = launch(
        "join",
        join_kernel,
        [info, *parts],
        [SMEM] + [VMEM] * len(parts),
        [pltpu.HBM(shape, parts[0].dtype)],
        [AUTO],
        8,
        after=after,
    )
    return outs[0]


def mix_end_kernel(width, seqs, *refs):
    outs = refs[seqs:]
    tiles = [summed(refs[:seqs], slot) for slot in range(refs[0].shape[0])]
    for out_ref, value in zip(outs, unpack_lanes(tiles, len(outs), width)):
        out_ref[...] = value


def mix_end(ins, pieces, width, after):
    outs, _ = launch(
        "mix_end",
        functools.partial(mix_end_kernel, width, len(ins)),
        ins,
        [VMEM] * len(ins),
        [pltpu.HBM((ins[0].shape[1], width), jnp.float32)] * pieces,
        [AUTO] * pieces,
        8,
        after=after,
    )
    return outs


def sum_kernel(count, *refs):
    refs[count][...] = summed(refs[:count], slice(None)).astype(jnp.bfloat16)


def sum_of(name, terms, after):
    return pl.pallas_call(
        ordered(functools.partial(sum_kernel, len(terms)), len(terms), after),
        out_shape=jax.ShapeDtypeStruct(terms[0].shape, jnp.bfloat16),
        in_specs=[VMEM] * len(terms) + [ANY] * len(after),
        out_specs=VMEM,
        compiler_params=params(8),
        cost_estimate=cost(1),
        name=name,
    )(*terms, *after)


def unpack_kernel(vocab, chips, info_ref, *refs):
    shares = refs[: 2 * chips]
    embed_ref, filter_ref, score_ref, first_ref, second_ref, bias_ref, whole_ref = refs[2 * chips :]
    share = shares[0].shape[1]
    me = info_ref[0]
    for place in range(chips):
        for odd in range(2):
            start = pl.multiple_of((me ^ (2 * place + odd)) * share, 16)
            whole_ref[pl.ds(start, share), :] = shares[odd * chips + place][0].astype(jnp.float32)
    embed_ref[...] = whole_ref[:vocab]
    filter_ref[...] = whole_ref[vocab : vocab + 4]
    for i, ref in enumerate((score_ref, first_ref, second_ref)):
        ref[...] = whole_ref[vocab + 4 + i, :]
    heads, buckets = bias_ref.shape
    bias_ref[...] = whole_ref[vocab + 7 : vocab + 7 + heads, :buckets]


def unpack(info, mine, others, vocab, buckets, heads, after):
    chips = len(mine)
    _, share, features = mine[0].shape
    full = lambda *shape: pltpu.HBM(shape, jnp.float32)
    return pl.pallas_call(
        ordered(functools.partial(unpack_kernel, vocab, chips), 1 + 2 * chips, after),
        out_shape=[
            full(vocab, features),
            full(4, features),
            full(features),
            full(features),
            full(features),
            full(heads, buckets),
        ],
        in_specs=[SMEM] + [VMEM] * (2 * chips) + [ANY] * len(after),
        out_specs=[AUTO] * 6,
        scratch_shapes=[pltpu.VMEM((2 * chips * share, features), jnp.float32)],
        compiler_params=params(8),
        cost_estimate=cost(1),
        name="unpack",
    )(info, *mine, *others, *after)


AXES = ("batch", "seq")


def across_cores(x):
    count = lax.axis_size("batch")
    return lax.ppermute(x, "batch", [(i, i ^ 1) for i in range(count)])


def across_chips(x, chip):
    count = lax.axis_size("batch")
    return lax.ppermute(x, "batch", [(i, i ^ (2 * chip)) for i in range(count)])


def across_seq(x, d):
    count = lax.axis_size("seq")
    return lax.ppermute(x, "seq", [(i, i ^ d) for i in range(count)])


class Halving:
    def __init__(self, pairs, where):
        self.pairs, self.where = pairs, where

    def split(self, chosen, bit):
        keys = [key for key in self.where if chosen(key)]
        keep = [key for key in keys if not key[-1] & (1 << bit)]
        send = [key[:-1] + (key[-1] | (1 << bit),) for key in keep]
        return keep, send

    def picks(self, keys):
        return [self.where[key] for key in keys]


def exchange(name, info, state, plans, after=(), carry=(), held_back=False):
    lists, kept = [], []
    for chosen, bit in plans:
        keep, send = state.split(chosen, bit)
        kept.append(keep)
        lists += [state.picks(keep), state.picks(send)]
    outs, carried = fold(name, info, state.pairs, lists, after, carry)

    def start(sends):
        pairs, where = [], {}
        for place, ((_, bit), keep) in enumerate(zip(plans, kept)):
            pairs.append((outs[2 * place], across_chips(sends[place], 1 << bit)))
            where.update({key: (place, slot) for slot, key in enumerate(keep)})
        return Halving(pairs, where)

    return start if held_back else start(outs[1::2]), outs, carried


class Plan:
    def __init__(self, held):
        self.count = lax.axis_size("batch")
        self.seqs = lax.axis_size("seq")
        self.held = held
        self.group = self.seqs // (2 * held)
        me = lax.axis_index("batch")
        place = lax.axis_index("seq")
        self.me, self.place = me, place
        self.core = me % 2
        self.row = place // self.group
        self.part = 2 * (place % self.group) + self.core
        self.parts = 2 * self.group
        self.perms = []
        for phase in range(held):
            perm = []
            for b in range(self.count):
                for s in range(self.seqs):
                    row = held * (b % 2) + (s + phase) % held
                    part = s // held
                    target = (b - b % 2 + part % 2, self.group * row + part // 2)
                    perm.append((b * self.seqs + s, target[0] * self.seqs + target[1]))
            self.perms.append(perm)

    def blocks_of(self, x):
        return [
            lax.dynamic_index_in_dim(x, (self.place + phase) % self.held, 0, keepdims=False)
            for phase in range(self.held)
        ]

    def parts_of(self, x):
        return [lax.ppermute(x, AXES, perm) for x, perm in zip(self.blocks_of(x), self.perms)]

    def bytes_of(self, x):
        held = self.held
        main = self.parts_of(x)
        ends = jnp.concatenate([x[:, :4], x[:, -4:]], axis=1)
        sides = []
        for phase in range(held):
            perm = []
            for b in range(self.count):
                for s in range(self.seqs):
                    row = held * (b % 2) + (s + phase) % held
                    part = s // held + {0: -1, held - 1: 1}.get(s % held, self.parts)
                    if 0 <= part < self.parts:
                        target = (b - b % 2 + part % 2, self.group * row + part // 2)
                        perm.append((b * self.seqs + s, target[0] * self.seqs + target[1]))
            send = lax.dynamic_index_in_dim(ends, (self.place + phase) % held, 0, keepdims=False)
            sides.append(lax.ppermute(send, AXES, perm))
        low = lax.dynamic_index_in_dim(
            jnp.stack(sides), (self.row + 1) % held, 0, keepdims=False
        )[4:]
        high = lax.dynamic_index_in_dim(jnp.stack(sides), self.row % held, 0, keepdims=False)[:4]
        low = jnp.where(self.part > 0, low, -1)
        high = jnp.where(self.part < self.parts - 1, high, -1)
        order = (self.row - jnp.arange(held)) % held
        middle = jnp.take(jnp.stack(main), order, axis=0).reshape(-1)
        return jnp.concatenate([low, middle, high]).reshape(-1, 4)

    def gather(self, x):
        other = across_cores(x)
        pair = jnp.stack([jnp.where(self.core == 0, x, other), jnp.where(self.core == 0, other, x)])
        if self.group > 1:
            groups = [
                list(range(first, first + self.group))
                for first in range(0, self.seqs, self.group)
            ]
            pair = lax.all_gather(pair, "seq", axis_index_groups=groups)
        return pair.reshape((-1,) + x.shape[1:])

    def scatter(self, x):
        if self.group > 1:
            groups = [
                list(range(first, first + self.group))
                for first in range(0, self.seqs, self.group)
            ]
            x = lax.psum_scatter(
                x, "seq", scatter_dimension=0, axis_index_groups=groups, tiled=True
            )
        pair = x.reshape((2, -1) + x.shape[1:])
        got = across_cores(lax.dynamic_index_in_dim(pair, 1 - self.core, 0, keepdims=False))
        mine = lax.dynamic_index_in_dim(pair, self.core, 0, keepdims=False)
        return mine.astype(jnp.float32) + got.astype(jnp.float32)


def shards(
    byte_values,
    segments,
    byte_mask,
    embedding,
    filter_weight,
    score_weight,
    first_gain,
    query_weight,
    key_weight,
    value_weight,
    merge_weight,
    position_bias,
    second_gain,
    gate_weight,
    up_weight,
    down_weight,
    cotangent,
):
    count = lax.axis_size("batch")
    seqs = lax.axis_size("seq")
    held, width = byte_values.shape
    row_len = segments.shape[1]
    vocab, features = embedding.shape
    hidden_size = gate_weight.shape[1]
    heads = position_bias.shape[1]
    bucket_count = position_bias.shape[0]
    total = row_len // 2
    plan = Plan(held)
    tokens = total // plan.parts
    chips = count // 2
    levels = chips.bit_length() - 1
    blocks = tokens // BLOCK
    other_part = plan.part ^ 1

    bases = [plan.part * blocks, other_part * blocks] if plan.group == 1 else [0, 0]
    info = jnp.stack(
        [
            jnp.asarray(value, jnp.int32)
            for value in (
                plan.me,
                plan.core,
                plan.row % held,
                plan.part * blocks,
                plan.part * 2 * tokens,
                bases[0],
                bases[1],
                plan.me // chips,
                plan.place,
            )
        ]
    )
    ids = plan.bytes_of(jnp.where(byte_mask > 0, byte_values, -1))
    groups = tokens // 2
    spare = -(groups + 2) % 8
    ids = jnp.concatenate([ids[1:], jnp.full((spare, 4), -1, jnp.int32), ids[:1]])
    cuts = jnp.sum((segments[:, :, None] < jnp.arange(1, 4)).astype(jnp.int32), axis=1)
    cuts = (cuts + 1) // 2
    both = jnp.concatenate([cuts, across_cores(cuts)])
    own_first = jnp.where(plan.row // held == plan.core, 0, held)
    cuts = lax.dynamic_index_in_dim(both, own_first + plan.row % held, 0, keepdims=False)
    bias = hbm(bias_tiles(position_bias.T))
    embedding = hbm(embedding)
    gate_weight, up_weight, down_weight = map(hbm, (gate_weight, up_weight, down_weight))
    query_weight, key_weight, value_weight = map(hbm, (query_weight, key_weight, value_weight))
    merge_weight = hbm(merge_weight)
    head_size = features // heads
    words = -(-(vocab + 7 + heads) // (16 * count)) * (16 * count)
    vectors = jnp.stack([score_weight, first_gain, second_gain])
    stream, normed, q, kv = mixer_forward(
        info,
        ids,
        embedding,
        filter_weight,
        vectors,
        query_weight,
        key_weight,
        value_weight,
        tokens,
        row_len,
        [bias],
    )
    normed, stream = hbm(normed), hbm(stream)
    ends = (stream, merge_weight, vectors)
    cot_blocks = plan.blocks_of(cotangent)
    if plan.group == 1:
        kvs = [kv, across_cores(kv)]
        begun, later = attention_forward(
            "attention_own", head_size, info, q, kvs[0], bias, cuts, carry=cot_blocks[1:]
        )
        (att, lse, resid, normed_two), _ = attention_forward(
            "attention_other", head_size, info, q, kvs[1], bias, cuts, begun, ends
        )
    else:
        kvs = [jnp.stack([plan.gather(kv[0]), plan.gather(kv[1])])]
        later = cot_blocks[1:]
        (att, lse, resid, normed_two), _ = attention_forward(
            "attention_all", head_size, info, q, kvs[0], bias, cuts, (), ends
        )
    cots = [lax.ppermute(x, AXES, perm) for x, perm in zip([cot_blocks[0], *later], plan.perms)]

    weights = (gate_weight, up_weight, down_weight)
    acc, grad_two, *grads, cot, cot_turned, normed_turned = feed_forward(
        0, info, normed_two, [*cots, resid], *weights, held, count
    )
    halves = [grads]
    *results, grad_two, gu_keep, gu_send, d_keep, d_send = feed_forward(
        1,
        info,
        normed_two,
        [acc, grad_two, cot, cot_turned, normed_turned],
        *weights,
        held,
        count,
    )
    halves.append([gu_keep, gu_send, d_keep, d_send])
    early = count // 4

    def upwards(key):
        return key[0] == "down" or key[3] < early

    def downwards(key):
        return not upwards(key)

    states = []

    def start_half(half, after):
        gu_keep, gu_send, d_keep, d_send = halves[half]
        pairs = [(gu_keep, across_cores(gu_send)), (d_keep, across_cores(d_send))]
        where = {}
        for r in range(chips):
            for n in range(count):
                where["gu", half, 0, n, r] = (0, r * count + n)
        for r in range(chips // 2):
            for n in range(count):
                where["down", half, 0, n, r] = (1, r * count + n)
        state = Halving(pairs, where)
        first = None
        for level in range(levels - 1):
            state, outs, _ = exchange(
                f"feed_{half}_{level}",
                info,
                state,
                [(upwards, level), (downwards, levels - 1 - level)],
                after if level == 0 else (),
            )
            first = first or outs
        states.append(state)
        return first

    first = start_half(0, [grad_two])
    (grad_resid, att_grad, m_keep, m_send, second_part), later = between(
        info, grad_two, resid, vectors, cot, att, merge_weight, count, [first[0]], results[1:]
    )
    out_parts = [
        lax.ppermute(x, AXES, [(b, a) for a, b in perm])
        for x, perm in zip([results[0], *later], plan.perms)
    ]
    first = start_half(1, [second_part])
    dq, dkvs, tiles = attention_backward(
        head_size, info, hbm(q), att_grad, [hbm(kvs[0]), *kvs[1:]], bias, cuts, lse, att, [first[0]]
    )

    where = {}
    for half, state in enumerate(states):
        for key, (pair, slot) in state.where.items():
            where[key] = (2 * half + pair, slot)
    top = 1 << (levels - 1)
    for key in [key for key in where if key[0] == "down"]:
        _, half, kind, n, r = key
        mine, other = where["down", 0, 0, n, 0], where["down", 1, 0, n, 0]
        if half == 0:
            where["one", 2, 0, n, 0] = mine + other
            where["one", 2, 0, n, top] = other + mine
    where = {key: value for key, value in where.items() if key[0] != "down"}
    state = Halving(states[0].pairs + states[1].pairs, where)
    layer_output = join(info, out_parts, [dq])
    crossing = [dkvs[1]] if plan.group == 1 else []
    state, lasts, crossing = exchange(
        "feed_last",
        info,
        state,
        [
            (lambda key: key[0] == "one" or key[3] < early, levels - 1),
            (lambda key: key[0] == "gu" and key[3] >= early, 0),
        ],
        [layer_output],
        crossing,
    )
    if plan.group == 1:
        mine, got = hbm(dkvs[0]), across_cores(crossing[0])
    else:
        mine = jnp.stack([plan.scatter(dkvs[0][i]).astype(jnp.bfloat16) for i in range(2)])
        got = jnp.zeros_like(mine)
    bias_part = bucket_sums(tiles, [lasts[0]])
    q_keep, qm_send, back, turned = project_q(
        info, hbm(dq), normed, query_weight, m_send, count, [bias_part]
    )
    qm_got = across_cores(qm_send)
    kv_keep, kv_send, grad_stream, first_part = project_kv(
        mine,
        got,
        turned,
        back,
        stream,
        hbm(grad_resid),
        vectors,
        key_weight,
        value_weight,
        count,
        [],
    )

    each = count // seqs
    picks = []
    for key, pick in state.where.items():
        if key[0] == "one":
            picks.append((pick, key[3] // each, 2 * each + key[3] % each))
        else:
            kind, block = key[3] // chips, key[1] * chips + key[3] % chips
            picks.append((pick, block // each, kind * each + block % each))
    slots = 3 * each
    groups = [list(range(0, seqs, 2)), list(range(1, seqs, 2))]
    (z_keep, z_send), (kv_send,) = fold_seq(
        "feed_seq", info, state.pairs, picks, seqs, slots, groups, after=[first_part], carry=[kv_send]
    )
    kv_got = across_cores(kv_send)
    z_got = across_seq(z_send, 1)
    where = {}
    for r in range(chips):
        where["p", 0, r] = (0, r)
        where["p", 3, r] = (1, (r, chips + r))
        for kind in (1, 2):
            where["p", kind, r] = (2, (kind - 1) * chips + r)
    mixes = Halving([(q_keep, qm_got), (hbm(m_keep), qm_got), (kv_keep, kv_got)], where)

    def mix_step(mixes, level, after, carry=(), held_back=False):
        return exchange(
            f"mix_{level}",
            info,
            mixes,
            [
                (lambda key: key[1] in (1, 3), level),
                (lambda key: key[1] in (0, 2), levels - 1 - level),
            ],
            after,
            carry,
            held_back,
        )

    mixes, outs, _ = mix_step(mixes, 0, [z_keep])
    e_keep, e_send = mixer_backward(
        info,
        ids,
        embedding,
        filter_weight,
        vectors,
        grad_stream,
        first_part,
        second_part,
        bias_part,
        row_len,
        vocab,
        words,
        count,
        [z_keep, outs[0]],
    )

    def seq_step(name, z_keep, z_got, slots, step, after, carry):
        held_now = z_keep.shape[0] // slots
        lists = [
            [(0, d * slots + i) for d in range(first, held_now, 2) for i in range(slots)]
            for first in range(2)
        ]
        (z_keep, z_send), carried = fold(
            f"{name}_seq_{step}", info, [(z_keep, z_got)], lists, after, carry
        )
        return z_keep, across_seq(z_send, step), carried

    last, step, carry = e_keep, 2, [e_send]
    while step < seqs:
        z_keep, z_got, carry = seq_step("feed", z_keep, z_got, slots, step, [last], carry)
        last = z_keep
        step *= 2
    for level in range(1, levels):
        mixes, outs, _ = mix_step(mixes, level, [last], (), level == levels - 1)
        last = outs[0]
    e_got = across_cores(carry[0])
    small = Halving([(e_keep, e_got)], {("e", r): (0, r) for r in range(chips)})
    sends = outs[1::2]
    for level in range(levels):
        small, outs, sends = exchange(
            f"small_{level}",
            info,
            small,
            [(lambda key: True, level)],
            [last] if level == 0 else [],
            sends if level == 0 else [],
        )
        if level == 0:
            mixes = mixes(sends)
    (share,), _ = fold("small_chips", info, small.pairs, [small.picks([("e", 0)])])
    seq_parts = [share] + [across_seq(share, d) for d in range(1, seqs)]
    picks = [(pick, None, key[1]) for key, pick in mixes.where.items()]
    gate_grad, up_grad, down_grad = feed_end([z_keep, z_got], [share])
    share_width = features // seqs
    mix_sends, _ = fold_seq(
        "mix_seq",
        info,
        mixes.pairs,
        picks,
        seqs,
        tile_count(4, share_width),
        [[d] for d in range(seqs)],
        share_width,
        after=[gate_grad],
    )
    mix_arrived = [mix_sends[0]] + [across_seq(mix_sends[d], d) for d in range(1, seqs)]
    share = sum_of("small_seq", seq_parts, [mix_sends[0]])
    shares = [share] + [across_chips(share, r) for r in range(1, chips)]
    embed, filters, score, first, second, bias_sum = unpack(
        info, shares, [across_cores(x) for x in shares], vocab, bucket_count, heads, []
    )
    query_grad, key_grad, value_grad, merge_grad = mix_end(mix_arrived, 4, share_width, [score])
    return (
        layer_output,
        embed,
        filters,
        score,
        first,
        query_grad,
        key_grad,
        value_grad,
        merge_grad,
        bias_sum.T,
        second,
        gate_grad,
        up_grad,
        down_grad.T,
    )


def solution(mesh):
    in_specs = (
        P("batch", "seq"),
        P("batch", None),
        P("batch", "seq"),
        P(),
        P(),
        P(),
        P(),
        P(),
        P(),
        P(),
        P(),
        P(),
        P(),
        P(),
        P(),
        P(),
        P("batch", "seq", None),
    )
    out_specs = (
        P("batch", "seq", None),
        P(),
        P(),
        P(),
        P(),
        P("batch", "seq"),
        P("batch", "seq"),
        P("batch", "seq"),
        P("batch", "seq"),
        P(),
        P(),
        P("batch", "seq"),
        P("batch", "seq"),
        P("batch", "seq"),
    )
    return jax.shard_map(shards, mesh=mesh, in_specs=in_specs, out_specs=out_specs, check_vma=False)
```

```python
import functools

import jax
import jax.numpy as jnp
from jax import lax
from jax.experimental import pallas as pl
from jax.experimental.pallas import tpu as pltpu
from jax.sharding import PartitionSpec as P

EPS = 1e-06
LIMITS = (12, 16, 23, 32, 46, 64, 91)
NEG = -1e30
LANES = 128
BLOCK = 128
FAR = 2
CUBE = 0.044715
SLOPE = 0.7978845608028654
MEGA = 1 << 20


def dot(a, b):
    return lax.dot_general(a, b, (((1,), (0,)), ((), ())), preferred_element_type=jnp.float32)


def dot_nt(a, b):
    return lax.dot_general(a, b, (((1,), (1,)), ((), ())), preferred_element_type=jnp.float32)


def params(megabytes):
    return pltpu.CompilerParams(vmem_limit_bytes=megabytes * MEGA)


def cost(microseconds):
    return pl.CostEstimate(flops=int(microseconds * 1e+09), bytes_accessed=1, transcendentals=0)


VMEM = pl.BlockSpec(memory_space=pltpu.VMEM)
ANY = pl.BlockSpec(memory_space=pl.ANY)
HBM = pl.BlockSpec(memory_space=pltpu.HBM)
AUTO = pl.BlockSpec()
SMEM = pl.BlockSpec(memory_space=pltpu.SMEM)


def hbm(x):
    return pltpu.with_memory_space_constraint(x, pltpu.HBM)


def ordered(kernel, inputs, after):
    def with_others(*refs):
        kernel(*refs[:inputs], *refs[inputs + len(after) :])

    return with_others


def launch(name, kernel, ins, in_specs, outs, out_specs, megabytes, scratch=(), after=(), carry=(), microseconds=1.0
):
    given, made = len(ins), len(outs)
    skip = len(after) + len(carry)

    def body(*refs):
        rest = refs[given + skip :]
        kernel(*refs[:given], *rest[:made], *rest[made + len(carry) :])

    results = pl.pallas_call(
        body,
        out_shape=[*outs, *[jax.ShapeDtypeStruct(x.shape, x.dtype) for x in carry]],
        in_specs=[*in_specs, *[ANY] * skip],
        out_specs=[*out_specs, *[ANY] * len(carry)],
        scratch_shapes=list(scratch),
        input_output_aliases={given + len(after) + i: made + i for i in range(len(carry))},
        compiler_params=params(megabytes),
        cost_estimate=cost(microseconds),
        name=name,
    )(*ins, *after, *carry)
    return results[:made], results[made:]


def bucket_of(relative):
    distance = jnp.abs(relative)
    far = jnp.full_like(distance, 8)
    for limit in LIMITS:
        far = far + jnp.where(distance >= limit, 1, 0)
    return jnp.where(distance < 8, distance, far) + jnp.where(relative > 0, 16, 0)


def split_three(x):
    parts = []
    for _ in range(3):
        high = x.astype(jnp.bfloat16)
        parts.append(high)
        x = x - high.astype(jnp.float32)
    return parts


def bias_kernel(table_ref, out_ref, tile_ref, sems):
    copies = []
    heads, buckets = table_ref.shape
    wide = 2 * BLOCK
    parts = split_three(table_ref[...])
    bucket = lax.broadcasted_iota(jnp.int32, (buckets, wide), 0)
    entry = lax.broadcasted_iota(jnp.int32, (buckets, wide), 1)
    gap = jnp.where(entry < BLOCK, entry, entry - wide)
    for delta in range(3):
        hot = jnp.where(bucket_of((delta - 1) * BLOCK - gap) == bucket, 1.0, 0.0)
        hot = hot.astype(jnp.bfloat16)
        rows = (dot(parts[2], hot) + dot(parts[1], hot)) + dot(parts[0], hot)
        for h in range(heads):
            row = jnp.broadcast_to(rows[h : h + 1], (BLOCK, wide))
            tile_ref[delta, h] = pltpu.roll(row, 0, 1, stride=1, stride_axis=0)[:, :BLOCK]
        copies.append(pltpu.make_async_copy(tile_ref.at[delta], out_ref.at[delta], sems.at[delta]))
        copies[-1].start()
    for copy in copies:
        copy.wait()


def bias_tiles(table):
    outs, _ = launch(
        "bias_tiles",
        bias_kernel,
        [table],
        [VMEM],
        [pltpu.HBM((3, table.shape[0], BLOCK, BLOCK), jnp.float32)],
        [HBM],
        6,
        [
            pltpu.VMEM((3, table.shape[0], BLOCK, BLOCK), jnp.float32),
            pltpu.SemaphoreType.DMA((3,)),
        ],
        microseconds=2,
    )
    return outs[0]


def fill_tiles(near_ref, h, tile_ref):
    for delta in range(3):
        tile_ref[1 + delta] = near_ref[delta, h]
    tile_ref[0] = jnp.broadcast_to(near_ref[0, h, :1, BLOCK - 1 :], (BLOCK, BLOCK))
    tile_ref[4] = jnp.broadcast_to(near_ref[2, h, BLOCK - 1 :, :1], (BLOCK, BLOCK))


def by_head(turned, size):
    empty = jnp.zeros((size, turned.shape[1]), turned.dtype)
    left = jnp.concatenate([turned[:size], empty], axis=0)
    right = jnp.concatenate([empty, turned[size:]], axis=0)
    return jnp.concatenate([left, right], axis=1)


def lower_rows(cut_ref, start, rows, heads):
    count = rows[0].shape[1] if rows else heads[1]
    place = start + lax.broadcasted_iota(jnp.int32, (16, count), 1)
    row = lax.broadcasted_iota(jnp.int32, (16, count), 0)
    segment = sum(jnp.where(place >= cut_ref[i], 1, 0) for i in range(3))
    mask = jnp.where((row < 4) & (segment != row), NEG, 0.0)
    blocks = []
    for head in range(heads[0]):
        block = mask
        if rows:
            for i, part in enumerate(split_three(rows[head])):
                block = jnp.where(row == 4 + i, part.astype(jnp.float32), block)
        blocks.append(block.astype(jnp.bfloat16))
    block = jnp.concatenate(blocks, axis=1)
    return jnp.concatenate([block, jnp.zeros((LANES - 16, block.shape[1]), jnp.bfloat16)], axis=0)


def segment_hots(cut_ref, start, count, inside, outside):
    place = start + lax.broadcasted_iota(jnp.int32, (count, LANES), 0)
    lane = lax.broadcasted_iota(jnp.int32, (count, LANES), 1)
    segment = sum(jnp.where(place >= cut_ref[i], 1, 0) for i in range(3))
    value = jnp.where(segment == lane, inside, outside)
    return jnp.where(lane < 4, value, 0.0).astype(jnp.bfloat16)


TILE = 32
FORWARD_TILE = 64
GUARD = 8
MAIN = 24


def row_of(ref):
    return ref[...].reshape(1, -1)


def tile_rows(base, size=TILE):
    return pl.ds(pl.multiple_of(base, 8), size)


def with_sides(ref, lead, base, lanes, size=TILE):
    return ref[(*lead, pl.ds(pl.multiple_of(base - 8, 8), size + 16), lanes)]


def middle(x):
    return x[8:-8]


def down(x):
    return middle(pltpu.roll(x, 1, 0))


def up(x):
    return middle(pltpu.roll(x, x.shape[0] - 1, 0))


def lane_sum(x):
    return jnp.broadcast_to(jnp.sum(x, axis=1, keepdims=True), x.shape)


def offsets_of(rows):
    return {
        -2: down(rows[2]),
        -1: down(rows[3]),
        0: middle(rows[0]),
        1: middle(rows[1]),
        2: middle(rows[2]),
        3: middle(rows[3]),
        4: up(rows[0]),
        5: up(rows[1]),
    }


def spread_of(phase, j, one, two, three, four, coefs):
    pair = j - j % 2
    third = three / 3.0
    zero = jnp.zeros_like(third)
    half, quarter = two * 0.5, four * 0.25

    def add(o, value):
        coefs[o] = coefs[o] + value if o in coefs else value

    add(j, one + third)
    for o in (pair, pair + 1):
        add(o, half)
    for o in range(4):
        add(o, quarter)
    add(j + 1, jnp.where(phase <= 1, third, zero))
    add(j + 2, jnp.where(phase == 0, third, zero))
    add(j - 1, jnp.where(phase >= 1, third, zero))
    add(j - 2, jnp.where(phase == 2, third, zero))


def pooled_dots(phase, j, dots):
    pair = j - j % 2
    zero = jnp.zeros_like(dots[0])
    two = 0.5 * (dots[pair] + dots[pair + 1])
    four = 0.25 * ((dots[0] + dots[1]) + (dots[2] + dots[3]))
    three = dots[j] + jnp.where(phase <= 1, dots[j + 1], zero)
    three = three + jnp.where(phase == 0, dots[j + 2], zero)
    three = three + jnp.where(phase >= 1, dots[j - 1], zero)
    three = three + jnp.where(phase == 2, dots[j - 2], zero)
    return dots[j], two, three / 3.0, four


def lane_chunks(features):
    return [slice(i, i + LANES) for i in range(0, features, LANES)]


def over_tiles(first, rows, body, size=TILE):
    def step(t, carry):
        body(first + t * size)
        return carry

    lax.fori_loop(0, rows // size, step, 0)


def convolve_all(info_ref, ids_ref, emb_ref, filt_ref, score_ref, e_ref, c_ref, dot_ref, row_len):
    count = ids_ref.shape[0]
    words, features = emb_ref.shape
    score = row_of(score_ref)
    group = info_ref[4] // 4
    vocab = lax.broadcasted_iota(jnp.int32, (count, words), 1)
    edge = jnp.zeros((GUARD, LANES), jnp.float32)
    for j in range(4):
        hot = jnp.where(ids_ref[:, j : j + 1] == vocab, 1.0, 0.0).astype(jnp.bfloat16)
        e_ref[j] = dot(hot, emb_ref[...])
        dot_ref[j, :GUARD] = edge
        dot_ref[j, count - GUARD :] = edge

    def tile(base):
        parts = [jnp.zeros((TILE, LANES), jnp.float32) for _ in range(4)]
        for lanes in lane_chunks(features):
            near = offsets_of([with_sides(e_ref, (j,), base, lanes) for j in range(4)])
            taps = [filt_ref[k : k + 1, lanes] for k in range(4)]
            for j in range(4):
                value = taps[0] * near[j - 2]
                for k in range(1, 4):
                    value = value + taps[k] * near[j + k - 2]
                c_ref[j, tile_rows(base), lanes] = value
                parts[j] = parts[j] + value * score[:, lanes]
        places = base - MAIN + group + lax.broadcasted_iota(jnp.int32, (TILE, LANES), 0)
        for j in range(4):
            inside = 4 * places + j < row_len
            dot_ref[j, tile_rows(base)] = jnp.where(inside, lane_sum(parts[j]), 0.0)

    over_tiles(GUARD, count - 2 * GUARD, tile)


def tile_weights(info_ref, dot_ref, base, row_len, size):
    dots = offsets_of([with_sides(dot_ref, (j,), base, slice(None), size) for j in range(4)])
    places = base - MAIN + info_ref[4] // 4
    places = places + lax.broadcasted_iota(jnp.int32, (size, LANES), 0)
    phases, weights = [], []
    for j in range(4):
        phase = lax.rem(places + 3 + j, 3)
        scores = pooled_dots(phase, j, dots)
        highest = jnp.maximum(jnp.maximum(scores[0], scores[1]), jnp.maximum(scores[2], scores[3]))
        powers = [jnp.exp(score - highest) for score in scores]
        share = 1.0 / ((powers[0] + powers[1]) + (powers[2] + powers[3]))
        phases.append(phase)
        weights.append([power * share for power in powers])
    limits = {o: (4 * places + o < row_len) for o in (4, 5)}
    return phases, weights, limits


def token_coefs(phases, weights, limits, scale):
    result = []
    for h in range(2):
        coefs = {}
        for j in (2 * h, 2 * h + 1):
            spread_of(phases[j], j, *weights[j], coefs)
        for o in coefs:
            if o in limits:
                coefs[o] = jnp.where(limits[o], coefs[o], 0.0)
            coefs[o] = coefs[o] * scale
        result.append(coefs)
    return result


COEFS = [(0, o) for o in range(-2, 4)] + [(1, o) for o in range(6)]


def mixer_kernel(
    row_len,
    info_ref,
    ids_ref,
    emb_ref,
    filt_ref,
    score_ref,
    gain_ref,
    wq_ref,
    wk_ref,
    wv_ref,
    stream_out_ref,
    normed_out_ref,
    q_ref,
    kv_ref,
    e_ref,
    c_ref,
    dot_ref,
    pair_ref,
    root_ref,
    weight_ref,
    sems,
    stream_ref,
    normed_ref,
):
    copies = [
        pltpu.make_async_copy(w_ref, weight_ref.at[i], sems.at[i])
        for i, w_ref in enumerate((wk_ref, wv_ref, wq_ref))
    ]
    for copy in copies:
        copy.start()
    tokens, features = stream_ref.shape
    gain = row_of(gain_ref)
    chunks = lane_chunks(features)
    convolve_all(
        info_ref, ids_ref, emb_ref, filt_ref, score_ref, e_ref, c_ref, dot_ref, row_len
    )

    size = pair_ref.shape[1] // 2

    def tile(base):
        coefs = token_coefs(*tile_weights(info_ref, dot_ref, base, row_len, size), 0.5)
        squares = [jnp.zeros((size, LANES), jnp.float32) for _ in range(2)]
        rows = pl.ds(pl.multiple_of(2 * (base - MAIN), 2 * size), 2 * size)
        for i, lanes in enumerate(chunks):
            conv = offsets_of([with_sides(c_ref, (j,), base, lanes, size) for j in range(4)])
            for h in range(2):
                mixed = None
                for o, coef in coefs[h].items():
                    term = coef * conv[o]
                    mixed = term if mixed is None else mixed + term
                squares[h] = squares[h] + mixed * mixed
                pair_ref[i, pl.ds(h, size, stride=2), :] = mixed
        for h in range(2):
            root = lax.rsqrt(lane_sum(squares[h]) / features + EPS)
            root_ref[pl.ds(h, size, stride=2), :] = root
        for i, lanes in enumerate(chunks):
            stream = pair_ref[i]
            stream_ref[rows, lanes] = stream
            normed = stream * root_ref[...] * gain[:, lanes]
            normed_ref[rows, lanes] = normed.astype(jnp.bfloat16)

    over_tiles(MAIN, tokens // 2, tile, size)
    kept = [
        pltpu.make_async_copy(stream_ref, stream_out_ref, sems.at[3]),
        pltpu.make_async_copy(normed_ref, normed_out_ref, sems.at[4]),
    ]
    for copy in kept:
        copy.start()
    for i in range(2):
        copies[i].wait()
        kv_ref[i] = dot(normed_ref[...], weight_ref[i]).astype(jnp.bfloat16)
    copies[2].wait()
    q_ref[...] = dot(normed_ref[...], weight_ref[2]).astype(jnp.bfloat16)
    for copy in kept:
        copy.wait()


def mixer_forward(info, ids, emb, filt, score, gain, wq, wk, wv, tokens, row_len, after):
    features = emb.shape[1]
    count = ids.shape[0]
    low = jnp.bfloat16
    full = jnp.float32
    outs, _ = launch(
        "mixer_forward",
        functools.partial(mixer_kernel, row_len),
        [info, ids, emb, filt, score, gain, wq, wk, wv],
        [SMEM] + [VMEM] * 5 + [HBM] * 3,
        [
            pltpu.HBM((tokens, features), full),
            pltpu.HBM((tokens, features), low),
            jax.ShapeDtypeStruct((tokens, features), low),
            jax.ShapeDtypeStruct((2, tokens, features), low),
        ],
        [HBM, HBM, VMEM, VMEM],
        24,
        [
            pltpu.VMEM((4, count, features), full),
            pltpu.VMEM((4, count, features), full),
            pltpu.VMEM((4, count, LANES), full),
            pltpu.VMEM((features // LANES, 2 * FORWARD_TILE, LANES), full),
            pltpu.VMEM((2 * FORWARD_TILE, LANES), full),
            pltpu.VMEM((3, features, features), low),
            pltpu.SemaphoreType.DMA((5,)),
            pltpu.VMEM((tokens, features), full),
            pltpu.VMEM((tokens, features), low),
        ],
        after=after,
        microseconds=8,
    )
    return outs


def mixer_back_kernel(
    row_len,
    vocab_size,
    info_ref,
    ids_ref,
    emb_ref,
    filt_ref,
    score_ref,
    grad_ref,
    first_ref,
    second_ref,
    bias_ref,
    keep_ref,
    send_ref,
    e_ref,
    c_ref,
    dot_ref,
    coef_ref,
    g_ref,
    low_ref,
    turn_ref,
    embed_ref,
    small_ref,
):
    tokens, features = grad_ref.shape
    groups = tokens // 2
    chunks = lane_chunks(features)
    count = ids_ref.shape[0]
    inner = count - 2 * GUARD
    score_row = row_of(score_ref)
    convolve_all(
        info_ref, ids_ref, emb_ref, filt_ref, score_ref, e_ref, c_ref, dot_ref, row_len
    )
    before = jnp.zeros((MAIN, LANES), jnp.float32)
    behind = jnp.zeros((count - MAIN - groups, LANES), jnp.float32)
    for i, lanes in enumerate(chunks):
        turn_ref[i] = grad_ref[:, lanes]
        for h in range(2):
            g_ref[h, :MAIN, lanes] = before
            g_ref[h, MAIN + groups :, lanes] = behind
            g_ref[h, MAIN : MAIN + groups, lanes] = turn_ref[i, pl.ds(h, groups, stride=2), :]
    for place in range(2 * len(COEFS)):
        coef_ref[place, :MAIN] = before
        coef_ref[place, MAIN + groups :] = behind
    small_ref[...] = jnp.zeros_like(small_ref)

    def pull_tile(base):
        phases, weights, limits = tile_weights(info_ref, dot_ref, base, row_len, TILE)
        coefs = token_coefs(phases, weights, limits, 0.5)
        sums = {}
        for lanes in chunks:
            conv = offsets_of([with_sides(c_ref, (j,), base, lanes) for j in range(4)])
            grads = [g_ref[h, tile_rows(base), lanes] for h in range(2)]
            for h, o in COEFS:
                term = grads[h] * conv[o]
                sums[h, o] = sums[h, o] + term if (h, o) in sums else term
        pulls = []
        for h in range(2):
            dots = {}
            for side, o in COEFS:
                if side == h:
                    value = lane_sum(sums[h, o]) * 0.5
                    dots[o] = jnp.where(limits[o], value, 0.0) if o in limits else value
            for j in (2 * h, 2 * h + 1):
                grads = pooled_dots(phases[j], j, dots)
                mean = sum(weights[j][i] * grads[i] for i in range(4))
                pulls.append([weights[j][i] * (grads[i] - mean) for i in range(4)])
        score_coefs = token_coefs(phases, pulls, limits, 1.0)
        for place, (h, o) in enumerate(COEFS):
            coef_ref[place, tile_rows(base)] = coefs[h][o]
            coef_ref[len(COEFS) + place, tile_rows(base)] = score_coefs[h][o]

    over_tiles(MAIN, groups, pull_tile)

    def fold_rows(x):
        return sum(x[i : i + 8] for i in range(0, TILE, 8))

    def grad_tile(base):
        def coef(h, o, score=False):
            return with_sides(coef_ref, (COEFS.index((h, o)) + len(COEFS) * score,), base, slice(None))

        own = [[middle(coef(h, j)) for j in range(4)] for h in range(2)]
        side = [down(coef(1, 4 + j)) if j < 2 else up(coef(0, j - 4)) for j in range(4)]
        kappa = []
        for j in range(4):
            far = down(coef(1, 4 + j, True)) if j < 2 else up(coef(0, j - 4, True))
            kappa.append(middle(coef(0, j, True)) + middle(coef(1, j, True)) + far)
        for lanes in chunks:
            first, second = (with_sides(g_ref, (h,), base, lanes) for h in range(2))
            above, below = down(second), up(first)
            first, second = middle(first), middle(second)
            near = offsets_of([with_sides(e_ref, (j,), base, lanes) for j in range(4)])
            score = score_row[:, lanes]
            taps = [None] * 4
            score_sum = None
            for j in range(4):
                value = own[0][j] * first + own[1][j] * second
                value = value + side[j] * (above if j < 2 else below) + kappa[j] * score
                term = kappa[j] * c_ref[j, tile_rows(base), lanes]
                score_sum = term if score_sum is None else score_sum + term
                c_ref[j, tile_rows(base), lanes] = value
                for k in range(4):
                    term = value * near[j + k - 2]
                    taps[k] = term if taps[k] is None else taps[k] + term
            for k in range(4):
                small_ref[k, :, lanes] += fold_rows(taps[k])
            small_ref[4, :, lanes] += fold_rows(score_sum)

    over_tiles(GUARD, inner, grad_tile)
    edge = jnp.zeros((GUARD, features), jnp.float32)
    for j in range(4):
        c_ref[j, :GUARD] = edge
        c_ref[j, count - GUARD :] = edge

    def back_tile(base):
        start = pl.multiple_of(base - GUARD, TILE)
        for lanes in chunks:
            d = offsets_of([with_sides(c_ref, (j,), base, lanes) for j in range(4)])
            taps = [filt_ref[k : k + 1, lanes] for k in range(4)]
            for j in range(4):
                value = taps[0] * d[j + 2]
                for k in range(1, 4):
                    value = value + taps[k] * d[j + 2 - k]
                low_ref[pl.ds(j * inner + start, TILE), lanes] = value.astype(jnp.bfloat16)

    over_tiles(GUARD, inner, back_tile)
    lane = lax.broadcasted_iota(jnp.int32, (inner, LANES), 1)
    spread = jnp.zeros((inner, LANES), jnp.float32)
    for j in range(4):
        ids = ids_ref[GUARD : GUARD + inner, j : j + 1].astype(jnp.float32)
        spread = jnp.where(lane == j, ids, spread)
    spare = jnp.zeros((-inner % LANES, LANES), jnp.float32)
    turned = jnp.concatenate([spread, spare], axis=0).T.astype(jnp.int32)
    flat = jnp.concatenate([turned[j : j + 1, :inner] for j in range(4)], axis=1)
    words = -(-vocab_size // 16) * 16
    vocab = lax.broadcasted_iota(jnp.int32, (words, 4 * inner), 0)
    hot = jnp.where(flat == vocab, 1.0, 0.0).astype(jnp.bfloat16)
    embed_ref[:words] = dot(hot, low_ref[...])
    embed_ref[words:] = jnp.zeros((embed_ref.shape[0] - words, features), jnp.float32)
    for i in range(5):
        embed_ref[vocab_size + i : vocab_size + i + 1] = jnp.sum(small_ref[i], axis=0, keepdims=True)
    embed_ref[vocab_size + 5 : vocab_size + 6] = first_ref[...]
    embed_ref[vocab_size + 6 : vocab_size + 7] = second_ref[...]
    heads = bias_ref.shape[0]
    embed_ref[vocab_size + 7 : vocab_size + 7 + heads, :LANES] = bias_ref[...]
    share = keep_ref.shape[1]
    chips = keep_ref.shape[0]
    me = info_ref[0]
    for place in range(chips):
        for odd, out_ref in enumerate((keep_ref, send_ref)):
            start = pl.multiple_of((me ^ (2 * place + odd)) * share, 16)
            out_ref[place] = embed_ref[pl.ds(start, share), :].astype(jnp.bfloat16)


def mixer_backward(
    info, ids, emb, filt, score, grad, first, second, bias, row_len, vocab, embed_rows, devices, after
):
    tokens, features = grad.shape
    count = ids.shape[0]
    full = jnp.float32
    piece = jax.ShapeDtypeStruct((devices // 2, embed_rows // devices, features), jnp.bfloat16)
    outs, _ = launch(
        "mixer_backward",
        functools.partial(mixer_back_kernel, row_len, vocab),
        [info, ids, emb, filt, score, grad, first, second, bias],
        [SMEM] + [VMEM] * 8,
        [piece, piece],
        [VMEM] * 2,
        26,
        [
            pltpu.VMEM((4, count, features), full),
            pltpu.VMEM((4, count, features), full),
            pltpu.VMEM((4, count, LANES), full),
            pltpu.VMEM((2 * len(COEFS), count, LANES), full),
            pltpu.VMEM((2, count, features), full),
            pltpu.VMEM((4 * (count - 2 * GUARD), features), jnp.bfloat16),
            pltpu.VMEM((features // LANES, tokens, LANES), full),
            pltpu.VMEM((embed_rows, features), full),
            pltpu.VMEM((5, 8, features), full),
        ],
        after=after,
        microseconds=11,
    )
    return outs


def scores_of(info_ref, part, raw, tile_ref):
    keys, tokens = raw.shape
    base, own = info_ref[part], info_ref[3]
    rows = []
    for kb in range(keys // BLOCK):
        tiles = [
            tile_ref[jnp.clip(base + kb - own - qb, -FAR, FAR) + FAR]
            for qb in range(tokens // BLOCK)
        ]
        rows.append(raw[kb * BLOCK : (kb + 1) * BLOCK] + jnp.concatenate(tiles, axis=1))
    return rows


def only_head(x, h, size):
    lane = lax.broadcasted_iota(jnp.int32, x.shape, 1)
    return jnp.where((lane >= h * size) & (lane < (h + 1) * size), x, jnp.zeros_like(x))


def attention_kernel(
    size,
    carried,
    last,
    info_ref,
    q_ref,
    kv_ref,
    bias_ref,
    cut_ref,
    *refs,
):
    if last:
        *refs, plain_ref, weight_ref, sems = refs
    *refs, tile_ref, q_low_ref, k_hot_ref = refs
    if carried:
        before_ref, state_ref, *refs = refs
    if last:
        stream_ref, wm_ref, gain_ref, att_ref, lse_ref, resid_ref, normed_ref = refs
    else:
        mixed_ref, stat_ref = refs
    step = pl.program_id(0)
    part = 5 + carried
    low = []
    tokens = q_ref.shape[0]

    @pl.when(step == 0)
    def _():
        q_low_ref[...] = lower_rows(cut_ref, info_ref[3] * BLOCK, [], (2, tokens))
        k_hot_ref[...] = segment_hots(cut_ref, info_ref[part] * BLOCK, kv_ref.shape[1], 1.0, 0.0)

    both = jnp.concatenate([by_head(q_ref[...].T, size), q_low_ref[...]], axis=0)
    raws = dot(jnp.concatenate([kv_ref[0], k_hot_ref[...]], axis=1), both)
    turned = kv_ref[1].T
    ones = jnp.ones((16, turned.shape[1]), jnp.bfloat16)
    for h in range(2):
        fill_tiles(bias_ref, h, tile_ref.at[h])
    for h in range(2):
        raw = raws[:, h * tokens : (h + 1) * tokens]
        rows = scores_of(info_ref, part, raw, tile_ref.at[h])
        highest = None
        for row in rows:
            top = jnp.max(row, axis=0, keepdims=True)
            highest = top if highest is None else jnp.maximum(highest, top)
        if carried:
            highest = jnp.maximum(highest, state_ref[0, h : h + 1])
        weights = jnp.concatenate([jnp.exp(row - highest).astype(jnp.bfloat16) for row in rows], axis=0)
        mixed = dot(jnp.concatenate([turned[h * size : (h + 1) * size], ones], axis=0), weights)
        mixed, summed = mixed[:size], mixed[size : size + 1]
        if carried:
            shrink = jnp.exp(state_ref[0, h : h + 1] - highest)
            summed = summed + state_ref[0, 2 + h : 3 + h] * shrink
            mixed = mixed + before_ref[h * size : (h + 1) * size] * shrink
        if last:
            lse_ref[0, h : h + 1] = highest + jnp.log(summed)
            low.append(mixed * (1.0 / summed))
        else:
            stat_ref[0, h : h + 1] = highest
            stat_ref[0, 2 + h : 3 + h] = summed
            mixed_ref[h * size : (h + 1) * size] = mixed
    if not last:
        return
    features = stream_ref.shape[1]
    turned = jnp.concatenate(low, axis=0)
    att_ref[...] = turned
    plain_ref[step] = turned.T.astype(jnp.bfloat16)
    copies = [
        pltpu.make_async_copy(wm_ref, weight_ref, sems.at[0]),
        pltpu.make_async_copy(stream_ref, resid_ref, sems.at[1]),
    ]

    @pl.when(step == 0)
    def _():
        for copy in copies:
            copy.start()

    @pl.when(step == pl.num_programs(0) - 1)
    def _():
        for copy in copies:
            copy.wait()
        attended = jnp.concatenate([plain_ref[p] for p in range(plain_ref.shape[0])], axis=1)
        resid = resid_ref[...] + dot(attended, weight_ref[...])
        resid_ref[...] = resid
        root = lax.rsqrt(jnp.sum(resid * resid, axis=1, keepdims=True) / features + EPS)
        normed_ref[...] = (resid * root * row_of(gain_ref)).astype(jnp.bfloat16)


def attention_forward(name, size, info, q, kv, bias, cuts, carried=(), last=(), carry=()):
    tokens, features = q.shape
    heads = features // size
    pairs = heads // 2
    wide = 2 * size
    whole = lambda shape: pl.BlockSpec(shape, lambda p: (0,) * len(shape))
    by_rows = pl.BlockSpec((wide, tokens), lambda p: (p, 0))
    stat = pl.BlockSpec((1, 8, tokens), lambda p: (p, 0, 0))
    stat_shape = jax.ShapeDtypeStruct((pairs, 8, tokens), jnp.float32)
    ins = [info, q, kv, bias, cuts, *carried, *last]
    in_specs = [
        SMEM,
        pl.BlockSpec((tokens, wide), lambda p: (0, p)),
        pl.BlockSpec((2, kv.shape[1], wide), lambda p: (0, 0, p)),
        pl.BlockSpec((3, 2, BLOCK, BLOCK), lambda p: (0, p, 0, 0)),
        SMEM,
    ]
    if carried:
        in_specs += [by_rows, stat]
    if last:
        stream, wm, gain = last
        in_specs += [
            HBM,
            HBM,
            whole(gain.shape),
        ]
        shapes = [
            jax.ShapeDtypeStruct((features, tokens), jnp.float32),
            stat_shape,
            jax.ShapeDtypeStruct((tokens, features), jnp.float32),
            jax.ShapeDtypeStruct((tokens, features), jnp.bfloat16),
        ]
        out_specs = [by_rows, stat, whole((tokens, features)), whole((tokens, features))]
    else:
        shapes = [jax.ShapeDtypeStruct((features, tokens), jnp.float32), stat_shape]
        out_specs = [by_rows, stat]
    merging = [
        pltpu.VMEM((pairs, tokens, wide), jnp.bfloat16),
        pltpu.VMEM((features, features), jnp.bfloat16),
        pltpu.SemaphoreType.DMA((2,)),
    ]
    kernel = functools.partial(attention_kernel, size, int(bool(carried)), bool(last))
    made = len(shapes)

    def body(*refs):
        rest = refs[len(ins) + len(carry) :]
        kernel(*refs[: len(ins)], *rest[:made], *rest[made + len(carry) :])

    results = pl.pallas_call(
        body,
        grid=(pairs,),
        out_shape=[*shapes, *[jax.ShapeDtypeStruct(x.shape, x.dtype) for x in carry]],
        in_specs=in_specs + [ANY] * len(carry),
        out_specs=[*out_specs, *[ANY] * len(carry)],
        input_output_aliases={len(ins) + i: made + i for i in range(len(carry))},
        scratch_shapes=[
            pltpu.VMEM((2, 2 * FAR + 1, BLOCK, BLOCK), jnp.float32),
            pltpu.VMEM((LANES, 2 * tokens), jnp.bfloat16),
            pltpu.VMEM((kv.shape[1], LANES), jnp.bfloat16),
            *(merging if last else []),
        ],
        compiler_params=params(12),
        cost_estimate=cost(9),
        name=name,
    )(*ins, *carry)
    return results[:made], results[made:]


def diagonal_sums(tile_ref, sums_ref):
    wide = 2 * BLOCK
    row = lax.broadcasted_iota(jnp.int32, (BLOCK, BLOCK), 0)
    column = lax.broadcasted_iota(jnp.int32, (BLOCK, BLOCK), 1)
    flip = jnp.where(row + column == BLOCK - 1, 1.0, 0.0).astype(jnp.bfloat16)
    near = jnp.concatenate([tile_ref[h, 1 + delta] for h in range(2) for delta in range(3)], axis=1)
    high = near.astype(jnp.bfloat16)
    rest = (near - high.astype(jnp.float32)).astype(jnp.bfloat16)
    flipped = dot(flip, high) + dot(flip, rest)
    empty = jnp.zeros((BLOCK, BLOCK), jnp.float32)
    for h in range(2):
        for delta in range(3):
            start = (3 * h + delta) * BLOCK
            padded = jnp.concatenate([flipped[:, start : start + BLOCK], empty], axis=1)
            slid = pltpu.roll(padded, 0, 1, stride=1, stride_axis=0)
            place = 5 * h + 1 + delta
            sums_ref[0, place : place + 1] = jnp.sum(slid, axis=0, keepdims=True)
        for far in (0, 2 * FAR):
            place = 5 * h + far
            total = jnp.sum(tile_ref[h, far], axis=0, keepdims=True)
            sums_ref[0, place : place + 1] = jnp.concatenate([total, empty[:1]], axis=1)


def attention_back_kernel(
    parts,
    size,
    info_ref,
    q_ref,
    g_ref,
    *refs,
):
    kv_refs = refs[:parts]
    bias_ref, cut_ref, lse_ref, att_ref = refs[parts : parts + 4]
    dq_ref, *dkv_refs, sums_ref, bias_tile_ref, tile_ref = refs[-4 - 2 * parts : len(refs) - parts]
    k_hot_refs = refs[len(refs) - parts :]
    tokens = q_ref.shape[0]
    blocks = tokens // BLOCK
    own = info_ref[3]
    for h in range(2):
        fill_tiles(bias_ref, h, bias_tile_ref.at[h])

    @pl.when(pl.program_id(0) == 0)
    def _():
        lane = lax.broadcasted_iota(jnp.int32, (1, LANES), 1)
        one = jnp.where((lane >= 4) & (lane < 7), 1.0, 0.0).astype(jnp.bfloat16)
        for part in range(parts):
            hots = segment_hots(cut_ref, info_ref[5 + part] * BLOCK, kv_refs[part].shape[1], 1.0, 0.0)
            k_hot_refs[part][...] = hots + one

    q_both = jnp.concatenate([only_head(q_ref[...], h, size) for h in range(2)], axis=0)
    g_both = jnp.concatenate([only_head(g_ref[...], h, size) for h in range(2)], axis=0)
    turned = g_ref[...].T
    logs = [-lse_ref[0, h : h + 1] for h in range(2)]
    q_wide = jnp.concatenate(
        [by_head(q_ref[...].T, size), lower_rows(cut_ref, own * BLOCK, logs, (2, tokens))], axis=0
    )
    g_wide = by_head(turned, size)
    products = turned.astype(jnp.float32) * att_ref[...]
    correction = jnp.concatenate(
        [jnp.sum(products[h * size : (h + 1) * size], axis=0, keepdims=True) for h in range(2)], axis=1
    )
    tile_ref[...] = jnp.zeros_like(tile_ref)
    dq = None
    for part in range(parts):
        base = info_ref[5 + part]
        keys = kv_refs[part].shape[1]
        hots = k_hot_refs[part][...]
        raw = dot(jnp.concatenate([kv_refs[part][0], hots], axis=1), q_wide)
        pull = dot(kv_refs[part][1], g_wide)
        shares, grads, sums = [], [], {}
        for kb in range(keys // BLOCK):
            rows = slice(kb * BLOCK, (kb + 1) * BLOCK)
            tiles = [
                bias_tile_ref[h, jnp.clip(base + kb - own - qb, -FAR, FAR) + FAR]
                for h in range(2)
                for qb in range(blocks)
            ]
            probs = jnp.exp(raw[rows] + jnp.concatenate(tiles, axis=1))
            grad = probs * (pull[rows] - correction)
            shares.append(probs.astype(jnp.bfloat16))
            grads.append(grad.astype(jnp.bfloat16))
            for h in range(2):
                for qb in range(blocks):
                    start = (h * blocks + qb) * BLOCK
                    here = grad[:, start : start + BLOCK]
                    key = (h, kb - qb)
                    sums[key] = sums[key] + here if key in sums else here
        for (h, delta), tile in sums.items():
            place = jnp.clip(base - own + delta, -FAR, FAR) + FAR
            tile_ref[h, place] += tile
        shares = jnp.concatenate(shares, axis=0)
        grads = jnp.concatenate(grads, axis=0)
        dkv_refs[part][0] = dot(grads, q_both).astype(jnp.bfloat16)
        dkv_refs[part][1] = dot(shares, g_both).astype(jnp.bfloat16)
        term = dot(kv_refs[part][0].T, grads)
        dq = term if dq is None else dq + term
    dq = jnp.concatenate([dq[:size, :tokens], dq[size:, tokens:]], axis=0)
    dq_ref[...] = dq.T.astype(jnp.bfloat16)
    diagonal_sums(tile_ref, sums_ref)


def attention_backward(size, info, q, g, kvs, bias, cuts, lse, att, after):
    tokens, features = q.shape
    pairs = features // size // 2
    parts = len(kvs)
    wide = 2 * size
    by_pair = [pl.BlockSpec((2, x.shape[1], wide), lambda p: (0, 0, p)) for x in kvs]
    own = pl.BlockSpec((tokens, wide), lambda p: (0, p))
    sums = pl.BlockSpec((1, 16, 2 * BLOCK), lambda p: (p, 0, 0))
    tiles = pltpu.VMEM((2, 2 * FAR + 1, BLOCK, BLOCK), jnp.float32)
    shapes = [jax.ShapeDtypeStruct(x.shape, jnp.bfloat16) for x in kvs]
    if parts > 1:
        shapes[0] = pltpu.HBM(kvs[0].shape, jnp.bfloat16)
    result = pl.pallas_call(
        functools.partial(attention_back_kernel, parts, size),
        grid=(pairs,),
        out_shape=[pltpu.HBM(q.shape, jnp.bfloat16), *shapes]
        + [jax.ShapeDtypeStruct((pairs, 16, 2 * BLOCK), jnp.float32)],
        in_specs=[
            SMEM,
            own,
            own,
            *by_pair,
            pl.BlockSpec((3, 2, BLOCK, BLOCK), lambda p: (0, p, 0, 0)),
            SMEM,
            pl.BlockSpec((1, 8, tokens), lambda p: (p, 0, 0)),
            pl.BlockSpec((wide, tokens), lambda p: (p, 0)),
            *[ANY] * len(after),
        ],
        out_specs=[own, *by_pair, sums],
        scratch_shapes=[
            tiles,
            tiles,
            *[pltpu.VMEM((x.shape[1], LANES), jnp.bfloat16) for x in kvs],
        ],
        compiler_params=params(18),
        cost_estimate=cost(20),
        name="attention_backward",
    )(info, q, g, *kvs, bias, cuts, lse, att, *after)
    return result[0], result[1 : 1 + parts], result[-1]


def bucket_kernel(sums_ref, out_ref):
    pairs = sums_ref.shape[0]
    wide = 2 * BLOCK
    spot = lax.broadcasted_iota(jnp.int32, (wide, LANES), 1)
    entry = lax.broadcasted_iota(jnp.int32, (wide, LANES), 0)
    gap = entry - (BLOCK - 1)
    total = None
    for delta in range(5):
        if delta in (0, 2 * FAR):
            hot = jnp.where(spot == (15 if delta == 0 else 31), 1.0, 0.0)
        else:
            hot = jnp.where(spot == bucket_of((delta - FAR) * BLOCK - gap), 1.0, 0.0)
        hot = hot.astype(jnp.bfloat16)
        rows = [sums_ref[p, 5 * h + delta : 5 * h + delta + 1] for p in range(pairs) for h in range(2)]
        rows = jnp.concatenate(rows, axis=0)
        for part in split_three(rows):
            here = dot(part, hot)
            total = here if total is None else total + here
    out_ref[...] = total


def bucket_sums(sums, after):
    outs, _ = launch(
        "bucket_sums",
        bucket_kernel,
        [sums],
        [VMEM],
        [jax.ShapeDtypeStruct((2 * sums.shape[0], LANES), jnp.float32)],
        [VMEM],
        4,
        after=after,
    )
    return outs[0]


def relative_rows(me, count, src_ref, dst_ref):
    size = src_ref.shape[0] // count
    for place in range(count):
        r = 2 * (place % (count // 2)) + place // (count // 2)
        start = pl.multiple_of((me ^ r) * size, 16)
        dst_ref[place * size : (place + 1) * size] = src_ref[pl.ds(start, size), :]


def feed_kernel(
    held,
    count,
    half,
    info_ref,
    normed_ref,
    *refs,
):
    if half == 0:
        cot_refs = refs[:held]
        (
            resid_ref,
            wg_ref,
            wu_ref,
            wd_ref,
            acc_ref,
            grad_ref,
            keep_ref,
            send_ref,
            cot_ref,
            cot_turned_ref,
            normed_turned_ref,
            turned_ref,
        ) = refs[held:]
        grad_in_ref = None
    else:
        (
            resid_ref,
            grad_in_ref,
            cot_ref,
            cot_turned_ref,
            normed_turned_ref,
            wg_ref,
            wu_ref,
            wd_ref,
            *out_refs,
            grad_ref,
            keep_ref,
            send_ref,
            acc_ref,
        ) = refs
    step = pl.program_id(0)
    core = info_ref[1]
    if half == 0:
        span = cot_refs[0].shape[0]

        @pl.when(step == 0)
        def _():
            for phase in range(held):
                start = pl.multiple_of(lax.rem(info_ref[2] + held - phase, held) * span, span)
                cot_ref[pl.ds(start, span), :] = cot_refs[phase][...]
            cot_turned_ref[...] = cot_ref[...].T
            turned_ref[...] = normed_ref[...].T
            relative_rows(info_ref[0], count, turned_ref, normed_turned_ref)

    normed, cot = normed_ref[...], cot_ref[...]
    gate = dot(normed, wg_ref[...])
    up_value = dot(normed, wu_ref[...])
    grad_hidden = dot_nt(cot, wd_ref[...])
    square = gate * gate
    bend = jnp.tanh(gate * (SLOPE + (SLOPE * CUBE) * square))
    middle = 0.5 + 0.5 * bend
    gelu = gate * middle
    slope = middle * (1.0 + (1.0 - bend) * (gate * (SLOPE + (3.0 * SLOPE * CUBE) * square)))
    hidden = (gelu * up_value).astype(jnp.bfloat16)
    grad_gate = (grad_hidden * up_value * slope).astype(jnp.bfloat16)
    grad_up = (grad_hidden * gelu).astype(jnp.bfloat16)
    rb, cb = keep_ref.shape[-2:]
    chips = count // 2
    half_rows = chips * rb
    turned = normed_turned_ref[...]
    for kind, grad in enumerate((grad_gate, grad_up)):
        part = dot(turned, grad).astype(jnp.bfloat16)
        for e in range(2):
            columns = part[:, e * cb : (e + 1) * cb]
            tiles = slice((2 * kind + e) * chips, (2 * kind + e + 1) * chips)
            keep_ref[0, tiles] = columns[:half_rows].reshape(chips, rb, cb)
            send_ref[0, tiles] = columns[half_rows:].reshape(chips, rb, cb)
    part = dot(cot_turned_ref[...], hidden)
    first, second = part[:, :cb], part[:, cb:]
    mine = core == 0
    keep = jnp.where(mine, first, second).astype(jnp.bfloat16)
    send = jnp.where(mine, second, first).astype(jnp.bfloat16)
    keep_ref[0, 4 * chips :] = keep.reshape(count, rb, cb)
    send_ref[0, 4 * chips :] = send.reshape(count, rb, cb)
    result = dot(hidden, wd_ref[...])
    back = dot_nt(grad_gate, wg_ref[...]) + dot_nt(grad_up, wu_ref[...])

    @pl.when(step == 0)
    def _():
        acc_ref[...] = resid_ref[...] + result
        grad_ref[...] = back if grad_in_ref is None else grad_in_ref[...] + back

    @pl.when(step > 0)
    def _():
        acc_ref[...] += result
        grad_ref[...] += back

    if half == 1:

        @pl.when(step == pl.num_programs(0) - 1)
        def _():
            span = out_refs[0].shape[0]
            for phase in range(held):
                start = pl.multiple_of(lax.rem(info_ref[2] + held - phase, held) * span, span)
                out_refs[phase][...] = acc_ref[pl.ds(start, span), :].astype(jnp.bfloat16)


def feed_forward(half, info, normed, ins, wg, wu, wd, held, count):
    tokens, features = normed.shape
    width = wg.shape[1]
    chips = count // 2
    steps = chips // 2
    rb, cb = features // count, width // count
    whole = lambda shape: pl.BlockSpec(shape, lambda j, info: (0,) * len(shape))
    low = jnp.bfloat16
    slab = (4 * chips + count, rb, cb)
    tiles = jax.ShapeDtypeStruct((steps,) + slab, low)
    tile_spec = pl.BlockSpec((1,) + slab, lambda j, info: (j, 0, 0, 0))
    natural, turned = (tokens, features), (features, tokens)
    full = jax.ShapeDtypeStruct(natural, jnp.float32)
    shapes = [full, tiles, tiles]
    specs = [whole(natural), tile_spec, tile_spec]
    if half == 0:
        shapes, specs = [full] + shapes, [whole(natural)] + specs
    else:
        span = (tokens // held, features)
        shapes = [jax.ShapeDtypeStruct(span, low)] * held + shapes
        specs = [whole(span)] * held + specs
    scratch = [pltpu.VMEM(natural, jnp.float32)]
    if half == 0:
        shapes += [
            jax.ShapeDtypeStruct(natural, low),
            jax.ShapeDtypeStruct(turned, low),
            jax.ShapeDtypeStruct(turned, low),
        ]
        specs += [whole(natural), whole(turned), whole(turned)]
        scratch = [pltpu.VMEM(turned, low)]
    return pl.pallas_call(
        functools.partial(feed_kernel, held, count, half),
        grid_spec=pltpu.PrefetchScalarGridSpec(
            num_scalar_prefetch=1,
            grid=(steps,),
            in_specs=[
                whole(normed.shape),
                *[whole(x.shape) for x in ins],
                pl.BlockSpec((features, 2 * cb), lambda j, info: (0, j + half * steps)),
                pl.BlockSpec((features, 2 * cb), lambda j, info: (0, j + half * steps)),
                pl.BlockSpec((2 * cb, features), lambda j, info: (j + half * steps, 0)),
            ],
            out_specs=specs,
            scratch_shapes=scratch,
        ),
        out_shape=shapes,
        compiler_params=params(28),
        cost_estimate=cost(11),
        name=f"feed_forward_{half}",
    )(info, normed, *ins, wg, wu, wd)


def between_kernel(
    count,
    info_ref,
    grad_ref,
    resid_ref,
    gain_ref,
    cot_ref,
    att_ref,
    wm_ref,
    *refs,
):
    (
        out_hbm_ref,
        att_grad_ref,
        keep_hbm_ref,
        send_ref,
        gain_grad_ref,
        turned_ref,
        low_ref,
        out_ref,
        keep_ref,
        sems,
    ) = refs[-10:]
    features = resid_ref.shape[1]
    resid = resid_ref[...]
    root = lax.rsqrt(jnp.sum(resid * resid, axis=1, keepdims=True) / features + EPS)
    grad = grad_ref[...]
    unit = resid * root
    gain_grad_ref[...] = jnp.sum(grad * unit, axis=0, keepdims=True)
    pulled = grad * row_of(gain_ref)
    mean = jnp.sum(unit * pulled, axis=1, keepdims=True) / features
    result = cot_ref[...].astype(jnp.float32) + root * (pulled - unit * mean)
    out_ref[...] = result
    copies = [
        pltpu.make_async_copy(out_ref, out_hbm_ref, sems.at[0]),
        pltpu.make_async_copy(keep_ref, keep_hbm_ref, sems.at[1]),
    ]
    copies[0].start()
    mixed = result.astype(jnp.bfloat16)
    low_ref[...] = att_ref[...].astype(jnp.bfloat16)
    relative_rows(info_ref[0], count, low_ref, turned_ref)
    part = dot(turned_ref[...], mixed).astype(jnp.bfloat16)
    half = features // 2
    keep_ref[...] = part[:half].reshape(keep_ref.shape)
    copies[1].start()
    send_ref[...] = part[half:].reshape(send_ref.shape)
    att_grad_ref[...] = dot_nt(mixed, wm_ref[...]).astype(jnp.bfloat16)
    for copy in copies:
        copy.wait()


def between(info, grad, resid, gain, cot, att, wm, count, after, carry):
    tokens, features = grad.shape
    rb = features // count
    low = jnp.bfloat16
    piece = jax.ShapeDtypeStruct((count // 2, rb, features), low)
    ins = [info, grad, resid, gain, cot, att, wm]
    return launch(
        "between",
        functools.partial(between_kernel, count),
        ins,
        [SMEM] + [VMEM] * 6,
        [
            pltpu.HBM((tokens, features), jnp.float32),
            jax.ShapeDtypeStruct((tokens, features), low),
            pltpu.HBM(piece.shape, low),
            piece,
            jax.ShapeDtypeStruct((1, features), jnp.float32),
        ],
        [HBM, VMEM, HBM, VMEM, VMEM],
        16,
        [
            pltpu.VMEM((features, tokens), low),
            pltpu.VMEM((features, tokens), low),
            pltpu.VMEM((tokens, features), jnp.float32),
            pltpu.VMEM(piece.shape, low),
            pltpu.SemaphoreType.DMA((2,)),
        ],
        after=after,
        carry=carry,
        microseconds=3,
    )


def project_q_kernel(
    count,
    info_ref,
    dq_ref,
    normed_ref,
    wq_ref,
    other_ref,
    keep_ref,
    send_ref,
    back_ref,
    turned_ref,
    plain_ref,
):
    plain_ref[...] = normed_ref[...].T
    relative_rows(info_ref[0], count, plain_ref, turned_ref)
    dq = dq_ref[...]
    part = dot(turned_ref[...], dq).astype(jnp.bfloat16)
    half = part.shape[0] // 2
    keep_ref[...] = part[:half].reshape(keep_ref.shape)
    send_ref[0] = part[half:].reshape(send_ref.shape[1:])
    send_ref[1] = other_ref[...]
    back_ref[...] = dot_nt(dq, wq_ref[...])


def project_q(info, dq, normed, wq, other, count, after, carry):
    tokens, features = dq.shape
    low = jnp.bfloat16
    piece = jax.ShapeDtypeStruct((count // 2, features // count, features), low)
    return launch(
        "project_q",
        functools.partial(project_q_kernel, count),
        [info, dq, normed, wq, other],
        [SMEM] + [VMEM] * 4,
        [
            piece,
            jax.ShapeDtypeStruct((2,) + piece.shape, low),
            jax.ShapeDtypeStruct((tokens, features), jnp.float32),
            jax.ShapeDtypeStruct((features, tokens), low),
        ],
        [VMEM] * 4,
        14,
        [pltpu.VMEM((features, tokens), low)],
        after=after,
        carry=carry,
    )


def project_kv_kernel(
    mine_ref,
    got_ref,
    turned_ref,
    back_ref,
    stream_ref,
    grad_ref,
    gain_ref,
    wk_ref,
    wv_ref,
    keep_ref,
    send_ref,
    out_ref,
    gain_grad_ref,
):
    features = stream_ref.shape[1]
    half = features // 2
    total = back_ref[...]
    for i, w_ref in enumerate((wk_ref, wv_ref)):
        grad = mine_ref[i] + got_ref[i]
        part = dot(turned_ref[...], grad).astype(jnp.bfloat16)
        keep_ref[i] = part[:half].reshape(keep_ref.shape[1:])
        send_ref[i] = part[half:].reshape(send_ref.shape[1:])
        total = total + dot_nt(grad, w_ref[...])
    stream = stream_ref[...]
    root = lax.rsqrt(jnp.sum(stream * stream, axis=1, keepdims=True) / features + EPS)
    unit = stream * root
    gain_grad_ref[...] = jnp.sum(total * unit, axis=0, keepdims=True)
    pulled = total * row_of(gain_ref)
    mean = jnp.sum(unit * pulled, axis=1, keepdims=True) / features
    out_ref[...] = grad_ref[...] + root * (pulled - unit * mean)


def project_kv(mine, got, turned, back, stream, grad, gain, wk, wv, count, after):
    tokens, features = stream.shape
    piece = jax.ShapeDtypeStruct((2, count // 2, features // count, features), jnp.bfloat16)
    outs, _ = launch(
        "project_kv",
        project_kv_kernel,
        [mine, got, turned, back, stream, grad, gain, wk, wv],
        [VMEM] * 9,
        [piece] * 2
        + [
            jax.ShapeDtypeStruct((tokens, features), jnp.float32),
            jax.ShapeDtypeStruct((1, features), jnp.float32),
        ],
        [VMEM] * 4,
        18,
        after=after,
    )
    return outs


def pick_of(pairs, info_ref):
    def tile(pair, at):
        if callable(at):
            at = at(info_ref)
        first, second = at if isinstance(at, tuple) else (at, at)
        return pairs[pair][0][first] + pairs[pair][1][second]

    def value(pick):
        if len(pick) == 2:
            return tile(*pick)
        return jnp.where(info_ref[7] == 0, tile(*pick[:2]), tile(*pick[2:]))

    return value


def tiles_of(pairs):
    return [tuple(x.reshape((-1,) + x.shape[-2:]) for x in pair) for pair in pairs]


def fold(name, info, pairs, picks, after=(), carry=()):
    pairs = tiles_of(pairs)
    shape = pairs[0][0].shape[1:]

    def kernel(info_ref, *refs):
        ins, outs = refs[: 2 * len(pairs)], refs[2 * len(pairs) :]
        value = pick_of([ins[2 * i : 2 * i + 2] for i in range(len(pairs))], info_ref)
        for out_ref, chosen in zip(outs, picks):
            for slot, pick in enumerate(chosen):
                out_ref[slot] = value(pick)

    return launch(
        name,
        kernel,
        [info, *sum(pairs, ())],
        [SMEM] + [VMEM] * (2 * len(pairs)),
        [jax.ShapeDtypeStruct((len(chosen),) + shape, jnp.bfloat16) for chosen in picks],
        [VMEM] * len(picks),
        16,
        after=after,
        carry=carry,
    )


def lane_tiles(width):
    whole = width // LANES
    rest = width - whole * LANES
    return whole, rest, LANES // rest if rest else 1


def tile_count(pieces, width):
    whole, rest, each = lane_tiles(width)
    return pieces * whole + (-(-pieces // each) if rest else 0)


def pack_lanes(pieces):
    width = pieces[0].shape[1]
    whole, rest, each = lane_tiles(width)
    tiles = [piece[:, i * LANES : (i + 1) * LANES] for piece in pieces for i in range(whole)]
    if rest:
        ends = [piece[:, whole * LANES :] for piece in pieces]
        for i in range(0, len(ends), each):
            group = ends[i : i + each]
            spare = LANES - rest * len(group)
            if spare:
                group = group + [jnp.zeros((group[0].shape[0], spare), group[0].dtype)]
            tiles.append(jnp.concatenate(group, axis=1))
    return tiles


def unpack_lanes(tiles, pieces, width):
    whole, rest, each = lane_tiles(width)
    result = []
    for piece in range(pieces):
        parts = [tiles[piece * whole + i] for i in range(whole)]
        if rest:
            tile = tiles[pieces * whole + piece // each]
            start = piece % each * rest
            parts.append(tile[:, start : start + rest])
        result.append(jnp.concatenate(parts, axis=1) if len(parts) > 1 else parts[0])
    return result


def fold_seq(name, info, pairs, picks, seqs, slots, groups, width=None, after=(), carry=()):
    pairs = tiles_of(pairs)
    tall, wide = pairs[0][0].shape[1:]
    shape = (tall, LANES if width else wide)

    def kernel(info_ref, *refs):
        ins, outs, scratch_ref = refs[: 2 * len(pairs)], refs[2 * len(pairs) : -1], refs[-1]
        value = pick_of([ins[2 * i : 2 * i + 2] for i in range(len(pairs))], info_ref)
        here = info_ref[8]
        if width is None:
            for pick, block, slot in picks:
                scratch_ref[block ^ here, slot] = value(pick)
        else:
            totals = [value(pick) for pick, _, _ in sorted(picks, key=lambda x: x[2])]
            for s in range(seqs):
                pieces = [total[:, s * width : (s + 1) * width] for total in totals]
                for slot, tile in enumerate(pack_lanes(pieces)):
                    scratch_ref[s ^ here, slot] = tile
        for out_ref, group in zip(outs, groups):
            for i, d in enumerate(group):
                out_ref[i * slots : (i + 1) * slots] = scratch_ref[d]

    return launch(
        name,
        kernel,
        [info, *sum(pairs, ())],
        [SMEM] + [VMEM] * (2 * len(pairs)),
        [jax.ShapeDtypeStruct((len(group) * slots,) + shape, jnp.bfloat16) for group in groups],
        [VMEM] * len(groups),
        16,
        [pltpu.VMEM((seqs, slots) + shape, jnp.bfloat16)],
        after=after,
        carry=carry,
    )


def summed(refs, at):
    terms = [ref[at].astype(jnp.float32) for ref in refs]
    while len(terms) > 1:
        terms = [terms[i] + terms[i + 1] for i in range(0, len(terms), 2)]
    return terms[0]


def feed_end_kernel(seqs, *refs):
    ins, (gate_ref, up_ref, down_ref) = refs[:seqs], refs[seqs:]
    slots, rb, cb = ins[0].shape
    each = slots // 3
    for q in range(each):
        gate_ref[:, q * cb : (q + 1) * cb] = summed(ins, q)
        up_ref[:, q * cb : (q + 1) * cb] = summed(ins, each + q)
    for q in range(each):
        down_ref[q * rb : (q + 1) * rb] = summed(ins, 2 * each + q)


def feed_end(ins, after):
    slots, rb, cb = ins[0].shape
    each = slots // 3
    wide = pltpu.HBM((rb, each * cb), jnp.float32)
    return pl.pallas_call(
        ordered(functools.partial(feed_end_kernel, len(ins)), len(ins), after),
        out_shape=[wide, wide, pltpu.HBM((each * rb, cb), jnp.float32)],
        in_specs=[VMEM] * len(ins) + [ANY] * len(after),
        out_specs=[AUTO] * 3,
        compiler_params=params(8),
        cost_estimate=cost(1),
        name="feed_end",
    )(*ins, *after)


def join_kernel(info_ref, *refs):
    held = len(refs) - 1
    for phase in range(held):
        refs[held][lax.rem(info_ref[8] + phase, held)] = refs[phase][...]


def join(info, parts, after):
    shape = (len(parts),) + parts[0].shape
    outs, _ = launch(
        "join",
        join_kernel,
        [info, *parts],
        [SMEM] + [VMEM] * len(parts),
        [pltpu.HBM(shape, parts[0].dtype)],
        [AUTO],
        8,
        after=after,
    )
    return outs[0]


def mix_end_kernel(width, seqs, *refs):
    outs = refs[seqs:]
    tiles = [summed(refs[:seqs], slot) for slot in range(refs[0].shape[0])]
    for out_ref, value in zip(outs, unpack_lanes(tiles, len(outs), width)):
        out_ref[...] = value


def mix_end(ins, pieces, width, after):
    outs, _ = launch(
        "mix_end",
        functools.partial(mix_end_kernel, width, len(ins)),
        ins,
        [VMEM] * len(ins),
        [pltpu.HBM((ins[0].shape[1], width), jnp.float32)] * pieces,
        [AUTO] * pieces,
        8,
        after=after,
    )
    return outs


def sum_kernel(count, *refs):
    refs[count][...] = summed(refs[:count], slice(None)).astype(jnp.bfloat16)


def sum_of(name, terms, after):
    return pl.pallas_call(
        ordered(functools.partial(sum_kernel, len(terms)), len(terms), after),
        out_shape=jax.ShapeDtypeStruct(terms[0].shape, jnp.bfloat16),
        in_specs=[VMEM] * len(terms) + [ANY] * len(after),
        out_specs=VMEM,
        compiler_params=params(8),
        cost_estimate=cost(1),
        name=name,
    )(*terms, *after)


def unpack_kernel(vocab, chips, info_ref, *refs):
    shares = refs[: 2 * chips]
    embed_ref, filter_ref, score_ref, first_ref, second_ref, bias_ref, whole_ref = refs[2 * chips :]
    share = shares[0].shape[1]
    me = info_ref[0]
    for place in range(chips):
        for odd in range(2):
            start = pl.multiple_of((me ^ (2 * place + odd)) * share, 16)
            whole_ref[pl.ds(start, share), :] = shares[odd * chips + place][0].astype(jnp.float32)
    embed_ref[...] = whole_ref[:vocab]
    filter_ref[...] = whole_ref[vocab : vocab + 4]
    for i, ref in enumerate((score_ref, first_ref, second_ref)):
        ref[...] = whole_ref[vocab + 4 + i, :]
    heads, buckets = bias_ref.shape
    bias_ref[...] = whole_ref[vocab + 7 : vocab + 7 + heads, :buckets]


def unpack(info, mine, others, vocab, buckets, heads, after):
    chips = len(mine)
    _, share, features = mine[0].shape
    full = lambda *shape: pltpu.HBM(shape, jnp.float32)
    return pl.pallas_call(
        ordered(functools.partial(unpack_kernel, vocab, chips), 1 + 2 * chips, after),
        out_shape=[
            full(vocab, features),
            full(4, features),
            full(features),
            full(features),
            full(features),
            full(heads, buckets),
        ],
        in_specs=[SMEM] + [VMEM] * (2 * chips) + [ANY] * len(after),
        out_specs=[AUTO] * 6,
        scratch_shapes=[pltpu.VMEM((2 * chips * share, features), jnp.float32)],
        compiler_params=params(8),
        cost_estimate=cost(1),
        name="unpack",
    )(info, *mine, *others, *after)


AXES = ("batch", "seq")


def across_cores(x):
    count = lax.axis_size("batch")
    return lax.ppermute(x, "batch", [(i, i ^ 1) for i in range(count)])


def across_chips(x, chip):
    count = lax.axis_size("batch")
    return lax.ppermute(x, "batch", [(i, i ^ (2 * chip)) for i in range(count)])


def across_seq(x, d):
    count = lax.axis_size("seq")
    return lax.ppermute(x, "seq", [(i, i ^ d) for i in range(count)])


class Halving:
    def __init__(self, pairs, where):
        self.pairs, self.where = pairs, where

    def split(self, chosen, bit):
        keys = [key for key in self.where if chosen(key)]
        keep = [key for key in keys if not key[-1] & (1 << bit)]
        send = [key[:-1] + (key[-1] | (1 << bit),) for key in keep]
        return keep, send

    def picks(self, keys):
        return [self.where[key] for key in keys]


def exchange(name, info, state, plans, after=(), carry=(), held_back=False):
    lists, kept = [], []
    for chosen, bit in plans:
        keep, send = state.split(chosen, bit)
        kept.append(keep)
        lists += [state.picks(keep), state.picks(send)]
    outs, carried = fold(name, info, state.pairs, lists, after, carry)

    def start(sends):
        pairs, where = [], {}
        for place, ((_, bit), keep) in enumerate(zip(plans, kept)):
            pairs.append((outs[2 * place], across_chips(sends[place], 1 << bit)))
            where.update({key: (place, slot) for slot, key in enumerate(keep)})
        return Halving(pairs, where)

    return start if held_back else start(outs[1::2]), outs, carried


class Plan:
    def __init__(self, held):
        self.count = lax.axis_size("batch")
        self.seqs = lax.axis_size("seq")
        self.held = held
        self.group = self.seqs // (2 * held)
        me = lax.axis_index("batch")
        place = lax.axis_index("seq")
        self.me, self.place = me, place
        self.core = me % 2
        self.row = place // self.group
        self.part = 2 * (place % self.group) + self.core
        self.parts = 2 * self.group
        self.perms = []
        for phase in range(held):
            perm = []
            for b in range(self.count):
                for s in range(self.seqs):
                    row = held * (b % 2) + (s + phase) % held
                    part = s // held
                    target = (b - b % 2 + part % 2, self.group * row + part // 2)
                    perm.append((b * self.seqs + s, target[0] * self.seqs + target[1]))
            self.perms.append(perm)

    def blocks_of(self, x):
        return [
            lax.dynamic_index_in_dim(x, (self.place + phase) % self.held, 0, keepdims=False)
            for phase in range(self.held)
        ]

    def parts_of(self, x):
        return [lax.ppermute(x, AXES, perm) for x, perm in zip(self.blocks_of(x), self.perms)]

    def bytes_of(self, x):
        held = self.held
        main = self.parts_of(x)
        ends = jnp.concatenate([x[:, :4], x[:, -4:]], axis=1)
        sides = []
        for phase in range(held):
            perm = []
            for b in range(self.count):
                for s in range(self.seqs):
                    row = held * (b % 2) + (s + phase) % held
                    part = s // held + {0: -1, held - 1: 1}.get(s % held, self.parts)
                    if 0 <= part < self.parts:
                        target = (b - b % 2 + part % 2, self.group * row + part // 2)
                        perm.append((b * self.seqs + s, target[0] * self.seqs + target[1]))
            send = lax.dynamic_index_in_dim(ends, (self.place + phase) % held, 0, keepdims=False)
            sides.append(lax.ppermute(send, AXES, perm))
        low = lax.dynamic_index_in_dim(
            jnp.stack(sides), (self.row + 1) % held, 0, keepdims=False
        )[4:]
        high = lax.dynamic_index_in_dim(jnp.stack(sides), self.row % held, 0, keepdims=False)[:4]
        low = jnp.where(self.part > 0, low, -1)
        high = jnp.where(self.part < self.parts - 1, high, -1)
        order = (self.row - jnp.arange(held)) % held
        middle = jnp.take(jnp.stack(main), order, axis=0).reshape(-1)
        return jnp.concatenate([low, middle, high]).reshape(-1, 4)

    def gather(self, x):
        other = across_cores(x)
        pair = jnp.stack([jnp.where(self.core == 0, x, other), jnp.where(self.core == 0, other, x)])
        if self.group > 1:
            groups = [
                list(range(first, first + self.group))
                for first in range(0, self.seqs, self.group)
            ]
            pair = lax.all_gather(pair, "seq", axis_index_groups=groups)
        return pair.reshape((-1,) + x.shape[1:])

    def scatter(self, x):
        if self.group > 1:
            groups = [
                list(range(first, first + self.group))
                for first in range(0, self.seqs, self.group)
            ]
            x = lax.psum_scatter(
                x, "seq", scatter_dimension=0, axis_index_groups=groups, tiled=True
            )
        pair = x.reshape((2, -1) + x.shape[1:])
        got = across_cores(lax.dynamic_index_in_dim(pair, 1 - self.core, 0, keepdims=False))
        mine = lax.dynamic_index_in_dim(pair, self.core, 0, keepdims=False)
        return mine.astype(jnp.float32) + got.astype(jnp.float32)


def shards(
    byte_values,
    segments,
    byte_mask,
    embedding,
    filter_weight,
    score_weight,
    first_gain,
    query_weight,
    key_weight,
    value_weight,
    merge_weight,
    position_bias,
    second_gain,
    gate_weight,
    up_weight,
    down_weight,
    cotangent,
):
    count = lax.axis_size("batch")
    seqs = lax.axis_size("seq")
    held, width = byte_values.shape
    row_len = segments.shape[1]
    vocab, features = embedding.shape
    hidden_size = gate_weight.shape[1]
    heads = position_bias.shape[1]
    bucket_count = position_bias.shape[0]
    total = row_len // 2
    plan = Plan(held)
    tokens = total // plan.parts
    chips = count // 2
    levels = chips.bit_length() - 1
    blocks = tokens // BLOCK
    other_part = plan.part ^ 1

    bases = [plan.part * blocks, other_part * blocks] if plan.group == 1 else [0, 0]
    info = jnp.stack(
        [
            jnp.asarray(value, jnp.int32)
            for value in (
                plan.me,
                plan.core,
                plan.row % held,
                plan.part * blocks,
                plan.part * 2 * tokens,
                bases[0],
                bases[1],
                plan.me // chips,
                plan.place,
            )
        ]
    )
    ids = plan.bytes_of(jnp.where(byte_mask > 0, byte_values, -1))
    ids = jnp.pad(ids, ((MAIN - 1, MAIN - 1), (0, 0)), constant_values=-1)
    cuts = jnp.sum((segments[:, :, None] < jnp.arange(1, 4)).astype(jnp.int32), axis=1)
    cuts = (cuts + 1) // 2
    both = jnp.concatenate([cuts, across_cores(cuts)])
    own_first = jnp.where(plan.row // held == plan.core, 0, held)
    cuts = lax.dynamic_index_in_dim(both, own_first + plan.row % held, 0, keepdims=False)
    bias = hbm(bias_tiles(position_bias.T))
    embedding, filter_weight, score_weight = map(hbm, (embedding, filter_weight, score_weight))
    first_gain, second_gain = hbm(first_gain), hbm(second_gain)
    query_weight, key_weight, value_weight = map(hbm, (query_weight, key_weight, value_weight))
    merge_weight = hbm(merge_weight)
    head_size = features // heads
    words = -(-(vocab + 7 + heads) // (16 * count)) * (16 * count)
    stream, normed, q, kv = mixer_forward(
        info,
        ids,
        embedding,
        filter_weight,
        score_weight,
        first_gain,
        query_weight,
        key_weight,
        value_weight,
        tokens,
        row_len,
        [],
    )
    normed, stream = hbm(normed), hbm(stream)
    ends = (stream, merge_weight, second_gain)
    cot_blocks = plan.blocks_of(cotangent)
    if plan.group == 1:
        kvs = [kv, across_cores(kv)]
        begun, later = attention_forward(
            "attention_own", head_size, info, q, kvs[0], bias, cuts, carry=cot_blocks[1:]
        )
        (att, lse, resid, normed_two), _ = attention_forward(
            "attention_other", head_size, info, q, kvs[1], bias, cuts, begun, ends
        )
    else:
        kvs = [jnp.stack([plan.gather(kv[0]), plan.gather(kv[1])])]
        later = cot_blocks[1:]
        (att, lse, resid, normed_two), _ = attention_forward(
            "attention_all", head_size, info, q, kvs[0], bias, cuts, (), ends
        )
    cots = [lax.ppermute(x, AXES, perm) for x, perm in zip([cot_blocks[0], *later], plan.perms)]

    weights = (gate_weight, up_weight, down_weight)
    acc, grad_two, *grads, cot, cot_turned, normed_turned = feed_forward(
        0, info, normed_two, [*cots, resid], *weights, held, count
    )
    halves = [grads]
    *results, grad_two, keep, send = feed_forward(
        1,
        info,
        normed_two,
        [acc, grad_two, cot, cot_turned, normed_turned],
        *weights,
        held,
        count,
    )
    halves.append([keep, send])
    early = count // 4

    def upwards(key):
        return key[0] == "down" or key[3] < early

    def downwards(key):
        return not upwards(key)

    states = []

    def start_half(half, after):
        keep, send = halves[half]
        pairs = [(keep, across_cores(send))]
        steps = chips // 2
        slab = 4 * chips + count
        where = {}
        for r in range(chips):
            for n in range(count):
                kind, block = n // chips, n % chips
                place = block // 2 * slab + (2 * kind + block % 2) * chips + r
                where["gu", half, 0, n, r] = (0, place)

        def down_at(r, n):
            return lambda info: (r ^ lax.rem(info[0] // 2, steps)) * slab + 4 * chips + n

        for r in range(steps):
            for n in range(count):
                where["down", half, 0, n, r] = (0, down_at(r, n))
        state = Halving(pairs, where)
        first = None
        for level in range(levels - 1):
            state, outs, _ = exchange(
                f"feed_{half}_{level}",
                info,
                state,
                [(upwards, level), (downwards, levels - 1 - level)],
                after if level == 0 else (),
            )
            first = first or outs
        states.append(state)
        return first

    back_perms = [[(b, a) for a, b in perm] for perm in plan.perms]
    out_parts = [lax.ppermute(x, AXES, perm) for x, perm in zip(results, back_perms)]
    first = start_half(0, [grad_two])
    (grad_resid, att_grad, m_keep, m_send, second_part), _ = between(
        info, grad_two, resid, second_gain, cot, att, merge_weight, count, [first[0]], []
    )
    first = start_half(1, [second_part])
    dq, dkvs, tiles = attention_backward(
        head_size, info, hbm(q), att_grad, [hbm(kvs[0]), *kvs[1:]], bias, cuts, lse, att, [first[0]]
    )

    where = {}
    for half, state in enumerate(states):
        for key, (pair, slot) in state.where.items():
            where[key] = (2 * half + pair, slot)
    top = 1 << (levels - 1)
    for key in [key for key in where if key[0] == "down"]:
        _, half, kind, n, r = key
        mine, other = where["down", 0, 0, n, 0], where["down", 1, 0, n, 0]
        if half == 0:
            where["one", 2, 0, n, 0] = mine + other
            where["one", 2, 0, n, top] = other + mine
    where = {key: value for key, value in where.items() if key[0] != "down"}
    state = Halving(states[0].pairs + states[1].pairs, where)
    crossing = [dkvs[1]] if plan.group == 1 else []
    state, lasts, crossing = exchange(
        "feed_last",
        info,
        state,
        [
            (lambda key: key[0] == "one" or key[3] < early, levels - 1),
            (lambda key: key[0] == "gu" and key[3] >= early, 0),
        ],
        [hbm(dq), out_parts[0]],
        crossing,
    )
    if plan.group == 1:
        mine, got = hbm(dkvs[0]), across_cores(crossing[0])
    else:
        mine = jnp.stack([plan.scatter(dkvs[0][i]).astype(jnp.bfloat16) for i in range(2)])
        got = jnp.zeros_like(mine)
    bias_part = bucket_sums(tiles, [lasts[0]])
    (q_keep, qm_send, back, turned), later = project_q(
        info, hbm(dq), normed, query_weight, m_send, count, [bias_part], []
    )
    qm_got = across_cores(qm_send)
    kv_keep, kv_send, grad_stream, first_part = project_kv(
        mine,
        got,
        turned,
        back,
        stream,
        hbm(grad_resid),
        first_gain,
        key_weight,
        value_weight,
        count,
        [],
    )

    each = count // seqs
    picks = []
    for key, pick in state.where.items():
        if key[0] == "one":
            picks.append((pick, key[3] // each, 2 * each + key[3] % each))
        else:
            kind, block = key[3] // chips, key[1] * chips + key[3] % chips
            picks.append((pick, block // each, kind * each + block % each))
    slots = 3 * each
    groups = [list(range(0, seqs, 2)), list(range(1, seqs, 2))]
    (z_keep, z_send), (kv_send,) = fold_seq(
        "feed_seq", info, state.pairs, picks, seqs, slots, groups, after=[first_part, *out_parts[1:]], carry=[kv_send]
    )
    kv_got = across_cores(kv_send)
    z_got = across_seq(z_send, 1)
    where = {}
    for r in range(chips):
        where["p", 0, r] = (0, r)
        where["p", 3, r] = (1, (r, chips + r))
        for kind in (1, 2):
            where["p", kind, r] = (2, (kind - 1) * chips + r)
    mixes = Halving([(q_keep, qm_got), (hbm(m_keep), qm_got), (kv_keep, kv_got)], where)

    def mix_step(mixes, level, after, carry=(), held_back=False):
        return exchange(
            f"mix_{level}",
            info,
            mixes,
            [
                (lambda key: key[1] in (1, 3), level),
                (lambda key: key[1] in (0, 2), levels - 1 - level),
            ],
            after,
            carry,
            held_back,
        )

    layer_output = join(info, out_parts, [z_keep])
    mixes, outs, _ = mix_step(mixes, 0, [hbm(layer_output)])
    e_keep, e_send = mixer_backward(
        info,
        ids,
        embedding,
        filter_weight,
        score_weight,
        grad_stream,
        first_part,
        second_part,
        bias_part,
        row_len,
        vocab,
        words,
        count,
        [z_keep, outs[0]],
    )

    def seq_step(name, z_keep, z_got, slots, step, after, carry):
        held_now = z_keep.shape[0] // slots
        lists = [
            [(0, d * slots + i) for d in range(first, held_now, 2) for i in range(slots)]
            for first in range(2)
        ]
        (z_keep, z_send), carried = fold(
            f"{name}_seq_{step}", info, [(z_keep, z_got)], lists, after, carry
        )
        return z_keep, across_seq(z_send, step), carried

    last, step, carry = e_keep, 2, [e_send]
    while step < seqs:
        z_keep, z_got, carry = seq_step("feed", z_keep, z_got, slots, step, [last], carry)
        last = z_keep
        step *= 2
    for level in range(1, levels):
        mixes, outs, _ = mix_step(mixes, level, [last], (), level == levels - 1)
        last = outs[0]
    e_got = across_cores(carry[0])
    small = Halving([(e_keep, e_got)], {("e", r): (0, r) for r in range(chips)})
    sends = outs[1::2]
    for level in range(levels):
        small, outs, sends = exchange(
            f"small_{level}",
            info,
            small,
            [(lambda key: True, level)],
            [last] if level == 0 else [],
            sends if level == 0 else [],
        )
        if level == 0:
            mixes = mixes(sends)
    (share,), _ = fold("small_chips", info, small.pairs, [small.picks([("e", 0)])])
    seq_parts = [share] + [across_seq(share, d) for d in range(1, seqs)]
    picks = [(pick, None, key[1]) for key, pick in mixes.where.items()]
    gate_grad, up_grad, down_grad = feed_end([z_keep, z_got], [share])
    share_width = features // seqs
    mix_sends, _ = fold_seq(
        "mix_seq",
        info,
        mixes.pairs,
        picks,
        seqs,
        tile_count(4, share_width),
        [[d] for d in range(seqs)],
        share_width,
        after=[hbm(gate_grad)],
    )
    mix_arrived = [mix_sends[0]] + [across_seq(mix_sends[d], d) for d in range(1, seqs)]
    share = sum_of("small_seq", seq_parts, [mix_sends[0]])
    shares = [share] + [across_chips(share, r) for r in range(1, chips)]
    query_grad, key_grad, value_grad, merge_grad = mix_end(mix_arrived, 4, share_width, [share])
    embed, filters, score, first, second, bias_sum = unpack(
        info, shares, [across_cores(x) for x in shares], vocab, bucket_count, heads, [hbm(query_grad)]
    )
    return (
        layer_output,
        embed,
        filters,
        score,
        first,
        query_grad,
        key_grad,
        value_grad,
        merge_grad,
        bias_sum.T,
        second,
        gate_grad,
        up_grad,
        down_grad.T,
    )


def solution(mesh):
    in_specs = (
        P("batch", "seq"),
        P("batch", None),
        P("batch", "seq"),
        P(),
        P(),
        P(),
        P(),
        P(),
        P(),
        P(),
        P(),
        P(),
        P(),
        P(),
        P(),
        P(),
        P("batch", "seq", None),
    )
    out_specs = (
        P("batch", "seq", None),
        P(),
        P(),
        P(),
        P(),
        P("batch", "seq"),
        P("batch", "seq"),
        P("batch", "seq"),
        P("batch", "seq"),
        P(),
        P(),
        P("batch", "seq"),
        P("batch", "seq"),
        P("batch", "seq"),
    )
    return jax.shard_map(shards, mesh=mesh, in_specs=in_specs, out_specs=out_specs, check_vma=False)
```

```python
import functools

import jax
import jax.numpy as jnp
from jax import lax
from jax.experimental import pallas as pl
from jax.experimental.pallas import tpu as pltpu
from jax.sharding import PartitionSpec as P

EPS = 1e-06
LIMITS = (12, 16, 23, 32, 46, 64, 91)
NEG = -1e30
LANES = 128
BLOCK = 128
FAR = 2
CUBE = 0.044715
SLOPE = 0.7978845608028654
MEGA = 1 << 20


def dot(a, b):
    return lax.dot_general(a, b, (((1,), (0,)), ((), ())), preferred_element_type=jnp.float32)


def dot_nt(a, b):
    return lax.dot_general(a, b, (((1,), (1,)), ((), ())), preferred_element_type=jnp.float32)


def params(megabytes):
    return pltpu.CompilerParams(vmem_limit_bytes=megabytes * MEGA)


def cost(microseconds):
    return pl.CostEstimate(flops=int(microseconds * 1e+09), bytes_accessed=1, transcendentals=0)


VMEM = pl.BlockSpec(memory_space=pltpu.VMEM)
ANY = pl.BlockSpec(memory_space=pl.ANY)
HBM = pl.BlockSpec(memory_space=pltpu.HBM)
AUTO = pl.BlockSpec()
SMEM = pl.BlockSpec(memory_space=pltpu.SMEM)


def hbm(x):
    return pltpu.with_memory_space_constraint(x, pltpu.HBM)


def ordered(kernel, inputs, after):
    def with_others(*refs):
        kernel(*refs[:inputs], *refs[inputs + len(after) :])

    return with_others


def launch(name, kernel, ins, in_specs, outs, out_specs, megabytes, scratch=(), after=(), carry=(), microseconds=1.0
):
    given, made = len(ins), len(outs)
    skip = len(after) + len(carry)

    def body(*refs):
        rest = refs[given + skip :]
        kernel(*refs[:given], *rest[:made], *rest[made + len(carry) :])

    results = pl.pallas_call(
        body,
        out_shape=[*outs, *[jax.ShapeDtypeStruct(x.shape, x.dtype) for x in carry]],
        in_specs=[*in_specs, *[ANY] * skip],
        out_specs=[*out_specs, *[ANY] * len(carry)],
        scratch_shapes=list(scratch),
        input_output_aliases={given + len(after) + i: made + i for i in range(len(carry))},
        compiler_params=params(megabytes),
        cost_estimate=cost(microseconds),
        name=name,
    )(*ins, *after, *carry)
    return results[:made], results[made:]


def bucket_of(relative):
    distance = jnp.abs(relative)
    far = jnp.full_like(distance, 8)
    for limit in LIMITS:
        far = far + jnp.where(distance >= limit, 1, 0)
    return jnp.where(distance < 8, distance, far) + jnp.where(relative > 0, 16, 0)


def split_three(x):
    parts = []
    for _ in range(3):
        high = x.astype(jnp.bfloat16)
        parts.append(high)
        x = x - high.astype(jnp.float32)
    return parts


def bias_kernel(table_ref, out_ref, tile_ref, sems):
    copies = []
    heads, buckets = table_ref.shape
    wide = 2 * BLOCK
    parts = split_three(table_ref[...])
    bucket = lax.broadcasted_iota(jnp.int32, (buckets, wide), 0)
    entry = lax.broadcasted_iota(jnp.int32, (buckets, wide), 1)
    gap = jnp.where(entry < BLOCK, entry, entry - wide)
    for delta in range(3):
        hot = jnp.where(bucket_of((delta - 1) * BLOCK - gap) == bucket, 1.0, 0.0)
        hot = hot.astype(jnp.bfloat16)
        rows = (dot(parts[2], hot) + dot(parts[1], hot)) + dot(parts[0], hot)
        for h in range(heads):
            row = jnp.broadcast_to(rows[h : h + 1], (BLOCK, wide))
            tile_ref[delta, h] = pltpu.roll(row, 0, 1, stride=1, stride_axis=0)[:, :BLOCK]
        copies.append(pltpu.make_async_copy(tile_ref.at[delta], out_ref.at[delta], sems.at[delta]))
        copies[-1].start()
    for copy in copies:
        copy.wait()


def bias_tiles(table, after, carry):
    return launch(
        "bias_tiles",
        bias_kernel,
        [table],
        [VMEM],
        [pltpu.HBM((3, table.shape[0], BLOCK, BLOCK), jnp.float32)],
        [HBM],
        6,
        [
            pltpu.VMEM((3, table.shape[0], BLOCK, BLOCK), jnp.float32),
            pltpu.SemaphoreType.DMA((3,)),
        ],
        after=after,
        carry=carry,
        microseconds=2,
    )


def fill_tiles(near_ref, h, tile_ref):
    for delta in range(3):
        tile_ref[1 + delta] = near_ref[delta, h]
    tile_ref[0] = jnp.broadcast_to(near_ref[0, h, :1, BLOCK - 1 :], (BLOCK, BLOCK))
    tile_ref[4] = jnp.broadcast_to(near_ref[2, h, BLOCK - 1 :, :1], (BLOCK, BLOCK))


def by_head(turned, size):
    empty = jnp.zeros((size, turned.shape[1]), turned.dtype)
    left = jnp.concatenate([turned[:size], empty], axis=0)
    right = jnp.concatenate([empty, turned[size:]], axis=0)
    return jnp.concatenate([left, right], axis=1)


def lower_rows(cut_ref, start, rows, heads):
    count = rows[0].shape[1] if rows else heads[1]
    place = start + lax.broadcasted_iota(jnp.int32, (16, count), 1)
    row = lax.broadcasted_iota(jnp.int32, (16, count), 0)
    segment = sum(jnp.where(place >= cut_ref[i], 1, 0) for i in range(3))
    mask = jnp.where((row < 4) & (segment != row), NEG, 0.0)
    blocks = []
    for head in range(heads[0]):
        block = mask
        if rows:
            for i, part in enumerate(split_three(rows[head])):
                block = jnp.where(row == 4 + i, part.astype(jnp.float32), block)
        blocks.append(block.astype(jnp.bfloat16))
    block = jnp.concatenate(blocks, axis=1)
    return jnp.concatenate([block, jnp.zeros((LANES - 16, block.shape[1]), jnp.bfloat16)], axis=0)


def segment_hots(cut_ref, start, count, inside, outside):
    place = start + lax.broadcasted_iota(jnp.int32, (count, LANES), 0)
    lane = lax.broadcasted_iota(jnp.int32, (count, LANES), 1)
    segment = sum(jnp.where(place >= cut_ref[i], 1, 0) for i in range(3))
    value = jnp.where(segment == lane, inside, outside)
    return jnp.where(lane < 4, value, 0.0).astype(jnp.bfloat16)


TILE = 32
FORWARD_TILE = 64
GUARD = 8
MAIN = 24


def row_of(ref):
    return ref[...].reshape(1, -1)


def tile_rows(base, size=TILE):
    return pl.ds(pl.multiple_of(base, 8), size)


def with_sides(ref, lead, base, lanes, size=TILE):
    return ref[(*lead, pl.ds(pl.multiple_of(base - 8, 8), size + 16), lanes)]


def middle(x):
    return x[8:-8]


def down(x):
    return middle(pltpu.roll(x, 1, 0))


def up(x):
    return middle(pltpu.roll(x, x.shape[0] - 1, 0))


def lane_sum(x):
    return jnp.broadcast_to(jnp.sum(x, axis=1, keepdims=True), x.shape)


def offsets_of(rows):
    return {
        -2: down(rows[2]),
        -1: down(rows[3]),
        0: middle(rows[0]),
        1: middle(rows[1]),
        2: middle(rows[2]),
        3: middle(rows[3]),
        4: up(rows[0]),
        5: up(rows[1]),
    }


def spread_of(phase, j, one, two, three, four, coefs):
    pair = j - j % 2
    third = three / 3.0
    zero = jnp.zeros_like(third)
    half, quarter = two * 0.5, four * 0.25

    def add(o, value):
        coefs[o] = coefs[o] + value if o in coefs else value

    add(j, one + third)
    for o in (pair, pair + 1):
        add(o, half)
    for o in range(4):
        add(o, quarter)
    add(j + 1, jnp.where(phase <= 1, third, zero))
    add(j + 2, jnp.where(phase == 0, third, zero))
    add(j - 1, jnp.where(phase >= 1, third, zero))
    add(j - 2, jnp.where(phase == 2, third, zero))


def pooled_dots(phase, j, dots):
    pair = j - j % 2
    zero = jnp.zeros_like(dots[0])
    two = 0.5 * (dots[pair] + dots[pair + 1])
    four = 0.25 * ((dots[0] + dots[1]) + (dots[2] + dots[3]))
    three = dots[j] + jnp.where(phase <= 1, dots[j + 1], zero)
    three = three + jnp.where(phase == 0, dots[j + 2], zero)
    three = three + jnp.where(phase >= 1, dots[j - 1], zero)
    three = three + jnp.where(phase == 2, dots[j - 2], zero)
    return dots[j], two, three / 3.0, four


def lane_chunks(features):
    return [slice(i, i + LANES) for i in range(0, features, LANES)]


def over_tiles(first, rows, body, size=TILE):
    def step(t, carry):
        body(first + t * size)
        return carry

    lax.fori_loop(0, rows // size, step, 0)


def convolve_all(info_ref, ids_ref, emb_ref, filt_ref, score_ref, e_ref, c_ref, dot_ref, row_len):
    count = ids_ref.shape[0]
    words, features = emb_ref.shape
    score = row_of(score_ref)
    group = info_ref[4] // 4
    vocab = lax.broadcasted_iota(jnp.int32, (count, words), 1)
    edge = jnp.zeros((GUARD, LANES), jnp.float32)
    for j in range(4):
        hot = jnp.where(ids_ref[:, j : j + 1] == vocab, 1.0, 0.0).astype(jnp.bfloat16)
        e_ref[j] = dot(hot, emb_ref[...])
        dot_ref[j, :GUARD] = edge
        dot_ref[j, count - GUARD :] = edge

    def tile(base):
        parts = [jnp.zeros((TILE, LANES), jnp.float32) for _ in range(4)]
        for lanes in lane_chunks(features):
            near = offsets_of([with_sides(e_ref, (j,), base, lanes) for j in range(4)])
            taps = [filt_ref[k : k + 1, lanes] for k in range(4)]
            for j in range(4):
                value = taps[0] * near[j - 2]
                for k in range(1, 4):
                    value = value + taps[k] * near[j + k - 2]
                c_ref[j, tile_rows(base), lanes] = value
                parts[j] = parts[j] + value * score[:, lanes]
        places = base - MAIN + group + lax.broadcasted_iota(jnp.int32, (TILE, LANES), 0)
        for j in range(4):
            inside = 4 * places + j < row_len
            dot_ref[j, tile_rows(base)] = jnp.where(inside, lane_sum(parts[j]), 0.0)

    over_tiles(GUARD, count - 2 * GUARD, tile)


def tile_weights(info_ref, dot_ref, base, row_len, size):
    dots = offsets_of([with_sides(dot_ref, (j,), base, slice(None), size) for j in range(4)])
    places = base - MAIN + info_ref[4] // 4
    places = places + lax.broadcasted_iota(jnp.int32, (size, LANES), 0)
    phases, weights = [], []
    for j in range(4):
        phase = lax.rem(places + 3 + j, 3)
        scores = pooled_dots(phase, j, dots)
        highest = jnp.maximum(jnp.maximum(scores[0], scores[1]), jnp.maximum(scores[2], scores[3]))
        powers = [jnp.exp(score - highest) for score in scores]
        share = 1.0 / ((powers[0] + powers[1]) + (powers[2] + powers[3]))
        phases.append(phase)
        weights.append([power * share for power in powers])
    limits = {o: (4 * places + o < row_len) for o in (4, 5)}
    return phases, weights, limits


def token_coefs(phases, weights, limits, scale):
    result = []
    for h in range(2):
        coefs = {}
        for j in (2 * h, 2 * h + 1):
            spread_of(phases[j], j, *weights[j], coefs)
        for o in coefs:
            if o in limits:
                coefs[o] = jnp.where(limits[o], coefs[o], 0.0)
            coefs[o] = coefs[o] * scale
        result.append(coefs)
    return result


COEFS = [(0, o) for o in range(-2, 4)] + [(1, o) for o in range(6)]


def mixer_kernel(
    row_len,
    info_ref,
    ids_ref,
    emb_ref,
    filt_ref,
    score_ref,
    gain_ref,
    wq_ref,
    wk_ref,
    wv_ref,
    stream_out_ref,
    normed_out_ref,
    q_ref,
    kv_ref,
    e_ref,
    c_ref,
    dot_ref,
    pair_ref,
    root_ref,
    weight_ref,
    sems,
    stream_ref,
    normed_ref,
):
    copies = [
        pltpu.make_async_copy(w_ref, weight_ref.at[i], sems.at[i])
        for i, w_ref in enumerate((wk_ref, wv_ref, wq_ref))
    ]
    for copy in copies:
        copy.start()
    tokens, features = stream_ref.shape
    gain = row_of(gain_ref)
    chunks = lane_chunks(features)
    convolve_all(
        info_ref, ids_ref, emb_ref, filt_ref, score_ref, e_ref, c_ref, dot_ref, row_len
    )

    size = pair_ref.shape[1] // 2

    def tile(base):
        coefs = token_coefs(*tile_weights(info_ref, dot_ref, base, row_len, size), 0.5)
        squares = [jnp.zeros((size, LANES), jnp.float32) for _ in range(2)]
        rows = pl.ds(pl.multiple_of(2 * (base - MAIN), 2 * size), 2 * size)
        for i, lanes in enumerate(chunks):
            conv = offsets_of([with_sides(c_ref, (j,), base, lanes, size) for j in range(4)])
            for h in range(2):
                mixed = None
                for o, coef in coefs[h].items():
                    term = coef * conv[o]
                    mixed = term if mixed is None else mixed + term
                squares[h] = squares[h] + mixed * mixed
                pair_ref[i, pl.ds(h, size, stride=2), :] = mixed
        for h in range(2):
            root = lax.rsqrt(lane_sum(squares[h]) / features + EPS)
            root_ref[pl.ds(h, size, stride=2), :] = root
        for i, lanes in enumerate(chunks):
            stream = pair_ref[i]
            stream_ref[rows, lanes] = stream
            normed = stream * root_ref[...] * gain[:, lanes]
            normed_ref[rows, lanes] = normed.astype(jnp.bfloat16)

    over_tiles(MAIN, tokens // 2, tile, size)
    kept = [
        pltpu.make_async_copy(stream_ref, stream_out_ref, sems.at[3]),
        pltpu.make_async_copy(normed_ref, normed_out_ref, sems.at[4]),
    ]
    for copy in kept:
        copy.start()
    for i in range(2):
        copies[i].wait()
        kv_ref[i] = dot(normed_ref[...], weight_ref[i]).astype(jnp.bfloat16)
    copies[2].wait()
    q_ref[...] = dot(normed_ref[...], weight_ref[2]).astype(jnp.bfloat16)
    for copy in kept:
        copy.wait()


def mixer_forward(info, ids, emb, filt, score, gain, wq, wk, wv, tokens, row_len, after):
    features = emb.shape[1]
    count = ids.shape[0]
    low = jnp.bfloat16
    full = jnp.float32
    outs, _ = launch(
        "mixer_forward",
        functools.partial(mixer_kernel, row_len),
        [info, ids, emb, filt, score, gain, wq, wk, wv],
        [SMEM] + [VMEM] * 5 + [HBM] * 3,
        [
            pltpu.HBM((tokens, features), full),
            pltpu.HBM((tokens, features), low),
            jax.ShapeDtypeStruct((tokens, features), low),
            jax.ShapeDtypeStruct((2, tokens, features), low),
        ],
        [HBM, HBM, VMEM, VMEM],
        24,
        [
            pltpu.VMEM((4, count, features), full),
            pltpu.VMEM((4, count, features), full),
            pltpu.VMEM((4, count, LANES), full),
            pltpu.VMEM((features // LANES, 2 * FORWARD_TILE, LANES), full),
            pltpu.VMEM((2 * FORWARD_TILE, LANES), full),
            pltpu.VMEM((3, features, features), low),
            pltpu.SemaphoreType.DMA((5,)),
            pltpu.VMEM((tokens, features), full),
            pltpu.VMEM((tokens, features), low),
        ],
        after=after,
        microseconds=8,
    )
    return outs


def mixer_back_kernel(
    row_len,
    vocab_size,
    info_ref,
    ids_ref,
    emb_ref,
    filt_ref,
    score_ref,
    grad_ref,
    first_ref,
    second_ref,
    bias_ref,
    keep_ref,
    send_ref,
    e_ref,
    c_ref,
    dot_ref,
    coef_ref,
    g_ref,
    low_ref,
    turn_ref,
    embed_ref,
    small_ref,
):
    tokens, features = grad_ref.shape
    groups = tokens // 2
    chunks = lane_chunks(features)
    count = ids_ref.shape[0]
    inner = count - 2 * GUARD
    score_row = row_of(score_ref)
    convolve_all(
        info_ref, ids_ref, emb_ref, filt_ref, score_ref, e_ref, c_ref, dot_ref, row_len
    )
    before = jnp.zeros((MAIN, LANES), jnp.float32)
    behind = jnp.zeros((count - MAIN - groups, LANES), jnp.float32)
    for i, lanes in enumerate(chunks):
        turn_ref[i] = grad_ref[:, lanes]
        for h in range(2):
            g_ref[h, :MAIN, lanes] = before
            g_ref[h, MAIN + groups :, lanes] = behind
            g_ref[h, MAIN : MAIN + groups, lanes] = turn_ref[i, pl.ds(h, groups, stride=2), :]
    for place in range(2 * len(COEFS)):
        coef_ref[place, :MAIN] = before
        coef_ref[place, MAIN + groups :] = behind
    small_ref[...] = jnp.zeros_like(small_ref)

    def pull_tile(base):
        phases, weights, limits = tile_weights(info_ref, dot_ref, base, row_len, TILE)
        coefs = token_coefs(phases, weights, limits, 0.5)
        sums = {}
        for lanes in chunks:
            conv = offsets_of([with_sides(c_ref, (j,), base, lanes) for j in range(4)])
            grads = [g_ref[h, tile_rows(base), lanes] for h in range(2)]
            for h, o in COEFS:
                term = grads[h] * conv[o]
                sums[h, o] = sums[h, o] + term if (h, o) in sums else term
        pulls = []
        for h in range(2):
            dots = {}
            for side, o in COEFS:
                if side == h:
                    value = lane_sum(sums[h, o]) * 0.5
                    dots[o] = jnp.where(limits[o], value, 0.0) if o in limits else value
            for j in (2 * h, 2 * h + 1):
                grads = pooled_dots(phases[j], j, dots)
                mean = sum(weights[j][i] * grads[i] for i in range(4))
                pulls.append([weights[j][i] * (grads[i] - mean) for i in range(4)])
        score_coefs = token_coefs(phases, pulls, limits, 1.0)
        for place, (h, o) in enumerate(COEFS):
            coef_ref[place, tile_rows(base)] = coefs[h][o]
            coef_ref[len(COEFS) + place, tile_rows(base)] = score_coefs[h][o]

    over_tiles(MAIN, groups, pull_tile)

    def fold_rows(x):
        return sum(x[i : i + 8] for i in range(0, TILE, 8))

    def grad_tile(base):
        def coef(h, o, score=False):
            return with_sides(coef_ref, (COEFS.index((h, o)) + len(COEFS) * score,), base, slice(None))

        own = [[middle(coef(h, j)) for j in range(4)] for h in range(2)]
        side = [down(coef(1, 4 + j)) if j < 2 else up(coef(0, j - 4)) for j in range(4)]
        kappa = []
        for j in range(4):
            far = down(coef(1, 4 + j, True)) if j < 2 else up(coef(0, j - 4, True))
            kappa.append(middle(coef(0, j, True)) + middle(coef(1, j, True)) + far)
        for lanes in chunks:
            first, second = (with_sides(g_ref, (h,), base, lanes) for h in range(2))
            above, below = down(second), up(first)
            first, second = middle(first), middle(second)
            near = offsets_of([with_sides(e_ref, (j,), base, lanes) for j in range(4)])
            score = score_row[:, lanes]
            taps = [None] * 4
            score_sum = None
            for j in range(4):
                value = own[0][j] * first + own[1][j] * second
                value = value + side[j] * (above if j < 2 else below) + kappa[j] * score
                term = kappa[j] * c_ref[j, tile_rows(base), lanes]
                score_sum = term if score_sum is None else score_sum + term
                c_ref[j, tile_rows(base), lanes] = value
                for k in range(4):
                    term = value * near[j + k - 2]
                    taps[k] = term if taps[k] is None else taps[k] + term
            for k in range(4):
                small_ref[k, :, lanes] += fold_rows(taps[k])
            small_ref[4, :, lanes] += fold_rows(score_sum)

    over_tiles(GUARD, inner, grad_tile)
    edge = jnp.zeros((GUARD, features), jnp.float32)
    for j in range(4):
        c_ref[j, :GUARD] = edge
        c_ref[j, count - GUARD :] = edge

    def back_tile(base):
        start = pl.multiple_of(base - GUARD, TILE)
        for lanes in chunks:
            d = offsets_of([with_sides(c_ref, (j,), base, lanes) for j in range(4)])
            taps = [filt_ref[k : k + 1, lanes] for k in range(4)]
            for j in range(4):
                value = taps[0] * d[j + 2]
                for k in range(1, 4):
                    value = value + taps[k] * d[j + 2 - k]
                low_ref[pl.ds(j * inner + start, TILE), lanes] = value.astype(jnp.bfloat16)

    over_tiles(GUARD, inner, back_tile)
    lane = lax.broadcasted_iota(jnp.int32, (inner, LANES), 1)
    spread = jnp.zeros((inner, LANES), jnp.float32)
    for j in range(4):
        ids = ids_ref[GUARD : GUARD + inner, j : j + 1].astype(jnp.float32)
        spread = jnp.where(lane == j, ids, spread)
    spare = jnp.zeros((-inner % LANES, LANES), jnp.float32)
    turned = jnp.concatenate([spread, spare], axis=0).T.astype(jnp.int32)
    flat = jnp.concatenate([turned[j : j + 1, :inner] for j in range(4)], axis=1)
    words = -(-vocab_size // 16) * 16
    vocab = lax.broadcasted_iota(jnp.int32, (words, 4 * inner), 0)
    hot = jnp.where(flat == vocab, 1.0, 0.0).astype(jnp.bfloat16)
    embed_ref[:words] = dot(hot, low_ref[...])
    embed_ref[words:] = jnp.zeros((embed_ref.shape[0] - words, features), jnp.float32)
    for i in range(5):
        embed_ref[vocab_size + i : vocab_size + i + 1] = jnp.sum(small_ref[i], axis=0, keepdims=True)
    embed_ref[vocab_size + 5 : vocab_size + 6] = first_ref[...]
    embed_ref[vocab_size + 6 : vocab_size + 7] = second_ref[...]
    heads = bias_ref.shape[0]
    embed_ref[vocab_size + 7 : vocab_size + 7 + heads, :LANES] = bias_ref[...]
    share = keep_ref.shape[1]
    chips = keep_ref.shape[0]
    me = info_ref[0]
    for place in range(chips):
        for odd, out_ref in enumerate((keep_ref, send_ref)):
            start = pl.multiple_of((me ^ (2 * place + odd)) * share, 16)
            out_ref[place] = embed_ref[pl.ds(start, share), :].astype(jnp.bfloat16)


def mixer_backward(
    info, ids, emb, filt, score, grad, first, second, bias, row_len, vocab, embed_rows, devices, after
):
    tokens, features = grad.shape
    count = ids.shape[0]
    full = jnp.float32
    piece = jax.ShapeDtypeStruct((devices // 2, embed_rows // devices, features), jnp.bfloat16)
    outs, _ = launch(
        "mixer_backward",
        functools.partial(mixer_back_kernel, row_len, vocab),
        [info, ids, emb, filt, score, grad, first, second, bias],
        [SMEM] + [VMEM] * 8,
        [piece, piece],
        [VMEM] * 2,
        26,
        [
            pltpu.VMEM((4, count, features), full),
            pltpu.VMEM((4, count, features), full),
            pltpu.VMEM((4, count, LANES), full),
            pltpu.VMEM((2 * len(COEFS), count, LANES), full),
            pltpu.VMEM((2, count, features), full),
            pltpu.VMEM((4 * (count - 2 * GUARD), features), jnp.bfloat16),
            pltpu.VMEM((features // LANES, tokens, LANES), full),
            pltpu.VMEM((embed_rows, features), full),
            pltpu.VMEM((5, 8, features), full),
        ],
        after=after,
        microseconds=11,
    )
    return outs


def scores_of(info_ref, part, raw, tile_ref):
    keys, tokens = raw.shape
    base, own = info_ref[part], info_ref[3]
    rows = []
    for kb in range(keys // BLOCK):
        tiles = [
            tile_ref[jnp.clip(base + kb - own - qb, -FAR, FAR) + FAR]
            for qb in range(tokens // BLOCK)
        ]
        rows.append(raw[kb * BLOCK : (kb + 1) * BLOCK] + jnp.concatenate(tiles, axis=1))
    return rows


def only_head(x, h, size):
    lane = lax.broadcasted_iota(jnp.int32, x.shape, 1)
    return jnp.where((lane >= h * size) & (lane < (h + 1) * size), x, jnp.zeros_like(x))


def attention_kernel(
    size,
    carried,
    last,
    info_ref,
    q_ref,
    kv_ref,
    bias_ref,
    cut_ref,
    *refs,
):
    if last:
        *refs, plain_ref, weight_ref, sems = refs
    *refs, tile_ref, q_low_ref, k_hot_ref = refs
    if carried:
        before_ref, state_ref, *refs = refs
    if last:
        stream_ref, wm_ref, gain_ref, att_ref, lse_ref, resid_ref, normed_ref = refs
    else:
        mixed_ref, stat_ref = refs
    step = pl.program_id(0)
    part = 5 + carried
    low = []
    tokens = q_ref.shape[0]

    @pl.when(step == 0)
    def _():
        q_low_ref[...] = lower_rows(cut_ref, info_ref[3] * BLOCK, [], (2, tokens))
        k_hot_ref[...] = segment_hots(cut_ref, info_ref[part] * BLOCK, kv_ref.shape[1], 1.0, 0.0)

    both = jnp.concatenate([by_head(q_ref[...].T, size), q_low_ref[...]], axis=0)
    raws = dot(jnp.concatenate([kv_ref[0], k_hot_ref[...]], axis=1), both)
    turned = kv_ref[1].T
    ones = jnp.ones((16, turned.shape[1]), jnp.bfloat16)
    for h in range(2):
        fill_tiles(bias_ref, h, tile_ref.at[h])
    for h in range(2):
        raw = raws[:, h * tokens : (h + 1) * tokens]
        rows = scores_of(info_ref, part, raw, tile_ref.at[h])
        highest = None
        for row in rows:
            top = jnp.max(row, axis=0, keepdims=True)
            highest = top if highest is None else jnp.maximum(highest, top)
        if carried:
            highest = jnp.maximum(highest, state_ref[0, h : h + 1])
        weights = jnp.concatenate([jnp.exp(row - highest).astype(jnp.bfloat16) for row in rows], axis=0)
        mixed = dot(jnp.concatenate([turned[h * size : (h + 1) * size], ones], axis=0), weights)
        mixed, summed = mixed[:size], mixed[size : size + 1]
        if carried:
            shrink = jnp.exp(state_ref[0, h : h + 1] - highest)
            summed = summed + state_ref[0, 2 + h : 3 + h] * shrink
            mixed = mixed + before_ref[h * size : (h + 1) * size] * shrink
        if last:
            lse_ref[0, h : h + 1] = highest + jnp.log(summed)
            low.append(mixed * (1.0 / summed))
        else:
            stat_ref[0, h : h + 1] = highest
            stat_ref[0, 2 + h : 3 + h] = summed
            mixed_ref[h * size : (h + 1) * size] = mixed
    if not last:
        return
    features = stream_ref.shape[1]
    turned = jnp.concatenate(low, axis=0)
    att_ref[...] = turned
    plain_ref[step] = turned.T.astype(jnp.bfloat16)
    copies = [
        pltpu.make_async_copy(wm_ref, weight_ref, sems.at[0]),
        pltpu.make_async_copy(stream_ref, resid_ref, sems.at[1]),
    ]

    @pl.when(step == 0)
    def _():
        for copy in copies:
            copy.start()

    @pl.when(step == pl.num_programs(0) - 1)
    def _():
        for copy in copies:
            copy.wait()
        attended = jnp.concatenate([plain_ref[p] for p in range(plain_ref.shape[0])], axis=1)
        resid = resid_ref[...] + dot(attended, weight_ref[...])
        resid_ref[...] = resid
        root = lax.rsqrt(jnp.sum(resid * resid, axis=1, keepdims=True) / features + EPS)
        normed_ref[...] = (resid * root * row_of(gain_ref)).astype(jnp.bfloat16)


def attention_forward(name, size, info, q, kv, bias, cuts, carried=(), last=(), carry=()):
    tokens, features = q.shape
    heads = features // size
    pairs = heads // 2
    wide = 2 * size
    whole = lambda shape: pl.BlockSpec(shape, lambda p: (0,) * len(shape))
    by_rows = pl.BlockSpec((wide, tokens), lambda p: (p, 0))
    stat = pl.BlockSpec((1, 8, tokens), lambda p: (p, 0, 0))
    stat_shape = jax.ShapeDtypeStruct((pairs, 8, tokens), jnp.float32)
    ins = [info, q, kv, bias, cuts, *carried, *last]
    in_specs = [
        SMEM,
        pl.BlockSpec((tokens, wide), lambda p: (0, p)),
        pl.BlockSpec((2, kv.shape[1], wide), lambda p: (0, 0, p)),
        pl.BlockSpec((3, 2, BLOCK, BLOCK), lambda p: (0, p, 0, 0)),
        SMEM,
    ]
    if carried:
        in_specs += [by_rows, stat]
    if last:
        stream, wm, gain = last
        in_specs += [
            HBM,
            HBM,
            whole(gain.shape),
        ]
        shapes = [
            jax.ShapeDtypeStruct((features, tokens), jnp.float32),
            stat_shape,
            jax.ShapeDtypeStruct((tokens, features), jnp.float32),
            jax.ShapeDtypeStruct((tokens, features), jnp.bfloat16),
        ]
        out_specs = [by_rows, stat, whole((tokens, features)), whole((tokens, features))]
    else:
        shapes = [jax.ShapeDtypeStruct((features, tokens), jnp.float32), stat_shape]
        out_specs = [by_rows, stat]
    merging = [
        pltpu.VMEM((pairs, tokens, wide), jnp.bfloat16),
        pltpu.VMEM((features, features), jnp.bfloat16),
        pltpu.SemaphoreType.DMA((2,)),
    ]
    kernel = functools.partial(attention_kernel, size, int(bool(carried)), bool(last))
    made = len(shapes)

    def body(*refs):
        rest = refs[len(ins) + len(carry) :]
        kernel(*refs[: len(ins)], *rest[:made], *rest[made + len(carry) :])

    results = pl.pallas_call(
        body,
        grid=(pairs,),
        out_shape=[*shapes, *[jax.ShapeDtypeStruct(x.shape, x.dtype) for x in carry]],
        in_specs=in_specs + [ANY] * len(carry),
        out_specs=[*out_specs, *[ANY] * len(carry)],
        input_output_aliases={len(ins) + i: made + i for i in range(len(carry))},
        scratch_shapes=[
            pltpu.VMEM((2, 2 * FAR + 1, BLOCK, BLOCK), jnp.float32),
            pltpu.VMEM((LANES, 2 * tokens), jnp.bfloat16),
            pltpu.VMEM((kv.shape[1], LANES), jnp.bfloat16),
            *(merging if last else []),
        ],
        compiler_params=params(12),
        cost_estimate=cost(9),
        name=name,
    )(*ins, *carry)
    return results[:made], results[made:]


def diagonal_sums(tile_ref, sums_ref):
    wide = 2 * BLOCK
    row = lax.broadcasted_iota(jnp.int32, (BLOCK, BLOCK), 0)
    column = lax.broadcasted_iota(jnp.int32, (BLOCK, BLOCK), 1)
    flip = jnp.where(row + column == BLOCK - 1, 1.0, 0.0).astype(jnp.bfloat16)
    near = jnp.concatenate([tile_ref[h, 1 + delta] for h in range(2) for delta in range(3)], axis=1)
    high = near.astype(jnp.bfloat16)
    rest = (near - high.astype(jnp.float32)).astype(jnp.bfloat16)
    flipped = dot(flip, high) + dot(flip, rest)
    empty = jnp.zeros((BLOCK, BLOCK), jnp.float32)
    for h in range(2):
        for delta in range(3):
            start = (3 * h + delta) * BLOCK
            padded = jnp.concatenate([flipped[:, start : start + BLOCK], empty], axis=1)
            slid = pltpu.roll(padded, 0, 1, stride=1, stride_axis=0)
            place = 5 * h + 1 + delta
            sums_ref[0, place : place + 1] = jnp.sum(slid, axis=0, keepdims=True)
        for far in (0, 2 * FAR):
            place = 5 * h + far
            total = jnp.sum(tile_ref[h, far], axis=0, keepdims=True)
            sums_ref[0, place : place + 1] = jnp.concatenate([total, empty[:1]], axis=1)


def attention_back_kernel(
    parts,
    size,
    info_ref,
    q_ref,
    g_ref,
    *refs,
):
    kv_refs = refs[:parts]
    bias_ref, cut_ref, lse_ref, att_ref = refs[parts : parts + 4]
    dq_ref, *dkv_refs, sums_ref, bias_tile_ref, tile_ref = refs[-4 - 2 * parts : len(refs) - parts]
    k_hot_refs = refs[len(refs) - parts :]
    tokens = q_ref.shape[0]
    blocks = tokens // BLOCK
    own = info_ref[3]
    for h in range(2):
        fill_tiles(bias_ref, h, bias_tile_ref.at[h])

    @pl.when(pl.program_id(0) == 0)
    def _():
        lane = lax.broadcasted_iota(jnp.int32, (1, LANES), 1)
        one = jnp.where((lane >= 4) & (lane < 7), 1.0, 0.0).astype(jnp.bfloat16)
        for part in range(parts):
            hots = segment_hots(cut_ref, info_ref[5 + part] * BLOCK, kv_refs[part].shape[1], 1.0, 0.0)
            k_hot_refs[part][...] = hots + one

    q_both = jnp.concatenate([only_head(q_ref[...], h, size) for h in range(2)], axis=0)
    g_both = jnp.concatenate([only_head(g_ref[...], h, size) for h in range(2)], axis=0)
    turned = g_ref[...].T
    logs = [-lse_ref[0, h : h + 1] for h in range(2)]
    q_wide = jnp.concatenate(
        [by_head(q_ref[...].T, size), lower_rows(cut_ref, own * BLOCK, logs, (2, tokens))], axis=0
    )
    g_wide = by_head(turned, size)
    products = turned.astype(jnp.float32) * att_ref[...]
    correction = jnp.concatenate(
        [jnp.sum(products[h * size : (h + 1) * size], axis=0, keepdims=True) for h in range(2)], axis=1
    )
    tile_ref[...] = jnp.zeros_like(tile_ref)
    dq = None
    for part in range(parts):
        base = info_ref[5 + part]
        keys = kv_refs[part].shape[1]
        hots = k_hot_refs[part][...]
        raw = dot(jnp.concatenate([kv_refs[part][0], hots], axis=1), q_wide)
        pull = dot(kv_refs[part][1], g_wide)
        shares, grads, sums = [], [], {}
        for kb in range(keys // BLOCK):
            rows = slice(kb * BLOCK, (kb + 1) * BLOCK)
            tiles = [
                bias_tile_ref[h, jnp.clip(base + kb - own - qb, -FAR, FAR) + FAR]
                for h in range(2)
                for qb in range(blocks)
            ]
            probs = jnp.exp(raw[rows] + jnp.concatenate(tiles, axis=1))
            grad = probs * (pull[rows] - correction)
            shares.append(probs.astype(jnp.bfloat16))
            grads.append(grad.astype(jnp.bfloat16))
            for h in range(2):
                for qb in range(blocks):
                    start = (h * blocks + qb) * BLOCK
                    here = grad[:, start : start + BLOCK]
                    key = (h, kb - qb)
                    sums[key] = sums[key] + here if key in sums else here
        for (h, delta), tile in sums.items():
            place = jnp.clip(base - own + delta, -FAR, FAR) + FAR
            tile_ref[h, place] += tile
        shares = jnp.concatenate(shares, axis=0)
        grads = jnp.concatenate(grads, axis=0)
        dkv_refs[part][0] = dot(grads, q_both).astype(jnp.bfloat16)
        dkv_refs[part][1] = dot(shares, g_both).astype(jnp.bfloat16)
        term = dot(kv_refs[part][0].T, grads)
        dq = term if dq is None else dq + term
    dq = jnp.concatenate([dq[:size, :tokens], dq[size:, tokens:]], axis=0)
    dq_ref[...] = dq.T.astype(jnp.bfloat16)
    diagonal_sums(tile_ref, sums_ref)


def attention_backward(size, info, q, g, kvs, bias, cuts, lse, att, after):
    tokens, features = q.shape
    pairs = features // size // 2
    parts = len(kvs)
    wide = 2 * size
    by_pair = [pl.BlockSpec((2, x.shape[1], wide), lambda p: (0, 0, p)) for x in kvs]
    own = pl.BlockSpec((tokens, wide), lambda p: (0, p))
    sums = pl.BlockSpec((1, 16, 2 * BLOCK), lambda p: (p, 0, 0))
    tiles = pltpu.VMEM((2, 2 * FAR + 1, BLOCK, BLOCK), jnp.float32)
    shapes = [jax.ShapeDtypeStruct(x.shape, jnp.bfloat16) for x in kvs]
    if parts > 1:
        shapes[0] = pltpu.HBM(kvs[0].shape, jnp.bfloat16)
    result = pl.pallas_call(
        functools.partial(attention_back_kernel, parts, size),
        grid=(pairs,),
        out_shape=[pltpu.HBM(q.shape, jnp.bfloat16), *shapes]
        + [jax.ShapeDtypeStruct((pairs, 16, 2 * BLOCK), jnp.float32)],
        in_specs=[
            SMEM,
            own,
            own,
            *by_pair,
            pl.BlockSpec((3, 2, BLOCK, BLOCK), lambda p: (0, p, 0, 0)),
            SMEM,
            pl.BlockSpec((1, 8, tokens), lambda p: (p, 0, 0)),
            pl.BlockSpec((wide, tokens), lambda p: (p, 0)),
            *[ANY] * len(after),
        ],
        out_specs=[own, *by_pair, sums],
        scratch_shapes=[
            tiles,
            tiles,
            *[pltpu.VMEM((x.shape[1], LANES), jnp.bfloat16) for x in kvs],
        ],
        compiler_params=params(18),
        cost_estimate=cost(20),
        name="attention_backward",
    )(info, q, g, *kvs, bias, cuts, lse, att, *after)
    return result[0], result[1 : 1 + parts], result[-1]


def bucket_kernel(sums_ref, out_ref):
    pairs = sums_ref.shape[0]
    wide = 2 * BLOCK
    spot = lax.broadcasted_iota(jnp.int32, (wide, LANES), 1)
    entry = lax.broadcasted_iota(jnp.int32, (wide, LANES), 0)
    gap = entry - (BLOCK - 1)
    total = None
    for delta in range(5):
        if delta in (0, 2 * FAR):
            hot = jnp.where(spot == (15 if delta == 0 else 31), 1.0, 0.0)
        else:
            hot = jnp.where(spot == bucket_of((delta - FAR) * BLOCK - gap), 1.0, 0.0)
        hot = hot.astype(jnp.bfloat16)
        rows = [sums_ref[p, 5 * h + delta : 5 * h + delta + 1] for p in range(pairs) for h in range(2)]
        rows = jnp.concatenate(rows, axis=0)
        for part in split_three(rows):
            here = dot(part, hot)
            total = here if total is None else total + here
    out_ref[...] = total


def bucket_sums(sums, after):
    outs, _ = launch(
        "bucket_sums",
        bucket_kernel,
        [sums],
        [VMEM],
        [jax.ShapeDtypeStruct((2 * sums.shape[0], LANES), jnp.float32)],
        [VMEM],
        4,
        after=after,
    )
    return outs[0]


def relative_rows(me, count, src_ref, dst_ref):
    size = src_ref.shape[0] // count
    for place in range(count):
        r = 2 * (place % (count // 2)) + place // (count // 2)
        start = pl.multiple_of((me ^ r) * size, 16)
        dst_ref[place * size : (place + 1) * size] = src_ref[pl.ds(start, size), :]


def feed_kernel(
    held,
    count,
    half,
    info_ref,
    normed_ref,
    *refs,
):
    if half == 0:
        cot_refs = refs[:held]
        (
            resid_ref,
            wg_ref,
            wu_ref,
            wd_ref,
            acc_ref,
            grad_ref,
            keep_ref,
            send_ref,
            cot_ref,
            cot_turned_ref,
            normed_turned_ref,
            turned_ref,
        ) = refs[held:]
        grad_in_ref = None
    else:
        (
            resid_ref,
            grad_in_ref,
            cot_ref,
            cot_turned_ref,
            normed_turned_ref,
            wg_ref,
            wu_ref,
            wd_ref,
            *out_refs,
            grad_ref,
            keep_ref,
            send_ref,
            acc_ref,
        ) = refs
    step = pl.program_id(0)
    core = info_ref[1]
    if half == 0:
        span = cot_refs[0].shape[0]

        @pl.when(step == 0)
        def _():
            for phase in range(held):
                start = pl.multiple_of(lax.rem(info_ref[2] + held - phase, held) * span, span)
                cot_ref[pl.ds(start, span), :] = cot_refs[phase][...]
            cot_turned_ref[...] = cot_ref[...].T
            turned_ref[...] = normed_ref[...].T
            relative_rows(info_ref[0], count, turned_ref, normed_turned_ref)

    normed, cot = normed_ref[...], cot_ref[...]
    gate = dot(normed, wg_ref[...])
    up_value = dot(normed, wu_ref[...])
    grad_hidden = dot_nt(cot, wd_ref[...])
    square = gate * gate
    bend = jnp.tanh(gate * (SLOPE + (SLOPE * CUBE) * square))
    middle = 0.5 + 0.5 * bend
    gelu = gate * middle
    slope = middle * (1.0 + (1.0 - bend) * (gate * (SLOPE + (3.0 * SLOPE * CUBE) * square)))
    hidden = (gelu * up_value).astype(jnp.bfloat16)
    grad_gate = (grad_hidden * up_value * slope).astype(jnp.bfloat16)
    grad_up = (grad_hidden * gelu).astype(jnp.bfloat16)
    rb, cb = keep_ref.shape[-2:]
    chips = count // 2
    half_rows = chips * rb
    turned = normed_turned_ref[...]
    for kind, grad in enumerate((grad_gate, grad_up)):
        part = dot(turned, grad).astype(jnp.bfloat16)
        for e in range(2):
            columns = part[:, e * cb : (e + 1) * cb]
            tiles = slice((2 * kind + e) * chips, (2 * kind + e + 1) * chips)
            keep_ref[0, tiles] = columns[:half_rows].reshape(chips, rb, cb)
            send_ref[0, tiles] = columns[half_rows:].reshape(chips, rb, cb)
    part = dot(cot_turned_ref[...], hidden)
    first, second = part[:, :cb], part[:, cb:]
    mine = core == 0
    keep = jnp.where(mine, first, second).astype(jnp.bfloat16)
    send = jnp.where(mine, second, first).astype(jnp.bfloat16)
    keep_ref[0, 4 * chips :] = keep.reshape(count, rb, cb)
    send_ref[0, 4 * chips :] = send.reshape(count, rb, cb)
    result = dot(hidden, wd_ref[...])
    back = dot_nt(grad_gate, wg_ref[...]) + dot_nt(grad_up, wu_ref[...])

    @pl.when(step == 0)
    def _():
        acc_ref[...] = resid_ref[...] + result
        grad_ref[...] = back if grad_in_ref is None else grad_in_ref[...] + back

    @pl.when(step > 0)
    def _():
        acc_ref[...] += result
        grad_ref[...] += back

    if half == 1:

        @pl.when(step == pl.num_programs(0) - 1)
        def _():
            span = out_refs[0].shape[0]
            for phase in range(held):
                start = pl.multiple_of(lax.rem(info_ref[2] + held - phase, held) * span, span)
                out_refs[phase][...] = acc_ref[pl.ds(start, span), :].astype(jnp.bfloat16)


def feed_forward(half, info, normed, ins, wg, wu, wd, held, count):
    tokens, features = normed.shape
    width = wg.shape[1]
    chips = count // 2
    steps = chips // 2
    rb, cb = features // count, width // count
    whole = lambda shape: pl.BlockSpec(shape, lambda j, info: (0,) * len(shape))
    low = jnp.bfloat16
    slab = (4 * chips + count, rb, cb)
    tiles = jax.ShapeDtypeStruct((steps,) + slab, low)
    tile_spec = pl.BlockSpec((1,) + slab, lambda j, info: (j, 0, 0, 0))
    natural, turned = (tokens, features), (features, tokens)
    full = jax.ShapeDtypeStruct(natural, jnp.float32)
    shapes = [full, tiles, tiles]
    specs = [whole(natural), tile_spec, tile_spec]
    if half == 0:
        shapes, specs = [full] + shapes, [whole(natural)] + specs
    else:
        span = (tokens // held, features)
        shapes = [jax.ShapeDtypeStruct(span, low)] * held + shapes
        specs = [whole(span)] * held + specs
    scratch = [pltpu.VMEM(natural, jnp.float32)]
    if half == 0:
        shapes += [
            jax.ShapeDtypeStruct(natural, low),
            jax.ShapeDtypeStruct(turned, low),
            jax.ShapeDtypeStruct(turned, low),
        ]
        specs += [whole(natural), whole(turned), whole(turned)]
        scratch = [pltpu.VMEM(turned, low)]
    return pl.pallas_call(
        functools.partial(feed_kernel, held, count, half),
        grid_spec=pltpu.PrefetchScalarGridSpec(
            num_scalar_prefetch=1,
            grid=(steps,),
            in_specs=[
                whole(normed.shape),
                *[whole(x.shape) for x in ins],
                pl.BlockSpec((features, 2 * cb), lambda j, info: (0, j + half * steps)),
                pl.BlockSpec((features, 2 * cb), lambda j, info: (0, j + half * steps)),
                pl.BlockSpec((2 * cb, features), lambda j, info: (j + half * steps, 0)),
            ],
            out_specs=specs,
            scratch_shapes=scratch,
        ),
        out_shape=shapes,
        compiler_params=params(28),
        cost_estimate=cost(11),
        name=f"feed_forward_{half}",
    )(info, normed, *ins, wg, wu, wd)


def between_kernel(
    count,
    info_ref,
    grad_ref,
    resid_ref,
    gain_ref,
    cot_ref,
    att_ref,
    wm_ref,
    *refs,
):
    (
        out_hbm_ref,
        att_grad_ref,
        keep_hbm_ref,
        send_ref,
        gain_grad_ref,
        turned_ref,
        low_ref,
        out_ref,
        keep_ref,
        sems,
    ) = refs[-10:]
    features = resid_ref.shape[1]
    resid = resid_ref[...]
    root = lax.rsqrt(jnp.sum(resid * resid, axis=1, keepdims=True) / features + EPS)
    grad = grad_ref[...]
    unit = resid * root
    gain_grad_ref[...] = jnp.sum(grad * unit, axis=0, keepdims=True)
    pulled = grad * row_of(gain_ref)
    mean = jnp.sum(unit * pulled, axis=1, keepdims=True) / features
    result = cot_ref[...].astype(jnp.float32) + root * (pulled - unit * mean)
    out_ref[...] = result
    copies = [
        pltpu.make_async_copy(out_ref, out_hbm_ref, sems.at[0]),
        pltpu.make_async_copy(keep_ref, keep_hbm_ref, sems.at[1]),
    ]
    copies[0].start()
    mixed = result.astype(jnp.bfloat16)
    low_ref[...] = att_ref[...].astype(jnp.bfloat16)
    relative_rows(info_ref[0], count, low_ref, turned_ref)
    part = dot(turned_ref[...], mixed).astype(jnp.bfloat16)
    half = features // 2
    keep_ref[...] = part[:half].reshape(keep_ref.shape)
    copies[1].start()
    send_ref[...] = part[half:].reshape(send_ref.shape)
    att_grad_ref[...] = dot_nt(mixed, wm_ref[...]).astype(jnp.bfloat16)
    for copy in copies:
        copy.wait()


def between(info, grad, resid, gain, cot, att, wm, count, after, carry):
    tokens, features = grad.shape
    rb = features // count
    low = jnp.bfloat16
    piece = jax.ShapeDtypeStruct((count // 2, rb, features), low)
    ins = [info, grad, resid, gain, cot, att, wm]
    return launch(
        "between",
        functools.partial(between_kernel, count),
        ins,
        [SMEM] + [VMEM] * 6,
        [
            pltpu.HBM((tokens, features), jnp.float32),
            jax.ShapeDtypeStruct((tokens, features), low),
            pltpu.HBM(piece.shape, low),
            piece,
            jax.ShapeDtypeStruct((1, features), jnp.float32),
        ],
        [HBM, VMEM, HBM, VMEM, VMEM],
        16,
        [
            pltpu.VMEM((features, tokens), low),
            pltpu.VMEM((features, tokens), low),
            pltpu.VMEM((tokens, features), jnp.float32),
            pltpu.VMEM(piece.shape, low),
            pltpu.SemaphoreType.DMA((2,)),
        ],
        after=after,
        carry=carry,
        microseconds=3,
    )


def project_q_kernel(
    count,
    info_ref,
    dq_ref,
    normed_ref,
    wq_ref,
    other_ref,
    keep_ref,
    send_ref,
    back_ref,
    turned_ref,
    plain_ref,
):
    plain_ref[...] = normed_ref[...].T
    relative_rows(info_ref[0], count, plain_ref, turned_ref)
    dq = dq_ref[...]
    part = dot(turned_ref[...], dq).astype(jnp.bfloat16)
    half = part.shape[0] // 2
    keep_ref[...] = part[:half].reshape(keep_ref.shape)
    send_ref[0] = part[half:].reshape(send_ref.shape[1:])
    send_ref[1] = other_ref[...]
    back_ref[...] = dot_nt(dq, wq_ref[...])


def project_q(info, dq, normed, wq, other, count, after, carry):
    tokens, features = dq.shape
    low = jnp.bfloat16
    piece = jax.ShapeDtypeStruct((count // 2, features // count, features), low)
    return launch(
        "project_q",
        functools.partial(project_q_kernel, count),
        [info, dq, normed, wq, other],
        [SMEM] + [VMEM] * 4,
        [
            piece,
            jax.ShapeDtypeStruct((2,) + piece.shape, low),
            jax.ShapeDtypeStruct((tokens, features), jnp.float32),
            jax.ShapeDtypeStruct((features, tokens), low),
        ],
        [VMEM] * 4,
        14,
        [pltpu.VMEM((features, tokens), low)],
        after=after,
        carry=carry,
    )


def project_kv_kernel(
    mine_ref,
    got_ref,
    turned_ref,
    back_ref,
    stream_ref,
    grad_ref,
    gain_ref,
    wk_ref,
    wv_ref,
    keep_ref,
    send_ref,
    out_ref,
    gain_grad_ref,
):
    features = stream_ref.shape[1]
    half = features // 2
    total = back_ref[...]
    for i, w_ref in enumerate((wk_ref, wv_ref)):
        grad = mine_ref[i] + got_ref[i]
        part = dot(turned_ref[...], grad).astype(jnp.bfloat16)
        keep_ref[i] = part[:half].reshape(keep_ref.shape[1:])
        send_ref[i] = part[half:].reshape(send_ref.shape[1:])
        total = total + dot_nt(grad, w_ref[...])
    stream = stream_ref[...]
    root = lax.rsqrt(jnp.sum(stream * stream, axis=1, keepdims=True) / features + EPS)
    unit = stream * root
    gain_grad_ref[...] = jnp.sum(total * unit, axis=0, keepdims=True)
    pulled = total * row_of(gain_ref)
    mean = jnp.sum(unit * pulled, axis=1, keepdims=True) / features
    out_ref[...] = grad_ref[...] + root * (pulled - unit * mean)


def project_kv(mine, got, turned, back, stream, grad, gain, wk, wv, count, after):
    tokens, features = stream.shape
    piece = jax.ShapeDtypeStruct((2, count // 2, features // count, features), jnp.bfloat16)
    outs, _ = launch(
        "project_kv",
        project_kv_kernel,
        [mine, got, turned, back, stream, grad, gain, wk, wv],
        [VMEM] * 9,
        [piece] * 2
        + [
            jax.ShapeDtypeStruct((tokens, features), jnp.float32),
            jax.ShapeDtypeStruct((1, features), jnp.float32),
        ],
        [VMEM] * 4,
        18,
        after=after,
    )
    return outs


def pick_of(pairs, info_ref):
    def tile(pair, at):
        if callable(at):
            at = at(info_ref)
        first, second = at if isinstance(at, tuple) else (at, at)
        return pairs[pair][0][first] + pairs[pair][1][second]

    def value(pick):
        if len(pick) == 2:
            return tile(*pick)
        return jnp.where(info_ref[7] == 0, tile(*pick[:2]), tile(*pick[2:]))

    return value


def tiles_of(pairs):
    return [tuple(x.reshape((-1,) + x.shape[-2:]) for x in pair) for pair in pairs]


def fold(name, info, pairs, picks, after=(), carry=()):
    pairs = tiles_of(pairs)
    shape = pairs[0][0].shape[1:]

    def kernel(info_ref, *refs):
        ins, outs = refs[: 2 * len(pairs)], refs[2 * len(pairs) :]
        value = pick_of([ins[2 * i : 2 * i + 2] for i in range(len(pairs))], info_ref)
        for out_ref, chosen in zip(outs, picks):
            for slot, pick in enumerate(chosen):
                out_ref[slot] = value(pick)

    return launch(
        name,
        kernel,
        [info, *sum(pairs, ())],
        [SMEM] + [VMEM] * (2 * len(pairs)),
        [jax.ShapeDtypeStruct((len(chosen),) + shape, jnp.bfloat16) for chosen in picks],
        [VMEM] * len(picks),
        16,
        after=after,
        carry=carry,
    )


def lane_tiles(width):
    whole = width // LANES
    rest = width - whole * LANES
    return whole, rest, LANES // rest if rest else 1


def tile_count(pieces, width):
    whole, rest, each = lane_tiles(width)
    return pieces * whole + (-(-pieces // each) if rest else 0)


def pack_lanes(pieces):
    width = pieces[0].shape[1]
    whole, rest, each = lane_tiles(width)
    tiles = [piece[:, i * LANES : (i + 1) * LANES] for piece in pieces for i in range(whole)]
    if rest:
        ends = [piece[:, whole * LANES :] for piece in pieces]
        for i in range(0, len(ends), each):
            group = ends[i : i + each]
            spare = LANES - rest * len(group)
            if spare:
                group = group + [jnp.zeros((group[0].shape[0], spare), group[0].dtype)]
            tiles.append(jnp.concatenate(group, axis=1))
    return tiles


def unpack_lanes(tiles, pieces, width):
    whole, rest, each = lane_tiles(width)
    result = []
    for piece in range(pieces):
        parts = [tiles[piece * whole + i] for i in range(whole)]
        if rest:
            tile = tiles[pieces * whole + piece // each]
            start = piece % each * rest
            parts.append(tile[:, start : start + rest])
        result.append(jnp.concatenate(parts, axis=1) if len(parts) > 1 else parts[0])
    return result


def fold_seq(name, info, pairs, picks, seqs, slots, groups, width=None, after=(), carry=()):
    pairs = tiles_of(pairs)
    tall, wide = pairs[0][0].shape[1:]
    shape = (tall, LANES if width else wide)

    def kernel(info_ref, *refs):
        ins, outs, scratch_ref = refs[: 2 * len(pairs)], refs[2 * len(pairs) : -1], refs[-1]
        value = pick_of([ins[2 * i : 2 * i + 2] for i in range(len(pairs))], info_ref)
        here = info_ref[8]
        if width is None:
            for pick, block, slot in picks:
                scratch_ref[block ^ here, slot] = value(pick)
        else:
            totals = [value(pick) for pick, _, _ in sorted(picks, key=lambda x: x[2])]
            for s in range(seqs):
                pieces = [total[:, s * width : (s + 1) * width] for total in totals]
                for slot, tile in enumerate(pack_lanes(pieces)):
                    scratch_ref[s ^ here, slot] = tile
        for out_ref, group in zip(outs, groups):
            for i, d in enumerate(group):
                out_ref[i * slots : (i + 1) * slots] = scratch_ref[d]

    return launch(
        name,
        kernel,
        [info, *sum(pairs, ())],
        [SMEM] + [VMEM] * (2 * len(pairs)),
        [jax.ShapeDtypeStruct((len(group) * slots,) + shape, jnp.bfloat16) for group in groups],
        [VMEM] * len(groups),
        16,
        [pltpu.VMEM((seqs, slots) + shape, jnp.bfloat16)],
        after=after,
        carry=carry,
    )


def summed(refs, at):
    terms = [ref[at].astype(jnp.float32) for ref in refs]
    while len(terms) > 1:
        terms = [terms[i] + terms[i + 1] for i in range(0, len(terms), 2)]
    return terms[0]


def feed_end_kernel(seqs, *refs):
    ins, (gate_ref, up_ref, down_ref) = refs[:seqs], refs[seqs:]
    slots, rb, cb = ins[0].shape
    each = slots // 3
    for q in range(each):
        gate_ref[:, q * cb : (q + 1) * cb] = summed(ins, q)
        up_ref[:, q * cb : (q + 1) * cb] = summed(ins, each + q)
    for q in range(each):
        down_ref[q * rb : (q + 1) * rb] = summed(ins, 2 * each + q)


def feed_end(ins, after):
    slots, rb, cb = ins[0].shape
    each = slots // 3
    wide = pltpu.HBM((rb, each * cb), jnp.float32)
    return pl.pallas_call(
        ordered(functools.partial(feed_end_kernel, len(ins)), len(ins), after),
        out_shape=[wide, wide, pltpu.HBM((each * rb, cb), jnp.float32)],
        in_specs=[VMEM] * len(ins) + [ANY] * len(after),
        out_specs=[AUTO] * 3,
        compiler_params=params(8),
        cost_estimate=cost(1),
        name="feed_end",
    )(*ins, *after)


def join_kernel(info_ref, *refs):
    held = len(refs) - 1
    for phase in range(held):
        refs[held][lax.rem(info_ref[8] + phase, held)] = refs[phase][...]


def join(info, parts, after):
    shape = (len(parts),) + parts[0].shape
    outs, _ = launch(
        "join",
        join_kernel,
        [info, *parts],
        [SMEM] + [VMEM] * len(parts),
        [pltpu.HBM(shape, parts[0].dtype)],
        [AUTO],
        8,
        after=after,
    )
    return outs[0]


def mix_end_kernel(width, seqs, *refs):
    outs = refs[seqs:]
    tiles = [summed(refs[:seqs], slot) for slot in range(refs[0].shape[0])]
    for out_ref, value in zip(outs, unpack_lanes(tiles, len(outs), width)):
        out_ref[...] = value


def mix_end(ins, pieces, width, after):
    outs, _ = launch(
        "mix_end",
        functools.partial(mix_end_kernel, width, len(ins)),
        ins,
        [VMEM] * len(ins),
        [pltpu.HBM((ins[0].shape[1], width), jnp.float32)] * pieces,
        [AUTO] * pieces,
        8,
        after=after,
    )
    return outs


def sum_kernel(count, *refs):
    refs[count][...] = summed(refs[:count], slice(None)).astype(jnp.bfloat16)


def sum_of(name, terms, after):
    return pl.pallas_call(
        ordered(functools.partial(sum_kernel, len(terms)), len(terms), after),
        out_shape=jax.ShapeDtypeStruct(terms[0].shape, jnp.bfloat16),
        in_specs=[VMEM] * len(terms) + [ANY] * len(after),
        out_specs=VMEM,
        compiler_params=params(8),
        cost_estimate=cost(1),
        name=name,
    )(*terms, *after)


def unpack_kernel(vocab, chips, info_ref, *refs):
    shares = refs[: 2 * chips]
    embed_ref, filter_ref, score_ref, first_ref, second_ref, bias_ref, whole_ref = refs[2 * chips :]
    share = shares[0].shape[1]
    me = info_ref[0]
    for place in range(chips):
        for odd in range(2):
            start = pl.multiple_of((me ^ (2 * place + odd)) * share, 16)
            whole_ref[pl.ds(start, share), :] = shares[odd * chips + place][0].astype(jnp.float32)
    embed_ref[...] = whole_ref[:vocab]
    filter_ref[...] = whole_ref[vocab : vocab + 4]
    for i, ref in enumerate((score_ref, first_ref, second_ref)):
        ref[...] = whole_ref[vocab + 4 + i, :]
    heads, buckets = bias_ref.shape
    bias_ref[...] = whole_ref[vocab + 7 : vocab + 7 + heads, :buckets]


def unpack(info, mine, others, vocab, buckets, heads, after):
    chips = len(mine)
    _, share, features = mine[0].shape
    full = lambda *shape: pltpu.HBM(shape, jnp.float32)
    return pl.pallas_call(
        ordered(functools.partial(unpack_kernel, vocab, chips), 1 + 2 * chips, after),
        out_shape=[
            full(vocab, features),
            full(4, features),
            full(features),
            full(features),
            full(features),
            full(heads, buckets),
        ],
        in_specs=[SMEM] + [VMEM] * (2 * chips) + [ANY] * len(after),
        out_specs=[AUTO] * 6,
        scratch_shapes=[pltpu.VMEM((2 * chips * share, features), jnp.float32)],
        compiler_params=params(8),
        cost_estimate=cost(1),
        name="unpack",
    )(info, *mine, *others, *after)


AXES = ("batch", "seq")


def across_cores(x):
    count = lax.axis_size("batch")
    return lax.ppermute(x, "batch", [(i, i ^ 1) for i in range(count)])


def across_chips(x, chip):
    count = lax.axis_size("batch")
    return lax.ppermute(x, "batch", [(i, i ^ (2 * chip)) for i in range(count)])


def across_seq(x, d):
    count = lax.axis_size("seq")
    return lax.ppermute(x, "seq", [(i, i ^ d) for i in range(count)])


class Halving:
    def __init__(self, pairs, where):
        self.pairs, self.where = pairs, where

    def split(self, chosen, bit):
        keys = [key for key in self.where if chosen(key)]
        keep = [key for key in keys if not key[-1] & (1 << bit)]
        send = [key[:-1] + (key[-1] | (1 << bit),) for key in keep]
        return keep, send

    def picks(self, keys):
        return [self.where[key] for key in keys]


def exchange(name, info, state, plans, after=(), carry=(), held_back=False):
    lists, kept = [], []
    for chosen, bit in plans:
        keep, send = state.split(chosen, bit)
        kept.append(keep)
        lists += [state.picks(keep), state.picks(send)]
    outs, carried = fold(name, info, state.pairs, lists, after, carry)

    def start(sends):
        pairs, where = [], {}
        for place, ((_, bit), keep) in enumerate(zip(plans, kept)):
            pairs.append((outs[2 * place], across_chips(sends[place], 1 << bit)))
            where.update({key: (place, slot) for slot, key in enumerate(keep)})
        return Halving(pairs, where)

    return start if held_back else start(outs[1::2]), outs, carried


class Plan:
    def __init__(self, held):
        self.count = lax.axis_size("batch")
        self.seqs = lax.axis_size("seq")
        self.held = held
        self.group = self.seqs // (2 * held)
        me = lax.axis_index("batch")
        place = lax.axis_index("seq")
        self.me, self.place = me, place
        self.core = me % 2
        self.row = place // self.group
        self.part = 2 * (place % self.group) + self.core
        self.parts = 2 * self.group
        self.perms = []
        for phase in range(held):
            perm = []
            for b in range(self.count):
                for s in range(self.seqs):
                    row = held * (b % 2) + (s + phase) % held
                    part = s // held
                    target = (b - b % 2 + part % 2, self.group * row + part // 2)
                    perm.append((b * self.seqs + s, target[0] * self.seqs + target[1]))
            self.perms.append(perm)

    def blocks_of(self, x):
        return [
            lax.dynamic_index_in_dim(x, (self.place + phase) % self.held, 0, keepdims=False)
            for phase in range(self.held)
        ]

    def parts_of(self, x):
        return [lax.ppermute(x, AXES, perm) for x, perm in zip(self.blocks_of(x), self.perms)]

    def bytes_of(self, x):
        held = self.held
        main = self.parts_of(x)
        ends = jnp.concatenate([x[:, :4], x[:, -4:]], axis=1)
        sides = []
        for phase in range(held):
            perm = []
            for b in range(self.count):
                for s in range(self.seqs):
                    row = held * (b % 2) + (s + phase) % held
                    part = s // held + {0: -1, held - 1: 1}.get(s % held, self.parts)
                    if 0 <= part < self.parts:
                        target = (b - b % 2 + part % 2, self.group * row + part // 2)
                        perm.append((b * self.seqs + s, target[0] * self.seqs + target[1]))
            send = lax.dynamic_index_in_dim(ends, (self.place + phase) % held, 0, keepdims=False)
            sides.append(lax.ppermute(send, AXES, perm))
        low = lax.dynamic_index_in_dim(
            jnp.stack(sides), (self.row + 1) % held, 0, keepdims=False
        )[4:]
        high = lax.dynamic_index_in_dim(jnp.stack(sides), self.row % held, 0, keepdims=False)[:4]
        low = jnp.where(self.part > 0, low, -1)
        high = jnp.where(self.part < self.parts - 1, high, -1)
        order = (self.row - jnp.arange(held)) % held
        middle = jnp.take(jnp.stack(main), order, axis=0).reshape(-1)
        return jnp.concatenate([low, middle, high]).reshape(-1, 4)

    def gather(self, x):
        other = across_cores(x)
        pair = jnp.stack([jnp.where(self.core == 0, x, other), jnp.where(self.core == 0, other, x)])
        if self.group > 1:
            groups = [
                list(range(first, first + self.group))
                for first in range(0, self.seqs, self.group)
            ]
            pair = lax.all_gather(pair, "seq", axis_index_groups=groups)
        return pair.reshape((-1,) + x.shape[1:])

    def scatter(self, x):
        if self.group > 1:
            groups = [
                list(range(first, first + self.group))
                for first in range(0, self.seqs, self.group)
            ]
            x = lax.psum_scatter(
                x, "seq", scatter_dimension=0, axis_index_groups=groups, tiled=True
            )
        pair = x.reshape((2, -1) + x.shape[1:])
        got = across_cores(lax.dynamic_index_in_dim(pair, 1 - self.core, 0, keepdims=False))
        mine = lax.dynamic_index_in_dim(pair, self.core, 0, keepdims=False)
        return mine.astype(jnp.float32) + got.astype(jnp.float32)


def shards(
    byte_values,
    segments,
    byte_mask,
    embedding,
    filter_weight,
    score_weight,
    first_gain,
    query_weight,
    key_weight,
    value_weight,
    merge_weight,
    position_bias,
    second_gain,
    gate_weight,
    up_weight,
    down_weight,
    cotangent,
):
    count = lax.axis_size("batch")
    seqs = lax.axis_size("seq")
    held, width = byte_values.shape
    row_len = segments.shape[1]
    vocab, features = embedding.shape
    hidden_size = gate_weight.shape[1]
    heads = position_bias.shape[1]
    bucket_count = position_bias.shape[0]
    total = row_len // 2
    plan = Plan(held)
    tokens = total // plan.parts
    chips = count // 2
    levels = chips.bit_length() - 1
    blocks = tokens // BLOCK
    other_part = plan.part ^ 1

    bases = [plan.part * blocks, other_part * blocks] if plan.group == 1 else [0, 0]
    info = jnp.stack(
        [
            jnp.asarray(value, jnp.int32)
            for value in (
                plan.me,
                plan.core,
                plan.row % held,
                plan.part * blocks,
                plan.part * 2 * tokens,
                bases[0],
                bases[1],
                plan.me // chips,
                plan.place,
            )
        ]
    )
    ids = plan.bytes_of(jnp.where(byte_mask > 0, byte_values, -1))
    ids = jnp.pad(ids, ((MAIN - 1, MAIN - 1), (0, 0)), constant_values=-1)
    cuts = jnp.sum((segments[:, :, None] < jnp.arange(1, 4)).astype(jnp.int32), axis=1)
    cuts = (cuts + 1) // 2
    both = jnp.concatenate([cuts, across_cores(cuts)])
    own_first = jnp.where(plan.row // held == plan.core, 0, held)
    cuts = lax.dynamic_index_in_dim(both, own_first + plan.row % held, 0, keepdims=False)
    embedding, filter_weight, score_weight = map(hbm, (embedding, filter_weight, score_weight))
    first_gain, second_gain = hbm(first_gain), hbm(second_gain)
    query_weight, key_weight, value_weight = map(hbm, (query_weight, key_weight, value_weight))
    merge_weight = hbm(merge_weight)
    head_size = features // heads
    words = -(-(vocab + 7 + heads) // (16 * count)) * (16 * count)
    stream, normed, q, kv = mixer_forward(
        info,
        ids,
        embedding,
        filter_weight,
        score_weight,
        first_gain,
        query_weight,
        key_weight,
        value_weight,
        tokens,
        row_len,
        [],
    )
    normed, stream = hbm(normed), hbm(stream)
    cot_blocks = plan.blocks_of(cotangent)
    cots = [lax.ppermute(cot_blocks[0], AXES, plan.perms[0])]
    (bias,), (kv,) = bias_tiles(position_bias.T, [*cots, cuts], [kv])
    bias = hbm(bias)
    ends = (stream, merge_weight, second_gain)
    if plan.group == 1:
        kvs = [kv, across_cores(kv)]
        begun, later = attention_forward(
            "attention_own", head_size, info, q, kvs[0], bias, cuts, carry=cot_blocks[1:]
        )
        (att, lse, resid, normed_two), _ = attention_forward(
            "attention_other", head_size, info, q, kvs[1], bias, cuts, begun, ends
        )
    else:
        kvs = [jnp.stack([plan.gather(kv[0]), plan.gather(kv[1])])]
        later = cot_blocks[1:]
        (att, lse, resid, normed_two), _ = attention_forward(
            "attention_all", head_size, info, q, kvs[0], bias, cuts, (), ends
        )
    cots += [lax.ppermute(x, AXES, perm) for x, perm in zip(later, plan.perms[1:])]

    weights = (gate_weight, up_weight, down_weight)
    acc, grad_two, *grads, cot, cot_turned, normed_turned = feed_forward(
        0, info, normed_two, [*cots, resid], *weights, held, count
    )
    halves = [grads]
    *results, grad_two, keep, send = feed_forward(
        1,
        info,
        normed_two,
        [acc, grad_two, cot, cot_turned, normed_turned],
        *weights,
        held,
        count,
    )
    halves.append([keep, send])
    early = count // 4

    def upwards(key):
        return key[0] == "down" or key[3] < early

    def downwards(key):
        return not upwards(key)

    states = []

    def start_half(half, after):
        keep, send = halves[half]
        pairs = [(keep, across_cores(send))]
        steps = chips // 2
        slab = 4 * chips + count
        where = {}
        for r in range(chips):
            for n in range(count):
                kind, block = n // chips, n % chips
                place = block // 2 * slab + (2 * kind + block % 2) * chips + r
                where["gu", half, 0, n, r] = (0, place)

        def down_at(r, n):
            return lambda info: (r ^ lax.rem(info[0] // 2, steps)) * slab + 4 * chips + n

        for r in range(steps):
            for n in range(count):
                where["down", half, 0, n, r] = (0, down_at(r, n))
        state = Halving(pairs, where)
        first = None
        for level in range(levels - 1):
            state, outs, _ = exchange(
                f"feed_{half}_{level}",
                info,
                state,
                [(upwards, level), (downwards, levels - 1 - level)],
                after if level == 0 else (),
            )
            first = first or outs
        states.append(state)
        return first

    back_perms = [[(b, a) for a, b in perm] for perm in plan.perms]
    out_parts = [lax.ppermute(x, AXES, perm) for x, perm in zip(results, back_perms)]
    first = start_half(0, [grad_two])
    (grad_resid, att_grad, m_keep, m_send, second_part), _ = between(
        info, grad_two, resid, second_gain, cot, att, merge_weight, count, [first[0]], []
    )
    first = start_half(1, [second_part])
    dq, dkvs, tiles = attention_backward(
        head_size, info, hbm(q), att_grad, [hbm(kvs[0]), *kvs[1:]], bias, cuts, lse, att, [first[0]]
    )

    where = {}
    for half, state in enumerate(states):
        for key, (pair, slot) in state.where.items():
            where[key] = (2 * half + pair, slot)
    top = 1 << (levels - 1)
    for key in [key for key in where if key[0] == "down"]:
        _, half, kind, n, r = key
        mine, other = where["down", 0, 0, n, 0], where["down", 1, 0, n, 0]
        if half == 0:
            where["one", 2, 0, n, 0] = mine + other
            where["one", 2, 0, n, top] = other + mine
    where = {key: value for key, value in where.items() if key[0] != "down"}
    state = Halving(states[0].pairs + states[1].pairs, where)
    crossing = [dkvs[1]] if plan.group == 1 else []
    state, lasts, crossing = exchange(
        "feed_last",
        info,
        state,
        [
            (lambda key: key[0] == "one" or key[3] < early, levels - 1),
            (lambda key: key[0] == "gu" and key[3] >= early, 0),
        ],
        [hbm(dq), out_parts[0]],
        crossing,
    )
    if plan.group == 1:
        mine, got = hbm(dkvs[0]), across_cores(crossing[0])
    else:
        mine = jnp.stack([plan.scatter(dkvs[0][i]).astype(jnp.bfloat16) for i in range(2)])
        got = jnp.zeros_like(mine)
    bias_part = bucket_sums(tiles, [lasts[0]])
    (q_keep, qm_send, back, turned), later = project_q(
        info, hbm(dq), normed, query_weight, m_send, count, [bias_part], []
    )
    qm_got = across_cores(qm_send)
    kv_keep, kv_send, grad_stream, first_part = project_kv(
        mine,
        got,
        turned,
        back,
        stream,
        hbm(grad_resid),
        first_gain,
        key_weight,
        value_weight,
        count,
        [],
    )

    each = count // seqs
    picks = []
    for key, pick in state.where.items():
        if key[0] == "one":
            picks.append((pick, key[3] // each, 2 * each + key[3] % each))
        else:
            kind, block = key[3] // chips, key[1] * chips + key[3] % chips
            picks.append((pick, block // each, kind * each + block % each))
    slots = 3 * each
    groups = [list(range(0, seqs, 2)), list(range(1, seqs, 2))]
    (z_keep, z_send), (kv_send,) = fold_seq(
        "feed_seq", info, state.pairs, picks, seqs, slots, groups, after=[first_part, *out_parts[1:]], carry=[kv_send]
    )
    kv_got = across_cores(kv_send)
    z_got = across_seq(z_send, 1)
    where = {}
    for r in range(chips):
        where["p", 0, r] = (0, r)
        where["p", 3, r] = (1, (r, chips + r))
        for kind in (1, 2):
            where["p", kind, r] = (2, (kind - 1) * chips + r)
    mixes = Halving([(q_keep, qm_got), (hbm(m_keep), qm_got), (kv_keep, kv_got)], where)

    def mix_step(mixes, level, after, carry=(), held_back=False):
        return exchange(
            f"mix_{level}",
            info,
            mixes,
            [
                (lambda key: key[1] in (1, 3), level),
                (lambda key: key[1] in (0, 2), levels - 1 - level),
            ],
            after,
            carry,
            held_back,
        )

    layer_output = join(info, out_parts, [z_keep])
    mixes, outs, _ = mix_step(mixes, 0, [hbm(layer_output)])
    e_keep, e_send = mixer_backward(
        info,
        ids,
        embedding,
        filter_weight,
        score_weight,
        grad_stream,
        first_part,
        second_part,
        bias_part,
        row_len,
        vocab,
        words,
        count,
        [z_keep, outs[0]],
    )

    def seq_step(name, z_keep, z_got, slots, step, after, carry):
        held_now = z_keep.shape[0] // slots
        lists = [
            [(0, d * slots + i) for d in range(first, held_now, 2) for i in range(slots)]
            for first in range(2)
        ]
        (z_keep, z_send), carried = fold(
            f"{name}_seq_{step}", info, [(z_keep, z_got)], lists, after, carry
        )
        return z_keep, across_seq(z_send, step), carried

    last, step, carry = e_keep, 2, [e_send]
    while step < seqs:
        z_keep, z_got, carry = seq_step("feed", z_keep, z_got, slots, step, [last], carry)
        last = z_keep
        step *= 2
    for level in range(1, levels):
        mixes, outs, _ = mix_step(mixes, level, [last], (), level == levels - 1)
        last = outs[0]
    e_got = across_cores(carry[0])
    small = Halving([(e_keep, e_got)], {("e", r): (0, r) for r in range(chips)})
    sends = outs[1::2]
    for level in range(levels):
        small, outs, sends = exchange(
            f"small_{level}",
            info,
            small,
            [(lambda key: True, level)],
            [last] if level == 0 else [],
            sends if level == 0 else [],
        )
        if level == 0:
            mixes = mixes(sends)
    (share,), _ = fold("small_chips", info, small.pairs, [small.picks([("e", 0)])])
    share_got = across_seq(share, 1)
    picks = [(pick, None, key[1]) for key, pick in mixes.where.items()]
    gate_grad, up_grad, down_grad = feed_end([z_keep, z_got], [share])
    share_width = features // seqs
    mix_sends, _ = fold_seq(
        "mix_seq",
        info,
        mixes.pairs,
        picks,
        seqs,
        tile_count(4, share_width),
        [[d] for d in range(seqs)],
        share_width,
        after=[hbm(gate_grad)],
    )
    mix_arrived = [mix_sends[0]] + [across_seq(mix_sends[d], d) for d in range(1, seqs)]
    distance = 1
    while distance < seqs:
        share = sum_of(f"small_seq_{distance}", [share, share_got], [mix_sends[0]])
        distance *= 2
        if distance < seqs:
            share_got = across_seq(share, distance)
    shares = [share] + [across_chips(share, r) for r in range(1, chips)]
    query_grad, key_grad, value_grad, merge_grad = mix_end(mix_arrived, 4, share_width, [share])
    embed, filters, score, first, second, bias_sum = unpack(
        info, shares, [across_cores(x) for x in shares], vocab, bucket_count, heads, [hbm(query_grad)]
    )
    return (
        layer_output,
        embed,
        filters,
        score,
        first,
        query_grad,
        key_grad,
        value_grad,
        merge_grad,
        bias_sum.T,
        second,
        gate_grad,
        up_grad,
        down_grad.T,
    )


def solution(mesh):
    in_specs = (
        P("batch", "seq"),
        P("batch", None),
        P("batch", "seq"),
        P(),
        P(),
        P(),
        P(),
        P(),
        P(),
        P(),
        P(),
        P(),
        P(),
        P(),
        P(),
        P(),
        P("batch", "seq", None),
    )
    out_specs = (
        P("batch", "seq", None),
        P(),
        P(),
        P(),
        P(),
        P("batch", "seq"),
        P("batch", "seq"),
        P("batch", "seq"),
        P("batch", "seq"),
        P(),
        P(),
        P("batch", "seq"),
        P("batch", "seq"),
        P("batch", "seq"),
    )
    return jax.shard_map(shards, mesh=mesh, in_specs=in_specs, out_specs=out_specs, check_vma=False)
```

```python
import functools

import jax
import jax.numpy as jnp
from jax import lax
from jax.experimental import pallas as pl
from jax.experimental.pallas import tpu as pltpu
from jax.sharding import PartitionSpec as P

EPS = 1e-06
LIMITS = (12, 16, 23, 32, 46, 64, 91)
NEG = -1e30
LANES = 128
BLOCK = 128
FAR = 2
CUBE = 0.044715
SLOPE = 0.7978845608028654
MEGA = 1 << 20


def dot(a, b):
    return lax.dot_general(a, b, (((1,), (0,)), ((), ())), preferred_element_type=jnp.float32)


def dot_nt(a, b):
    return lax.dot_general(a, b, (((1,), (1,)), ((), ())), preferred_element_type=jnp.float32)


def params(megabytes):
    return pltpu.CompilerParams(vmem_limit_bytes=megabytes * MEGA)


def cost(microseconds):
    return pl.CostEstimate(flops=int(microseconds * 1e+09), bytes_accessed=1, transcendentals=0)


VMEM = pl.BlockSpec(memory_space=pltpu.VMEM)
ANY = pl.BlockSpec(memory_space=pl.ANY)
HBM = pl.BlockSpec(memory_space=pltpu.HBM)
AUTO = pl.BlockSpec()
SMEM = pl.BlockSpec(memory_space=pltpu.SMEM)


def hbm(x):
    return pltpu.with_memory_space_constraint(x, pltpu.HBM)


def ordered(kernel, inputs, after):
    def with_others(*refs):
        kernel(*refs[:inputs], *refs[inputs + len(after) :])

    return with_others


def launch(name, kernel, ins, in_specs, outs, out_specs, megabytes, scratch=(), after=(), carry=(), microseconds=1.0
):
    given, made = len(ins), len(outs)
    skip = len(after) + len(carry)

    def body(*refs):
        rest = refs[given + skip :]
        kernel(*refs[:given], *rest[:made], *rest[made + len(carry) :])

    results = pl.pallas_call(
        body,
        out_shape=[*outs, *[jax.ShapeDtypeStruct(x.shape, x.dtype) for x in carry]],
        in_specs=[*in_specs, *[ANY] * skip],
        out_specs=[*out_specs, *[ANY] * len(carry)],
        scratch_shapes=list(scratch),
        input_output_aliases={given + len(after) + i: made + i for i in range(len(carry))},
        compiler_params=params(megabytes),
        cost_estimate=cost(microseconds),
        name=name,
    )(*ins, *after, *carry)
    return results[:made], results[made:]


def bucket_of(relative):
    distance = jnp.abs(relative)
    far = jnp.full_like(distance, 8)
    for limit in LIMITS:
        far = far + jnp.where(distance >= limit, 1, 0)
    return jnp.where(distance < 8, distance, far) + jnp.where(relative > 0, 16, 0)


def split_three(x):
    parts = []
    for _ in range(3):
        high = x.astype(jnp.bfloat16)
        parts.append(high)
        x = x - high.astype(jnp.float32)
    return parts


def bias_kernel(table_ref, out_ref, tile_ref, sems):
    copies = []
    heads, buckets = table_ref.shape
    wide = 2 * BLOCK
    parts = split_three(table_ref[...])
    bucket = lax.broadcasted_iota(jnp.int32, (buckets, wide), 0)
    entry = lax.broadcasted_iota(jnp.int32, (buckets, wide), 1)
    gap = jnp.where(entry < BLOCK, entry, entry - wide)
    for delta in range(3):
        hot = jnp.where(bucket_of((delta - 1) * BLOCK - gap) == bucket, 1.0, 0.0)
        hot = hot.astype(jnp.bfloat16)
        rows = (dot(parts[2], hot) + dot(parts[1], hot)) + dot(parts[0], hot)
        for h in range(heads):
            row = jnp.broadcast_to(rows[h : h + 1], (BLOCK, wide))
            tile_ref[delta, h] = pltpu.roll(row, 0, 1, stride=1, stride_axis=0)[:, :BLOCK]
        copies.append(pltpu.make_async_copy(tile_ref.at[delta], out_ref.at[delta], sems.at[delta]))
        copies[-1].start()
    for copy in copies:
        copy.wait()


def bias_tiles(table):
    outs, _ = launch(
        "bias_tiles",
        bias_kernel,
        [table],
        [VMEM],
        [pltpu.HBM((3, table.shape[0], BLOCK, BLOCK), jnp.float32)],
        [HBM],
        6,
        [
            pltpu.VMEM((3, table.shape[0], BLOCK, BLOCK), jnp.float32),
            pltpu.SemaphoreType.DMA((3,)),
        ],
        microseconds=2,
    )
    return outs[0]


def fill_tiles(near_ref, h, tile_ref):
    for delta in range(3):
        tile_ref[1 + delta] = near_ref[delta, h]
    tile_ref[0] = jnp.broadcast_to(near_ref[0, h, :1, BLOCK - 1 :], (BLOCK, BLOCK))
    tile_ref[4] = jnp.broadcast_to(near_ref[2, h, BLOCK - 1 :, :1], (BLOCK, BLOCK))


def by_head(turned, size):
    empty = jnp.zeros((size, turned.shape[1]), turned.dtype)
    left = jnp.concatenate([turned[:size], empty], axis=0)
    right = jnp.concatenate([empty, turned[size:]], axis=0)
    return jnp.concatenate([left, right], axis=1)


def lower_rows(cut_ref, start, rows, heads):
    count = rows[0].shape[1] if rows else heads[1]
    place = start + lax.broadcasted_iota(jnp.int32, (16, count), 1)
    row = lax.broadcasted_iota(jnp.int32, (16, count), 0)
    segment = sum(jnp.where(place >= cut_ref[i], 1, 0) for i in range(3))
    mask = jnp.where((row < 4) & (segment != row), NEG, 0.0)
    blocks = []
    for head in range(heads[0]):
        block = mask
        if rows:
            for i, part in enumerate(split_three(rows[head])):
                block = jnp.where(row == 4 + i, part.astype(jnp.float32), block)
        blocks.append(block.astype(jnp.bfloat16))
    block = jnp.concatenate(blocks, axis=1)
    return jnp.concatenate([block, jnp.zeros((LANES - 16, block.shape[1]), jnp.bfloat16)], axis=0)


def segment_hots(cut_ref, start, count, inside, outside):
    place = start + lax.broadcasted_iota(jnp.int32, (count, LANES), 0)
    lane = lax.broadcasted_iota(jnp.int32, (count, LANES), 1)
    segment = sum(jnp.where(place >= cut_ref[i], 1, 0) for i in range(3))
    value = jnp.where(segment == lane, inside, outside)
    return jnp.where(lane < 4, value, 0.0).astype(jnp.bfloat16)


TILE = 32
FORWARD_TILE = 64
GUARD = 8
MAIN = 24


def row_of(ref):
    return ref[...].reshape(1, -1)


def tile_rows(base, size=TILE):
    return pl.ds(pl.multiple_of(base, 8), size)


def with_sides(ref, lead, base, lanes, size=TILE):
    return ref[(*lead, pl.ds(pl.multiple_of(base - 8, 8), size + 16), lanes)]


def middle(x):
    return x[8:-8]


def down(x):
    return middle(pltpu.roll(x, 1, 0))


def up(x):
    return middle(pltpu.roll(x, x.shape[0] - 1, 0))


def lane_sum(x):
    return jnp.broadcast_to(jnp.sum(x, axis=1, keepdims=True), x.shape)


def offsets_of(rows):
    return {
        -2: down(rows[2]),
        -1: down(rows[3]),
        0: middle(rows[0]),
        1: middle(rows[1]),
        2: middle(rows[2]),
        3: middle(rows[3]),
        4: up(rows[0]),
        5: up(rows[1]),
    }


def spread_of(phase, j, one, two, three, four, coefs):
    pair = j - j % 2
    third = three / 3.0
    zero = jnp.zeros_like(third)
    half, quarter = two * 0.5, four * 0.25

    def add(o, value):
        coefs[o] = coefs[o] + value if o in coefs else value

    add(j, one + third)
    for o in (pair, pair + 1):
        add(o, half)
    for o in range(4):
        add(o, quarter)
    add(j + 1, jnp.where(phase <= 1, third, zero))
    add(j + 2, jnp.where(phase == 0, third, zero))
    add(j - 1, jnp.where(phase >= 1, third, zero))
    add(j - 2, jnp.where(phase == 2, third, zero))


def pooled_dots(phase, j, dots):
    pair = j - j % 2
    zero = jnp.zeros_like(dots[0])
    two = 0.5 * (dots[pair] + dots[pair + 1])
    four = 0.25 * ((dots[0] + dots[1]) + (dots[2] + dots[3]))
    three = dots[j] + jnp.where(phase <= 1, dots[j + 1], zero)
    three = three + jnp.where(phase == 0, dots[j + 2], zero)
    three = three + jnp.where(phase >= 1, dots[j - 1], zero)
    three = three + jnp.where(phase == 2, dots[j - 2], zero)
    return dots[j], two, three / 3.0, four


def lane_chunks(features):
    return [slice(i, i + LANES) for i in range(0, features, LANES)]


def over_tiles(first, rows, body, size=TILE):
    def step(t, carry):
        body(first + t * size)
        return carry

    lax.fori_loop(0, rows // size, step, 0)


def convolve_all(info_ref, ids_ref, emb_ref, filt_ref, score_ref, e_ref, c_ref, dot_ref, row_len):
    count = ids_ref.shape[0]
    words, features = emb_ref.shape
    score = row_of(score_ref)
    group = info_ref[4] // 4
    vocab = lax.broadcasted_iota(jnp.int32, (count, words), 1)
    edge = jnp.zeros((GUARD, LANES), jnp.float32)
    for j in range(4):
        hot = jnp.where(ids_ref[:, j : j + 1] == vocab, 1.0, 0.0).astype(jnp.bfloat16)
        e_ref[j] = dot(hot, emb_ref[...])
        dot_ref[j, :GUARD] = edge
        dot_ref[j, count - GUARD :] = edge

    def tile(base):
        parts = [jnp.zeros((TILE, LANES), jnp.float32) for _ in range(4)]
        for lanes in lane_chunks(features):
            near = offsets_of([with_sides(e_ref, (j,), base, lanes) for j in range(4)])
            taps = [filt_ref[k : k + 1, lanes] for k in range(4)]
            for j in range(4):
                value = taps[0] * near[j - 2]
                for k in range(1, 4):
                    value = value + taps[k] * near[j + k - 2]
                c_ref[j, tile_rows(base), lanes] = value
                parts[j] = parts[j] + value * score[:, lanes]
        places = base - MAIN + group + lax.broadcasted_iota(jnp.int32, (TILE, LANES), 0)
        for j in range(4):
            inside = 4 * places + j < row_len
            dot_ref[j, tile_rows(base)] = jnp.where(inside, lane_sum(parts[j]), 0.0)

    over_tiles(GUARD, count - 2 * GUARD, tile)


def tile_weights(info_ref, dot_ref, base, row_len, size):
    dots = offsets_of([with_sides(dot_ref, (j,), base, slice(None), size) for j in range(4)])
    places = base - MAIN + info_ref[4] // 4
    places = places + lax.broadcasted_iota(jnp.int32, (size, LANES), 0)
    phases, weights = [], []
    for j in range(4):
        phase = lax.rem(places + 3 + j, 3)
        scores = pooled_dots(phase, j, dots)
        highest = jnp.maximum(jnp.maximum(scores[0], scores[1]), jnp.maximum(scores[2], scores[3]))
        powers = [jnp.exp(score - highest) for score in scores]
        share = 1.0 / ((powers[0] + powers[1]) + (powers[2] + powers[3]))
        phases.append(phase)
        weights.append([power * share for power in powers])
    limits = {o: (4 * places + o < row_len) for o in (4, 5)}
    return phases, weights, limits


def token_coefs(phases, weights, limits, scale):
    result = []
    for h in range(2):
        coefs = {}
        for j in (2 * h, 2 * h + 1):
            spread_of(phases[j], j, *weights[j], coefs)
        for o in coefs:
            if o in limits:
                coefs[o] = jnp.where(limits[o], coefs[o], 0.0)
            coefs[o] = coefs[o] * scale
        result.append(coefs)
    return result


COEFS = [(0, o) for o in range(-2, 4)] + [(1, o) for o in range(6)]


def mixer_kernel(
    row_len,
    info_ref,
    ids_ref,
    emb_ref,
    filt_ref,
    score_ref,
    gain_ref,
    wq_ref,
    wk_ref,
    wv_ref,
    stream_out_ref,
    normed_out_ref,
    q_ref,
    kv_ref,
    e_ref,
    c_ref,
    dot_ref,
    pair_ref,
    root_ref,
    weight_ref,
    sems,
    stream_ref,
    normed_ref,
):
    copies = [
        pltpu.make_async_copy(w_ref, weight_ref.at[i], sems.at[i])
        for i, w_ref in enumerate((wk_ref, wv_ref, wq_ref))
    ]
    for copy in copies:
        copy.start()
    tokens, features = stream_ref.shape
    gain = row_of(gain_ref)
    chunks = lane_chunks(features)
    convolve_all(
        info_ref, ids_ref, emb_ref, filt_ref, score_ref, e_ref, c_ref, dot_ref, row_len
    )

    size = pair_ref.shape[1] // 2

    def tile(base):
        coefs = token_coefs(*tile_weights(info_ref, dot_ref, base, row_len, size), 0.5)
        squares = [jnp.zeros((size, LANES), jnp.float32) for _ in range(2)]
        rows = pl.ds(pl.multiple_of(2 * (base - MAIN), 2 * size), 2 * size)
        for i, lanes in enumerate(chunks):
            conv = offsets_of([with_sides(c_ref, (j,), base, lanes, size) for j in range(4)])
            for h in range(2):
                mixed = None
                for o, coef in coefs[h].items():
                    term = coef * conv[o]
                    mixed = term if mixed is None else mixed + term
                squares[h] = squares[h] + mixed * mixed
                pair_ref[i, pl.ds(h, size, stride=2), :] = mixed
        for h in range(2):
            root = lax.rsqrt(lane_sum(squares[h]) / features + EPS)
            root_ref[pl.ds(h, size, stride=2), :] = root
        for i, lanes in enumerate(chunks):
            stream = pair_ref[i]
            stream_ref[rows, lanes] = stream
            normed = stream * root_ref[...] * gain[:, lanes]
            normed_ref[rows, lanes] = normed.astype(jnp.bfloat16)

    over_tiles(MAIN, tokens // 2, tile, size)
    kept = [
        pltpu.make_async_copy(stream_ref, stream_out_ref, sems.at[3]),
        pltpu.make_async_copy(normed_ref, normed_out_ref, sems.at[4]),
    ]
    for copy in kept:
        copy.start()
    for i in range(2):
        copies[i].wait()
        kv_ref[i] = dot(normed_ref[...], weight_ref[i]).astype(jnp.bfloat16)
    copies[2].wait()
    q_ref[...] = dot(normed_ref[...], weight_ref[2]).astype(jnp.bfloat16)
    for copy in kept:
        copy.wait()


def mixer_forward(info, ids, emb, filt, score, gain, wq, wk, wv, tokens, row_len, after):
    features = emb.shape[1]
    count = ids.shape[0]
    low = jnp.bfloat16
    full = jnp.float32
    outs, _ = launch(
        "mixer_forward",
        functools.partial(mixer_kernel, row_len),
        [info, ids, emb, filt, score, gain, wq, wk, wv],
        [SMEM] + [VMEM] * 5 + [HBM] * 3,
        [
            pltpu.HBM((tokens, features), full),
            pltpu.HBM((tokens, features), low),
            jax.ShapeDtypeStruct((tokens, features), low),
            jax.ShapeDtypeStruct((2, tokens, features), low),
        ],
        [HBM, HBM, VMEM, VMEM],
        24,
        [
            pltpu.VMEM((4, count, features), full),
            pltpu.VMEM((4, count, features), full),
            pltpu.VMEM((4, count, LANES), full),
            pltpu.VMEM((features // LANES, 2 * FORWARD_TILE, LANES), full),
            pltpu.VMEM((2 * FORWARD_TILE, LANES), full),
            pltpu.VMEM((3, features, features), low),
            pltpu.SemaphoreType.DMA((5,)),
            pltpu.VMEM((tokens, features), full),
            pltpu.VMEM((tokens, features), low),
        ],
        after=after,
        microseconds=8,
    )
    return outs


def mixer_back_kernel(
    row_len,
    vocab_size,
    info_ref,
    ids_ref,
    emb_ref,
    filt_ref,
    score_ref,
    grad_ref,
    first_ref,
    second_ref,
    bias_ref,
    keep_ref,
    send_ref,
    e_ref,
    c_ref,
    dot_ref,
    coef_ref,
    g_ref,
    low_ref,
    turn_ref,
    embed_ref,
    small_ref,
):
    tokens, features = grad_ref.shape
    groups = tokens // 2
    chunks = lane_chunks(features)
    count = ids_ref.shape[0]
    inner = count - 2 * GUARD
    score_row = row_of(score_ref)
    convolve_all(
        info_ref, ids_ref, emb_ref, filt_ref, score_ref, e_ref, c_ref, dot_ref, row_len
    )
    before = jnp.zeros((MAIN, LANES), jnp.float32)
    behind = jnp.zeros((count - MAIN - groups, LANES), jnp.float32)
    for i, lanes in enumerate(chunks):
        turn_ref[i] = grad_ref[:, lanes]
        for h in range(2):
            g_ref[h, :MAIN, lanes] = before
            g_ref[h, MAIN + groups :, lanes] = behind
            g_ref[h, MAIN : MAIN + groups, lanes] = turn_ref[i, pl.ds(h, groups, stride=2), :]
    for place in range(2 * len(COEFS)):
        coef_ref[place, :MAIN] = before
        coef_ref[place, MAIN + groups :] = behind
    small_ref[...] = jnp.zeros_like(small_ref)

    def pull_tile(base):
        phases, weights, limits = tile_weights(info_ref, dot_ref, base, row_len, TILE)
        coefs = token_coefs(phases, weights, limits, 0.5)
        sums = {}
        for lanes in chunks:
            conv = offsets_of([with_sides(c_ref, (j,), base, lanes) for j in range(4)])
            grads = [g_ref[h, tile_rows(base), lanes] for h in range(2)]
            for h, o in COEFS:
                term = grads[h] * conv[o]
                sums[h, o] = sums[h, o] + term if (h, o) in sums else term
        pulls = []
        for h in range(2):
            dots = {}
            for side, o in COEFS:
                if side == h:
                    value = lane_sum(sums[h, o]) * 0.5
                    dots[o] = jnp.where(limits[o], value, 0.0) if o in limits else value
            for j in (2 * h, 2 * h + 1):
                grads = pooled_dots(phases[j], j, dots)
                mean = sum(weights[j][i] * grads[i] for i in range(4))
                pulls.append([weights[j][i] * (grads[i] - mean) for i in range(4)])
        score_coefs = token_coefs(phases, pulls, limits, 1.0)
        for place, (h, o) in enumerate(COEFS):
            coef_ref[place, tile_rows(base)] = coefs[h][o]
            coef_ref[len(COEFS) + place, tile_rows(base)] = score_coefs[h][o]

    over_tiles(MAIN, groups, pull_tile)

    def fold_rows(x):
        return sum(x[i : i + 8] for i in range(0, TILE, 8))

    def grad_tile(base):
        def coef(h, o, score=False):
            return with_sides(coef_ref, (COEFS.index((h, o)) + len(COEFS) * score,), base, slice(None))

        own = [[middle(coef(h, j)) for j in range(4)] for h in range(2)]
        side = [down(coef(1, 4 + j)) if j < 2 else up(coef(0, j - 4)) for j in range(4)]
        kappa = []
        for j in range(4):
            far = down(coef(1, 4 + j, True)) if j < 2 else up(coef(0, j - 4, True))
            kappa.append(middle(coef(0, j, True)) + middle(coef(1, j, True)) + far)
        for lanes in chunks:
            first, second = (with_sides(g_ref, (h,), base, lanes) for h in range(2))
            above, below = down(second), up(first)
            first, second = middle(first), middle(second)
            near = offsets_of([with_sides(e_ref, (j,), base, lanes) for j in range(4)])
            score = score_row[:, lanes]
            taps = [None] * 4
            score_sum = None
            for j in range(4):
                value = own[0][j] * first + own[1][j] * second
                value = value + side[j] * (above if j < 2 else below) + kappa[j] * score
                term = kappa[j] * c_ref[j, tile_rows(base), lanes]
                score_sum = term if score_sum is None else score_sum + term
                c_ref[j, tile_rows(base), lanes] = value
                for k in range(4):
                    term = value * near[j + k - 2]
                    taps[k] = term if taps[k] is None else taps[k] + term
            for k in range(4):
                small_ref[k, :, lanes] += fold_rows(taps[k])
            small_ref[4, :, lanes] += fold_rows(score_sum)

    over_tiles(GUARD, inner, grad_tile)
    edge = jnp.zeros((GUARD, features), jnp.float32)
    for j in range(4):
        c_ref[j, :GUARD] = edge
        c_ref[j, count - GUARD :] = edge

    def back_tile(base):
        start = pl.multiple_of(base - GUARD, TILE)
        for lanes in chunks:
            d = offsets_of([with_sides(c_ref, (j,), base, lanes) for j in range(4)])
            taps = [filt_ref[k : k + 1, lanes] for k in range(4)]
            for j in range(4):
                value = taps[0] * d[j + 2]
                for k in range(1, 4):
                    value = value + taps[k] * d[j + 2 - k]
                low_ref[pl.ds(j * inner + start, TILE), lanes] = value.astype(jnp.bfloat16)

    over_tiles(GUARD, inner, back_tile)
    lane = lax.broadcasted_iota(jnp.int32, (inner, LANES), 1)
    spread = jnp.zeros((inner, LANES), jnp.float32)
    for j in range(4):
        ids = ids_ref[GUARD : GUARD + inner, j : j + 1].astype(jnp.float32)
        spread = jnp.where(lane == j, ids, spread)
    spare = jnp.zeros((-inner % LANES, LANES), jnp.float32)
    turned = jnp.concatenate([spread, spare], axis=0).T.astype(jnp.int32)
    flat = jnp.concatenate([turned[j : j + 1, :inner] for j in range(4)], axis=1)
    words = -(-vocab_size // 16) * 16
    vocab = lax.broadcasted_iota(jnp.int32, (words, 4 * inner), 0)
    hot = jnp.where(flat == vocab, 1.0, 0.0).astype(jnp.bfloat16)
    embed_ref[:words] = dot(hot, low_ref[...])
    embed_ref[words:] = jnp.zeros((embed_ref.shape[0] - words, features), jnp.float32)
    for i in range(5):
        embed_ref[vocab_size + i : vocab_size + i + 1] = jnp.sum(small_ref[i], axis=0, keepdims=True)
    embed_ref[vocab_size + 5 : vocab_size + 6] = first_ref[...]
    embed_ref[vocab_size + 6 : vocab_size + 7] = second_ref[...]
    heads = bias_ref.shape[0]
    embed_ref[vocab_size + 7 : vocab_size + 7 + heads, :LANES] = bias_ref[...]
    share = keep_ref.shape[1]
    chips = keep_ref.shape[0]
    me = info_ref[0]
    for place in range(chips):
        for odd, out_ref in enumerate((keep_ref, send_ref)):
            start = pl.multiple_of((me ^ (2 * place + odd)) * share, 16)
            out_ref[place] = embed_ref[pl.ds(start, share), :].astype(jnp.bfloat16)


def mixer_backward(
    info, ids, emb, filt, score, grad, first, second, bias, row_len, vocab, embed_rows, devices, after
):
    tokens, features = grad.shape
    count = ids.shape[0]
    full = jnp.float32
    piece = jax.ShapeDtypeStruct((devices // 2, embed_rows // devices, features), jnp.bfloat16)
    outs, _ = launch(
        "mixer_backward",
        functools.partial(mixer_back_kernel, row_len, vocab),
        [info, ids, emb, filt, score, grad, first, second, bias],
        [SMEM] + [VMEM] * 8,
        [piece, piece],
        [VMEM] * 2,
        26,
        [
            pltpu.VMEM((4, count, features), full),
            pltpu.VMEM((4, count, features), full),
            pltpu.VMEM((4, count, LANES), full),
            pltpu.VMEM((2 * len(COEFS), count, LANES), full),
            pltpu.VMEM((2, count, features), full),
            pltpu.VMEM((4 * (count - 2 * GUARD), features), jnp.bfloat16),
            pltpu.VMEM((features // LANES, tokens, LANES), full),
            pltpu.VMEM((embed_rows, features), full),
            pltpu.VMEM((5, 8, features), full),
        ],
        after=after,
        microseconds=11,
    )
    return outs


def scores_of(info_ref, part, raw, tile_ref):
    keys, tokens = raw.shape
    base, own = info_ref[part], info_ref[3]
    rows = []
    for kb in range(keys // BLOCK):
        tiles = [
            tile_ref[jnp.clip(base + kb - own - qb, -FAR, FAR) + FAR]
            for qb in range(tokens // BLOCK)
        ]
        rows.append(raw[kb * BLOCK : (kb + 1) * BLOCK] + jnp.concatenate(tiles, axis=1))
    return rows


def only_head(x, h, size):
    lane = lax.broadcasted_iota(jnp.int32, x.shape, 1)
    return jnp.where((lane >= h * size) & (lane < (h + 1) * size), x, jnp.zeros_like(x))


def attention_kernel(
    size,
    carried,
    last,
    info_ref,
    q_ref,
    kv_ref,
    bias_ref,
    cut_ref,
    *refs,
):
    if last:
        *refs, plain_ref, weight_ref, sems = refs
    *refs, tile_ref, q_low_ref, k_hot_ref = refs
    if carried:
        before_ref, state_ref, *refs = refs
    if last:
        stream_ref, wm_ref, gain_ref, att_ref, lse_ref, resid_ref, normed_ref = refs
    else:
        mixed_ref, stat_ref = refs
    step = pl.program_id(0)
    part = 5 + carried
    low = []
    tokens = q_ref.shape[0]

    @pl.when(step == 0)
    def _():
        q_low_ref[...] = lower_rows(cut_ref, info_ref[3] * BLOCK, [], (2, tokens))
        k_hot_ref[...] = segment_hots(cut_ref, info_ref[part] * BLOCK, kv_ref.shape[1], 1.0, 0.0)

    both = jnp.concatenate([by_head(q_ref[...].T, size), q_low_ref[...]], axis=0)
    raws = dot(jnp.concatenate([kv_ref[0], k_hot_ref[...]], axis=1), both)
    turned = kv_ref[1].T
    ones = jnp.ones((16, turned.shape[1]), jnp.bfloat16)
    for h in range(2):
        fill_tiles(bias_ref, h, tile_ref.at[h])
    for h in range(2):
        raw = raws[:, h * tokens : (h + 1) * tokens]
        rows = scores_of(info_ref, part, raw, tile_ref.at[h])
        highest = None
        for row in rows:
            top = jnp.max(row, axis=0, keepdims=True)
            highest = top if highest is None else jnp.maximum(highest, top)
        if carried:
            highest = jnp.maximum(highest, state_ref[0, h : h + 1])
        weights = jnp.concatenate([jnp.exp(row - highest).astype(jnp.bfloat16) for row in rows], axis=0)
        mixed = dot(jnp.concatenate([turned[h * size : (h + 1) * size], ones], axis=0), weights)
        mixed, summed = mixed[:size], mixed[size : size + 1]
        if carried:
            shrink = jnp.exp(state_ref[0, h : h + 1] - highest)
            summed = summed + state_ref[0, 2 + h : 3 + h] * shrink
            mixed = mixed + before_ref[h * size : (h + 1) * size] * shrink
        if last:
            lse_ref[0, h : h + 1] = highest + jnp.log(summed)
            low.append(mixed * (1.0 / summed))
        else:
            stat_ref[0, h : h + 1] = highest
            stat_ref[0, 2 + h : 3 + h] = summed
            mixed_ref[h * size : (h + 1) * size] = mixed
    if not last:
        return
    features = stream_ref.shape[1]
    turned = jnp.concatenate(low, axis=0)
    att_ref[...] = turned
    plain_ref[step] = turned.T.astype(jnp.bfloat16)
    copies = [
        pltpu.make_async_copy(wm_ref, weight_ref, sems.at[0]),
        pltpu.make_async_copy(stream_ref, resid_ref, sems.at[1]),
    ]

    @pl.when(step == 0)
    def _():
        for copy in copies:
            copy.start()

    @pl.when(step == pl.num_programs(0) - 1)
    def _():
        for copy in copies:
            copy.wait()
        attended = jnp.concatenate([plain_ref[p] for p in range(plain_ref.shape[0])], axis=1)
        resid = resid_ref[...] + dot(attended, weight_ref[...])
        resid_ref[...] = resid
        root = lax.rsqrt(jnp.sum(resid * resid, axis=1, keepdims=True) / features + EPS)
        normed_ref[...] = (resid * root * row_of(gain_ref)).astype(jnp.bfloat16)


def attention_forward(name, size, info, q, kv, bias, cuts, carried=(), last=(), carry=()):
    tokens, features = q.shape
    heads = features // size
    pairs = heads // 2
    wide = 2 * size
    whole = lambda shape: pl.BlockSpec(shape, lambda p: (0,) * len(shape))
    by_rows = pl.BlockSpec((wide, tokens), lambda p: (p, 0))
    stat = pl.BlockSpec((1, 8, tokens), lambda p: (p, 0, 0))
    stat_shape = jax.ShapeDtypeStruct((pairs, 8, tokens), jnp.float32)
    ins = [info, q, kv, bias, cuts, *carried, *last]
    in_specs = [
        SMEM,
        pl.BlockSpec((tokens, wide), lambda p: (0, p)),
        pl.BlockSpec((2, kv.shape[1], wide), lambda p: (0, 0, p)),
        pl.BlockSpec((3, 2, BLOCK, BLOCK), lambda p: (0, p, 0, 0)),
        SMEM,
    ]
    if carried:
        in_specs += [by_rows, stat]
    if last:
        stream, wm, gain = last
        in_specs += [
            HBM,
            HBM,
            whole(gain.shape),
        ]
        shapes = [
            jax.ShapeDtypeStruct((features, tokens), jnp.float32),
            stat_shape,
            jax.ShapeDtypeStruct((tokens, features), jnp.float32),
            jax.ShapeDtypeStruct((tokens, features), jnp.bfloat16),
        ]
        out_specs = [by_rows, stat, whole((tokens, features)), whole((tokens, features))]
    else:
        shapes = [jax.ShapeDtypeStruct((features, tokens), jnp.float32), stat_shape]
        out_specs = [by_rows, stat]
    merging = [
        pltpu.VMEM((pairs, tokens, wide), jnp.bfloat16),
        pltpu.VMEM((features, features), jnp.bfloat16),
        pltpu.SemaphoreType.DMA((2,)),
    ]
    kernel = functools.partial(attention_kernel, size, int(bool(carried)), bool(last))
    made = len(shapes)

    def body(*refs):
        rest = refs[len(ins) + len(carry) :]
        kernel(*refs[: len(ins)], *rest[:made], *rest[made + len(carry) :])

    results = pl.pallas_call(
        body,
        grid=(pairs,),
        out_shape=[*shapes, *[jax.ShapeDtypeStruct(x.shape, x.dtype) for x in carry]],
        in_specs=in_specs + [ANY] * len(carry),
        out_specs=[*out_specs, *[ANY] * len(carry)],
        input_output_aliases={len(ins) + i: made + i for i in range(len(carry))},
        scratch_shapes=[
            pltpu.VMEM((2, 2 * FAR + 1, BLOCK, BLOCK), jnp.float32),
            pltpu.VMEM((LANES, 2 * tokens), jnp.bfloat16),
            pltpu.VMEM((kv.shape[1], LANES), jnp.bfloat16),
            *(merging if last else []),
        ],
        compiler_params=params(12),
        cost_estimate=cost(9),
        name=name,
    )(*ins, *carry)
    return results[:made], results[made:]


def diagonal_sums(tile_ref, sums_ref):
    wide = 2 * BLOCK
    row = lax.broadcasted_iota(jnp.int32, (BLOCK, BLOCK), 0)
    column = lax.broadcasted_iota(jnp.int32, (BLOCK, BLOCK), 1)
    flip = jnp.where(row + column == BLOCK - 1, 1.0, 0.0).astype(jnp.bfloat16)
    near = jnp.concatenate([tile_ref[h, 1 + delta] for h in range(2) for delta in range(3)], axis=1)
    high = near.astype(jnp.bfloat16)
    rest = (near - high.astype(jnp.float32)).astype(jnp.bfloat16)
    flipped = dot(flip, high) + dot(flip, rest)
    empty = jnp.zeros((BLOCK, BLOCK), jnp.float32)
    for h in range(2):
        for delta in range(3):
            start = (3 * h + delta) * BLOCK
            padded = jnp.concatenate([flipped[:, start : start + BLOCK], empty], axis=1)
            slid = pltpu.roll(padded, 0, 1, stride=1, stride_axis=0)
            place = 5 * h + 1 + delta
            sums_ref[0, place : place + 1] = jnp.sum(slid, axis=0, keepdims=True)
        for far in (0, 2 * FAR):
            place = 5 * h + far
            total = jnp.sum(tile_ref[h, far], axis=0, keepdims=True)
            sums_ref[0, place : place + 1] = jnp.concatenate([total, empty[:1]], axis=1)


def attention_back_kernel(
    parts,
    size,
    info_ref,
    q_ref,
    g_ref,
    *refs,
):
    kv_refs = refs[:parts]
    bias_ref, cut_ref, lse_ref, att_ref = refs[parts : parts + 4]
    dq_ref, *dkv_refs, sums_ref, bias_tile_ref, tile_ref = refs[-4 - 2 * parts : len(refs) - parts]
    k_hot_refs = refs[len(refs) - parts :]
    tokens = q_ref.shape[0]
    blocks = tokens // BLOCK
    own = info_ref[3]
    for h in range(2):
        fill_tiles(bias_ref, h, bias_tile_ref.at[h])

    @pl.when(pl.program_id(0) == 0)
    def _():
        lane = lax.broadcasted_iota(jnp.int32, (1, LANES), 1)
        one = jnp.where((lane >= 4) & (lane < 7), 1.0, 0.0).astype(jnp.bfloat16)
        for part in range(parts):
            hots = segment_hots(cut_ref, info_ref[5 + part] * BLOCK, kv_refs[part].shape[1], 1.0, 0.0)
            k_hot_refs[part][...] = hots + one

    q_both = jnp.concatenate([only_head(q_ref[...], h, size) for h in range(2)], axis=0)
    g_both = jnp.concatenate([only_head(g_ref[...], h, size) for h in range(2)], axis=0)
    turned = g_ref[...].T
    logs = [-lse_ref[0, h : h + 1] for h in range(2)]
    q_wide = jnp.concatenate(
        [by_head(q_ref[...].T, size), lower_rows(cut_ref, own * BLOCK, logs, (2, tokens))], axis=0
    )
    g_wide = by_head(turned, size)
    products = turned.astype(jnp.float32) * att_ref[...]
    correction = jnp.concatenate(
        [jnp.sum(products[h * size : (h + 1) * size], axis=0, keepdims=True) for h in range(2)], axis=1
    )
    tile_ref[...] = jnp.zeros_like(tile_ref)
    dq = None
    for part in range(parts):
        base = info_ref[5 + part]
        keys = kv_refs[part].shape[1]
        hots = k_hot_refs[part][...]
        raw = dot(jnp.concatenate([kv_refs[part][0], hots], axis=1), q_wide)
        pull = dot(kv_refs[part][1], g_wide)
        shares, grads, sums = [], [], {}
        for kb in range(keys // BLOCK):
            rows = slice(kb * BLOCK, (kb + 1) * BLOCK)
            tiles = [
                bias_tile_ref[h, jnp.clip(base + kb - own - qb, -FAR, FAR) + FAR]
                for h in range(2)
                for qb in range(blocks)
            ]
            probs = jnp.exp(raw[rows] + jnp.concatenate(tiles, axis=1))
            grad = probs * (pull[rows] - correction)
            shares.append(probs.astype(jnp.bfloat16))
            grads.append(grad.astype(jnp.bfloat16))
            for h in range(2):
                for qb in range(blocks):
                    start = (h * blocks + qb) * BLOCK
                    here = grad[:, start : start + BLOCK]
                    key = (h, kb - qb)
                    sums[key] = sums[key] + here if key in sums else here
        for (h, delta), tile in sums.items():
            place = jnp.clip(base - own + delta, -FAR, FAR) + FAR
            tile_ref[h, place] += tile
        shares = jnp.concatenate(shares, axis=0)
        grads = jnp.concatenate(grads, axis=0)
        dkv_refs[part][0] = dot(grads, q_both).astype(jnp.bfloat16)
        dkv_refs[part][1] = dot(shares, g_both).astype(jnp.bfloat16)
        term = dot(kv_refs[part][0].T, grads)
        dq = term if dq is None else dq + term
    dq = jnp.concatenate([dq[:size, :tokens], dq[size:, tokens:]], axis=0)
    dq_ref[...] = dq.T.astype(jnp.bfloat16)
    diagonal_sums(tile_ref, sums_ref)


def attention_backward(size, info, q, g, kvs, bias, cuts, lse, att, after):
    tokens, features = q.shape
    pairs = features // size // 2
    parts = len(kvs)
    wide = 2 * size
    by_pair = [pl.BlockSpec((2, x.shape[1], wide), lambda p: (0, 0, p)) for x in kvs]
    own = pl.BlockSpec((tokens, wide), lambda p: (0, p))
    sums = pl.BlockSpec((1, 16, 2 * BLOCK), lambda p: (p, 0, 0))
    tiles = pltpu.VMEM((2, 2 * FAR + 1, BLOCK, BLOCK), jnp.float32)
    shapes = [jax.ShapeDtypeStruct(x.shape, jnp.bfloat16) for x in kvs]
    if parts > 1:
        shapes[0] = pltpu.HBM(kvs[0].shape, jnp.bfloat16)
    result = pl.pallas_call(
        functools.partial(attention_back_kernel, parts, size),
        grid=(pairs,),
        out_shape=[pltpu.HBM(q.shape, jnp.bfloat16), *shapes]
        + [jax.ShapeDtypeStruct((pairs, 16, 2 * BLOCK), jnp.float32)],
        in_specs=[
            SMEM,
            own,
            own,
            *by_pair,
            pl.BlockSpec((3, 2, BLOCK, BLOCK), lambda p: (0, p, 0, 0)),
            SMEM,
            pl.BlockSpec((1, 8, tokens), lambda p: (p, 0, 0)),
            pl.BlockSpec((wide, tokens), lambda p: (p, 0)),
            *[ANY] * len(after),
        ],
        out_specs=[own, *by_pair, sums],
        scratch_shapes=[
            tiles,
            tiles,
            *[pltpu.VMEM((x.shape[1], LANES), jnp.bfloat16) for x in kvs],
        ],
        compiler_params=params(18),
        cost_estimate=cost(20),
        name="attention_backward",
    )(info, q, g, *kvs, bias, cuts, lse, att, *after)
    return result[0], result[1 : 1 + parts], result[-1]


def bucket_kernel(sums_ref, out_ref):
    pairs = sums_ref.shape[0]
    wide = 2 * BLOCK
    spot = lax.broadcasted_iota(jnp.int32, (wide, LANES), 1)
    entry = lax.broadcasted_iota(jnp.int32, (wide, LANES), 0)
    gap = entry - (BLOCK - 1)
    total = None
    for delta in range(5):
        if delta in (0, 2 * FAR):
            hot = jnp.where(spot == (15 if delta == 0 else 31), 1.0, 0.0)
        else:
            hot = jnp.where(spot == bucket_of((delta - FAR) * BLOCK - gap), 1.0, 0.0)
        hot = hot.astype(jnp.bfloat16)
        rows = [sums_ref[p, 5 * h + delta : 5 * h + delta + 1] for p in range(pairs) for h in range(2)]
        rows = jnp.concatenate(rows, axis=0)
        for part in split_three(rows):
            here = dot(part, hot)
            total = here if total is None else total + here
    out_ref[...] = total


def bucket_sums(sums, after):
    outs, _ = launch(
        "bucket_sums",
        bucket_kernel,
        [sums],
        [VMEM],
        [jax.ShapeDtypeStruct((2 * sums.shape[0], LANES), jnp.float32)],
        [VMEM],
        4,
        after=after,
    )
    return outs[0]


def relative_rows(me, count, src_ref, dst_ref):
    size = src_ref.shape[0] // count
    for place in range(count):
        r = 2 * (place % (count // 2)) + place // (count // 2)
        start = pl.multiple_of((me ^ r) * size, 16)
        dst_ref[place * size : (place + 1) * size] = src_ref[pl.ds(start, size), :]


def feed_kernel(
    held,
    count,
    half,
    info_ref,
    normed_ref,
    *refs,
):
    if half == 0:
        cot_refs = refs[:held]
        (
            resid_ref,
            wg_ref,
            wu_ref,
            wd_ref,
            acc_ref,
            grad_ref,
            keep_ref,
            send_ref,
            cot_ref,
            cot_turned_ref,
            normed_turned_ref,
            turned_ref,
        ) = refs[held:]
        grad_in_ref = None
    else:
        (
            resid_ref,
            grad_in_ref,
            cot_ref,
            cot_turned_ref,
            normed_turned_ref,
            wg_ref,
            wu_ref,
            wd_ref,
            *out_refs,
            grad_ref,
            keep_ref,
            send_ref,
            acc_ref,
        ) = refs
    step = pl.program_id(0)
    core = info_ref[1]
    if half == 0:
        span = cot_refs[0].shape[0]

        @pl.when(step == 0)
        def _():
            for phase in range(held):
                start = pl.multiple_of(lax.rem(info_ref[2] + held - phase, held) * span, span)
                cot_ref[pl.ds(start, span), :] = cot_refs[phase][...]
            cot_turned_ref[...] = cot_ref[...].T
            turned_ref[...] = normed_ref[...].T
            relative_rows(info_ref[0], count, turned_ref, normed_turned_ref)

    normed, cot = normed_ref[...], cot_ref[...]
    gate = dot(normed, wg_ref[...])
    up_value = dot(normed, wu_ref[...])
    grad_hidden = dot_nt(cot, wd_ref[...])
    square = gate * gate
    bend = jnp.tanh(gate * (SLOPE + (SLOPE * CUBE) * square))
    middle = 0.5 + 0.5 * bend
    gelu = gate * middle
    slope = middle * (1.0 + (1.0 - bend) * (gate * (SLOPE + (3.0 * SLOPE * CUBE) * square)))
    hidden = (gelu * up_value).astype(jnp.bfloat16)
    grad_gate = (grad_hidden * up_value * slope).astype(jnp.bfloat16)
    grad_up = (grad_hidden * gelu).astype(jnp.bfloat16)
    rb, cb = keep_ref.shape[-2:]
    chips = count // 2
    half_rows = chips * rb
    turned = normed_turned_ref[...]
    for kind, grad in enumerate((grad_gate, grad_up)):
        part = dot(turned, grad).astype(jnp.bfloat16)
        for e in range(2):
            columns = part[:, e * cb : (e + 1) * cb]
            tiles = slice((2 * kind + e) * chips, (2 * kind + e + 1) * chips)
            keep_ref[0, tiles] = columns[:half_rows].reshape(chips, rb, cb)
            send_ref[0, tiles] = columns[half_rows:].reshape(chips, rb, cb)
    part = dot(cot_turned_ref[...], hidden)
    first, second = part[:, :cb], part[:, cb:]
    mine = core == 0
    keep = jnp.where(mine, first, second).astype(jnp.bfloat16)
    send = jnp.where(mine, second, first).astype(jnp.bfloat16)
    keep_ref[0, 4 * chips :] = keep.reshape(count, rb, cb)
    send_ref[0, 4 * chips :] = send.reshape(count, rb, cb)
    result = dot(hidden, wd_ref[...])
    back = dot_nt(grad_gate, wg_ref[...]) + dot_nt(grad_up, wu_ref[...])

    @pl.when(step == 0)
    def _():
        acc_ref[...] = resid_ref[...] + result
        grad_ref[...] = back if grad_in_ref is None else grad_in_ref[...] + back

    @pl.when(step > 0)
    def _():
        acc_ref[...] += result
        grad_ref[...] += back

    if half == 1:

        @pl.when(step == pl.num_programs(0) - 1)
        def _():
            span = out_refs[0].shape[0]
            for phase in range(held):
                start = pl.multiple_of(lax.rem(info_ref[2] + held - phase, held) * span, span)
                out_refs[phase][...] = acc_ref[pl.ds(start, span), :].astype(jnp.bfloat16)


def feed_forward(half, info, normed, ins, wg, wu, wd, held, count):
    tokens, features = normed.shape
    width = wg.shape[1]
    chips = count // 2
    steps = chips // 2
    rb, cb = features // count, width // count
    whole = lambda shape: pl.BlockSpec(shape, lambda j, info: (0,) * len(shape))
    low = jnp.bfloat16
    slab = (4 * chips + count, rb, cb)
    tiles = jax.ShapeDtypeStruct((steps,) + slab, low)
    tile_spec = pl.BlockSpec((1,) + slab, lambda j, info: (j, 0, 0, 0))
    natural, turned = (tokens, features), (features, tokens)
    full = jax.ShapeDtypeStruct(natural, jnp.float32)
    shapes = [full, tiles, tiles]
    specs = [whole(natural), tile_spec, tile_spec]
    if half == 0:
        shapes, specs = [full] + shapes, [whole(natural)] + specs
    else:
        span = (tokens // held, features)
        shapes = [jax.ShapeDtypeStruct(span, low)] * held + shapes
        specs = [whole(span)] * held + specs
    scratch = [pltpu.VMEM(natural, jnp.float32)]
    if half == 0:
        shapes += [
            jax.ShapeDtypeStruct(natural, low),
            jax.ShapeDtypeStruct(turned, low),
            jax.ShapeDtypeStruct(turned, low),
        ]
        specs += [whole(natural), whole(turned), whole(turned)]
        scratch = [pltpu.VMEM(turned, low)]
    return pl.pallas_call(
        functools.partial(feed_kernel, held, count, half),
        grid_spec=pltpu.PrefetchScalarGridSpec(
            num_scalar_prefetch=1,
            grid=(steps,),
            in_specs=[
                whole(normed.shape),
                *[whole(x.shape) for x in ins],
                pl.BlockSpec((features, 2 * cb), lambda j, info: (0, j + half * steps)),
                pl.BlockSpec((features, 2 * cb), lambda j, info: (0, j + half * steps)),
                pl.BlockSpec((2 * cb, features), lambda j, info: (j + half * steps, 0)),
            ],
            out_specs=specs,
            scratch_shapes=scratch,
        ),
        out_shape=shapes,
        compiler_params=params(28),
        cost_estimate=cost(11),
        name=f"feed_forward_{half}",
    )(info, normed, *ins, wg, wu, wd)


def between_kernel(
    count,
    info_ref,
    grad_ref,
    resid_ref,
    gain_ref,
    cot_ref,
    att_ref,
    wm_ref,
    *refs,
):
    (
        out_hbm_ref,
        att_grad_ref,
        keep_hbm_ref,
        send_ref,
        gain_grad_ref,
        turned_ref,
        low_ref,
        out_ref,
        keep_ref,
        sems,
    ) = refs[-10:]
    features = resid_ref.shape[1]
    resid = resid_ref[...]
    root = lax.rsqrt(jnp.sum(resid * resid, axis=1, keepdims=True) / features + EPS)
    grad = grad_ref[...]
    unit = resid * root
    gain_grad_ref[...] = jnp.sum(grad * unit, axis=0, keepdims=True)
    pulled = grad * row_of(gain_ref)
    mean = jnp.sum(unit * pulled, axis=1, keepdims=True) / features
    result = cot_ref[...].astype(jnp.float32) + root * (pulled - unit * mean)
    out_ref[...] = result
    copies = [
        pltpu.make_async_copy(out_ref, out_hbm_ref, sems.at[0]),
        pltpu.make_async_copy(keep_ref, keep_hbm_ref, sems.at[1]),
    ]
    copies[0].start()
    mixed = result.astype(jnp.bfloat16)
    low_ref[...] = att_ref[...].astype(jnp.bfloat16)
    relative_rows(info_ref[0], count, low_ref, turned_ref)
    part = dot(turned_ref[...], mixed).astype(jnp.bfloat16)
    half = features // 2
    keep_ref[...] = part[:half].reshape(keep_ref.shape)
    copies[1].start()
    send_ref[...] = part[half:].reshape(send_ref.shape)
    att_grad_ref[...] = dot_nt(mixed, wm_ref[...]).astype(jnp.bfloat16)
    for copy in copies:
        copy.wait()


def between(info, grad, resid, gain, cot, att, wm, count, after, carry):
    tokens, features = grad.shape
    rb = features // count
    low = jnp.bfloat16
    piece = jax.ShapeDtypeStruct((count // 2, rb, features), low)
    ins = [info, grad, resid, gain, cot, att, wm]
    return launch(
        "between",
        functools.partial(between_kernel, count),
        ins,
        [SMEM] + [VMEM] * 6,
        [
            pltpu.HBM((tokens, features), jnp.float32),
            jax.ShapeDtypeStruct((tokens, features), low),
            pltpu.HBM(piece.shape, low),
            piece,
            jax.ShapeDtypeStruct((1, features), jnp.float32),
        ],
        [HBM, VMEM, HBM, VMEM, VMEM],
        16,
        [
            pltpu.VMEM((features, tokens), low),
            pltpu.VMEM((features, tokens), low),
            pltpu.VMEM((tokens, features), jnp.float32),
            pltpu.VMEM(piece.shape, low),
            pltpu.SemaphoreType.DMA((2,)),
        ],
        after=after,
        carry=carry,
        microseconds=3,
    )


def project_q_kernel(
    count,
    info_ref,
    dq_ref,
    normed_ref,
    wq_ref,
    other_ref,
    keep_ref,
    send_ref,
    back_ref,
    turned_ref,
    plain_ref,
):
    plain_ref[...] = normed_ref[...].T
    relative_rows(info_ref[0], count, plain_ref, turned_ref)
    dq = dq_ref[...]
    part = dot(turned_ref[...], dq).astype(jnp.bfloat16)
    half = part.shape[0] // 2
    keep_ref[...] = part[:half].reshape(keep_ref.shape)
    send_ref[0] = part[half:].reshape(send_ref.shape[1:])
    send_ref[1] = other_ref[...]
    back_ref[...] = dot_nt(dq, wq_ref[...])


def project_q(info, dq, normed, wq, other, count, after, carry):
    tokens, features = dq.shape
    low = jnp.bfloat16
    piece = jax.ShapeDtypeStruct((count // 2, features // count, features), low)
    return launch(
        "project_q",
        functools.partial(project_q_kernel, count),
        [info, dq, normed, wq, other],
        [SMEM] + [VMEM] * 4,
        [
            piece,
            jax.ShapeDtypeStruct((2,) + piece.shape, low),
            jax.ShapeDtypeStruct((tokens, features), jnp.float32),
            jax.ShapeDtypeStruct((features, tokens), low),
        ],
        [VMEM] * 4,
        14,
        [pltpu.VMEM((features, tokens), low)],
        after=after,
        carry=carry,
    )


def project_kv_kernel(
    mine_ref,
    got_ref,
    turned_ref,
    back_ref,
    stream_ref,
    grad_ref,
    gain_ref,
    wk_ref,
    wv_ref,
    keep_ref,
    send_ref,
    out_ref,
    gain_grad_ref,
):
    features = stream_ref.shape[1]
    half = features // 2
    total = back_ref[...]
    for i, w_ref in enumerate((wk_ref, wv_ref)):
        grad = mine_ref[i] + got_ref[i]
        part = dot(turned_ref[...], grad).astype(jnp.bfloat16)
        keep_ref[i] = part[:half].reshape(keep_ref.shape[1:])
        send_ref[i] = part[half:].reshape(send_ref.shape[1:])
        total = total + dot_nt(grad, w_ref[...])
    stream = stream_ref[...]
    root = lax.rsqrt(jnp.sum(stream * stream, axis=1, keepdims=True) / features + EPS)
    unit = stream * root
    gain_grad_ref[...] = jnp.sum(total * unit, axis=0, keepdims=True)
    pulled = total * row_of(gain_ref)
    mean = jnp.sum(unit * pulled, axis=1, keepdims=True) / features
    out_ref[...] = grad_ref[...] + root * (pulled - unit * mean)


def project_kv(mine, got, turned, back, stream, grad, gain, wk, wv, count, after):
    tokens, features = stream.shape
    piece = jax.ShapeDtypeStruct((2, count // 2, features // count, features), jnp.bfloat16)
    outs, _ = launch(
        "project_kv",
        project_kv_kernel,
        [mine, got, turned, back, stream, grad, gain, wk, wv],
        [VMEM] * 9,
        [piece] * 2
        + [
            jax.ShapeDtypeStruct((tokens, features), jnp.float32),
            jax.ShapeDtypeStruct((1, features), jnp.float32),
        ],
        [VMEM] * 4,
        18,
        after=after,
    )
    return outs


def pick_of(pairs, info_ref):
    def tile(pair, at):
        if callable(at):
            at = at(info_ref)
        first, second = at if isinstance(at, tuple) else (at, at)
        return pairs[pair][0][first] + pairs[pair][1][second]

    def value(pick):
        if len(pick) == 2:
            return tile(*pick)
        return jnp.where(info_ref[7] == 0, tile(*pick[:2]), tile(*pick[2:]))

    return value


def tiles_of(pairs):
    return [tuple(x.reshape((-1,) + x.shape[-2:]) for x in pair) for pair in pairs]


def fold(name, info, pairs, picks, after=(), carry=()):
    pairs = tiles_of(pairs)
    shape = pairs[0][0].shape[1:]

    def kernel(info_ref, *refs):
        ins, outs = refs[: 2 * len(pairs)], refs[2 * len(pairs) :]
        value = pick_of([ins[2 * i : 2 * i + 2] for i in range(len(pairs))], info_ref)
        for out_ref, chosen in zip(outs, picks):
            for slot, pick in enumerate(chosen):
                out_ref[slot] = value(pick)

    return launch(
        name,
        kernel,
        [info, *sum(pairs, ())],
        [SMEM] + [VMEM] * (2 * len(pairs)),
        [jax.ShapeDtypeStruct((len(chosen),) + shape, jnp.bfloat16) for chosen in picks],
        [VMEM] * len(picks),
        16,
        after=after,
        carry=carry,
    )


def lane_tiles(width):
    whole = width // LANES
    rest = width - whole * LANES
    return whole, rest, LANES // rest if rest else 1


def tile_count(pieces, width):
    whole, rest, each = lane_tiles(width)
    return pieces * whole + (-(-pieces // each) if rest else 0)


def pack_lanes(pieces):
    width = pieces[0].shape[1]
    whole, rest, each = lane_tiles(width)
    tiles = [piece[:, i * LANES : (i + 1) * LANES] for piece in pieces for i in range(whole)]
    if rest:
        ends = [piece[:, whole * LANES :] for piece in pieces]
        for i in range(0, len(ends), each):
            group = ends[i : i + each]
            spare = LANES - rest * len(group)
            if spare:
                group = group + [jnp.zeros((group[0].shape[0], spare), group[0].dtype)]
            tiles.append(jnp.concatenate(group, axis=1))
    return tiles


def unpack_lanes(tiles, pieces, width):
    whole, rest, each = lane_tiles(width)
    result = []
    for piece in range(pieces):
        parts = [tiles[piece * whole + i] for i in range(whole)]
        if rest:
            tile = tiles[pieces * whole + piece // each]
            start = piece % each * rest
            parts.append(tile[:, start : start + rest])
        result.append(jnp.concatenate(parts, axis=1) if len(parts) > 1 else parts[0])
    return result


def fold_seq(name, info, pairs, picks, seqs, slots, groups, width=None, after=(), carry=()):
    pairs = tiles_of(pairs)
    tall, wide = pairs[0][0].shape[1:]
    shape = (tall, LANES if width else wide)

    def kernel(info_ref, *refs):
        ins, outs, scratch_ref = refs[: 2 * len(pairs)], refs[2 * len(pairs) : -1], refs[-1]
        value = pick_of([ins[2 * i : 2 * i + 2] for i in range(len(pairs))], info_ref)
        here = info_ref[8]
        if width is None:
            for pick, block, slot in picks:
                scratch_ref[block ^ here, slot] = value(pick)
        else:
            totals = [value(pick) for pick, _, _ in sorted(picks, key=lambda x: x[2])]
            for s in range(seqs):
                pieces = [total[:, s * width : (s + 1) * width] for total in totals]
                for slot, tile in enumerate(pack_lanes(pieces)):
                    scratch_ref[s ^ here, slot] = tile
        for out_ref, group in zip(outs, groups):
            for i, d in enumerate(group):
                out_ref[i * slots : (i + 1) * slots] = scratch_ref[d]

    return launch(
        name,
        kernel,
        [info, *sum(pairs, ())],
        [SMEM] + [VMEM] * (2 * len(pairs)),
        [jax.ShapeDtypeStruct((len(group) * slots,) + shape, jnp.bfloat16) for group in groups],
        [VMEM] * len(groups),
        16,
        [pltpu.VMEM((seqs, slots) + shape, jnp.bfloat16)],
        after=after,
        carry=carry,
    )


def summed(refs, at):
    terms = [ref[at].astype(jnp.float32) for ref in refs]
    while len(terms) > 1:
        terms = [terms[i] + terms[i + 1] for i in range(0, len(terms), 2)]
    return terms[0]


def feed_end_kernel(seqs, *refs):
    ins, (gate_ref, up_ref, down_ref) = refs[:seqs], refs[seqs:]
    slots, rb, cb = ins[0].shape
    each = slots // 3
    for q in range(each):
        gate_ref[:, q * cb : (q + 1) * cb] = summed(ins, q)
        up_ref[:, q * cb : (q + 1) * cb] = summed(ins, each + q)
    for q in range(each):
        down_ref[q * rb : (q + 1) * rb] = summed(ins, 2 * each + q)


def feed_end(ins, after):
    slots, rb, cb = ins[0].shape
    each = slots // 3
    wide = pltpu.HBM((rb, each * cb), jnp.float32)
    return pl.pallas_call(
        ordered(functools.partial(feed_end_kernel, len(ins)), len(ins), after),
        out_shape=[wide, wide, pltpu.HBM((each * rb, cb), jnp.float32)],
        in_specs=[VMEM] * len(ins) + [ANY] * len(after),
        out_specs=[AUTO] * 3,
        compiler_params=params(8),
        cost_estimate=cost(1),
        name="feed_end",
    )(*ins, *after)


def join_kernel(info_ref, *refs):
    held = len(refs) - 1
    for phase in range(held):
        refs[held][lax.rem(info_ref[8] + phase, held)] = refs[phase][...]


def join(info, parts, after):
    shape = (len(parts),) + parts[0].shape
    outs, _ = launch(
        "join",
        join_kernel,
        [info, *parts],
        [SMEM] + [VMEM] * len(parts),
        [pltpu.HBM(shape, parts[0].dtype)],
        [AUTO],
        8,
        after=after,
    )
    return outs[0]


def mix_end_kernel(width, seqs, *refs):
    outs = refs[seqs:]
    tiles = [summed(refs[:seqs], slot) for slot in range(refs[0].shape[0])]
    for out_ref, value in zip(outs, unpack_lanes(tiles, len(outs), width)):
        out_ref[...] = value


def mix_end(ins, pieces, width, after):
    outs, _ = launch(
        "mix_end",
        functools.partial(mix_end_kernel, width, len(ins)),
        ins,
        [VMEM] * len(ins),
        [pltpu.HBM((ins[0].shape[1], width), jnp.float32)] * pieces,
        [AUTO] * pieces,
        8,
        after=after,
    )
    return outs


def sum_kernel(count, *refs):
    refs[count][...] = summed(refs[:count], slice(None)).astype(jnp.bfloat16)


def sum_of(name, terms, after):
    return pl.pallas_call(
        ordered(functools.partial(sum_kernel, len(terms)), len(terms), after),
        out_shape=jax.ShapeDtypeStruct(terms[0].shape, jnp.bfloat16),
        in_specs=[VMEM] * len(terms) + [ANY] * len(after),
        out_specs=VMEM,
        compiler_params=params(8),
        cost_estimate=cost(1),
        name=name,
    )(*terms, *after)


def unpack_kernel(vocab, chips, info_ref, *refs):
    shares = refs[: 2 * chips]
    embed_ref, filter_ref, score_ref, first_ref, second_ref, bias_ref, whole_ref = refs[2 * chips :]
    share = shares[0].shape[1]
    me = info_ref[0]
    for place in range(chips):
        for odd in range(2):
            start = pl.multiple_of((me ^ (2 * place + odd)) * share, 16)
            whole_ref[pl.ds(start, share), :] = shares[odd * chips + place][0].astype(jnp.float32)
    embed_ref[...] = whole_ref[:vocab]
    filter_ref[...] = whole_ref[vocab : vocab + 4]
    for i, ref in enumerate((score_ref, first_ref, second_ref)):
        ref[...] = whole_ref[vocab + 4 + i, :]
    heads, buckets = bias_ref.shape
    bias_ref[...] = whole_ref[vocab + 7 : vocab + 7 + heads, :buckets]


def unpack(info, mine, others, vocab, buckets, heads, after):
    chips = len(mine)
    _, share, features = mine[0].shape
    full = lambda *shape: pltpu.HBM(shape, jnp.float32)
    return pl.pallas_call(
        ordered(functools.partial(unpack_kernel, vocab, chips), 1 + 2 * chips, after),
        out_shape=[
            full(vocab, features),
            full(4, features),
            full(features),
            full(features),
            full(features),
            full(heads, buckets),
        ],
        in_specs=[SMEM] + [VMEM] * (2 * chips) + [ANY] * len(after),
        out_specs=[AUTO] * 6,
        scratch_shapes=[pltpu.VMEM((2 * chips * share, features), jnp.float32)],
        compiler_params=params(8),
        cost_estimate=cost(1),
        name="unpack",
    )(info, *mine, *others, *after)


AXES = ("batch", "seq")


def across_cores(x):
    count = lax.axis_size("batch")
    return lax.ppermute(x, "batch", [(i, i ^ 1) for i in range(count)])


def across_chips(x, chip):
    count = lax.axis_size("batch")
    return lax.ppermute(x, "batch", [(i, i ^ (2 * chip)) for i in range(count)])


def across_seq(x, d):
    count = lax.axis_size("seq")
    return lax.ppermute(x, "seq", [(i, i ^ d) for i in range(count)])


class Halving:
    def __init__(self, pairs, where):
        self.pairs, self.where = pairs, where

    def split(self, chosen, bit):
        keys = [key for key in self.where if chosen(key)]
        keep = [key for key in keys if not key[-1] & (1 << bit)]
        send = [key[:-1] + (key[-1] | (1 << bit),) for key in keep]
        return keep, send

    def picks(self, keys):
        return [self.where[key] for key in keys]


def exchange(name, info, state, plans, after=(), carry=(), held_back=False):
    lists, kept = [], []
    for chosen, bit in plans:
        keep, send = state.split(chosen, bit)
        kept.append(keep)
        lists += [state.picks(keep), state.picks(send)]
    outs, carried = fold(name, info, state.pairs, lists, after, carry)

    def start(sends):
        pairs, where = [], {}
        for place, ((_, bit), keep) in enumerate(zip(plans, kept)):
            pairs.append((outs[2 * place], across_chips(sends[place], 1 << bit)))
            where.update({key: (place, slot) for slot, key in enumerate(keep)})
        return Halving(pairs, where)

    return start if held_back else start(outs[1::2]), outs, carried


class Plan:
    def __init__(self, held):
        self.count = lax.axis_size("batch")
        self.seqs = lax.axis_size("seq")
        self.held = held
        self.group = self.seqs // (2 * held)
        me = lax.axis_index("batch")
        place = lax.axis_index("seq")
        self.me, self.place = me, place
        self.core = me % 2
        self.row = place // self.group
        self.part = 2 * (place % self.group) + self.core
        self.parts = 2 * self.group
        self.perms = []
        for phase in range(held):
            perm = []
            for b in range(self.count):
                for s in range(self.seqs):
                    row = held * (b % 2) + (s + phase) % held
                    part = s // held
                    target = (b - b % 2 + part % 2, self.group * row + part // 2)
                    perm.append((b * self.seqs + s, target[0] * self.seqs + target[1]))
            self.perms.append(perm)

    def blocks_of(self, x):
        return [
            lax.dynamic_index_in_dim(x, (self.place + phase) % self.held, 0, keepdims=False)
            for phase in range(self.held)
        ]

    def parts_of(self, x):
        return [lax.ppermute(x, AXES, perm) for x, perm in zip(self.blocks_of(x), self.perms)]

    def bytes_of(self, x):
        held = self.held
        main = self.parts_of(x)
        ends = jnp.concatenate([x[:, :4], x[:, -4:]], axis=1)
        sides = []
        for phase in range(held):
            perm = []
            for b in range(self.count):
                for s in range(self.seqs):
                    row = held * (b % 2) + (s + phase) % held
                    part = s // held + {0: -1, held - 1: 1}.get(s % held, self.parts)
                    if 0 <= part < self.parts:
                        target = (b - b % 2 + part % 2, self.group * row + part // 2)
                        perm.append((b * self.seqs + s, target[0] * self.seqs + target[1]))
            send = lax.dynamic_index_in_dim(ends, (self.place + phase) % held, 0, keepdims=False)
            sides.append(lax.ppermute(send, AXES, perm))
        low = lax.dynamic_index_in_dim(
            jnp.stack(sides), (self.row + 1) % held, 0, keepdims=False
        )[4:]
        high = lax.dynamic_index_in_dim(jnp.stack(sides), self.row % held, 0, keepdims=False)[:4]
        low = jnp.where(self.part > 0, low, -1)
        high = jnp.where(self.part < self.parts - 1, high, -1)
        order = (self.row - jnp.arange(held)) % held
        middle = jnp.take(jnp.stack(main), order, axis=0).reshape(-1)
        return jnp.concatenate([low, middle, high]).reshape(-1, 4)

    def gather(self, x):
        other = across_cores(x)
        pair = jnp.stack([jnp.where(self.core == 0, x, other), jnp.where(self.core == 0, other, x)])
        if self.group > 1:
            groups = [
                list(range(first, first + self.group))
                for first in range(0, self.seqs, self.group)
            ]
            pair = lax.all_gather(pair, "seq", axis_index_groups=groups)
        return pair.reshape((-1,) + x.shape[1:])

    def scatter(self, x):
        if self.group > 1:
            groups = [
                list(range(first, first + self.group))
                for first in range(0, self.seqs, self.group)
            ]
            x = lax.psum_scatter(
                x, "seq", scatter_dimension=0, axis_index_groups=groups, tiled=True
            )
        pair = x.reshape((2, -1) + x.shape[1:])
        got = across_cores(lax.dynamic_index_in_dim(pair, 1 - self.core, 0, keepdims=False))
        mine = lax.dynamic_index_in_dim(pair, self.core, 0, keepdims=False)
        return mine.astype(jnp.float32) + got.astype(jnp.float32)


def shards(
    byte_values,
    segments,
    byte_mask,
    embedding,
    filter_weight,
    score_weight,
    first_gain,
    query_weight,
    key_weight,
    value_weight,
    merge_weight,
    position_bias,
    second_gain,
    gate_weight,
    up_weight,
    down_weight,
    cotangent,
):
    count = lax.axis_size("batch")
    seqs = lax.axis_size("seq")
    held, width = byte_values.shape
    row_len = segments.shape[1]
    vocab, features = embedding.shape
    hidden_size = gate_weight.shape[1]
    heads = position_bias.shape[1]
    bucket_count = position_bias.shape[0]
    total = row_len // 2
    plan = Plan(held)
    tokens = total // plan.parts
    chips = count // 2
    levels = chips.bit_length() - 1
    blocks = tokens // BLOCK
    other_part = plan.part ^ 1

    bases = [plan.part * blocks, other_part * blocks] if plan.group == 1 else [0, 0]
    info = jnp.stack(
        [
            jnp.asarray(value, jnp.int32)
            for value in (
                plan.me,
                plan.core,
                plan.row % held,
                plan.part * blocks,
                plan.part * 2 * tokens,
                bases[0],
                bases[1],
                plan.me // chips,
                plan.place,
            )
        ]
    )
    ids = plan.bytes_of(jnp.where(byte_mask > 0, byte_values, -1))
    ids = jnp.pad(ids, ((MAIN - 1, MAIN - 1), (0, 0)), constant_values=-1)
    cuts = jnp.sum((segments[:, :, None] < jnp.arange(1, 4)).astype(jnp.int32), axis=1)
    cuts = (cuts + 1) // 2
    both = jnp.concatenate([cuts, across_cores(cuts)])
    own_first = jnp.where(plan.row // held == plan.core, 0, held)
    cuts = lax.dynamic_index_in_dim(both, own_first + plan.row % held, 0, keepdims=False)
    bias = hbm(bias_tiles(position_bias.T))
    embedding, filter_weight, score_weight = map(hbm, (embedding, filter_weight, score_weight))
    first_gain, second_gain = hbm(first_gain), hbm(second_gain)
    query_weight, key_weight, value_weight = map(hbm, (query_weight, key_weight, value_weight))
    merge_weight = hbm(merge_weight)
    head_size = features // heads
    words = -(-(vocab + 7 + heads) // (16 * count)) * (16 * count)
    stream, normed, q, kv = mixer_forward(
        info,
        ids,
        embedding,
        filter_weight,
        score_weight,
        first_gain,
        query_weight,
        key_weight,
        value_weight,
        tokens,
        row_len,
        [],
    )
    normed, stream = hbm(normed), hbm(stream)
    ends = (stream, merge_weight, second_gain)
    cot_blocks = plan.blocks_of(cotangent)
    if plan.group == 1:
        kvs = [kv, across_cores(kv)]
        begun, later = attention_forward(
            "attention_own", head_size, info, q, kvs[0], bias, cuts, carry=cot_blocks[1:]
        )
        (att, lse, resid, normed_two), _ = attention_forward(
            "attention_other", head_size, info, q, kvs[1], bias, cuts, begun, ends
        )
    else:
        kvs = [jnp.stack([plan.gather(kv[0]), plan.gather(kv[1])])]
        later = cot_blocks[1:]
        (att, lse, resid, normed_two), _ = attention_forward(
            "attention_all", head_size, info, q, kvs[0], bias, cuts, (), ends
        )
    cots = [lax.ppermute(x, AXES, perm) for x, perm in zip([cot_blocks[0], *later], plan.perms)]

    weights = (gate_weight, up_weight, down_weight)
    acc, grad_two, *grads, cot, cot_turned, normed_turned = feed_forward(
        0, info, normed_two, [*cots, resid], *weights, held, count
    )
    halves = [grads]
    *results, grad_two, keep, send = feed_forward(
        1,
        info,
        normed_two,
        [acc, grad_two, cot, cot_turned, normed_turned],
        *weights,
        held,
        count,
    )
    halves.append([keep, send])
    early = count // 4

    def upwards(key):
        return key[0] == "down" or key[3] < early

    def downwards(key):
        return not upwards(key)

    states = []

    def start_half(half, after):
        keep, send = halves[half]
        pairs = [(keep, across_cores(send))]
        steps = chips // 2
        slab = 4 * chips + count
        where = {}
        for r in range(chips):
            for n in range(count):
                kind, block = n // chips, n % chips
                place = block // 2 * slab + (2 * kind + block % 2) * chips + r
                where["gu", half, 0, n, r] = (0, place)

        def down_at(r, n):
            return lambda info: (r ^ lax.rem(info[0] // 2, steps)) * slab + 4 * chips + n

        for r in range(steps):
            for n in range(count):
                where["down", half, 0, n, r] = (0, down_at(r, n))
        state = Halving(pairs, where)
        first = None
        for level in range(levels - 1):
            state, outs, _ = exchange(
                f"feed_{half}_{level}",
                info,
                state,
                [(upwards, level), (downwards, levels - 1 - level)],
                after if level == 0 else (),
            )
            first = first or outs
        states.append(state)
        return first

    back_perms = [[(b, a) for a, b in perm] for perm in plan.perms]
    out_parts = [lax.ppermute(x, AXES, perm) for x, perm in zip(results, back_perms)]
    first = start_half(0, [grad_two])
    (grad_resid, att_grad, m_keep, m_send, second_part), _ = between(
        info, grad_two, resid, second_gain, cot, att, merge_weight, count, [first[0]], []
    )
    first = start_half(1, [second_part])
    dq, dkvs, tiles = attention_backward(
        head_size, info, hbm(q), att_grad, [hbm(kvs[0]), *kvs[1:]], bias, cuts, lse, att, [first[0]]
    )

    where = {}
    for half, state in enumerate(states):
        for key, (pair, slot) in state.where.items():
            where[key] = (2 * half + pair, slot)
    top = 1 << (levels - 1)
    for key in [key for key in where if key[0] == "down"]:
        _, half, kind, n, r = key
        mine, other = where["down", 0, 0, n, 0], where["down", 1, 0, n, 0]
        if half == 0:
            where["one", 2, 0, n, 0] = mine + other
            where["one", 2, 0, n, top] = other + mine
    where = {key: value for key, value in where.items() if key[0] != "down"}
    state = Halving(states[0].pairs + states[1].pairs, where)
    crossing = [dkvs[1]] if plan.group == 1 else []
    state, lasts, crossing = exchange(
        "feed_last",
        info,
        state,
        [
            (lambda key: key[0] == "one" or key[3] < early, levels - 1),
            (lambda key: key[0] == "gu" and key[3] >= early, 0),
        ],
        [hbm(dq), out_parts[0]],
        crossing,
    )
    if plan.group == 1:
        mine, got = hbm(dkvs[0]), across_cores(crossing[0])
    else:
        mine = jnp.stack([plan.scatter(dkvs[0][i]).astype(jnp.bfloat16) for i in range(2)])
        got = jnp.zeros_like(mine)
    bias_part = bucket_sums(tiles, [lasts[0]])
    (q_keep, qm_send, back, turned), later = project_q(
        info, hbm(dq), normed, query_weight, m_send, count, [bias_part], []
    )
    qm_got = across_cores(qm_send)
    kv_keep, kv_send, grad_stream, first_part = project_kv(
        mine,
        got,
        turned,
        back,
        stream,
        hbm(grad_resid),
        first_gain,
        key_weight,
        value_weight,
        count,
        [],
    )

    each = count // seqs
    picks = []
    for key, pick in state.where.items():
        if key[0] == "one":
            picks.append((pick, key[3] // each, 2 * each + key[3] % each))
        else:
            kind, block = key[3] // chips, key[1] * chips + key[3] % chips
            picks.append((pick, block // each, kind * each + block % each))
    slots = 3 * each
    groups = [list(range(0, seqs, 2)), list(range(1, seqs, 2))]
    (z_keep, z_send), (kv_send,) = fold_seq(
        "feed_seq", info, state.pairs, picks, seqs, slots, groups, after=[first_part, *out_parts[1:]], carry=[kv_send]
    )
    kv_got = across_cores(kv_send)
    z_got = across_seq(z_send, 1)
    where = {}
    for r in range(chips):
        where["p", 0, r] = (0, r)
        where["p", 3, r] = (1, (r, chips + r))
        for kind in (1, 2):
            where["p", kind, r] = (2, (kind - 1) * chips + r)
    mixes = Halving([(q_keep, qm_got), (hbm(m_keep), qm_got), (kv_keep, kv_got)], where)

    def mix_step(mixes, level, after, carry=(), held_back=False):
        return exchange(
            f"mix_{level}",
            info,
            mixes,
            [
                (lambda key: key[1] in (1, 3), level),
                (lambda key: key[1] in (0, 2), levels - 1 - level),
            ],
            after,
            carry,
            held_back,
        )

    layer_output = join(info, out_parts, [z_keep])
    mixes, outs, _ = mix_step(mixes, 0, [hbm(layer_output)])
    e_keep, e_send = mixer_backward(
        info,
        ids,
        embedding,
        filter_weight,
        score_weight,
        grad_stream,
        first_part,
        second_part,
        bias_part,
        row_len,
        vocab,
        words,
        count,
        [z_keep, outs[0]],
    )

    def seq_step(name, z_keep, z_got, slots, step, after, carry):
        held_now = z_keep.shape[0] // slots
        lists = [
            [(0, d * slots + i) for d in range(first, held_now, 2) for i in range(slots)]
            for first in range(2)
        ]
        (z_keep, z_send), carried = fold(
            f"{name}_seq_{step}", info, [(z_keep, z_got)], lists, after, carry
        )
        return z_keep, across_seq(z_send, step), carried

    last, step, carry = e_keep, 2, [e_send]
    while step < seqs:
        z_keep, z_got, carry = seq_step("feed", z_keep, z_got, slots, step, [last], carry)
        last = z_keep
        step *= 2
    for level in range(1, levels):
        mixes, outs, _ = mix_step(mixes, level, [last], (), level == levels - 1)
        last = outs[0]
    e_got = across_cores(carry[0])
    small = Halving([(e_keep, e_got)], {("e", r): (0, r) for r in range(chips)})
    sends = outs[1::2]
    for level in range(levels):
        small, outs, sends = exchange(
            f"small_{level}",
            info,
            small,
            [(lambda key: True, level)],
            [last] if level == 0 else [],
            sends if level == 0 else [],
        )
        if level == 0:
            mixes = mixes(sends)
    (share,), _ = fold("small_chips", info, small.pairs, [small.picks([("e", 0)])])
    share_got = across_seq(share, 1)
    picks = [(pick, None, key[1]) for key, pick in mixes.where.items()]
    gate_grad, up_grad, down_grad = feed_end([z_keep, z_got], [share])
    share_width = features // seqs
    mix_sends, _ = fold_seq(
        "mix_seq",
        info,
        mixes.pairs,
        picks,
        seqs,
        tile_count(4, share_width),
        [[d] for d in range(seqs)],
        share_width,
        after=[hbm(gate_grad)],
    )
    mix_arrived = [mix_sends[0]] + [across_seq(mix_sends[d], d) for d in range(1, seqs)]
    distance = 1
    while distance < seqs:
        share = sum_of(f"small_seq_{distance}", [share, share_got], [mix_sends[0]])
        distance *= 2
        if distance < seqs:
            share_got = across_seq(share, distance)
    shares = [share] + [across_chips(share, r) for r in range(1, chips)]
    query_grad, key_grad, value_grad, merge_grad = mix_end(mix_arrived, 4, share_width, [share])
    embed, filters, score, first, second, bias_sum = unpack(
        info, shares, [across_cores(x) for x in shares], vocab, bucket_count, heads, [hbm(query_grad)]
    )
    return (
        layer_output,
        embed,
        filters,
        score,
        first,
        query_grad,
        key_grad,
        value_grad,
        merge_grad,
        bias_sum.T,
        second,
        gate_grad,
        up_grad,
        down_grad.T,
    )


def solution(mesh):
    in_specs = (
        P("batch", "seq"),
        P("batch", None),
        P("batch", "seq"),
        P(),
        P(),
        P(),
        P(),
        P(),
        P(),
        P(),
        P(),
        P(),
        P(),
        P(),
        P(),
        P(),
        P("batch", "seq", None),
    )
    out_specs = (
        P("batch", "seq", None),
        P(),
        P(),
        P(),
        P(),
        P("batch", "seq"),
        P("batch", "seq"),
        P("batch", "seq"),
        P("batch", "seq"),
        P(),
        P(),
        P("batch", "seq"),
        P("batch", "seq"),
        P("batch", "seq"),
    )
    return jax.shard_map(shards, mesh=mesh, in_specs=in_specs, out_specs=out_specs, check_vma=False)
```

```python
import functools

import jax
import jax.numpy as jnp
from jax import lax
from jax.experimental import pallas as pl
from jax.experimental.pallas import tpu as pltpu
from jax.sharding import PartitionSpec as P

EPS = 1e-06
LIMITS = (12, 16, 23, 32, 46, 64, 91)
NEG = -1e30
LANES = 128
BLOCK = 128
FAR = 2
CUBE = 0.044715
SLOPE = 0.7978845608028654
MEGA = 1 << 20


def dot(a, b):
    return lax.dot_general(a, b, (((1,), (0,)), ((), ())), preferred_element_type=jnp.float32)


def dot_nt(a, b):
    return lax.dot_general(a, b, (((1,), (1,)), ((), ())), preferred_element_type=jnp.float32)


def params(megabytes):
    return pltpu.CompilerParams(vmem_limit_bytes=megabytes * MEGA)


def cost(microseconds):
    return pl.CostEstimate(flops=int(microseconds * 1e+09), bytes_accessed=1, transcendentals=0)


VMEM = pl.BlockSpec(memory_space=pltpu.VMEM)
ANY = pl.BlockSpec(memory_space=pl.ANY)
HBM = pl.BlockSpec(memory_space=pltpu.HBM)
AUTO = pl.BlockSpec()
SMEM = pl.BlockSpec(memory_space=pltpu.SMEM)


def hbm(x):
    return pltpu.with_memory_space_constraint(x, pltpu.HBM)


def ordered(kernel, inputs, after):
    def with_others(*refs):
        kernel(*refs[:inputs], *refs[inputs + len(after) :])

    return with_others


def launch(name, kernel, ins, in_specs, outs, out_specs, megabytes, scratch=(), after=(), carry=(), microseconds=1.0
):
    given, made = len(ins), len(outs)
    skip = len(after) + len(carry)

    def body(*refs):
        rest = refs[given + skip :]
        kernel(*refs[:given], *rest[:made], *rest[made + len(carry) :])

    results = pl.pallas_call(
        body,
        out_shape=[*outs, *[jax.ShapeDtypeStruct(x.shape, x.dtype) for x in carry]],
        in_specs=[*in_specs, *[ANY] * skip],
        out_specs=[*out_specs, *[ANY] * len(carry)],
        scratch_shapes=list(scratch),
        input_output_aliases={given + len(after) + i: made + i for i in range(len(carry))},
        compiler_params=params(megabytes),
        cost_estimate=cost(microseconds),
        name=name,
    )(*ins, *after, *carry)
    return results[:made], results[made:]


def bucket_of(relative):
    distance = jnp.abs(relative)
    far = jnp.full_like(distance, 8)
    for limit in LIMITS:
        far = far + jnp.where(distance >= limit, 1, 0)
    return jnp.where(distance < 8, distance, far) + jnp.where(relative > 0, 16, 0)


def split_three(x):
    parts = []
    for _ in range(3):
        high = x.astype(jnp.bfloat16)
        parts.append(high)
        x = x - high.astype(jnp.float32)
    return parts


def bias_kernel(table_ref, out_ref, tile_ref, sems):
    copies = []
    heads, buckets = table_ref.shape
    wide = 2 * BLOCK
    parts = split_three(table_ref[...])
    bucket = lax.broadcasted_iota(jnp.int32, (buckets, wide), 0)
    entry = lax.broadcasted_iota(jnp.int32, (buckets, wide), 1)
    gap = jnp.where(entry < BLOCK, entry, entry - wide)
    for delta in range(3):
        hot = jnp.where(bucket_of((delta - 1) * BLOCK - gap) == bucket, 1.0, 0.0)
        hot = hot.astype(jnp.bfloat16)
        rows = (dot(parts[2], hot) + dot(parts[1], hot)) + dot(parts[0], hot)
        for h in range(heads):
            row = jnp.broadcast_to(rows[h : h + 1], (BLOCK, wide))
            tile_ref[delta, h] = pltpu.roll(row, 0, 1, stride=1, stride_axis=0)[:, :BLOCK]
        copies.append(pltpu.make_async_copy(tile_ref.at[delta], out_ref.at[delta], sems.at[delta]))
        copies[-1].start()
    for copy in copies:
        copy.wait()


def bias_tiles(table, after, carry):
    return launch(
        "bias_tiles",
        bias_kernel,
        [table],
        [VMEM],
        [pltpu.HBM((3, table.shape[0], BLOCK, BLOCK), jnp.float32)],
        [HBM],
        6,
        [
            pltpu.VMEM((3, table.shape[0], BLOCK, BLOCK), jnp.float32),
            pltpu.SemaphoreType.DMA((3,)),
        ],
        after=after,
        carry=carry,
        microseconds=2,
    )


def fill_tiles(near_ref, h, tile_ref):
    for delta in range(3):
        tile_ref[1 + delta] = near_ref[delta, h]
    tile_ref[0] = jnp.broadcast_to(near_ref[0, h, :1, BLOCK - 1 :], (BLOCK, BLOCK))
    tile_ref[4] = jnp.broadcast_to(near_ref[2, h, BLOCK - 1 :, :1], (BLOCK, BLOCK))


def by_head(turned, size):
    empty = jnp.zeros((size, turned.shape[1]), turned.dtype)
    left = jnp.concatenate([turned[:size], empty], axis=0)
    right = jnp.concatenate([empty, turned[size:]], axis=0)
    return jnp.concatenate([left, right], axis=1)


def lower_rows(cut_ref, start, rows, heads):
    count = rows[0].shape[1] if rows else heads[1]
    place = start + lax.broadcasted_iota(jnp.int32, (16, count), 1)
    row = lax.broadcasted_iota(jnp.int32, (16, count), 0)
    segment = sum(jnp.where(place >= cut_ref[i], 1, 0) for i in range(3))
    mask = jnp.where((row < 4) & (segment != row), NEG, 0.0)
    blocks = []
    for head in range(heads[0]):
        block = mask
        if rows:
            for i, part in enumerate(split_three(rows[head])):
                block = jnp.where(row == 4 + i, part.astype(jnp.float32), block)
        blocks.append(block.astype(jnp.bfloat16))
    block = jnp.concatenate(blocks, axis=1)
    return jnp.concatenate([block, jnp.zeros((LANES - 16, block.shape[1]), jnp.bfloat16)], axis=0)


def segment_hots(cut_ref, start, count, inside, outside):
    place = start + lax.broadcasted_iota(jnp.int32, (count, LANES), 0)
    lane = lax.broadcasted_iota(jnp.int32, (count, LANES), 1)
    segment = sum(jnp.where(place >= cut_ref[i], 1, 0) for i in range(3))
    value = jnp.where(segment == lane, inside, outside)
    return jnp.where(lane < 4, value, 0.0).astype(jnp.bfloat16)


TILE = 32
FORWARD_TILE = 64
GUARD = 8
MAIN = 24


def row_of(ref):
    return ref[...].reshape(1, -1)


def tile_rows(base, size=TILE):
    return pl.ds(pl.multiple_of(base, 8), size)


def with_sides(ref, lead, base, lanes, size=TILE):
    return ref[(*lead, pl.ds(pl.multiple_of(base - 8, 8), size + 16), lanes)]


def middle(x):
    return x[8:-8]


def down(x):
    return middle(pltpu.roll(x, 1, 0))


def up(x):
    return middle(pltpu.roll(x, x.shape[0] - 1, 0))


def lane_sum(x):
    return jnp.broadcast_to(jnp.sum(x, axis=1, keepdims=True), x.shape)


def offsets_of(rows):
    return {
        -2: down(rows[2]),
        -1: down(rows[3]),
        0: middle(rows[0]),
        1: middle(rows[1]),
        2: middle(rows[2]),
        3: middle(rows[3]),
        4: up(rows[0]),
        5: up(rows[1]),
    }


def spread_of(phase, j, one, two, three, four, coefs):
    pair = j - j % 2
    third = three / 3.0
    zero = jnp.zeros_like(third)
    half, quarter = two * 0.5, four * 0.25

    def add(o, value):
        coefs[o] = coefs[o] + value if o in coefs else value

    add(j, one + third)
    for o in (pair, pair + 1):
        add(o, half)
    for o in range(4):
        add(o, quarter)
    add(j + 1, jnp.where(phase <= 1, third, zero))
    add(j + 2, jnp.where(phase == 0, third, zero))
    add(j - 1, jnp.where(phase >= 1, third, zero))
    add(j - 2, jnp.where(phase == 2, third, zero))


def pooled_dots(phase, j, dots):
    pair = j - j % 2
    zero = jnp.zeros_like(dots[0])
    two = 0.5 * (dots[pair] + dots[pair + 1])
    four = 0.25 * ((dots[0] + dots[1]) + (dots[2] + dots[3]))
    three = dots[j] + jnp.where(phase <= 1, dots[j + 1], zero)
    three = three + jnp.where(phase == 0, dots[j + 2], zero)
    three = three + jnp.where(phase >= 1, dots[j - 1], zero)
    three = three + jnp.where(phase == 2, dots[j - 2], zero)
    return dots[j], two, three / 3.0, four


def lane_chunks(features):
    return [slice(i, i + LANES) for i in range(0, features, LANES)]


def over_tiles(first, rows, body, size=TILE):
    def step(t, carry):
        body(first + t * size)
        return carry

    lax.fori_loop(0, rows // size, step, 0)


def convolve_all(info_ref, ids_ref, emb_ref, filt_ref, score_ref, e_ref, c_ref, dot_ref, row_len):
    count = ids_ref.shape[0]
    words, features = emb_ref.shape
    score = row_of(score_ref)
    group = info_ref[4] // 4
    vocab = lax.broadcasted_iota(jnp.int32, (count, words), 1)
    edge = jnp.zeros((GUARD, LANES), jnp.float32)
    for j in range(4):
        hot = jnp.where(ids_ref[:, j : j + 1] == vocab, 1.0, 0.0).astype(jnp.bfloat16)
        e_ref[j] = dot(hot, emb_ref[...])
        dot_ref[j, :GUARD] = edge
        dot_ref[j, count - GUARD :] = edge

    def tile(base):
        parts = [jnp.zeros((TILE, LANES), jnp.float32) for _ in range(4)]
        for lanes in lane_chunks(features):
            near = offsets_of([with_sides(e_ref, (j,), base, lanes) for j in range(4)])
            taps = [filt_ref[k : k + 1, lanes] for k in range(4)]
            for j in range(4):
                value = taps[0] * near[j - 2]
                for k in range(1, 4):
                    value = value + taps[k] * near[j + k - 2]
                c_ref[j, tile_rows(base), lanes] = value
                parts[j] = parts[j] + value * score[:, lanes]
        places = base - MAIN + group + lax.broadcasted_iota(jnp.int32, (TILE, LANES), 0)
        for j in range(4):
            inside = 4 * places + j < row_len
            dot_ref[j, tile_rows(base)] = jnp.where(inside, lane_sum(parts[j]), 0.0)

    over_tiles(GUARD, count - 2 * GUARD, tile)


def tile_weights(info_ref, dot_ref, base, row_len, size):
    dots = offsets_of([with_sides(dot_ref, (j,), base, slice(None), size) for j in range(4)])
    places = base - MAIN + info_ref[4] // 4
    places = places + lax.broadcasted_iota(jnp.int32, (size, LANES), 0)
    phases, weights = [], []
    for j in range(4):
        phase = lax.rem(places + 3 + j, 3)
        scores = pooled_dots(phase, j, dots)
        highest = jnp.maximum(jnp.maximum(scores[0], scores[1]), jnp.maximum(scores[2], scores[3]))
        powers = [jnp.exp(score - highest) for score in scores]
        share = 1.0 / ((powers[0] + powers[1]) + (powers[2] + powers[3]))
        phases.append(phase)
        weights.append([power * share for power in powers])
    limits = {o: (4 * places + o < row_len) for o in (4, 5)}
    return phases, weights, limits


def token_coefs(phases, weights, limits, scale):
    result = []
    for h in range(2):
        coefs = {}
        for j in (2 * h, 2 * h + 1):
            spread_of(phases[j], j, *weights[j], coefs)
        for o in coefs:
            if o in limits:
                coefs[o] = jnp.where(limits[o], coefs[o], 0.0)
            coefs[o] = coefs[o] * scale
        result.append(coefs)
    return result


COEFS = [(0, o) for o in range(-2, 4)] + [(1, o) for o in range(6)]


def mixer_kernel(
    row_len,
    info_ref,
    ids_ref,
    emb_ref,
    filt_ref,
    score_ref,
    gain_ref,
    wq_ref,
    wk_ref,
    wv_ref,
    stream_out_ref,
    normed_out_ref,
    q_ref,
    kv_ref,
    e_ref,
    c_ref,
    dot_ref,
    pair_ref,
    root_ref,
    weight_ref,
    sems,
    stream_ref,
    normed_ref,
):
    copies = [
        pltpu.make_async_copy(w_ref, weight_ref.at[i], sems.at[i])
        for i, w_ref in enumerate((wk_ref, wv_ref, wq_ref))
    ]
    for copy in copies:
        copy.start()
    tokens, features = stream_ref.shape
    gain = row_of(gain_ref)
    chunks = lane_chunks(features)
    convolve_all(
        info_ref, ids_ref, emb_ref, filt_ref, score_ref, e_ref, c_ref, dot_ref, row_len
    )

    size = pair_ref.shape[1] // 2

    def tile(base):
        coefs = token_coefs(*tile_weights(info_ref, dot_ref, base, row_len, size), 0.5)
        squares = [jnp.zeros((size, LANES), jnp.float32) for _ in range(2)]
        rows = pl.ds(pl.multiple_of(2 * (base - MAIN), 2 * size), 2 * size)
        for i, lanes in enumerate(chunks):
            conv = offsets_of([with_sides(c_ref, (j,), base, lanes, size) for j in range(4)])
            for h in range(2):
                mixed = None
                for o, coef in coefs[h].items():
                    term = coef * conv[o]
                    mixed = term if mixed is None else mixed + term
                squares[h] = squares[h] + mixed * mixed
                pair_ref[i, pl.ds(h, size, stride=2), :] = mixed
        for h in range(2):
            root = lax.rsqrt(lane_sum(squares[h]) / features + EPS)
            root_ref[pl.ds(h, size, stride=2), :] = root
        for i, lanes in enumerate(chunks):
            stream = pair_ref[i]
            stream_ref[rows, lanes] = stream
            normed = stream * root_ref[...] * gain[:, lanes]
            normed_ref[rows, lanes] = normed.astype(jnp.bfloat16)

    over_tiles(MAIN, tokens // 2, tile, size)
    kept = [
        pltpu.make_async_copy(stream_ref, stream_out_ref, sems.at[3]),
        pltpu.make_async_copy(normed_ref, normed_out_ref, sems.at[4]),
    ]
    for copy in kept:
        copy.start()
    for i in range(2):
        copies[i].wait()
        kv_ref[i] = dot(normed_ref[...], weight_ref[i]).astype(jnp.bfloat16)
    copies[2].wait()
    q_ref[...] = dot(normed_ref[...], weight_ref[2]).astype(jnp.bfloat16)
    for copy in kept:
        copy.wait()


def mixer_forward(info, ids, emb, filt, score, gain, wq, wk, wv, tokens, row_len, after):
    features = emb.shape[1]
    count = ids.shape[0]
    low = jnp.bfloat16
    full = jnp.float32
    outs, _ = launch(
        "mixer_forward",
        functools.partial(mixer_kernel, row_len),
        [info, ids, emb, filt, score, gain, wq, wk, wv],
        [SMEM] + [VMEM] * 5 + [HBM] * 3,
        [
            pltpu.HBM((tokens, features), full),
            pltpu.HBM((tokens, features), low),
            jax.ShapeDtypeStruct((tokens, features), low),
            jax.ShapeDtypeStruct((2, tokens, features), low),
        ],
        [HBM, HBM, VMEM, VMEM],
        24,
        [
            pltpu.VMEM((4, count, features), full),
            pltpu.VMEM((4, count, features), full),
            pltpu.VMEM((4, count, LANES), full),
            pltpu.VMEM((features // LANES, 2 * FORWARD_TILE, LANES), full),
            pltpu.VMEM((2 * FORWARD_TILE, LANES), full),
            pltpu.VMEM((3, features, features), low),
            pltpu.SemaphoreType.DMA((5,)),
            pltpu.VMEM((tokens, features), full),
            pltpu.VMEM((tokens, features), low),
        ],
        after=after,
        microseconds=8,
    )
    return outs


def mixer_back_kernel(
    row_len,
    vocab_size,
    info_ref,
    ids_ref,
    emb_ref,
    filt_ref,
    score_ref,
    grad_ref,
    first_ref,
    second_ref,
    bias_ref,
    keep_ref,
    send_ref,
    e_ref,
    c_ref,
    dot_ref,
    coef_ref,
    g_ref,
    low_ref,
    turn_ref,
    embed_ref,
    small_ref,
):
    tokens, features = grad_ref.shape
    groups = tokens // 2
    chunks = lane_chunks(features)
    count = ids_ref.shape[0]
    inner = count - 2 * GUARD
    score_row = row_of(score_ref)
    convolve_all(
        info_ref, ids_ref, emb_ref, filt_ref, score_ref, e_ref, c_ref, dot_ref, row_len
    )
    before = jnp.zeros((MAIN, LANES), jnp.float32)
    behind = jnp.zeros((count - MAIN - groups, LANES), jnp.float32)
    for i, lanes in enumerate(chunks):
        turn_ref[i] = grad_ref[:, lanes]
        for h in range(2):
            g_ref[h, :MAIN, lanes] = before
            g_ref[h, MAIN + groups :, lanes] = behind
            g_ref[h, MAIN : MAIN + groups, lanes] = turn_ref[i, pl.ds(h, groups, stride=2), :]
    for place in range(2 * len(COEFS)):
        coef_ref[place, :MAIN] = before
        coef_ref[place, MAIN + groups :] = behind
    small_ref[...] = jnp.zeros_like(small_ref)

    def pull_tile(base):
        phases, weights, limits = tile_weights(info_ref, dot_ref, base, row_len, TILE)
        coefs = token_coefs(phases, weights, limits, 0.5)
        sums = {}
        for lanes in chunks:
            conv = offsets_of([with_sides(c_ref, (j,), base, lanes) for j in range(4)])
            grads = [g_ref[h, tile_rows(base), lanes] for h in range(2)]
            for h, o in COEFS:
                term = grads[h] * conv[o]
                sums[h, o] = sums[h, o] + term if (h, o) in sums else term
        pulls = []
        for h in range(2):
            dots = {}
            for side, o in COEFS:
                if side == h:
                    value = lane_sum(sums[h, o]) * 0.5
                    dots[o] = jnp.where(limits[o], value, 0.0) if o in limits else value
            for j in (2 * h, 2 * h + 1):
                grads = pooled_dots(phases[j], j, dots)
                mean = sum(weights[j][i] * grads[i] for i in range(4))
                pulls.append([weights[j][i] * (grads[i] - mean) for i in range(4)])
        score_coefs = token_coefs(phases, pulls, limits, 1.0)
        for place, (h, o) in enumerate(COEFS):
            coef_ref[place, tile_rows(base)] = coefs[h][o]
            coef_ref[len(COEFS) + place, tile_rows(base)] = score_coefs[h][o]

    over_tiles(MAIN, groups, pull_tile)

    def fold_rows(x):
        return sum(x[i : i + 8] for i in range(0, TILE, 8))

    def grad_tile(base):
        def coef(h, o, score=False):
            return with_sides(coef_ref, (COEFS.index((h, o)) + len(COEFS) * score,), base, slice(None))

        own = [[middle(coef(h, j)) for j in range(4)] for h in range(2)]
        side = [down(coef(1, 4 + j)) if j < 2 else up(coef(0, j - 4)) for j in range(4)]
        kappa = []
        for j in range(4):
            far = down(coef(1, 4 + j, True)) if j < 2 else up(coef(0, j - 4, True))
            kappa.append(middle(coef(0, j, True)) + middle(coef(1, j, True)) + far)
        for lanes in chunks:
            first, second = (with_sides(g_ref, (h,), base, lanes) for h in range(2))
            above, below = down(second), up(first)
            first, second = middle(first), middle(second)
            near = offsets_of([with_sides(e_ref, (j,), base, lanes) for j in range(4)])
            score = score_row[:, lanes]
            taps = [None] * 4
            score_sum = None
            for j in range(4):
                value = own[0][j] * first + own[1][j] * second
                value = value + side[j] * (above if j < 2 else below) + kappa[j] * score
                term = kappa[j] * c_ref[j, tile_rows(base), lanes]
                score_sum = term if score_sum is None else score_sum + term
                c_ref[j, tile_rows(base), lanes] = value
                for k in range(4):
                    term = value * near[j + k - 2]
                    taps[k] = term if taps[k] is None else taps[k] + term
            for k in range(4):
                small_ref[k, :, lanes] += fold_rows(taps[k])
            small_ref[4, :, lanes] += fold_rows(score_sum)

    over_tiles(GUARD, inner, grad_tile)
    edge = jnp.zeros((GUARD, features), jnp.float32)
    for j in range(4):
        c_ref[j, :GUARD] = edge
        c_ref[j, count - GUARD :] = edge

    def back_tile(base):
        start = pl.multiple_of(base - GUARD, TILE)
        for lanes in chunks:
            d = offsets_of([with_sides(c_ref, (j,), base, lanes) for j in range(4)])
            taps = [filt_ref[k : k + 1, lanes] for k in range(4)]
            for j in range(4):
                value = taps[0] * d[j + 2]
                for k in range(1, 4):
                    value = value + taps[k] * d[j + 2 - k]
                low_ref[pl.ds(j * inner + start, TILE), lanes] = value.astype(jnp.bfloat16)

    over_tiles(GUARD, inner, back_tile)
    lane = lax.broadcasted_iota(jnp.int32, (inner, LANES), 1)
    spread = jnp.zeros((inner, LANES), jnp.float32)
    for j in range(4):
        ids = ids_ref[GUARD : GUARD + inner, j : j + 1].astype(jnp.float32)
        spread = jnp.where(lane == j, ids, spread)
    spare = jnp.zeros((-inner % LANES, LANES), jnp.float32)
    turned = jnp.concatenate([spread, spare], axis=0).T.astype(jnp.int32)
    flat = jnp.concatenate([turned[j : j + 1, :inner] for j in range(4)], axis=1)
    words = -(-vocab_size // 16) * 16
    vocab = lax.broadcasted_iota(jnp.int32, (words, 4 * inner), 0)
    hot = jnp.where(flat == vocab, 1.0, 0.0).astype(jnp.bfloat16)
    embed_ref[:words] = dot(hot, low_ref[...])
    embed_ref[words:] = jnp.zeros((embed_ref.shape[0] - words, features), jnp.float32)
    for i in range(5):
        embed_ref[vocab_size + i : vocab_size + i + 1] = jnp.sum(small_ref[i], axis=0, keepdims=True)
    embed_ref[vocab_size + 5 : vocab_size + 6] = first_ref[...]
    embed_ref[vocab_size + 6 : vocab_size + 7] = second_ref[...]
    heads = bias_ref.shape[0]
    embed_ref[vocab_size + 7 : vocab_size + 7 + heads, :LANES] = bias_ref[...]
    share = keep_ref.shape[1]
    chips = keep_ref.shape[0]
    me = info_ref[0]
    for place in range(chips):
        for odd, out_ref in enumerate((keep_ref, send_ref)):
            start = pl.multiple_of((me ^ (2 * place + odd)) * share, 16)
            out_ref[place] = embed_ref[pl.ds(start, share), :].astype(jnp.bfloat16)


def mixer_backward(
    info, ids, emb, filt, score, grad, first, second, bias, row_len, vocab, embed_rows, devices, after
):
    tokens, features = grad.shape
    count = ids.shape[0]
    full = jnp.float32
    piece = jax.ShapeDtypeStruct((devices // 2, embed_rows // devices, features), jnp.bfloat16)
    outs, _ = launch(
        "mixer_backward",
        functools.partial(mixer_back_kernel, row_len, vocab),
        [info, ids, emb, filt, score, grad, first, second, bias],
        [SMEM] + [VMEM] * 8,
        [piece, piece],
        [VMEM] * 2,
        26,
        [
            pltpu.VMEM((4, count, features), full),
            pltpu.VMEM((4, count, features), full),
            pltpu.VMEM((4, count, LANES), full),
            pltpu.VMEM((2 * len(COEFS), count, LANES), full),
            pltpu.VMEM((2, count, features), full),
            pltpu.VMEM((4 * (count - 2 * GUARD), features), jnp.bfloat16),
            pltpu.VMEM((features // LANES, tokens, LANES), full),
            pltpu.VMEM((embed_rows, features), full),
            pltpu.VMEM((5, 8, features), full),
        ],
        after=after,
        microseconds=11,
    )
    return outs


def scores_of(info_ref, part, raw, tile_ref):
    keys, tokens = raw.shape
    base, own = info_ref[part], info_ref[3]
    rows = []
    for kb in range(keys // BLOCK):
        tiles = [
            tile_ref[jnp.clip(base + kb - own - qb, -FAR, FAR) + FAR]
            for qb in range(tokens // BLOCK)
        ]
        rows.append(raw[kb * BLOCK : (kb + 1) * BLOCK] + jnp.concatenate(tiles, axis=1))
    return rows


def only_head(x, h, size):
    lane = lax.broadcasted_iota(jnp.int32, x.shape, 1)
    return jnp.where((lane >= h * size) & (lane < (h + 1) * size), x, jnp.zeros_like(x))


def attention_kernel(
    size,
    carried,
    last,
    info_ref,
    q_ref,
    kv_ref,
    bias_ref,
    cut_ref,
    *refs,
):
    if last:
        *refs, plain_ref, weight_ref, sems = refs
    *refs, tile_ref, q_low_ref, k_hot_ref = refs
    if carried:
        before_ref, state_ref, *refs = refs
    if last:
        stream_ref, wm_ref, gain_ref, att_ref, lse_ref, resid_ref, normed_ref = refs
    else:
        mixed_ref, stat_ref = refs
    step = pl.program_id(0)
    part = 5 + carried
    low = []
    tokens = q_ref.shape[0]

    @pl.when(step == 0)
    def _():
        q_low_ref[...] = lower_rows(cut_ref, info_ref[3] * BLOCK, [], (2, tokens))
        k_hot_ref[...] = segment_hots(cut_ref, info_ref[part] * BLOCK, kv_ref.shape[1], 1.0, 0.0)

    both = jnp.concatenate([by_head(q_ref[...].T, size), q_low_ref[...]], axis=0)
    raws = dot(jnp.concatenate([kv_ref[0], k_hot_ref[...]], axis=1), both)
    turned = kv_ref[1].T
    ones = jnp.ones((16, turned.shape[1]), jnp.bfloat16)
    for h in range(2):
        fill_tiles(bias_ref, h, tile_ref.at[h])
    for h in range(2):
        raw = raws[:, h * tokens : (h + 1) * tokens]
        rows = scores_of(info_ref, part, raw, tile_ref.at[h])
        highest = None
        for row in rows:
            top = jnp.max(row, axis=0, keepdims=True)
            highest = top if highest is None else jnp.maximum(highest, top)
        if carried:
            highest = jnp.maximum(highest, state_ref[0, h : h + 1])
        weights = jnp.concatenate([jnp.exp(row - highest).astype(jnp.bfloat16) for row in rows], axis=0)
        mixed = dot(jnp.concatenate([turned[h * size : (h + 1) * size], ones], axis=0), weights)
        mixed, summed = mixed[:size], mixed[size : size + 1]
        if carried:
            shrink = jnp.exp(state_ref[0, h : h + 1] - highest)
            summed = summed + state_ref[0, 2 + h : 3 + h] * shrink
            mixed = mixed + before_ref[h * size : (h + 1) * size] * shrink
        if last:
            lse_ref[0, h : h + 1] = highest + jnp.log(summed)
            low.append(mixed * (1.0 / summed))
        else:
            stat_ref[0, h : h + 1] = highest
            stat_ref[0, 2 + h : 3 + h] = summed
            mixed_ref[h * size : (h + 1) * size] = mixed
    if not last:
        return
    features = stream_ref.shape[1]
    turned = jnp.concatenate(low, axis=0)
    att_ref[...] = turned
    plain_ref[step] = turned.T.astype(jnp.bfloat16)
    copies = [
        pltpu.make_async_copy(wm_ref, weight_ref, sems.at[0]),
        pltpu.make_async_copy(stream_ref, resid_ref, sems.at[1]),
    ]

    @pl.when(step == 0)
    def _():
        for copy in copies:
            copy.start()

    @pl.when(step == pl.num_programs(0) - 1)
    def _():
        for copy in copies:
            copy.wait()
        attended = jnp.concatenate([plain_ref[p] for p in range(plain_ref.shape[0])], axis=1)
        resid = resid_ref[...] + dot(attended, weight_ref[...])
        resid_ref[...] = resid
        root = lax.rsqrt(jnp.sum(resid * resid, axis=1, keepdims=True) / features + EPS)
        normed_ref[...] = (resid * root * row_of(gain_ref)).astype(jnp.bfloat16)


def attention_forward(name, size, info, q, kv, bias, cuts, carried=(), last=(), carry=()):
    tokens, features = q.shape
    heads = features // size
    pairs = heads // 2
    wide = 2 * size
    whole = lambda shape: pl.BlockSpec(shape, lambda p: (0,) * len(shape))
    by_rows = pl.BlockSpec((wide, tokens), lambda p: (p, 0))
    stat = pl.BlockSpec((1, 8, tokens), lambda p: (p, 0, 0))
    stat_shape = jax.ShapeDtypeStruct((pairs, 8, tokens), jnp.float32)
    ins = [info, q, kv, bias, cuts, *carried, *last]
    in_specs = [
        SMEM,
        pl.BlockSpec((tokens, wide), lambda p: (0, p)),
        pl.BlockSpec((2, kv.shape[1], wide), lambda p: (0, 0, p)),
        pl.BlockSpec((3, 2, BLOCK, BLOCK), lambda p: (0, p, 0, 0)),
        SMEM,
    ]
    if carried:
        in_specs += [by_rows, stat]
    if last:
        stream, wm, gain = last
        in_specs += [
            HBM,
            HBM,
            whole(gain.shape),
        ]
        shapes = [
            jax.ShapeDtypeStruct((features, tokens), jnp.float32),
            stat_shape,
            jax.ShapeDtypeStruct((tokens, features), jnp.float32),
            jax.ShapeDtypeStruct((tokens, features), jnp.bfloat16),
        ]
        out_specs = [by_rows, stat, whole((tokens, features)), whole((tokens, features))]
    else:
        shapes = [jax.ShapeDtypeStruct((features, tokens), jnp.float32), stat_shape]
        out_specs = [by_rows, stat]
    merging = [
        pltpu.VMEM((pairs, tokens, wide), jnp.bfloat16),
        pltpu.VMEM((features, features), jnp.bfloat16),
        pltpu.SemaphoreType.DMA((2,)),
    ]
    kernel = functools.partial(attention_kernel, size, int(bool(carried)), bool(last))
    made = len(shapes)

    def body(*refs):
        rest = refs[len(ins) + len(carry) :]
        kernel(*refs[: len(ins)], *rest[:made], *rest[made + len(carry) :])

    results = pl.pallas_call(
        body,
        grid=(pairs,),
        out_shape=[*shapes, *[jax.ShapeDtypeStruct(x.shape, x.dtype) for x in carry]],
        in_specs=in_specs + [ANY] * len(carry),
        out_specs=[*out_specs, *[ANY] * len(carry)],
        input_output_aliases={len(ins) + i: made + i for i in range(len(carry))},
        scratch_shapes=[
            pltpu.VMEM((2, 2 * FAR + 1, BLOCK, BLOCK), jnp.float32),
            pltpu.VMEM((LANES, 2 * tokens), jnp.bfloat16),
            pltpu.VMEM((kv.shape[1], LANES), jnp.bfloat16),
            *(merging if last else []),
        ],
        compiler_params=params(12),
        cost_estimate=cost(9),
        name=name,
    )(*ins, *carry)
    return results[:made], results[made:]


def diagonal_sums(tile_ref, sums_ref):
    wide = 2 * BLOCK
    row = lax.broadcasted_iota(jnp.int32, (BLOCK, BLOCK), 0)
    column = lax.broadcasted_iota(jnp.int32, (BLOCK, BLOCK), 1)
    flip = jnp.where(row + column == BLOCK - 1, 1.0, 0.0).astype(jnp.bfloat16)
    near = jnp.concatenate([tile_ref[h, 1 + delta] for h in range(2) for delta in range(3)], axis=1)
    high = near.astype(jnp.bfloat16)
    rest = (near - high.astype(jnp.float32)).astype(jnp.bfloat16)
    flipped = dot(flip, high) + dot(flip, rest)
    empty = jnp.zeros((BLOCK, BLOCK), jnp.float32)
    for h in range(2):
        for delta in range(3):
            start = (3 * h + delta) * BLOCK
            padded = jnp.concatenate([flipped[:, start : start + BLOCK], empty], axis=1)
            slid = pltpu.roll(padded, 0, 1, stride=1, stride_axis=0)
            place = 5 * h + 1 + delta
            sums_ref[0, place : place + 1] = jnp.sum(slid, axis=0, keepdims=True)
        for far in (0, 2 * FAR):
            place = 5 * h + far
            total = jnp.sum(tile_ref[h, far], axis=0, keepdims=True)
            sums_ref[0, place : place + 1] = jnp.concatenate([total, empty[:1]], axis=1)


def attention_back_kernel(
    parts,
    size,
    info_ref,
    q_ref,
    g_ref,
    *refs,
):
    kv_refs = refs[:parts]
    bias_ref, cut_ref, lse_ref, att_ref = refs[parts : parts + 4]
    dq_ref, *dkv_refs, sums_ref, bias_tile_ref, tile_ref = refs[-4 - 2 * parts : len(refs) - parts]
    k_hot_refs = refs[len(refs) - parts :]
    tokens = q_ref.shape[0]
    blocks = tokens // BLOCK
    own = info_ref[3]
    for h in range(2):
        fill_tiles(bias_ref, h, bias_tile_ref.at[h])

    @pl.when(pl.program_id(0) == 0)
    def _():
        lane = lax.broadcasted_iota(jnp.int32, (1, LANES), 1)
        one = jnp.where((lane >= 4) & (lane < 7), 1.0, 0.0).astype(jnp.bfloat16)
        for part in range(parts):
            hots = segment_hots(cut_ref, info_ref[5 + part] * BLOCK, kv_refs[part].shape[1], 1.0, 0.0)
            k_hot_refs[part][...] = hots + one

    q_both = jnp.concatenate([only_head(q_ref[...], h, size) for h in range(2)], axis=0)
    g_both = jnp.concatenate([only_head(g_ref[...], h, size) for h in range(2)], axis=0)
    turned = g_ref[...].T
    logs = [-lse_ref[0, h : h + 1] for h in range(2)]
    q_wide = jnp.concatenate(
        [by_head(q_ref[...].T, size), lower_rows(cut_ref, own * BLOCK, logs, (2, tokens))], axis=0
    )
    g_wide = by_head(turned, size)
    products = turned.astype(jnp.float32) * att_ref[...]
    correction = jnp.concatenate(
        [jnp.sum(products[h * size : (h + 1) * size], axis=0, keepdims=True) for h in range(2)], axis=1
    )
    tile_ref[...] = jnp.zeros_like(tile_ref)
    dq = None
    for part in range(parts):
        base = info_ref[5 + part]
        keys = kv_refs[part].shape[1]
        hots = k_hot_refs[part][...]
        raw = dot(jnp.concatenate([kv_refs[part][0], hots], axis=1), q_wide)
        pull = dot(kv_refs[part][1], g_wide)
        shares, grads, sums = [], [], {}
        for kb in range(keys // BLOCK):
            rows = slice(kb * BLOCK, (kb + 1) * BLOCK)
            tiles = [
                bias_tile_ref[h, jnp.clip(base + kb - own - qb, -FAR, FAR) + FAR]
                for h in range(2)
                for qb in range(blocks)
            ]
            probs = jnp.exp(raw[rows] + jnp.concatenate(tiles, axis=1))
            grad = probs * (pull[rows] - correction)
            shares.append(probs.astype(jnp.bfloat16))
            grads.append(grad.astype(jnp.bfloat16))
            for h in range(2):
                for qb in range(blocks):
                    start = (h * blocks + qb) * BLOCK
                    here = grad[:, start : start + BLOCK]
                    key = (h, kb - qb)
                    sums[key] = sums[key] + here if key in sums else here
        for (h, delta), tile in sums.items():
            place = jnp.clip(base - own + delta, -FAR, FAR) + FAR
            tile_ref[h, place] += tile
        shares = jnp.concatenate(shares, axis=0)
        grads = jnp.concatenate(grads, axis=0)
        dkv_refs[part][0] = dot(grads, q_both).astype(jnp.bfloat16)
        dkv_refs[part][1] = dot(shares, g_both).astype(jnp.bfloat16)
        term = dot(kv_refs[part][0].T, grads)
        dq = term if dq is None else dq + term
    dq = jnp.concatenate([dq[:size, :tokens], dq[size:, tokens:]], axis=0)
    dq_ref[...] = dq.T.astype(jnp.bfloat16)
    diagonal_sums(tile_ref, sums_ref)


def attention_backward(size, info, q, g, kvs, bias, cuts, lse, att, after):
    tokens, features = q.shape
    pairs = features // size // 2
    parts = len(kvs)
    wide = 2 * size
    by_pair = [pl.BlockSpec((2, x.shape[1], wide), lambda p: (0, 0, p)) for x in kvs]
    own = pl.BlockSpec((tokens, wide), lambda p: (0, p))
    sums = pl.BlockSpec((1, 16, 2 * BLOCK), lambda p: (p, 0, 0))
    tiles = pltpu.VMEM((2, 2 * FAR + 1, BLOCK, BLOCK), jnp.float32)
    shapes = [jax.ShapeDtypeStruct(x.shape, jnp.bfloat16) for x in kvs]
    if parts > 1:
        shapes[0] = pltpu.HBM(kvs[0].shape, jnp.bfloat16)
    result = pl.pallas_call(
        functools.partial(attention_back_kernel, parts, size),
        grid=(pairs,),
        out_shape=[pltpu.HBM(q.shape, jnp.bfloat16), *shapes]
        + [jax.ShapeDtypeStruct((pairs, 16, 2 * BLOCK), jnp.float32)],
        in_specs=[
            SMEM,
            own,
            own,
            *by_pair,
            pl.BlockSpec((3, 2, BLOCK, BLOCK), lambda p: (0, p, 0, 0)),
            SMEM,
            pl.BlockSpec((1, 8, tokens), lambda p: (p, 0, 0)),
            pl.BlockSpec((wide, tokens), lambda p: (p, 0)),
            *[ANY] * len(after),
        ],
        out_specs=[own, *by_pair, sums],
        scratch_shapes=[
            tiles,
            tiles,
            *[pltpu.VMEM((x.shape[1], LANES), jnp.bfloat16) for x in kvs],
        ],
        compiler_params=params(18),
        cost_estimate=cost(20),
        name="attention_backward",
    )(info, q, g, *kvs, bias, cuts, lse, att, *after)
    return result[0], result[1 : 1 + parts], result[-1]


def bucket_kernel(sums_ref, out_ref):
    pairs = sums_ref.shape[0]
    wide = 2 * BLOCK
    spot = lax.broadcasted_iota(jnp.int32, (wide, LANES), 1)
    entry = lax.broadcasted_iota(jnp.int32, (wide, LANES), 0)
    gap = entry - (BLOCK - 1)
    total = None
    for delta in range(5):
        if delta in (0, 2 * FAR):
            hot = jnp.where(spot == (15 if delta == 0 else 31), 1.0, 0.0)
        else:
            hot = jnp.where(spot == bucket_of((delta - FAR) * BLOCK - gap), 1.0, 0.0)
        hot = hot.astype(jnp.bfloat16)
        rows = [sums_ref[p, 5 * h + delta : 5 * h + delta + 1] for p in range(pairs) for h in range(2)]
        rows = jnp.concatenate(rows, axis=0)
        for part in split_three(rows):
            here = dot(part, hot)
            total = here if total is None else total + here
    out_ref[...] = total


def bucket_sums(sums, after):
    outs, _ = launch(
        "bucket_sums",
        bucket_kernel,
        [sums],
        [VMEM],
        [jax.ShapeDtypeStruct((2 * sums.shape[0], LANES), jnp.float32)],
        [VMEM],
        4,
        after=after,
    )
    return outs[0]


def relative_rows(me, count, src_ref, dst_ref):
    size = src_ref.shape[0] // count
    for place in range(count):
        r = 2 * (place % (count // 2)) + place // (count // 2)
        start = pl.multiple_of((me ^ r) * size, 16)
        dst_ref[place * size : (place + 1) * size] = src_ref[pl.ds(start, size), :]


def feed_kernel(
    held,
    count,
    half,
    info_ref,
    normed_ref,
    *refs,
):
    if half == 0:
        cot_refs = refs[:held]
        (
            resid_ref,
            wg_ref,
            wu_ref,
            wd_ref,
            acc_ref,
            grad_ref,
            keep_ref,
            send_ref,
            cot_ref,
            cot_turned_ref,
            normed_turned_ref,
            turned_ref,
        ) = refs[held:]
        grad_in_ref = None
    else:
        (
            resid_ref,
            grad_in_ref,
            cot_ref,
            cot_turned_ref,
            normed_turned_ref,
            wg_ref,
            wu_ref,
            wd_ref,
            *out_refs,
            grad_ref,
            keep_ref,
            send_ref,
            acc_ref,
        ) = refs
    step = pl.program_id(0)
    core = info_ref[1]
    if half == 0:
        span = cot_refs[0].shape[0]

        @pl.when(step == 0)
        def _():
            for phase in range(held):
                start = pl.multiple_of(lax.rem(info_ref[2] + held - phase, held) * span, span)
                cot_ref[pl.ds(start, span), :] = cot_refs[phase][...]
            cot_turned_ref[...] = cot_ref[...].T
            turned_ref[...] = normed_ref[...].T
            relative_rows(info_ref[0], count, turned_ref, normed_turned_ref)

    normed, cot = normed_ref[...], cot_ref[...]
    gate = dot(normed, wg_ref[...])
    up_value = dot(normed, wu_ref[...])
    grad_hidden = dot_nt(cot, wd_ref[...])
    square = gate * gate
    bend = jnp.tanh(gate * (SLOPE + (SLOPE * CUBE) * square))
    middle = 0.5 + 0.5 * bend
    gelu = gate * middle
    slope = middle * (1.0 + (1.0 - bend) * (gate * (SLOPE + (3.0 * SLOPE * CUBE) * square)))
    hidden = (gelu * up_value).astype(jnp.bfloat16)
    grad_gate = (grad_hidden * up_value * slope).astype(jnp.bfloat16)
    grad_up = (grad_hidden * gelu).astype(jnp.bfloat16)
    rb, cb = keep_ref.shape[-2:]
    chips = count // 2
    half_rows = chips * rb
    turned = normed_turned_ref[...]
    for kind, grad in enumerate((grad_gate, grad_up)):
        part = dot(turned, grad).astype(jnp.bfloat16)
        for e in range(2):
            columns = part[:, e * cb : (e + 1) * cb]
            tiles = slice((2 * kind + e) * chips, (2 * kind + e + 1) * chips)
            keep_ref[0, tiles] = columns[:half_rows].reshape(chips, rb, cb)
            send_ref[0, tiles] = columns[half_rows:].reshape(chips, rb, cb)
    part = dot(cot_turned_ref[...], hidden)
    first, second = part[:, :cb], part[:, cb:]
    mine = core == 0
    keep = jnp.where(mine, first, second).astype(jnp.bfloat16)
    send = jnp.where(mine, second, first).astype(jnp.bfloat16)
    keep_ref[0, 4 * chips :] = keep.reshape(count, rb, cb)
    send_ref[0, 4 * chips :] = send.reshape(count, rb, cb)
    result = dot(hidden, wd_ref[...])
    back = dot_nt(grad_gate, wg_ref[...]) + dot_nt(grad_up, wu_ref[...])

    @pl.when(step == 0)
    def _():
        acc_ref[...] = resid_ref[...] + result
        grad_ref[...] = back if grad_in_ref is None else grad_in_ref[...] + back

    @pl.when(step > 0)
    def _():
        acc_ref[...] += result
        grad_ref[...] += back

    if half == 1:

        @pl.when(step == pl.num_programs(0) - 1)
        def _():
            span = out_refs[0].shape[0]
            for phase in range(held):
                start = pl.multiple_of(lax.rem(info_ref[2] + held - phase, held) * span, span)
                out_refs[phase][...] = acc_ref[pl.ds(start, span), :].astype(jnp.bfloat16)


def feed_forward(half, info, normed, ins, wg, wu, wd, held, count):
    tokens, features = normed.shape
    width = wg.shape[1]
    chips = count // 2
    steps = chips // 2
    rb, cb = features // count, width // count
    whole = lambda shape: pl.BlockSpec(shape, lambda j, info: (0,) * len(shape))
    low = jnp.bfloat16
    slab = (4 * chips + count, rb, cb)
    tiles = jax.ShapeDtypeStruct((steps,) + slab, low)
    tile_spec = pl.BlockSpec((1,) + slab, lambda j, info: (j, 0, 0, 0))
    natural, turned = (tokens, features), (features, tokens)
    full = jax.ShapeDtypeStruct(natural, jnp.float32)
    shapes = [full, tiles, tiles]
    specs = [whole(natural), tile_spec, tile_spec]
    if half == 0:
        shapes, specs = [full] + shapes, [whole(natural)] + specs
    else:
        span = (tokens // held, features)
        shapes = [jax.ShapeDtypeStruct(span, low)] * held + shapes
        specs = [whole(span)] * held + specs
    scratch = [pltpu.VMEM(natural, jnp.float32)]
    if half == 0:
        shapes += [
            jax.ShapeDtypeStruct(natural, low),
            jax.ShapeDtypeStruct(turned, low),
            jax.ShapeDtypeStruct(turned, low),
        ]
        specs += [whole(natural), whole(turned), whole(turned)]
        scratch = [pltpu.VMEM(turned, low)]
    return pl.pallas_call(
        functools.partial(feed_kernel, held, count, half),
        grid_spec=pltpu.PrefetchScalarGridSpec(
            num_scalar_prefetch=1,
            grid=(steps,),
            in_specs=[
                whole(normed.shape),
                *[whole(x.shape) for x in ins],
                pl.BlockSpec((features, 2 * cb), lambda j, info: (0, j + half * steps)),
                pl.BlockSpec((features, 2 * cb), lambda j, info: (0, j + half * steps)),
                pl.BlockSpec((2 * cb, features), lambda j, info: (j + half * steps, 0)),
            ],
            out_specs=specs,
            scratch_shapes=scratch,
        ),
        out_shape=shapes,
        compiler_params=params(28),
        cost_estimate=cost(11),
        name=f"feed_forward_{half}",
    )(info, normed, *ins, wg, wu, wd)


def between_kernel(
    count,
    info_ref,
    grad_ref,
    resid_ref,
    gain_ref,
    cot_ref,
    att_ref,
    wm_ref,
    *refs,
):
    (
        out_hbm_ref,
        att_grad_ref,
        keep_hbm_ref,
        send_ref,
        gain_grad_ref,
        turned_ref,
        low_ref,
        out_ref,
        keep_ref,
        sems,
    ) = refs[-10:]
    features = resid_ref.shape[1]
    resid = resid_ref[...]
    root = lax.rsqrt(jnp.sum(resid * resid, axis=1, keepdims=True) / features + EPS)
    grad = grad_ref[...]
    unit = resid * root
    gain_grad_ref[...] = jnp.sum(grad * unit, axis=0, keepdims=True)
    pulled = grad * row_of(gain_ref)
    mean = jnp.sum(unit * pulled, axis=1, keepdims=True) / features
    result = cot_ref[...].astype(jnp.float32) + root * (pulled - unit * mean)
    out_ref[...] = result
    copies = [
        pltpu.make_async_copy(out_ref, out_hbm_ref, sems.at[0]),
        pltpu.make_async_copy(keep_ref, keep_hbm_ref, sems.at[1]),
    ]
    copies[0].start()
    mixed = result.astype(jnp.bfloat16)
    low_ref[...] = att_ref[...].astype(jnp.bfloat16)
    relative_rows(info_ref[0], count, low_ref, turned_ref)
    part = dot(turned_ref[...], mixed).astype(jnp.bfloat16)
    half = features // 2
    keep_ref[...] = part[:half].reshape(keep_ref.shape)
    copies[1].start()
    send_ref[...] = part[half:].reshape(send_ref.shape)
    att_grad_ref[...] = dot_nt(mixed, wm_ref[...]).astype(jnp.bfloat16)
    for copy in copies:
        copy.wait()


def between(info, grad, resid, gain, cot, att, wm, count, after, carry):
    tokens, features = grad.shape
    rb = features // count
    low = jnp.bfloat16
    piece = jax.ShapeDtypeStruct((count // 2, rb, features), low)
    ins = [info, grad, resid, gain, cot, att, wm]
    return launch(
        "between",
        functools.partial(between_kernel, count),
        ins,
        [SMEM] + [VMEM] * 6,
        [
            pltpu.HBM((tokens, features), jnp.float32),
            jax.ShapeDtypeStruct((tokens, features), low),
            pltpu.HBM(piece.shape, low),
            piece,
            jax.ShapeDtypeStruct((1, features), jnp.float32),
        ],
        [HBM, VMEM, HBM, VMEM, VMEM],
        16,
        [
            pltpu.VMEM((features, tokens), low),
            pltpu.VMEM((features, tokens), low),
            pltpu.VMEM((tokens, features), jnp.float32),
            pltpu.VMEM(piece.shape, low),
            pltpu.SemaphoreType.DMA((2,)),
        ],
        after=after,
        carry=carry,
        microseconds=3,
    )


def project_q_kernel(
    count,
    info_ref,
    dq_ref,
    normed_ref,
    wq_ref,
    other_ref,
    keep_ref,
    send_ref,
    back_ref,
    turned_ref,
    plain_ref,
):
    plain_ref[...] = normed_ref[...].T
    relative_rows(info_ref[0], count, plain_ref, turned_ref)
    dq = dq_ref[...]
    part = dot(turned_ref[...], dq).astype(jnp.bfloat16)
    half = part.shape[0] // 2
    keep_ref[...] = part[:half].reshape(keep_ref.shape)
    send_ref[0] = part[half:].reshape(send_ref.shape[1:])
    send_ref[1] = other_ref[...]
    back_ref[...] = dot_nt(dq, wq_ref[...])


def project_q(info, dq, normed, wq, other, count, after, carry):
    tokens, features = dq.shape
    low = jnp.bfloat16
    piece = jax.ShapeDtypeStruct((count // 2, features // count, features), low)
    return launch(
        "project_q",
        functools.partial(project_q_kernel, count),
        [info, dq, normed, wq, other],
        [SMEM] + [VMEM] * 4,
        [
            piece,
            jax.ShapeDtypeStruct((2,) + piece.shape, low),
            jax.ShapeDtypeStruct((tokens, features), jnp.float32),
            jax.ShapeDtypeStruct((features, tokens), low),
        ],
        [VMEM] * 4,
        14,
        [pltpu.VMEM((features, tokens), low)],
        after=after,
        carry=carry,
    )


def project_kv_kernel(
    mine_ref,
    got_ref,
    turned_ref,
    back_ref,
    stream_ref,
    grad_ref,
    gain_ref,
    wk_ref,
    wv_ref,
    keep_ref,
    send_ref,
    out_ref,
    gain_grad_ref,
):
    features = stream_ref.shape[1]
    half = features // 2
    total = back_ref[...]
    for i, w_ref in enumerate((wk_ref, wv_ref)):
        grad = mine_ref[i] + got_ref[i]
        part = dot(turned_ref[...], grad).astype(jnp.bfloat16)
        keep_ref[i] = part[:half].reshape(keep_ref.shape[1:])
        send_ref[i] = part[half:].reshape(send_ref.shape[1:])
        total = total + dot_nt(grad, w_ref[...])
    stream = stream_ref[...]
    root = lax.rsqrt(jnp.sum(stream * stream, axis=1, keepdims=True) / features + EPS)
    unit = stream * root
    gain_grad_ref[...] = jnp.sum(total * unit, axis=0, keepdims=True)
    pulled = total * row_of(gain_ref)
    mean = jnp.sum(unit * pulled, axis=1, keepdims=True) / features
    out_ref[...] = grad_ref[...] + root * (pulled - unit * mean)


def project_kv(mine, got, turned, back, stream, grad, gain, wk, wv, count, after):
    tokens, features = stream.shape
    piece = jax.ShapeDtypeStruct((2, count // 2, features // count, features), jnp.bfloat16)
    outs, _ = launch(
        "project_kv",
        project_kv_kernel,
        [mine, got, turned, back, stream, grad, gain, wk, wv],
        [VMEM] * 9,
        [piece] * 2
        + [
            jax.ShapeDtypeStruct((tokens, features), jnp.float32),
            jax.ShapeDtypeStruct((1, features), jnp.float32),
        ],
        [VMEM] * 4,
        18,
        after=after,
    )
    return outs


def pick_of(pairs, info_ref):
    def tile(pair, at):
        if callable(at):
            at = at(info_ref)
        first, second = at if isinstance(at, tuple) else (at, at)
        return pairs[pair][0][first] + pairs[pair][1][second]

    def value(pick):
        if len(pick) == 2:
            return tile(*pick)
        return jnp.where(info_ref[7] == 0, tile(*pick[:2]), tile(*pick[2:]))

    return value


def tiles_of(pairs):
    return [tuple(x.reshape((-1,) + x.shape[-2:]) for x in pair) for pair in pairs]


def fold(name, info, pairs, picks, after=(), carry=()):
    pairs = tiles_of(pairs)
    shape = pairs[0][0].shape[1:]

    def kernel(info_ref, *refs):
        ins, outs = refs[: 2 * len(pairs)], refs[2 * len(pairs) :]
        value = pick_of([ins[2 * i : 2 * i + 2] for i in range(len(pairs))], info_ref)
        for out_ref, chosen in zip(outs, picks):
            for slot, pick in enumerate(chosen):
                out_ref[slot] = value(pick)

    return launch(
        name,
        kernel,
        [info, *sum(pairs, ())],
        [SMEM] + [VMEM] * (2 * len(pairs)),
        [jax.ShapeDtypeStruct((len(chosen),) + shape, jnp.bfloat16) for chosen in picks],
        [VMEM] * len(picks),
        16,
        after=after,
        carry=carry,
    )


def lane_tiles(width):
    whole = width // LANES
    rest = width - whole * LANES
    return whole, rest, LANES // rest if rest else 1


def tile_count(pieces, width):
    whole, rest, each = lane_tiles(width)
    return pieces * whole + (-(-pieces // each) if rest else 0)


def pack_lanes(pieces):
    width = pieces[0].shape[1]
    whole, rest, each = lane_tiles(width)
    tiles = [piece[:, i * LANES : (i + 1) * LANES] for piece in pieces for i in range(whole)]
    if rest:
        ends = [piece[:, whole * LANES :] for piece in pieces]
        for i in range(0, len(ends), each):
            group = ends[i : i + each]
            spare = LANES - rest * len(group)
            if spare:
                group = group + [jnp.zeros((group[0].shape[0], spare), group[0].dtype)]
            tiles.append(jnp.concatenate(group, axis=1))
    return tiles


def unpack_lanes(tiles, pieces, width):
    whole, rest, each = lane_tiles(width)
    result = []
    for piece in range(pieces):
        parts = [tiles[piece * whole + i] for i in range(whole)]
        if rest:
            tile = tiles[pieces * whole + piece // each]
            start = piece % each * rest
            parts.append(tile[:, start : start + rest])
        result.append(jnp.concatenate(parts, axis=1) if len(parts) > 1 else parts[0])
    return result


def fold_seq(name, info, pairs, picks, seqs, slots, groups, width=None, after=(), carry=()):
    pairs = tiles_of(pairs)
    tall, wide = pairs[0][0].shape[1:]
    shape = (tall, LANES if width else wide)

    def kernel(info_ref, *refs):
        ins, outs, scratch_ref = refs[: 2 * len(pairs)], refs[2 * len(pairs) : -1], refs[-1]
        value = pick_of([ins[2 * i : 2 * i + 2] for i in range(len(pairs))], info_ref)
        here = info_ref[8]
        if width is None:
            for pick, block, slot in picks:
                scratch_ref[block ^ here, slot] = value(pick)
        else:
            totals = [value(pick) for pick, _, _ in sorted(picks, key=lambda x: x[2])]
            for s in range(seqs):
                pieces = [total[:, s * width : (s + 1) * width] for total in totals]
                for slot, tile in enumerate(pack_lanes(pieces)):
                    scratch_ref[s ^ here, slot] = tile
        for out_ref, group in zip(outs, groups):
            for i, d in enumerate(group):
                out_ref[i * slots : (i + 1) * slots] = scratch_ref[d]

    return launch(
        name,
        kernel,
        [info, *sum(pairs, ())],
        [SMEM] + [VMEM] * (2 * len(pairs)),
        [jax.ShapeDtypeStruct((len(group) * slots,) + shape, jnp.bfloat16) for group in groups],
        [VMEM] * len(groups),
        16,
        [pltpu.VMEM((seqs, slots) + shape, jnp.bfloat16)],
        after=after,
        carry=carry,
    )


def summed(refs, at):
    terms = [ref[at].astype(jnp.float32) for ref in refs]
    while len(terms) > 1:
        terms = [terms[i] + terms[i + 1] for i in range(0, len(terms), 2)]
    return terms[0]


def feed_end_kernel(seqs, *refs):
    ins, (gate_ref, up_ref, down_ref) = refs[:seqs], refs[seqs:]
    slots, rb, cb = ins[0].shape
    each = slots // 3
    for q in range(each):
        gate_ref[:, q * cb : (q + 1) * cb] = summed(ins, q)
        up_ref[:, q * cb : (q + 1) * cb] = summed(ins, each + q)
    for q in range(each):
        down_ref[q * rb : (q + 1) * rb] = summed(ins, 2 * each + q)


def feed_end(ins, after):
    slots, rb, cb = ins[0].shape
    each = slots // 3
    wide = pltpu.HBM((rb, each * cb), jnp.float32)
    return pl.pallas_call(
        ordered(functools.partial(feed_end_kernel, len(ins)), len(ins), after),
        out_shape=[wide, wide, pltpu.HBM((each * rb, cb), jnp.float32)],
        in_specs=[VMEM] * len(ins) + [ANY] * len(after),
        out_specs=[AUTO] * 3,
        compiler_params=params(8),
        cost_estimate=cost(1),
        name="feed_end",
    )(*ins, *after)


def join_kernel(info_ref, *refs):
    held = len(refs) - 1
    for phase in range(held):
        refs[held][lax.rem(info_ref[8] + phase, held)] = refs[phase][...]


def join(info, parts, after):
    shape = (len(parts),) + parts[0].shape
    outs, _ = launch(
        "join",
        join_kernel,
        [info, *parts],
        [SMEM] + [VMEM] * len(parts),
        [pltpu.HBM(shape, parts[0].dtype)],
        [AUTO],
        8,
        after=after,
    )
    return outs[0]


def mix_end_kernel(width, seqs, *refs):
    outs = refs[seqs:]
    tiles = [summed(refs[:seqs], slot) for slot in range(refs[0].shape[0])]
    for out_ref, value in zip(outs, unpack_lanes(tiles, len(outs), width)):
        out_ref[...] = value


def mix_end(ins, pieces, width, after):
    outs, _ = launch(
        "mix_end",
        functools.partial(mix_end_kernel, width, len(ins)),
        ins,
        [VMEM] * len(ins),
        [pltpu.HBM((ins[0].shape[1], width), jnp.float32)] * pieces,
        [AUTO] * pieces,
        8,
        after=after,
    )
    return outs


def sum_kernel(count, *refs):
    refs[count][...] = summed(refs[:count], slice(None)).astype(jnp.bfloat16)


def sum_of(name, terms, after):
    return pl.pallas_call(
        ordered(functools.partial(sum_kernel, len(terms)), len(terms), after),
        out_shape=jax.ShapeDtypeStruct(terms[0].shape, jnp.bfloat16),
        in_specs=[VMEM] * len(terms) + [ANY] * len(after),
        out_specs=VMEM,
        compiler_params=params(8),
        cost_estimate=cost(1),
        name=name,
    )(*terms, *after)


def unpack_kernel(vocab, chips, info_ref, *refs):
    shares = refs[: 2 * chips]
    embed_ref, filter_ref, score_ref, first_ref, second_ref, bias_ref, whole_ref = refs[2 * chips :]
    share = shares[0].shape[1]
    me = info_ref[0]
    for place in range(chips):
        for odd in range(2):
            start = pl.multiple_of((me ^ (2 * place + odd)) * share, 16)
            whole_ref[pl.ds(start, share), :] = shares[odd * chips + place][0].astype(jnp.float32)
    embed_ref[...] = whole_ref[:vocab]
    filter_ref[...] = whole_ref[vocab : vocab + 4]
    for i, ref in enumerate((score_ref, first_ref, second_ref)):
        ref[...] = whole_ref[vocab + 4 + i, :]
    heads, buckets = bias_ref.shape
    bias_ref[...] = whole_ref[vocab + 7 : vocab + 7 + heads, :buckets]


def unpack(info, mine, others, vocab, buckets, heads, after):
    chips = len(mine)
    _, share, features = mine[0].shape
    full = lambda *shape: pltpu.HBM(shape, jnp.float32)
    return pl.pallas_call(
        ordered(functools.partial(unpack_kernel, vocab, chips), 1 + 2 * chips, after),
        out_shape=[
            full(vocab, features),
            full(4, features),
            full(features),
            full(features),
            full(features),
            full(heads, buckets),
        ],
        in_specs=[SMEM] + [VMEM] * (2 * chips) + [ANY] * len(after),
        out_specs=[AUTO] * 6,
        scratch_shapes=[pltpu.VMEM((2 * chips * share, features), jnp.float32)],
        compiler_params=params(8),
        cost_estimate=cost(1),
        name="unpack",
    )(info, *mine, *others, *after)


AXES = ("batch", "seq")


def across_cores(x):
    count = lax.axis_size("batch")
    return lax.ppermute(x, "batch", [(i, i ^ 1) for i in range(count)])


def across_chips(x, chip):
    count = lax.axis_size("batch")
    return lax.ppermute(x, "batch", [(i, i ^ (2 * chip)) for i in range(count)])


def across_seq(x, d):
    count = lax.axis_size("seq")
    return lax.ppermute(x, "seq", [(i, i ^ d) for i in range(count)])


class Halving:
    def __init__(self, pairs, where):
        self.pairs, self.where = pairs, where

    def split(self, chosen, bit):
        keys = [key for key in self.where if chosen(key)]
        keep = [key for key in keys if not key[-1] & (1 << bit)]
        send = [key[:-1] + (key[-1] | (1 << bit),) for key in keep]
        return keep, send

    def picks(self, keys):
        return [self.where[key] for key in keys]


def exchange(name, info, state, plans, after=(), carry=(), held_back=False):
    lists, kept = [], []
    for chosen, bit in plans:
        keep, send = state.split(chosen, bit)
        kept.append(keep)
        lists += [state.picks(keep), state.picks(send)]
    outs, carried = fold(name, info, state.pairs, lists, after, carry)

    def start(sends):
        pairs, where = [], {}
        for place, ((_, bit), keep) in enumerate(zip(plans, kept)):
            pairs.append((outs[2 * place], across_chips(sends[place], 1 << bit)))
            where.update({key: (place, slot) for slot, key in enumerate(keep)})
        return Halving(pairs, where)

    return start if held_back else start(outs[1::2]), outs, carried


class Plan:
    def __init__(self, held):
        self.count = lax.axis_size("batch")
        self.seqs = lax.axis_size("seq")
        self.held = held
        self.group = self.seqs // (2 * held)
        me = lax.axis_index("batch")
        place = lax.axis_index("seq")
        self.me, self.place = me, place
        self.core = me % 2
        self.row = place // self.group
        self.part = 2 * (place % self.group) + self.core
        self.parts = 2 * self.group
        self.perms = []
        for phase in range(held):
            perm = []
            for b in range(self.count):
                for s in range(self.seqs):
                    row = held * (b % 2) + (s + phase) % held
                    part = s // held
                    target = (b - b % 2 + part % 2, self.group * row + part // 2)
                    perm.append((b * self.seqs + s, target[0] * self.seqs + target[1]))
            self.perms.append(perm)

    def blocks_of(self, x):
        return [
            lax.dynamic_index_in_dim(x, (self.place + phase) % self.held, 0, keepdims=False)
            for phase in range(self.held)
        ]

    def parts_of(self, x):
        return [lax.ppermute(x, AXES, perm) for x, perm in zip(self.blocks_of(x), self.perms)]

    def bytes_of(self, x, more):
        held = self.held
        width = x.shape[1]
        main = self.parts_of(jnp.concatenate([x, more], axis=1))
        more = main[0][width:]
        main = [part[:width] for part in main]
        ends = jnp.concatenate([x[:, :4], x[:, -4:]], axis=1)
        sides = []
        for phase in range(held):
            perm = []
            for b in range(self.count):
                for s in range(self.seqs):
                    row = held * (b % 2) + (s + phase) % held
                    part = s // held + {0: -1, held - 1: 1}.get(s % held, self.parts)
                    if 0 <= part < self.parts:
                        target = (b - b % 2 + part % 2, self.group * row + part // 2)
                        perm.append((b * self.seqs + s, target[0] * self.seqs + target[1]))
            send = lax.dynamic_index_in_dim(ends, (self.place + phase) % held, 0, keepdims=False)
            sides.append(lax.ppermute(send, AXES, perm))
        low = lax.dynamic_index_in_dim(
            jnp.stack(sides), (self.row + 1) % held, 0, keepdims=False
        )[4:]
        high = lax.dynamic_index_in_dim(jnp.stack(sides), self.row % held, 0, keepdims=False)[:4]
        low = jnp.where(self.part > 0, low, -1)
        high = jnp.where(self.part < self.parts - 1, high, -1)
        order = (self.row - jnp.arange(held)) % held
        middle = jnp.take(jnp.stack(main), order, axis=0).reshape(-1)
        return jnp.concatenate([low, middle, high]).reshape(-1, 4), more

    def gather(self, x):
        other = across_cores(x)
        pair = jnp.stack([jnp.where(self.core == 0, x, other), jnp.where(self.core == 0, other, x)])
        if self.group > 1:
            groups = [
                list(range(first, first + self.group))
                for first in range(0, self.seqs, self.group)
            ]
            pair = lax.all_gather(pair, "seq", axis_index_groups=groups)
        return pair.reshape((-1,) + x.shape[1:])

    def scatter(self, x):
        if self.group > 1:
            groups = [
                list(range(first, first + self.group))
                for first in range(0, self.seqs, self.group)
            ]
            x = lax.psum_scatter(
                x, "seq", scatter_dimension=0, axis_index_groups=groups, tiled=True
            )
        pair = x.reshape((2, -1) + x.shape[1:])
        got = across_cores(lax.dynamic_index_in_dim(pair, 1 - self.core, 0, keepdims=False))
        mine = lax.dynamic_index_in_dim(pair, self.core, 0, keepdims=False)
        return mine.astype(jnp.float32) + got.astype(jnp.float32)


def shards(
    byte_values,
    segments,
    byte_mask,
    embedding,
    filter_weight,
    score_weight,
    first_gain,
    query_weight,
    key_weight,
    value_weight,
    merge_weight,
    position_bias,
    second_gain,
    gate_weight,
    up_weight,
    down_weight,
    cotangent,
):
    count = lax.axis_size("batch")
    seqs = lax.axis_size("seq")
    held, width = byte_values.shape
    row_len = segments.shape[1]
    vocab, features = embedding.shape
    hidden_size = gate_weight.shape[1]
    heads = position_bias.shape[1]
    bucket_count = position_bias.shape[0]
    total = row_len // 2
    plan = Plan(held)
    tokens = total // plan.parts
    chips = count // 2
    levels = chips.bit_length() - 1
    blocks = tokens // BLOCK
    other_part = plan.part ^ 1

    bases = [plan.part * blocks, other_part * blocks] if plan.group == 1 else [0, 0]
    info = jnp.stack(
        [
            jnp.asarray(value, jnp.int32)
            for value in (
                plan.me,
                plan.core,
                plan.row % held,
                plan.part * blocks,
                plan.part * 2 * tokens,
                bases[0],
                bases[1],
                plan.me // chips,
                plan.place,
            )
        ]
    )
    cuts = jnp.sum((segments[:, None, :] < jnp.arange(1, 4)[:, None]).astype(jnp.int32), axis=2)
    cuts = (cuts + 1) // 2
    ids, cuts = plan.bytes_of(jnp.where(byte_mask > 0, byte_values, -1), cuts)
    groups = tokens // 2
    ids = jnp.pad(ids, ((MAIN - 1, MAIN - 1), (0, 0)), constant_values=-1)
    embedding, filter_weight, score_weight = map(hbm, (embedding, filter_weight, score_weight))
    first_gain, second_gain = hbm(first_gain), hbm(second_gain)
    query_weight, key_weight, value_weight = map(hbm, (query_weight, key_weight, value_weight))
    merge_weight = hbm(merge_weight)
    head_size = features // heads
    words = -(-(vocab + 7 + heads) // (16 * count)) * (16 * count)
    stream, normed, q, kv = mixer_forward(
        info,
        ids,
        embedding,
        filter_weight,
        score_weight,
        first_gain,
        query_weight,
        key_weight,
        value_weight,
        tokens,
        row_len,
        [],
    )
    normed, stream = hbm(normed), hbm(stream)
    cot_blocks = plan.blocks_of(cotangent)
    cots = [lax.ppermute(cot_blocks[0], AXES, plan.perms[0])]
    (bias,), (kv,) = bias_tiles(position_bias.T, cots, [kv])
    bias = hbm(bias)
    ends = (stream, merge_weight, second_gain)
    if plan.group == 1:
        kvs = [kv, across_cores(kv)]
        begun, later = attention_forward(
            "attention_own", head_size, info, q, kvs[0], bias, cuts, carry=cot_blocks[1:]
        )
        (att, lse, resid, normed_two), _ = attention_forward(
            "attention_other", head_size, info, q, kvs[1], bias, cuts, begun, ends
        )
    else:
        kvs = [jnp.stack([plan.gather(kv[0]), plan.gather(kv[1])])]
        later = cot_blocks[1:]
        (att, lse, resid, normed_two), _ = attention_forward(
            "attention_all", head_size, info, q, kvs[0], bias, cuts, (), ends
        )
    cots += [lax.ppermute(x, AXES, perm) for x, perm in zip(later, plan.perms[1:])]

    weights = (gate_weight, up_weight, down_weight)
    acc, grad_two, *grads, cot, cot_turned, normed_turned = feed_forward(
        0, info, normed_two, [*cots, resid], *weights, held, count
    )
    halves = [grads]
    *results, grad_two, keep, send = feed_forward(
        1,
        info,
        normed_two,
        [acc, grad_two, cot, cot_turned, normed_turned],
        *weights,
        held,
        count,
    )
    halves.append([keep, send])
    early = count // 4

    def upwards(key):
        return key[0] == "down" or key[3] < early

    def downwards(key):
        return not upwards(key)

    states = []

    def start_half(half, after):
        keep, send = halves[half]
        pairs = [(keep, across_cores(send))]
        steps = chips // 2
        slab = 4 * chips + count
        where = {}
        for r in range(chips):
            for n in range(count):
                kind, block = n // chips, n % chips
                place = block // 2 * slab + (2 * kind + block % 2) * chips + r
                where["gu", half, 0, n, r] = (0, place)

        def down_at(r, n):
            return lambda info: (r ^ lax.rem(info[0] // 2, steps)) * slab + 4 * chips + n

        for r in range(steps):
            for n in range(count):
                where["down", half, 0, n, r] = (0, down_at(r, n))
        state = Halving(pairs, where)
        first = None
        for level in range(levels - 1):
            state, outs, _ = exchange(
                f"feed_{half}_{level}",
                info,
                state,
                [(upwards, level), (downwards, levels - 1 - level)],
                after if level == 0 else (),
            )
            first = first or outs
        states.append(state)
        return first

    back_perms = [[(b, a) for a, b in perm] for perm in plan.perms]
    out_parts = [lax.ppermute(x, AXES, perm) for x, perm in zip(results, back_perms)]
    first = start_half(0, [grad_two])
    (grad_resid, att_grad, m_keep, m_send, second_part), _ = between(
        info, grad_two, resid, second_gain, cot, att, merge_weight, count, [first[0]], []
    )
    first = start_half(1, [second_part])
    dq, dkvs, tiles = attention_backward(
        head_size, info, hbm(q), att_grad, [hbm(kvs[0]), *kvs[1:]], bias, cuts, lse, att, [first[0]]
    )

    where = {}
    for half, state in enumerate(states):
        for key, (pair, slot) in state.where.items():
            where[key] = (2 * half + pair, slot)
    top = 1 << (levels - 1)
    for key in [key for key in where if key[0] == "down"]:
        _, half, kind, n, r = key
        mine, other = where["down", 0, 0, n, 0], where["down", 1, 0, n, 0]
        if half == 0:
            where["one", 2, 0, n, 0] = mine + other
            where["one", 2, 0, n, top] = other + mine
    where = {key: value for key, value in where.items() if key[0] != "down"}
    state = Halving(states[0].pairs + states[1].pairs, where)
    crossing = [dkvs[1]] if plan.group == 1 else []
    state, lasts, crossing = exchange(
        "feed_last",
        info,
        state,
        [
            (lambda key: key[0] == "one" or key[3] < early, levels - 1),
            (lambda key: key[0] == "gu" and key[3] >= early, 0),
        ],
        [hbm(dq), out_parts[0]],
        crossing,
    )
    if plan.group == 1:
        mine, got = hbm(dkvs[0]), across_cores(crossing[0])
    else:
        mine = jnp.stack([plan.scatter(dkvs[0][i]).astype(jnp.bfloat16) for i in range(2)])
        got = jnp.zeros_like(mine)
    bias_part = bucket_sums(tiles, [lasts[0]])
    (q_keep, qm_send, back, turned), later = project_q(
        info, hbm(dq), normed, query_weight, m_send, count, [bias_part], []
    )
    qm_got = across_cores(qm_send)
    kv_keep, kv_send, grad_stream, first_part = project_kv(
        mine,
        got,
        turned,
        back,
        stream,
        hbm(grad_resid),
        first_gain,
        key_weight,
        value_weight,
        count,
        [],
    )

    each = count // seqs
    picks = []
    for key, pick in state.where.items():
        if key[0] == "one":
            picks.append((pick, key[3] // each, 2 * each + key[3] % each))
        else:
            kind, block = key[3] // chips, key[1] * chips + key[3] % chips
            picks.append((pick, block // each, kind * each + block % each))
    slots = 3 * each
    groups = [list(range(0, seqs, 2)), list(range(1, seqs, 2))]
    (z_keep, z_send), (kv_send,) = fold_seq(
        "feed_seq", info, state.pairs, picks, seqs, slots, groups, after=[first_part, *out_parts[1:]], carry=[kv_send]
    )
    kv_got = across_cores(kv_send)
    z_got = across_seq(z_send, 1)
    where = {}
    for r in range(chips):
        where["p", 0, r] = (0, r)
        where["p", 3, r] = (1, (r, chips + r))
        for kind in (1, 2):
            where["p", kind, r] = (2, (kind - 1) * chips + r)
    mixes = Halving([(q_keep, qm_got), (hbm(m_keep), qm_got), (kv_keep, kv_got)], where)

    def mix_step(mixes, level, after, carry=(), held_back=False):
        return exchange(
            f"mix_{level}",
            info,
            mixes,
            [
                (lambda key: key[1] in (1, 3), level),
                (lambda key: key[1] in (0, 2), levels - 1 - level),
            ],
            after,
            carry,
            held_back,
        )

    layer_output = join(info, out_parts, [z_keep])
    mixes, outs, _ = mix_step(mixes, 0, [hbm(layer_output)])
    e_keep, e_send = mixer_backward(
        info,
        ids,
        embedding,
        filter_weight,
        score_weight,
        grad_stream,
        first_part,
        second_part,
        bias_part,
        row_len,
        vocab,
        words,
        count,
        [z_keep, outs[0]],
    )

    def seq_step(name, z_keep, z_got, slots, step, after, carry):
        held_now = z_keep.shape[0] // slots
        lists = [
            [(0, d * slots + i) for d in range(first, held_now, 2) for i in range(slots)]
            for first in range(2)
        ]
        (z_keep, z_send), carried = fold(
            f"{name}_seq_{step}", info, [(z_keep, z_got)], lists, after, carry
        )
        return z_keep, across_seq(z_send, step), carried

    last, step, carry = e_keep, 2, [e_send]
    while step < seqs:
        z_keep, z_got, carry = seq_step("feed", z_keep, z_got, slots, step, [last], carry)
        last = z_keep
        step *= 2
    for level in range(1, levels):
        mixes, outs, _ = mix_step(mixes, level, [last], (), level == levels - 1)
        last = outs[0]
    e_got = across_cores(carry[0])
    small = Halving([(e_keep, e_got)], {("e", r): (0, r) for r in range(chips)})
    sends = outs[1::2]
    for level in range(levels):
        small, outs, sends = exchange(
            f"small_{level}",
            info,
            small,
            [(lambda key: True, level)],
            [last] if level == 0 else [],
            sends if level == 0 else [],
        )
        if level == 0:
            mixes = mixes(sends)
    (share,), _ = fold("small_chips", info, small.pairs, [small.picks([("e", 0)])])
    share_got = across_seq(share, 1)
    picks = [(pick, None, key[1]) for key, pick in mixes.where.items()]
    gate_grad, up_grad, down_grad = feed_end([z_keep, z_got], [share])
    share_width = features // seqs
    mix_sends, _ = fold_seq(
        "mix_seq",
        info,
        mixes.pairs,
        picks,
        seqs,
        tile_count(4, share_width),
        [[d] for d in range(seqs)],
        share_width,
        after=[hbm(gate_grad)],
    )
    mix_arrived = [mix_sends[0]] + [across_seq(mix_sends[d], d) for d in range(1, seqs)]
    distance = 1
    while distance < seqs:
        share = sum_of(f"small_seq_{distance}", [share, share_got], [mix_sends[0]])
        distance *= 2
        if distance < seqs:
            share_got = across_seq(share, distance)
    shares = [share] + [across_chips(share, r) for r in range(1, chips)]
    query_grad, key_grad, value_grad, merge_grad = mix_end(mix_arrived, 4, share_width, [share])
    embed, filters, score, first, second, bias_sum = unpack(
        info, shares, [across_cores(x) for x in shares], vocab, bucket_count, heads, [hbm(query_grad)]
    )
    return (
        layer_output,
        embed,
        filters,
        score,
        first,
        query_grad,
        key_grad,
        value_grad,
        merge_grad,
        bias_sum.T,
        second,
        gate_grad,
        up_grad,
        down_grad.T,
    )


def solution(mesh):
    in_specs = (
        P("batch", "seq"),
        P("batch", None),
        P("batch", "seq"),
        P(),
        P(),
        P(),
        P(),
        P(),
        P(),
        P(),
        P(),
        P(),
        P(),
        P(),
        P(),
        P(),
        P("batch", "seq", None),
    )
    out_specs = (
        P("batch", "seq", None),
        P(),
        P(),
        P(),
        P(),
        P("batch", "seq"),
        P("batch", "seq"),
        P("batch", "seq"),
        P("batch", "seq"),
        P(),
        P(),
        P("batch", "seq"),
        P("batch", "seq"),
        P("batch", "seq"),
    )
    return jax.shard_map(shards, mesh=mesh, in_specs=in_specs, out_specs=out_specs, check_vma=False)
```
